32 devices in a mesh: dom: 8 (over y, x, core), slab: 4 (over z).
Axes of the slice: x: 2, y: 2, z: 4, core: 2. Of those that a mesh axis runs over, the one named last changes fastest.
Arguments:
- particles: bfloat16 [4096, 320, 256], P('dom', 'slab'), may hold values from -8 to 8
- blocks: int32 [4096, 2], P('dom'), may hold values from 0 to 3, as said below
- references: bfloat16 [512, 320, 256], P(None, 'slab'), may hold values from -1 to 1
- inv_noise: float32 [320], P('slab'), may hold values from 0.5 to 2
- destination: int32 [320, 512], replicated, may hold values from 0 to 31, as said below
- row_index: int32 [320, 512], replicated, may hold values from 0 to 254
- fraction: float32 [320, 512], replicated, may hold values from 0 to 1
Outputs:
- volume_data: float32 [8192, 256], P(('dom', 'slab'))
- next_slab: bfloat16 [2048, 1024], P(None, 'slab')
The draws below stay inside these ranges and needn't reach their ends.
Inputs may be any that keep to these rules, and one draw needn't show every extreme that they name: Each particle names 2 different orientation blocks. destination is a device index in the order of the joined axes (dom, slab), dom major. Among the pieces whose group belongs to one index of slab and whose orientation belongs to one index of dom, no destination is named more than 256 times, and some destination exactly 256 times.
All inputs are finite; a program needn't handle non-finite values.
Results may differ from the reference program's by a relative error of at most 0.013.
Values may be sent and summed in bfloat16 or wider, within the bound.
No kernel may reach another device: no remote copies, remote signals or barrier semaphores. Data moves between devices by JAX's collectives and lax.ppermute only.
A program may use at most 256 MiB of HBM per device.

```python
import math
import jax
import jax.numpy as jnp
from jax import lax

COEF = 128
G = 320
OB = 128
TOPB = 2
O = 512
P_DEV = 512
RD = 256
PARTS_SIZE = 4096
CAP = 256
N_DOM = 8
N_SLAB = 4
DEVICES = 32


def make_references(key):
    spread = 2.0 / math.sqrt(G * 2 * COEF)
    return spread * jnp.clip(jax.random.normal(key, (O, G, 2 * COEF), jnp.float32), -6.0, 6.0)


def make_blocks(key):
    number = O // OB
    scores = jax.random.randint(key, (PARTS_SIZE, number), 0, 1024) * number + jnp.arange(number, dtype=jnp.int32)[None, :]
    _, picked = lax.top_k(scores, TOPB)
    return picked.astype(jnp.int32)


def draw_references(key, part):
    return make_references(jax.random.fold_in(key, 7)).astype(jnp.bfloat16)


def draw_blocks(key, part):
    return make_blocks(jax.random.fold_in(key, 11))


def draw_particles(key, part):
    layout = (PARTS_SIZE, G, 2 * COEF)
    return jnp.clip(jax.random.normal(jax.random.fold_in(key, 3), layout, jnp.float32), -6.0, 6.0).astype(jnp.bfloat16)


def draw_destination(key, part):
    group_share = G // N_SLAB
    orient_share = O // N_DOM
    block_size = group_share * orient_share
    slot_count = DEVICES * CAP
    popular = (jax.random.randint(jax.random.fold_in(key, 21), (DEVICES,), 0, 4) == 0).astype(jnp.int32) * 4096

    def one_block(block_key):
        key_a, key_b, key_c = jax.random.split(block_key, 3)
        favored = jax.random.randint(key_a, (), 0, DEVICES)
        owners = jnp.arange(slot_count, dtype=jnp.int32) // CAP
        bonuses = popular[owners] + jnp.where(owners == favored, 16384, 0)
        scores = (bonuses + jax.random.randint(key_b, (slot_count,), 0, 4096)) * 65536 + jnp.arange(slot_count, dtype=jnp.int32)
        _, picked = lax.top_k(scores, block_size)
        shuffle = jax.random.permutation(key_c, block_size)
        return (picked // CAP)[shuffle].astype(jnp.int32)
    block_keys = jax.random.split(jax.random.fold_in(key, 23), DEVICES)
    table = jax.vmap(one_block)(block_keys)
    table = table.reshape(N_DOM, N_SLAB, orient_share, group_share).transpose(1, 3, 0, 2)
    return table.reshape(G, O)


def with_ends(values, own_key, smallest, largest):
    shape = values.shape
    index_at = [jax.random.randint(jax.random.fold_in(own_key, axis), (), 0, shape[axis]) for axis in range(len(shape))]
    values = values.at[tuple(index_at)].set(smallest)
    longest = shape.index(max(shape))
    index_at[longest] = (index_at[longest] + 1) % shape[longest]
    return values.at[tuple(index_at)].set(largest)


def levels(stream_key, shape, cuts, smallest, largest):
    loudness = 1.0
    for dim, parts in cuts:
        heights = jax.random.uniform(jax.random.fold_in(jax.random.fold_in(stream_key, 6), dim), (parts,), jnp.float32, smallest / len(cuts), largest / len(cuts))
        loudness = loudness * jnp.repeat(jnp.exp(heights), shape[dim] // parts).reshape((-1,) + (1,) * (len(shape) - 1 - dim))
    return loudness


def setup_inputs(seed: int = 0) -> dict:
    keys = jax.random.split(jax.random.key(seed), 8)
    return {
        "particles": draw_particles(jax.random.fold_in(keys[7], 71), 0),
        "blocks": draw_blocks(jax.random.fold_in(keys[7], 71), 0),
        "references": draw_references(jax.random.fold_in(keys[7], 71), 0),
        "inv_noise": jnp.clip(jnp.exp(math.log(2.0) - 1.3862944 * jax.random.uniform(keys[3], (G,), jnp.float32) ** levels(keys[3], (G,), ((0, 4),), -0.2, 0.2)), 0.5, 2.0),
        "destination": draw_destination(jax.random.fold_in(keys[7], 71), 0),
        "row_index": with_ends(jax.random.randint(keys[5], (G, O), 0, RD - 1), jax.random.fold_in(keys[5], 1), 0, (RD - 1) - 1).astype(jnp.int32),
        "fraction": jnp.clip(jax.random.uniform(keys[6], (G, O), jnp.float32, 0.0, 1.0), 0.0, 1.0),
    }


def reference(particles, blocks, references, inv_noise, destination, row_index, fraction):
    row_width = 2 * COEF
    weighted = (references.astype(jnp.float32) * inv_noise[None, :, None]).astype(jnp.bfloat16)
    weighted = weighted.reshape(O, G * row_width)
    block_of = jnp.arange(O, dtype=jnp.int32) // OB
    flat_rows = particles.reshape(N_DOM, P_DEV, G * row_width)
    owners = blocks.reshape(N_DOM, P_DEV, TOPB)

    def one_owner(running, packed):
        images, chosen = packed
        scores = jnp.dot(images, weighted.T, preferred_element_type=jnp.float32)
        allowed = jnp.any(chosen[:, :, None] == block_of[None, None, :], axis=1)
        masked = jnp.where(allowed, scores, -jnp.inf)
        highest = jnp.max(masked, axis=1, keepdims=True)
        weights = jnp.where(allowed, jnp.exp(masked - highest), 0.0)
        posterior = (weights / jnp.sum(weights, axis=1, keepdims=True)).astype(jnp.bfloat16)
        partial_value = jnp.dot(posterior.T, images, preferred_element_type=jnp.float32).astype(jnp.bfloat16)
        return running + partial_value.astype(jnp.float32), None

    slices, _ = lax.scan(one_owner, jnp.zeros((O, G * row_width), jnp.float32), (flat_rows, owners))
    pieces = slices.reshape(O, G, row_width)
    target = (destination * RD + row_index).T
    lower_part = (1.0 - fraction).T[:, :, None] * pieces
    upper_part = fraction.T[:, :, None] * pieces
    rows_total = RD * N_DOM * N_SLAB
    volume = jnp.zeros((rows_total + 1, row_width), jnp.float32)
    volume = volume.at[target].add(lower_part).at[target + 1].add(upper_part)[:rows_total]
    next_slab = volume.astype(jnp.bfloat16).reshape(N_DOM, N_SLAB, RD, row_width)
    next_slab = next_slab.transpose(0, 2, 1, 3).reshape(N_DOM * RD, N_SLAB * row_width)
    return volume, next_slab
```

```python
import functools

import jax
import jax.numpy as jnp
from jax import lax
from jax.experimental import pallas as pl
from jax.experimental.pallas import tpu as pltpu
from jax.sharding import PartitionSpec as P

OB = 128
RD = 256
MB = 2**20
F32 = jnp.float32
BF16 = jnp.bfloat16


def group_block(groups):
    return 16 if groups % 16 == 0 else 8


def score_kernel(me_ref, noise_ref, perm_ref, x_ref, r_ref, blk_ref, flat_ref, *rest):
    *out_refs, w_ref, acc_ref = rest
    step = pl.program_id(0)
    particles, gb, width = x_ref.shape
    orients = r_ref.shape[0]

    @pl.when(step == 0)
    def _():
        acc_ref[...] = jnp.zeros_like(acc_ref)

    perm = perm_ref[...]

    def regroup(src_ref, dst_ref, scaled):
        def body(i, carry):
            at = pl.multiple_of(i * 16, 16)
            tile = src_ref[pl.ds(at, 16)].reshape(16 * gb, width)
            moved = jnp.dot(perm, tile, preferred_element_type=F32)
            for g in range(gb):
                part = moved[g * 16 : (g + 1) * 16]
                if scaled:
                    part = part * noise_ref[step * gb + g]
                dst_ref[pl.ds(at, 16), g * width : (g + 1) * width] = part.astype(BF16)
            return carry

        lax.fori_loop(0, src_ref.shape[0] // 16, body, 0, unroll=2)

    regroup(r_ref, w_ref, True)
    regroup(x_ref, flat_ref, False)
    half = min(256, orients)

    def product(n, carry):
        at = pl.multiple_of(n * half, half)
        acc_ref[n] += lax.dot_general(
            flat_ref[...],
            w_ref[pl.ds(at, half), :],
            (((1,), (1,)), ((), ())),
            preferred_element_type=F32,
        )
        return carry

    lax.fori_loop(0, orients // half, product, 0)

    @pl.when(step == pl.num_programs(0) - 1)
    def _():
        me = me_ref[0]
        share = particles // len(out_refs)
        per = half // OB
        for k, out_ref in enumerate(out_refs):
            at = pl.multiple_of((me ^ k) * share, share)
            for j in range(2):
                wanted = blk_ref[pl.ds(at, share), j : j + 1]
                chosen = jnp.zeros((share, OB), F32)
                for b in range(orients // OB):
                    lane = (b % per) * OB
                    chosen = jnp.where(
                        wanted == b, acc_ref[b // per, pl.ds(at, share), lane : lane + OB], chosen
                    )
                out_ref[:, j * OB : (j + 1) * OB] = chosen


def score_call(me, inv_noise, particles, references, blocks, slab_size):
    count, groups, width = particles.shape
    orients = references.shape[0]
    gb = group_block(groups)
    side = 16 * gb
    row = jnp.arange(side, dtype=jnp.int32)[:, None]
    col = jnp.arange(side, dtype=jnp.int32)[None, :]
    perm = ((row // 16 == col % gb) & (row % 16 == col // gb)).astype(BF16)
    share = count // slab_size
    half = min(256, orients)
    smem = pl.BlockSpec(memory_space=pltpu.SMEM)
    return pl.pallas_call(
        score_kernel,
        grid=(groups // gb,),
        out_shape=[jax.ShapeDtypeStruct((count, groups * width), BF16)]
        + [jax.ShapeDtypeStruct((share, 2 * OB), F32)] * slab_size,
        in_specs=[
            smem,
            smem,
            pl.BlockSpec((side, side), lambda i: (0, 0)),
            pl.BlockSpec((count, gb, width), lambda i: (0, i, 0)),
            pl.BlockSpec((orients, gb, width), lambda i: (0, i, 0)),
            pl.BlockSpec((count, 2), lambda i: (0, 0)),
        ],
        out_specs=[pl.BlockSpec((count, gb * width), lambda i: (0, i))]
        + [pl.BlockSpec((share, 2 * OB), lambda i: (0, 0))] * slab_size,
        scratch_shapes=[
            pltpu.VMEM((orients, gb * width), BF16),
            pltpu.VMEM((orients // half, count, half), F32),
        ],
        compiler_params=pltpu.CompilerParams(vmem_limit_bytes=56 * MB),
        cost_estimate=pl.CostEstimate(
            flops=4 * count * orients * groups * width,
            bytes_accessed=6 * count * groups * width,
            transcendentals=0,
        ),
    )(me, inv_noise, perm, particles, references, blocks)


def softmax_kernel(*refs):
    *parts, out_ref = refs
    total = parts[0][...]
    for part in parts[1:]:
        total = total + part[...]
    highest = jnp.max(total, axis=1, keepdims=True)
    weights = jnp.exp(total - highest)
    out_ref[...] = (weights / jnp.sum(weights, axis=1, keepdims=True)).astype(BF16)


def softmax_call(parts):
    return pl.pallas_call(
        softmax_kernel, out_shape=jax.ShapeDtypeStruct(parts[0].shape, BF16)
    )(*parts)


def insert_kernel(me_ref, row_ref, x_ref, frac_ref, blk_ref, *rest, share_count, copies):
    post_refs = rest[:share_count]
    send_ref, keep_ref = rest[share_count : share_count + 2]
    post_t, spread_ref, quad_ref = rest[share_count + 2 : share_count + 5]
    volumes = rest[share_count + 5 :]
    step = pl.program_id(0)
    count = x_ref.shape[0]
    orients = post_t.shape[0]
    gb = frac_ref.shape[2]
    width = x_ref.shape[1] // gb
    share = count // share_count

    @pl.when(step == 0)
    def _():
        for volume in volumes:
            volume[...] = jnp.zeros_like(volume)
        me = me_ref[0]
        for k, post_ref in enumerate(post_refs):
            at = pl.multiple_of((me ^ k) * share, share)
            post = post_ref[...].astype(F32)
            first = blk_ref[pl.ds(at, share), 0:1]
            second = blk_ref[pl.ds(at, share), 1:2]
            for b in range(orients // OB):
                spread = jnp.where(
                    first == b, post[:, :OB], jnp.where(second == b, post[:, OB:], 0.0)
                )
                spread_ref[pl.ds(at, share), b * OB : (b + 1) * OB] = spread
        for b in range(orients // OB):
            post_t[b * OB : (b + 1) * OB] = spread_ref[:, b * OB : (b + 1) * OB].T.astype(BF16)

    lanes = lax.broadcasted_iota(jnp.int32, (1, gb), 1)

    def one_group(g, carry):
        piece = jnp.dot(
            post_t[...],
            x_ref[:, pl.ds(pl.multiple_of(g * width, width), width)],
            preferred_element_type=F32,
        )
        upper = jnp.sum(jnp.where(lanes == g, frac_ref[0], 0.0), axis=1, keepdims=True)
        lower = 1.0 - upper
        quad_ref[pl.ds(0, orients, 4), :] = piece[:, :OB] * lower
        quad_ref[pl.ds(1, orients, 4), :] = piece[:, OB:] * lower
        quad_ref[pl.ds(2, orients, 4), :] = piece[:, :OB] * upper
        quad_ref[pl.ds(3, orients, 4), :] = piece[:, OB:] * upper
        burst = 32

        def rows(i, c):
            for u in range(burst):
                at = row_ref[0, g, i * burst + u]
                src = quad_ref[pl.ds(pl.multiple_of(i * (4 * burst), 4 * burst) + 4 * u, 4), :]
                volume = volumes[u % copies]
                volume[pl.ds(at, 4), :] = volume[pl.ds(at, 4), :] + src
            return c

        lax.fori_loop(0, orients // burst, rows, 0)
        return carry

    lax.fori_loop(0, gb, one_group, 0)

    @pl.when(step == pl.num_programs(0) - 1)
    def _():
        half = keep_ref.shape[0]
        tile = min(512, half)
        for base, out_ref in ((half, send_ref), (0, keep_ref)):
            def finish(i, carry, base=base, out_ref=out_ref):
                at = pl.multiple_of(i * tile, tile)
                for lane in range(2):
                    total = volumes[0][pl.ds(2 * (base + at) + lane, tile, 2), :]
                    for volume in volumes[1:]:
                        total = total + volume[pl.ds(2 * (base + at) + lane, tile, 2), :]
                    out_ref[pl.ds(at, tile), lane * OB : (lane + 1) * OB] = total.astype(BF16)
                return carry

            lax.fori_loop(0, half // tile, finish, 0)


def insert_call(me, rows, flat, fraction, blocks, posts, devices):
    count = flat.shape[0]
    steps, gb, orients = rows.shape
    width = flat.shape[1] // (steps * gb)
    total = devices * RD
    copies = max(1, min(4, 32 * MB // (total * width * 4)))
    smem = pl.BlockSpec(memory_space=pltpu.SMEM)
    share = posts[0].shape[0]
    return pl.pallas_call(
        functools.partial(insert_kernel, share_count=len(posts), copies=copies),
        grid=(steps,),
        out_shape=[jax.ShapeDtypeStruct((total // 2, width), BF16)] * 2,
        in_specs=[
            smem,
            pl.BlockSpec((1, gb, orients), lambda i: (i, 0, 0), memory_space=pltpu.SMEM),
            pl.BlockSpec((count, gb * width), lambda i: (0, i)),
            pl.BlockSpec((1, orients, gb), lambda i: (i, 0, 0)),
            pl.BlockSpec((count, 2), lambda i: (0, 0)),
        ]
        + [pl.BlockSpec((share, 2 * OB), lambda i: (0, 0))] * len(posts),
        out_specs=[pl.BlockSpec((total // 2, width), lambda i: (0, 0))] * 2,
        scratch_shapes=[
            pltpu.VMEM((orients, count), BF16),
            pltpu.VMEM((count, orients), F32),
            pltpu.VMEM((4 * orients, OB), F32),
        ]
        + [pltpu.VMEM((2 * total, OB), F32)] * copies,
        compiler_params=pltpu.CompilerParams(vmem_limit_bytes=60 * MB),
        cost_estimate=pl.CostEstimate(
            flops=2 * count * orients * steps * gb * width,
            bytes_accessed=2 * count * steps * gb * width,
            transcendentals=0,
        ),
    )(me, rows, flat, fraction, blocks, *posts)


def flip(value, axis, bit):
    size = lax.axis_size(axis)
    return lax.ppermute(value, axis, [(i, i ^ bit) for i in range(size)])


def shards(particles, blocks, references, inv_noise, destination, row_index, fraction):
    groups, width = particles.shape[1:]
    orients = references.shape[0]
    dom_size = lax.axis_size("dom")
    slab_size = lax.axis_size("slab")
    devices = dom_size * slab_size
    dom_pos = lax.axis_index("dom")
    slab_pos = lax.axis_index("slab")
    slab_me = slab_pos.astype(jnp.int32).reshape(1)
    dom_bits = [1 << i for i in range((dom_size - 1).bit_length())]
    slab_bits = [1 << i for i in range((slab_size - 1).bit_length())]

    flat, *scores = score_call(slab_me, inv_noise, particles, references, blocks, slab_size)
    parts = [scores[0]] + [flip(scores[k], "slab", k) for k in range(1, slab_size)]
    post = softmax_call(parts)
    posts = [post] + [flip(post, "slab", k) for k in range(1, slab_size)]

    gb = group_block(groups)
    steps = groups // gb
    take = lambda table: lax.dynamic_slice_in_dim(table, slab_pos * groups, groups, 0)
    owner = take(destination)
    dom_off = (owner // slab_size) ^ dom_pos
    slab_off = (owner % slab_size) ^ slab_pos
    place = jnp.zeros_like(owner)
    for bit in dom_bits:
        place = place * 2 + jnp.where(dom_off & bit != 0, 1, 0)
    for bit in slab_bits:
        place = place * 2 + jnp.where(slab_off & bit != 0, 1, 0)
    rows = ((place * RD + take(row_index)) * 2).reshape(steps, gb, orients)
    mine = take(fraction).reshape(steps, gb, orients).transpose(0, 2, 1)
    send, keep = insert_call(slab_me, rows, flat, mine, blocks, posts, devices)

    def merge(kept, got):
        return kept.astype(F32) + got.astype(F32)

    total = merge(keep, flip(send, "dom", dom_bits[0]))
    rest = dom_bits[1:]
    total = total.reshape((2,) * len(rest) + (slab_size * RD, width))
    halves = []
    for part, order in ((0, rest), (1, rest[::-1])):
        value = total[..., part * OB : (part + 1) * OB]
        axes = list(rest)
        for bit in order:
            axis = axes.index(bit)
            axes.pop(axis)
            kept = lax.index_in_dim(value, 0, axis, keepdims=False)
            sent = lax.index_in_dim(value, 1, axis, keepdims=False)
            value = merge(kept, flip(sent.astype(BF16), "dom", bit))
        halves.append(value)
    value = jnp.concatenate(halves, axis=1)
    for bit in slab_bits:
        near, far = jnp.split(value, 2, axis=0)
        value = merge(near, flip(far.astype(BF16), "slab", bit))
    volume = value

    own = volume.astype(BF16)
    columns = []
    for part, order in ((0, rest), (1, rest[::-1])):
        value = own[:, part * OB : (part + 1) * OB]
        done = []
        for bit in order:
            got = flip(value, "dom", bit)
            axis = len([b for b in done if b > bit])
            done.append(bit)
            mine_low = dom_pos & bit == 0
            value = jnp.where(
                mine_low, jnp.stack([value, got], axis), jnp.stack([got, value], axis)
            )
        columns.append(value)
    value = jnp.concatenate(columns, axis=-1)
    got = flip(value, "dom", dom_bits[0])
    value = jnp.where(
        dom_pos & dom_bits[0] == 0,
        jnp.stack([value, got], len(rest)),
        jnp.stack([got, value], len(rest)),
    )
    return volume, value.reshape(dom_size * RD, width)


def solution(mesh):
    return jax.shard_map(
        shards,
        mesh=mesh,
        in_specs=(
            P("dom", "slab", None),
            P("dom", None),
            P(None, "slab", None),
            P("slab"),
            P(),
            P(),
            P(),
        ),
        out_specs=(P(("dom", "slab"), None), P(None, "slab")),
        check_vma=False,
    )
```

```python
import functools

import jax
import jax.numpy as jnp
from jax import lax
from jax.experimental import pallas as pl
from jax.experimental.pallas import tpu as pltpu
from jax.sharding import PartitionSpec as P

OB = 128
RD = 256
MB = 2**20
F32 = jnp.float32
BF16 = jnp.bfloat16


def group_block(groups):
    return 16 if groups % 16 == 0 else 8


def score_kernel(me_ref, noise_ref, perm_ref, x_ref, r_ref, blk_ref, flat_ref, *rest):
    *out_refs, w_ref, acc_ref = rest
    step = pl.program_id(0)
    particles, gb, width = x_ref.shape
    orients = r_ref.shape[0]

    @pl.when(step == 0)
    def _():
        acc_ref[...] = jnp.zeros_like(acc_ref)

    perm = perm_ref[...]

    def regroup(src_ref, dst_ref, scaled):
        def body(i, carry):
            at = pl.multiple_of(i * 16, 16)
            tile = src_ref[pl.ds(at, 16)].reshape(16 * gb, width)
            moved = jnp.dot(perm, tile, preferred_element_type=F32)
            for g in range(gb):
                part = moved[g * 16 : (g + 1) * 16]
                if scaled:
                    part = part * noise_ref[step * gb + g]
                dst_ref[pl.ds(at, 16), g * width : (g + 1) * width] = part.astype(BF16)
            return carry

        lax.fori_loop(0, src_ref.shape[0] // 16, body, 0, unroll=8)

    regroup(r_ref, w_ref, True)
    regroup(x_ref, flat_ref, False)
    half = min(256, orients)

    def product(n, carry):
        at = pl.multiple_of(n * half, half)
        acc_ref[n] += lax.dot_general(
            flat_ref[...],
            w_ref[pl.ds(at, half), :],
            (((1,), (1,)), ((), ())),
            preferred_element_type=F32,
        )
        return carry

    lax.fori_loop(0, orients // half, product, 0)

    @pl.when(step == pl.num_programs(0) - 1)
    def _():
        me = me_ref[0]
        share = particles // len(out_refs)
        per = half // OB
        for k, out_ref in enumerate(out_refs):
            at = pl.multiple_of((me ^ k) * share, share)
            for j in range(2):
                wanted = blk_ref[pl.ds(at, share), j : j + 1]
                chosen = jnp.zeros((share, OB), F32)
                for b in range(orients // OB):
                    lane = (b % per) * OB
                    chosen = jnp.where(
                        wanted == b, acc_ref[b // per, pl.ds(at, share), lane : lane + OB], chosen
                    )
                out_ref[:, j * OB : (j + 1) * OB] = chosen


def score_call(me, inv_noise, particles, references, blocks, slab_size):
    count, groups, width = particles.shape
    orients = references.shape[0]
    gb = group_block(groups)
    side = 16 * gb
    row = jnp.arange(side, dtype=jnp.int32)[:, None]
    col = jnp.arange(side, dtype=jnp.int32)[None, :]
    perm = ((row // 16 == col % gb) & (row % 16 == col // gb)).astype(BF16)
    share = count // slab_size
    half = min(256, orients)
    smem = pl.BlockSpec(memory_space=pltpu.SMEM)
    return pl.pallas_call(
        score_kernel,
        grid=(groups // gb,),
        out_shape=[jax.ShapeDtypeStruct((count, groups * width), BF16)]
        + [jax.ShapeDtypeStruct((share, 2 * OB), F32)] * slab_size,
        in_specs=[
            smem,
            smem,
            pl.BlockSpec((side, side), lambda i: (0, 0)),
            pl.BlockSpec((count, gb, width), lambda i: (0, i, 0)),
            pl.BlockSpec((orients, gb, width), lambda i: (0, i, 0)),
            pl.BlockSpec((count, 2), lambda i: (0, 0)),
        ],
        out_specs=[pl.BlockSpec((count, gb * width), lambda i: (0, i))]
        + [pl.BlockSpec((share, 2 * OB), lambda i: (0, 0))] * slab_size,
        scratch_shapes=[
            pltpu.VMEM((orients, gb * width), BF16),
            pltpu.VMEM((orients // half, count, half), F32),
        ],
        compiler_params=pltpu.CompilerParams(vmem_limit_bytes=56 * MB),
        cost_estimate=pl.CostEstimate(
            flops=4 * count * orients * groups * width,
            bytes_accessed=6 * count * groups * width,
            transcendentals=0,
        ),
    )(me, inv_noise, perm, particles, references, blocks)


def softmax_kernel(*refs):
    *parts, out_ref = refs
    total = parts[0][...]
    for part in parts[1:]:
        total = total + part[...]
    highest = jnp.max(total, axis=1, keepdims=True)
    weights = jnp.exp(total - highest)
    out_ref[...] = (weights / jnp.sum(weights, axis=1, keepdims=True)).astype(BF16)


def softmax_call(parts):
    return pl.pallas_call(
        softmax_kernel, out_shape=jax.ShapeDtypeStruct(parts[0].shape, BF16)
    )(*parts)


def plan_kernel(place_ref, pos_ref, addr_ref, item_ref, hot_ref, count_ref, *, owners):
    _, gb, orients = place_ref.shape
    lanes = addr_ref.shape[2]
    owner = lax.broadcasted_iota(jnp.int32, (owners, 1), 0)
    for g in range(gb):
        hot = jnp.where(place_ref[0, g : g + 1, :] == owner, 1.0, 0.0)
        hot_ref[g * owners : (g + 1) * owners, :] = hot.astype(BF16)
    before = lax.broadcasted_iota(jnp.int32, (orients, orients), 0)
    after = lax.broadcasted_iota(jnp.int32, (orients, orients), 1)
    upto = jnp.where(before <= after, 1.0, 0.0).astype(BF16)
    count_ref[...] = jnp.dot(hot_ref[...], upto, preferred_element_type=F32)

    exact = functools.partial(
        jnp.dot, preferred_element_type=F32, precision=lax.Precision.HIGHEST
    )
    tri = lambda n, lower: jnp.where(
        (lax.broadcasted_iota(jnp.int32, (n, n), 0) > lax.broadcasted_iota(jnp.int32, (n, n), 1))
        == lower,
        1.0,
        0.0,
    )
    below = tri(owners, True)
    row = lax.broadcasted_iota(jnp.int32, (OB, OB), 0)
    col = lax.broadcasted_iota(jnp.int32, (OB, OB), 1)
    earlier = jnp.where(row < col, 1.0, 0.0)
    lane = lax.broadcasted_iota(jnp.int32, (owners, OB), 1)
    sizes = jnp.zeros((owners, OB), F32)
    for g in range(gb):
        size = count_ref[g * owners : (g + 1) * owners, orients - 1 : orients]
        size = jnp.floor((size + 7.0) * 0.125) * 8.0
        sizes = jnp.where(lane == g, size, sizes)
    base = exact(below, sizes)
    ahead = exact(sizes, earlier)
    total = jnp.sum(sizes, axis=1, keepdims=True)
    start = exact(below, jnp.broadcast_to(total, (owners, OB)))[:, :1]
    blocks = jnp.floor((total + (RD - 1.0)) * (1.0 / RD))
    first = exact(below, jnp.broadcast_to(blocks, (owners, OB)))[:, :1]
    owner_f = owner.astype(F32)

    slot = (lax.broadcasted_iota(jnp.int32, (1, lanes), 1) * 8).astype(F32)
    is_last = lax.broadcasted_iota(jnp.int32, (1, lanes), 1) == lanes - 1
    rows = gb * (orients + 7 * owners)
    for g in range(gb):
        low, size = base[:, g : g + 1], sizes[:, g : g + 1]
        hot = hot_ref[g * owners : (g + 1) * owners, :].astype(F32)
        rank = count_ref[g * owners : (g + 1) * owners, :] - 1.0 + low
        pos_ref[0, g : g + 1, :] = jnp.sum(hot * rank, axis=0, keepdims=True).astype(jnp.int32)
        inside = (slot >= low) & (slot < low + size)
        goal = jnp.where(inside, start + ahead[:, g : g + 1] - low + slot - rows, 0.0)
        goal = jnp.sum(goal, axis=0, keepdims=True) + rows
        used = jnp.sum(size, axis=0, keepdims=True)
        addr_ref[0, g : g + 1, :] = jnp.where(is_last, used, goal).astype(jnp.int32)

    wide = item_ref.shape[2]
    number = lax.broadcasted_iota(jnp.int32, (1, wide), 1).astype(F32)
    inside = (number >= first) & (number < first + blocks)
    done = (number - first) * RD
    pick = lambda value: jnp.sum(jnp.where(inside, value, 0.0), axis=0, keepdims=True)
    item_ref[0, 0:1, :] = pick(jnp.broadcast_to(owner_f, (owners, wide))).astype(jnp.int32)
    item_ref[0, 1:2, :] = pick(start + done).astype(jnp.int32)
    item_ref[0, 2:3, :] = pick(total - done).astype(jnp.int32)
    items = jnp.sum(jnp.broadcast_to(blocks, (owners, wide)), axis=0, keepdims=True)
    item_ref[0, 3:4, :] = items.astype(jnp.int32)


def up_to(value, step):
    return -(-value // step) * step


def plan_call(place, owners):
    steps, gb, orients = place.shape
    slots = orients + 7 * owners
    lanes = up_to(slots // 8 + 17, 128)
    wide = up_to(owners + gb * slots // RD + 4, 128)
    block = lambda *shape: pl.BlockSpec((1,) + shape, lambda i: (i, 0, 0))
    return pl.pallas_call(
        functools.partial(plan_kernel, owners=owners),
        grid=(steps,),
        out_shape=[
            jax.ShapeDtypeStruct((steps, gb, orients), jnp.int32),
            jax.ShapeDtypeStruct((steps, gb, lanes), jnp.int32),
            jax.ShapeDtypeStruct((steps, 4, wide), jnp.int32),
        ],
        in_specs=[block(gb, orients)],
        out_specs=[block(gb, orients), block(gb, lanes), block(4, wide)],
        scratch_shapes=[
            pltpu.VMEM((gb * owners, orients), BF16),
            pltpu.VMEM((gb * owners, orients), F32),
        ],
        compiler_params=pltpu.CompilerParams(vmem_limit_bytes=40 * MB),
        cost_estimate=pl.CostEstimate(
            flops=8 * steps * gb * owners * orients * orients,
            bytes_accessed=8 * steps * gb * orients,
            transcendentals=0,
        ),
    )(place)


def insert_kernel(me_ref, addr_ref, item_ref, x_ref, pos_ref, rowf_ref, blk_ref, *rest):
    *post_refs, send_ref, keep_ref = rest[:-8]
    post_t, spread_ref, slice_ref, buf_s, buf_t, volume, stage, sem = rest[-8:]
    step = pl.program_id(0)
    count = x_ref.shape[0]
    orients = post_t.shape[0]
    gb = pos_ref.shape[1]
    width = x_ref.shape[1] // gb
    share = count // len(post_refs)
    lanes = addr_ref.shape[2]

    @pl.when(step == 0)
    def _():
        volume[...] = jnp.zeros_like(volume)
        buf_s[...] = jnp.zeros_like(buf_s)
        buf_t[...] = jnp.zeros_like(buf_t)
        me = me_ref[0]
        for k, post_ref in enumerate(post_refs):
            at = pl.multiple_of((me ^ k) * share, share)
            post = post_ref[...].astype(F32)
            first = blk_ref[pl.ds(at, share), 0:1]
            second = blk_ref[pl.ds(at, share), 1:2]
            for b in range(orients // OB):
                spread = jnp.where(
                    first == b, post[:, :OB], jnp.where(second == b, post[:, OB:], 0.0)
                )
                spread_ref[pl.ds(at, share), b * OB : (b + 1) * OB] = spread
        for b in range(orients // OB):
            post_t[b * OB : (b + 1) * OB] = spread_ref[:, b * OB : (b + 1) * OB].T.astype(BF16)

    def one_slice(g, carry):
        at = pl.ds(pl.multiple_of(g * width, width), width)
        value = jnp.dot(post_t[...], x_ref[:, at], preferred_element_type=F32)
        slice_ref[:, at] = value.astype(BF16)
        return carry

    lax.fori_loop(0, gb, one_slice, 0, unroll=2)

    bins = lax.broadcasted_iota(jnp.int32, (RD, 1), 0).astype(F32)

    def one_group(g, carry):
        pos = pos_ref[0, pl.ds(g, 1), :]
        tent = jnp.maximum(1.0 - jnp.abs(bins - rowf_ref[0, pl.ds(g, 1), :]), 0.0).astype(BF16)
        piece = slice_ref[:, pl.ds(pl.multiple_of(g * width, width), width)]

        def emit(base, size):
            slot = lax.broadcasted_iota(jnp.int32, (size, 1), 0) + base
            order = jnp.where(slot == pos, 1.0, 0.0).astype(BF16)
            rows = jnp.dot(order, piece, preferred_element_type=F32)
            weights = lax.dot_general(
                order, tent, (((1,), (1,)), ((), ())), preferred_element_type=F32
            )
            for i in range(size // 8):
                at = pl.multiple_of(addr_ref[0, g, base // 8 + i], 8)
                buf_s[pl.ds(at, 8), :] = rows[8 * i : 8 * i + 8]
                buf_t[pl.ds(at, 8), :] = weights[8 * i : 8 * i + 8]

        sure = orients + 128
        emit(0, sure)

        def more(e, c):
            emit(sure + e * 128, 128)
            return c

        used = addr_ref[0, g, lanes - 1]
        lax.fori_loop(0, lax.div(jnp.maximum(used - sure, 0) + 127, 128), more, 0)
        return carry

    lax.fori_loop(0, gb, one_group, 0)

    line = lax.broadcasted_iota(jnp.int32, (RD, 1), 0)

    def some_items(q, carry):
        for u in range(4):
            j = q * 4 + u
            owner, at, left = item_ref[0, 0, j], item_ref[0, 1, j], item_ref[0, 2, j]
            span = pl.ds(pl.multiple_of(at, 8), RD)
            weights = jnp.where(line < left, buf_t[span, :], 0.0).T.astype(BF16)
            goal = pl.ds(pl.multiple_of(owner * RD, RD), RD)
            volume[goal, :] += jnp.dot(
                weights, buf_s[span, :].astype(BF16), preferred_element_type=F32
            )
        return carry

    lax.fori_loop(0, lax.div(item_ref[0, 3, 0] + 3, 4), some_items, 0)

    @pl.when(step == pl.num_programs(0) - 1)
    def _():
        half = keep_ref.shape[0]
        tile = stage.shape[1]
        copies = []
        number = 0
        for base, out_ref in ((half, send_ref), (0, keep_ref)):
            for at in range(0, half, tile):
                slot = number % 2
                if number >= 2:
                    copies[number - 2].wait()
                stage[slot] = volume[base + at : base + at + tile, :].astype(BF16)
                copy = pltpu.make_async_copy(
                    stage.at[slot], out_ref.at[pl.ds(at, tile)], sem.at[slot]
                )
                copy.start()
                copies.append(copy)
                number += 1
        for copy in copies[-2:]:
            copy.wait()


def insert_block(groups, orients, owners, count, width):
    room = 58 * MB - owners * RD * width * 4 - 6 * MB
    best = 1
    for gb in range(1, groups + 1):
        rows = gb * (orients + 7 * owners) + RD + 8
        need = rows * width * 8 + 4 * count * gb * width + 2 * orients * gb * width
        if groups % gb == 0 and need <= room:
            best = gb
    return best


def insert_call(me, addr, items, flat, pos, rowf, blocks, posts, owners):
    count = flat.shape[0]
    steps, gb, orients = pos.shape
    width = flat.shape[1] // (steps * gb)
    total = owners * RD
    share = posts[0].shape[0]
    rows = gb * (orients + 7 * owners) + RD + 8
    smem = pl.BlockSpec(memory_space=pltpu.SMEM)
    block = lambda shape, **kw: pl.BlockSpec((1,) + shape[1:], lambda i: (i, 0, 0), **kw)
    return pl.pallas_call(
        insert_kernel,
        grid=(steps,),
        out_shape=[jax.ShapeDtypeStruct((total // 2, width), BF16)] * 2,
        in_specs=[
            smem,
            block(addr.shape, memory_space=pltpu.SMEM),
            block(items.shape, memory_space=pltpu.SMEM),
            pl.BlockSpec((count, gb * width), lambda i: (0, i)),
            block(pos.shape),
            block(rowf.shape),
            pl.BlockSpec((count, 2), lambda i: (0, 0)),
        ]
        + [pl.BlockSpec((share, 2 * OB), lambda i: (0, 0))] * len(posts),
        out_specs=[pl.BlockSpec(memory_space=pl.ANY)] * 2,
        scratch_shapes=[
            pltpu.VMEM((orients, count), BF16),
            pltpu.VMEM((count, orients), F32),
            pltpu.VMEM((orients, gb * width), BF16),
            pltpu.VMEM((rows, width), F32),
            pltpu.VMEM((rows, RD), F32),
            pltpu.VMEM((total, width), F32),
            pltpu.VMEM((2, 512, width), BF16),
            pltpu.SemaphoreType.DMA((2,)),
        ],
        compiler_params=pltpu.CompilerParams(vmem_limit_bytes=62 * MB),
        cost_estimate=pl.CostEstimate(
            flops=8 * count * orients * steps * gb * width,
            bytes_accessed=2 * count * steps * gb * width,
            transcendentals=0,
        ),
    )(me, addr, items, flat, pos, rowf, blocks, *posts)


def flip(value, axis, bit):
    size = lax.axis_size(axis)
    return lax.ppermute(value, axis, [(i, i ^ bit) for i in range(size)])


def shards(particles, blocks, references, inv_noise, destination, row_index, fraction):
    groups, width = particles.shape[1:]
    orients = references.shape[0]
    dom_size = lax.axis_size("dom")
    slab_size = lax.axis_size("slab")
    devices = dom_size * slab_size
    dom_pos = lax.axis_index("dom")
    slab_pos = lax.axis_index("slab")
    slab_me = slab_pos.astype(jnp.int32).reshape(1)
    dom_bits = [1 << i for i in range((dom_size - 1).bit_length())]
    slab_bits = [1 << i for i in range((slab_size - 1).bit_length())]

    flat, *scores = score_call(slab_me, inv_noise, particles, references, blocks, slab_size)
    parts = [scores[0]] + [flip(scores[k], "slab", k) for k in range(1, slab_size)]
    post = softmax_call(parts)
    posts = [post] + [flip(post, "slab", k) for k in range(1, slab_size)]

    gb = insert_block(groups, orients, devices, particles.shape[0], width)
    table = (groups // gb, gb, orients)
    take = lambda array: lax.dynamic_slice_in_dim(array, slab_pos * groups, groups, 0)
    owner = take(destination)
    dom_off = (owner // slab_size) ^ dom_pos
    slab_off = (owner % slab_size) ^ slab_pos
    place = jnp.zeros_like(owner)
    for bit in dom_bits:
        place = place * 2 + jnp.where(dom_off & bit != 0, 1, 0)
    for bit in slab_bits:
        place = place * 2 + jnp.where(slab_off & bit != 0, 1, 0)
    rowf = (take(row_index).astype(F32) + take(fraction)).reshape(table)
    pos, addr, items = plan_call(place.reshape(table), devices)
    send, keep = insert_call(slab_me, addr, items, flat, pos, rowf, blocks, posts, devices)

    def merge(kept, got):
        return kept.astype(F32) + got.astype(F32)

    total = merge(keep, flip(send, "dom", dom_bits[0]))
    rest = dom_bits[1:]
    total = total.reshape((2,) * len(rest) + (slab_size * RD, width))
    halves = []
    for part, order in ((0, rest), (1, rest[::-1])):
        value = total[..., part * OB : (part + 1) * OB]
        axes = list(rest)
        for bit in order:
            axis = axes.index(bit)
            axes.pop(axis)
            kept = lax.index_in_dim(value, 0, axis, keepdims=False)
            sent = lax.index_in_dim(value, 1, axis, keepdims=False)
            value = merge(kept, flip(sent.astype(BF16), "dom", bit))
        halves.append(value)
    value = jnp.concatenate(halves, axis=1)
    for bit in slab_bits:
        near, far = jnp.split(value, 2, axis=0)
        value = merge(near, flip(far.astype(BF16), "slab", bit))
    volume = value

    own = volume.astype(BF16)
    columns = []
    for part, order in ((0, rest), (1, rest[::-1])):
        value = own[:, part * OB : (part + 1) * OB]
        done = []
        for bit in order:
            got = flip(value, "dom", bit)
            axis = len([b for b in done if b > bit])
            done.append(bit)
            mine_low = dom_pos & bit == 0
            value = jnp.where(
                mine_low, jnp.stack([value, got], axis), jnp.stack([got, value], axis)
            )
        columns.append(value)
    value = jnp.concatenate(columns, axis=-1)
    got = flip(value, "dom", dom_bits[0])
    value = jnp.where(
        dom_pos & dom_bits[0] == 0,
        jnp.stack([value, got], len(rest)),
        jnp.stack([got, value], len(rest)),
    )
    return volume, value.reshape(dom_size * RD, width)


def solution(mesh):
    return jax.shard_map(
        shards,
        mesh=mesh,
        in_specs=(
            P("dom", "slab", None),
            P("dom", None),
            P(None, "slab", None),
            P("slab"),
            P(),
            P(),
            P(),
        ),
        out_specs=(P(("dom", "slab"), None), P(None, "slab")),
        check_vma=False,
    )
```

```python
import functools

import jax
import jax.numpy as jnp
from jax import lax
from jax.experimental import pallas as pl
from jax.experimental.pallas import tpu as pltpu
from jax.sharding import PartitionSpec as P

OB = 128
RD = 256
MB = 2**20
F32 = jnp.float32
BF16 = jnp.bfloat16


def group_block(groups):
    return 16 if groups % 16 == 0 else 8


def score_kernel(me_ref, noise_ref, perm_ref, x_ref, r_ref, blk_ref, flat_ref, *rest):
    *out_refs, w_ref, acc_ref = rest
    step = pl.program_id(0)
    particles, gb, width = x_ref.shape
    orients = r_ref.shape[0]

    @pl.when(step == 0)
    def _():
        acc_ref[...] = jnp.zeros_like(acc_ref)

    perm = perm_ref[...]

    def regroup(src_ref, dst_ref, scaled, i):
        at = pl.multiple_of(i * 16, 16)
        tile = src_ref[pl.ds(at, 16)].reshape(16 * gb, width)
        moved = jnp.dot(perm, tile, preferred_element_type=F32)
        for g in range(gb):
            part = moved[g * 16 : (g + 1) * 16]
            if scaled:
                part = part * noise_ref[step * gb + g]
            dst_ref[pl.ds(at, 16), g * width : (g + 1) * width] = part.astype(BF16)

    def tiles(i, carry):
        regroup(r_ref, w_ref, True, i)
        regroup(x_ref, flat_ref, False, i)
        return carry

    def more_tiles(src_ref, dst_ref, scaled):
        def body(i, carry):
            regroup(src_ref, dst_ref, scaled, i)
            return carry

        lax.fori_loop(both, src_ref.shape[0] // 16, body, 0)

    both = min(particles, orients) // 16
    lax.fori_loop(0, both, tiles, 0, unroll=8)
    more_tiles(r_ref, w_ref, True)
    more_tiles(x_ref, flat_ref, False)
    half = min(256, orients)

    def product(n, carry):
        at = pl.multiple_of(n * half, half)
        acc_ref[n] += lax.dot_general(
            flat_ref[...],
            w_ref[pl.ds(at, half), :],
            (((1,), (1,)), ((), ())),
            preferred_element_type=F32,
        )
        return carry

    lax.fori_loop(0, orients // half, product, 0)

    @pl.when(step == pl.num_programs(0) - 1)
    def _():
        me = me_ref[0]
        share = particles // len(out_refs)
        per = half // OB
        for k, out_ref in enumerate(out_refs):
            at = pl.multiple_of((me ^ k) * share, share)
            for j in range(2):
                wanted = blk_ref[pl.ds(at, share), j : j + 1]
                chosen = jnp.zeros((share, OB), F32)
                for b in range(orients // OB):
                    lane = (b % per) * OB
                    chosen = jnp.where(
                        wanted == b, acc_ref[b // per, pl.ds(at, share), lane : lane + OB], chosen
                    )
                out_ref[:, j * OB : (j + 1) * OB] = chosen


def score_call(me, inv_noise, particles, references, blocks, slab_size):
    count, groups, width = particles.shape
    orients = references.shape[0]
    gb = group_block(groups)
    side = 16 * gb
    row = jnp.arange(side, dtype=jnp.int32)[:, None]
    col = jnp.arange(side, dtype=jnp.int32)[None, :]
    perm = ((row // 16 == col % gb) & (row % 16 == col // gb)).astype(BF16)
    share = count // slab_size
    half = min(256, orients)
    smem = pl.BlockSpec(memory_space=pltpu.SMEM)
    return pl.pallas_call(
        score_kernel,
        grid=(groups // gb,),
        out_shape=[jax.ShapeDtypeStruct((count, groups * width), BF16)]
        + [jax.ShapeDtypeStruct((share, 2 * OB), F32)] * slab_size,
        in_specs=[
            smem,
            smem,
            pl.BlockSpec((side, side), lambda i: (0, 0)),
            pl.BlockSpec((count, gb, width), lambda i: (0, i, 0)),
            pl.BlockSpec((orients, gb, width), lambda i: (0, i, 0)),
            pl.BlockSpec((count, 2), lambda i: (0, 0)),
        ],
        out_specs=[pl.BlockSpec((count, gb * width), lambda i: (0, i))]
        + [pl.BlockSpec((share, 2 * OB), lambda i: (0, 0))] * slab_size,
        scratch_shapes=[
            pltpu.VMEM((orients, gb * width), BF16),
            pltpu.VMEM((orients // half, count, half), F32),
        ],
        compiler_params=pltpu.CompilerParams(vmem_limit_bytes=56 * MB),
        cost_estimate=pl.CostEstimate(
            flops=4 * count * orients * groups * width,
            bytes_accessed=6 * count * groups * width,
            transcendentals=0,
        ),
    )(me, inv_noise, perm, particles, references, blocks)


def softmax_kernel(*refs):
    *parts, out_ref = refs
    total = parts[0][...]
    for part in parts[1:]:
        total = total + part[...]
    highest = jnp.max(total, axis=1, keepdims=True)
    weights = jnp.exp(total - highest)
    out_ref[...] = (weights / jnp.sum(weights, axis=1, keepdims=True)).astype(BF16)


def softmax_call(parts):
    return pl.pallas_call(
        softmax_kernel, out_shape=jax.ShapeDtypeStruct(parts[0].shape, BF16)
    )(*parts)


def plan_kernel(
    place_ref, rowf_ref, pos_ref, addr_ref, item_ref, meta_ref, hot_ref, count_ref, *, owners
):
    _, gb, orients = place_ref.shape
    lanes = addr_ref.shape[2]
    owner = lax.broadcasted_iota(jnp.int32, (owners, 1), 0)
    for g in range(gb):
        hot = jnp.where(place_ref[0, g : g + 1, :] == owner, 1.0, 0.0)
        hot_ref[g * owners : (g + 1) * owners, :] = hot.astype(BF16)
    before = lax.broadcasted_iota(jnp.int32, (orients, orients), 0)
    after = lax.broadcasted_iota(jnp.int32, (orients, orients), 1)
    upto = jnp.where(before <= after, 1.0, 0.0).astype(BF16)
    count_ref[...] = jnp.dot(hot_ref[...], upto, preferred_element_type=F32)

    exact = functools.partial(
        jnp.dot, preferred_element_type=F32, precision=lax.Precision.HIGHEST
    )
    tri = lambda n, lower: jnp.where(
        (lax.broadcasted_iota(jnp.int32, (n, n), 0) > lax.broadcasted_iota(jnp.int32, (n, n), 1))
        == lower,
        1.0,
        0.0,
    )
    below = tri(owners, True)
    row = lax.broadcasted_iota(jnp.int32, (OB, OB), 0)
    col = lax.broadcasted_iota(jnp.int32, (OB, OB), 1)
    earlier = jnp.where(row < col, 1.0, 0.0)
    lane = lax.broadcasted_iota(jnp.int32, (owners, OB), 1)
    sizes = jnp.zeros((owners, OB), F32)
    for g in range(gb):
        size = count_ref[g * owners : (g + 1) * owners, orients - 1 : orients]
        size = jnp.floor((size + 7.0) * 0.125) * 8.0
        sizes = jnp.where(lane == g, size, sizes)
    base = exact(below, sizes)
    ahead = exact(sizes, earlier)
    total = jnp.sum(sizes, axis=1, keepdims=True)
    start = exact(below, jnp.broadcast_to(total, (owners, OB)))[:, :1]
    blocks = jnp.floor((total + (RD - 1.0)) * (1.0 / RD))
    first = exact(below, jnp.broadcast_to(blocks, (owners, OB)))[:, :1]
    owner_f = owner.astype(F32)

    slot = (lax.broadcasted_iota(jnp.int32, (1, lanes), 1) * 8).astype(F32)
    eighth = lax.broadcasted_iota(jnp.int32, (meta_ref.shape[2], 1), 0).astype(F32)
    lane_of = (lax.broadcasted_iota(jnp.int32, (OB, 1), 0) % 8).astype(F32)
    is_last = lax.broadcasted_iota(jnp.int32, (1, lanes), 1) == lanes - 1
    rows = gb * (orients + 7 * owners)
    for g in range(gb):
        low, size = base[:, g : g + 1], sizes[:, g : g + 1]
        hot = hot_ref[g * owners : (g + 1) * owners, :].astype(F32)
        rank = count_ref[g * owners : (g + 1) * owners, :] - 1.0 + low
        pos = jnp.sum(hot * rank, axis=0, keepdims=True)
        pos_ref[0, g : g + 1, :] = pos.astype(jnp.int32)
        block = jnp.floor(pos * 0.125)
        value = rowf_ref[0, g : g + 1, :]
        coarse = value.astype(BF16).astype(F32)
        here = lane_of == pos - 8.0 * block
        spots = jnp.where(eighth == block, 1.0, 0.0).astype(BF16)
        meta = jnp.zeros((meta_ref.shape[2], OB), F32)
        for term in (coarse, value - coarse):
            meta = meta + lax.dot_general(
                spots,
                jnp.where(here, term, 0.0).astype(BF16),
                (((1,), (1,)), ((), ())),
                preferred_element_type=F32,
            )
        meta_ref[0, g] = meta
        inside = (slot >= low) & (slot < low + size)
        goal = jnp.where(inside, start + ahead[:, g : g + 1] - low + slot - rows, 0.0) * 0.125
        goal = jnp.sum(goal, axis=0, keepdims=True) + rows // 8
        used = jnp.sum(size, axis=0, keepdims=True)
        addr_ref[0, g : g + 1, :] = jnp.where(is_last, used, goal).astype(jnp.int32)

    wide = item_ref.shape[2]
    number = lax.broadcasted_iota(jnp.int32, (1, wide), 1).astype(F32)
    inside = (number >= first) & (number < first + blocks)
    done = (number - first) * RD
    pick = lambda value: jnp.sum(jnp.where(inside, value, 0.0), axis=0, keepdims=True)
    item_ref[0, 0:1, :] = pick(jnp.broadcast_to(owner_f, (owners, wide))).astype(jnp.int32)
    item_ref[0, 1:2, :] = pick((start + done) * 0.125).astype(jnp.int32)
    item_ref[0, 2:3, :] = pick(total - done).astype(jnp.int32)
    items = jnp.sum(jnp.broadcast_to(blocks, (owners, wide)), axis=0, keepdims=True)
    item_ref[0, 3:4, :] = items.astype(jnp.int32)


def up_to(value, step):
    return -(-value // step) * step


def sort_sizes(orients, owners):
    slots = orients + 7 * owners
    sure = orients + 144
    blocks = up_to((sure + up_to(max(0, slots - sure), 128)) // 8, 8)
    return slots, sure, blocks


def plan_call(place, rowf, owners):
    steps, gb, orients = place.shape
    slots, _, blocks = sort_sizes(orients, owners)
    lanes = up_to(blocks + 1, 128)
    wide = up_to(owners + gb * slots // RD + 8, 128)
    block = lambda *shape: pl.BlockSpec(
        (1,) + shape, lambda i, n=len(shape): (i,) + (0,) * n
    )
    return pl.pallas_call(
        functools.partial(plan_kernel, owners=owners),
        grid=(steps,),
        out_shape=[
            jax.ShapeDtypeStruct((steps, gb, orients), jnp.int32),
            jax.ShapeDtypeStruct((steps, gb, lanes), jnp.int32),
            jax.ShapeDtypeStruct((steps, 4, wide), jnp.int32),
            jax.ShapeDtypeStruct((steps, gb, blocks, OB), F32),
        ],
        in_specs=[block(gb, orients)] * 2,
        out_specs=[block(gb, orients), block(gb, lanes), block(4, wide), block(gb, blocks, OB)],
        scratch_shapes=[
            pltpu.VMEM((gb * owners, orients), BF16),
            pltpu.VMEM((gb * owners, orients), F32),
        ],
        compiler_params=pltpu.CompilerParams(vmem_limit_bytes=40 * MB),
        cost_estimate=pl.CostEstimate(
            flops=8 * steps * gb * owners * orients * orients,
            bytes_accessed=8 * steps * gb * orients,
            transcendentals=0,
        ),
    )(place, rowf)


def insert_kernel(me_ref, addr_ref, item_ref, x_ref, pos_ref, meta_ref, blk_ref, *rest):
    *post_refs, send_ref, keep_ref = rest[:-8]
    post_t, spread_ref, slice_ref, buf_s, buf_m, volume, stage, sem = rest[-8:]
    step = pl.program_id(0)
    count = x_ref.shape[0]
    orients = post_t.shape[0]
    gb = pos_ref.shape[1]
    width = x_ref.shape[1] // gb
    share = count // len(post_refs)
    lanes = addr_ref.shape[2]
    unroll = 4 if gb % 4 == 0 else 1

    @pl.when(step == 0)
    def _():
        volume[...] = jnp.zeros_like(volume)
        buf_s[...] = jnp.zeros_like(buf_s)
        buf_m[...] = jnp.zeros_like(buf_m)
        me = me_ref[0]
        for k, post_ref in enumerate(post_refs):
            at = pl.multiple_of((me ^ k) * share, share)
            post = post_ref[...].astype(F32)
            first = blk_ref[pl.ds(at, share), 0:1]
            second = blk_ref[pl.ds(at, share), 1:2]
            for b in range(orients // OB):
                spread = jnp.where(
                    first == b, post[:, :OB], jnp.where(second == b, post[:, OB:], 0.0)
                )
                spread_ref[pl.ds(at, share), b * OB : (b + 1) * OB] = spread
        for b in range(orients // OB):
            post_t[b * OB : (b + 1) * OB] = spread_ref[:, b * OB : (b + 1) * OB].T.astype(BF16)

    def one_slice(g, carry):
        at = pl.ds(pl.multiple_of(g * width, width), width)
        value = jnp.dot(post_t[...], x_ref[:, at], preferred_element_type=F32)
        slice_ref[:, at] = value.astype(BF16)
        return carry

    lax.fori_loop(0, gb, one_slice, 0, unroll=unroll)

    def emit(g, base, size):
        pos = pos_ref[0, pl.ds(g, 1), :]
        piece = slice_ref[:, pl.ds(pl.multiple_of(g * width, width), width)]
        slot = lax.broadcasted_iota(jnp.int32, (size, 1), 0) + base
        order = jnp.where(slot == pos, 1.0, 0.0).astype(BF16)
        rows = jnp.dot(order, piece, preferred_element_type=F32)
        for i in range(size // 8):
            at = addr_ref[0, g, base // 8 + i]
            buf_s[pl.ds(pl.multiple_of(at * 8, 8), 8), :] = rows[8 * i : 8 * i + 8]
            buf_m[pl.ds(at, 1), :] = meta_ref[0, g, pl.ds(base // 8 + i, 1), :]

    slots, sure, _ = sort_sizes(orients, volume.shape[0] // RD)

    def one_group(g, carry):
        emit(g, 0, sure)
        return carry

    lax.fori_loop(0, gb, one_group, 0, unroll=unroll)

    def rest_of_group(g, carry):
        def more(e, c):
            emit(g, sure + e * 128, 128)
            return c

        used = addr_ref[0, g, lanes - 1]
        return lax.fori_loop(0, lax.div(jnp.maximum(used - sure, 0) + 127, 128), more, carry)

    if slots > sure:
        lax.fori_loop(0, gb, rest_of_group, 0)

    bins = lax.broadcasted_iota(jnp.int32, (RD, 1), 0).astype(F32)
    side = RD // 2
    at_lane = lax.broadcasted_iota(jnp.int32, (side // 8, side), 1) // 8
    own_lane = at_lane == lax.broadcasted_iota(jnp.int32, (side // 8, side), 0)
    line = lax.broadcasted_iota(jnp.int32, (1, RD), 1)
    together = 8

    def some_items(q, carry):
        for u in range(together):
            j = q * together + u
            owner, at, left = item_ref[0, 0, j], item_ref[0, 1, j], item_ref[0, 2, j]
            places = [
                jnp.sum(
                    jnp.where(own_lane, buf_m[pl.ds(at + h * (side // 8), side // 8), :], 0.0),
                    axis=0,
                    keepdims=True,
                )
                for h in range(2)
            ]
            place = jnp.where(line < left, jnp.concatenate(places, axis=1), -9.0)
            weights = jnp.maximum(1.0 - jnp.abs(bins - place), 0.0).astype(BF16)
            values = buf_s[pl.ds(pl.multiple_of(at * 8, 8), RD), :].astype(BF16)
            goal = pl.ds(pl.multiple_of(owner * RD, RD), RD)
            volume[goal, :] += jnp.dot(weights, values, preferred_element_type=F32)
        return carry

    count_items = lax.div(item_ref[0, 3, 0] + together - 1, together)
    lax.fori_loop(0, count_items, some_items, 0)

    @pl.when(step == pl.num_programs(0) - 1)
    def _():
        half = keep_ref.shape[0]
        tile = stage.shape[1]
        copies = []
        number = 0
        for base, out_ref in ((half, send_ref), (0, keep_ref)):
            for at in range(0, half, tile):
                slot = number % 2
                if number >= 2:
                    copies[number - 2].wait()
                stage[slot] = volume[base + at : base + at + tile, :].astype(BF16)
                copy = pltpu.make_async_copy(
                    stage.at[slot], out_ref.at[pl.ds(at, tile)], sem.at[slot]
                )
                copy.start()
                copies.append(copy)
                number += 1
        for copy in copies[-2:]:
            copy.wait()


def insert_block(groups, orients, owners, count, width):
    room = 58 * MB - owners * RD * width * 4 - 6 * MB
    best = 1
    for gb in range(1, groups + 1):
        rows = gb * (orients + 7 * owners) + RD + 8
        need = rows * width * 4 + rows * OB // 2 + 4 * count * gb * width + 2 * orients * gb * width
        if groups % gb == 0 and need <= room:
            best = gb
    return best


def insert_call(me, addr, items, flat, pos, meta, blocks, posts, owners):
    count = flat.shape[0]
    steps, gb, orients = pos.shape
    width = flat.shape[1] // (steps * gb)
    total = owners * RD
    share = posts[0].shape[0]
    rows = gb * (orients + 7 * owners) + RD + 8
    smem = pl.BlockSpec(memory_space=pltpu.SMEM)
    block = lambda shape, **kw: pl.BlockSpec((1,) + shape[1:], lambda i: (i,) + (0,) * (len(shape) - 1), **kw)
    return pl.pallas_call(
        insert_kernel,
        grid=(steps,),
        out_shape=[jax.ShapeDtypeStruct((total // 2, width), BF16)] * 2,
        in_specs=[
            smem,
            block(addr.shape, memory_space=pltpu.SMEM),
            block(items.shape, memory_space=pltpu.SMEM),
            pl.BlockSpec((count, gb * width), lambda i: (0, i)),
            block(pos.shape),
            block(meta.shape),
            pl.BlockSpec((count, 2), lambda i: (0, 0)),
        ]
        + [pl.BlockSpec((share, 2 * OB), lambda i: (0, 0))] * len(posts),
        out_specs=[pl.BlockSpec(memory_space=pl.ANY)] * 2,
        scratch_shapes=[
            pltpu.VMEM((orients, count), BF16),
            pltpu.VMEM((count, orients), F32),
            pltpu.VMEM((orients, gb * width), BF16),
            pltpu.VMEM((rows, width), F32),
            pltpu.VMEM((rows // 8, OB), F32),
            pltpu.VMEM((total, width), F32),
            pltpu.VMEM((2, 512, width), BF16),
            pltpu.SemaphoreType.DMA((2,)),
        ],
        compiler_params=pltpu.CompilerParams(vmem_limit_bytes=62 * MB),
        cost_estimate=pl.CostEstimate(
            flops=8 * count * orients * steps * gb * width,
            bytes_accessed=2 * count * steps * gb * width,
            transcendentals=0,
        ),
    )(me, addr, items, flat, pos, meta, blocks, *posts)


def flip(value, axis, bit):
    size = lax.axis_size(axis)
    return lax.ppermute(value, axis, [(i, i ^ bit) for i in range(size)])


def shards(particles, blocks, references, inv_noise, destination, row_index, fraction):
    groups, width = particles.shape[1:]
    orients = references.shape[0]
    dom_size = lax.axis_size("dom")
    slab_size = lax.axis_size("slab")
    devices = dom_size * slab_size
    dom_pos = lax.axis_index("dom")
    slab_pos = lax.axis_index("slab")
    slab_me = slab_pos.astype(jnp.int32).reshape(1)
    dom_bits = [1 << i for i in range((dom_size - 1).bit_length())]
    slab_bits = [1 << i for i in range((slab_size - 1).bit_length())]

    flat, *scores = score_call(slab_me, inv_noise, particles, references, blocks, slab_size)
    parts = [scores[0]] + [flip(scores[k], "slab", k) for k in range(1, slab_size)]
    post = softmax_call(parts)
    posts = [post] + [flip(post, "slab", k) for k in range(1, slab_size)]

    gb = insert_block(groups, orients, devices, particles.shape[0], width)
    table = (groups // gb, gb, orients)
    take = lambda array: lax.dynamic_slice_in_dim(array, slab_pos * groups, groups, 0)
    owner = take(destination)
    dom_off = (owner // slab_size) ^ dom_pos
    slab_off = (owner % slab_size) ^ slab_pos
    place = jnp.zeros_like(owner)
    for bit in dom_bits:
        place = place * 2 + jnp.where(dom_off & bit != 0, 1, 0)
    for bit in slab_bits:
        place = place * 2 + jnp.where(slab_off & bit != 0, 1, 0)
    rowf = (take(row_index).astype(F32) + take(fraction)).reshape(table)
    pos, addr, items, meta = plan_call(place.reshape(table), rowf, devices)
    send, keep = insert_call(slab_me, addr, items, flat, pos, meta, blocks, posts, devices)

    def merge(kept, got):
        return kept.astype(F32) + got.astype(F32)

    total = merge(keep, flip(send, "dom", dom_bits[0]))
    rest = dom_bits[1:]
    total = total.reshape((2,) * len(rest) + (slab_size * RD, width))
    halves = []
    for part, order in ((0, rest), (1, rest[::-1])):
        value = total[..., part * OB : (part + 1) * OB]
        axes = list(rest)
        for bit in order:
            axis = axes.index(bit)
            axes.pop(axis)
            kept = lax.index_in_dim(value, 0, axis, keepdims=False)
            sent = lax.index_in_dim(value, 1, axis, keepdims=False)
            value = merge(kept, flip(sent.astype(BF16), "dom", bit))
        halves.append(value)
    value = jnp.concatenate(halves, axis=1)
    for bit in slab_bits:
        near, far = jnp.split(value, 2, axis=0)
        value = merge(near, flip(far.astype(BF16), "slab", bit))
    volume = value

    own = volume.astype(BF16)
    columns = []
    for part, order in ((0, rest), (1, rest[::-1])):
        value = own[:, part * OB : (part + 1) * OB]
        done = []
        for bit in order:
            got = flip(value, "dom", bit)
            axis = len([b for b in done if b > bit])
            done.append(bit)
            mine_low = dom_pos & bit == 0
            value = jnp.where(
                mine_low, jnp.stack([value, got], axis), jnp.stack([got, value], axis)
            )
        columns.append(value)
    value = jnp.concatenate(columns, axis=-1)
    got = flip(value, "dom", dom_bits[0])
    value = jnp.where(
        dom_pos & dom_bits[0] == 0,
        jnp.stack([value, got], len(rest)),
        jnp.stack([got, value], len(rest)),
    )
    return volume, value.reshape(dom_size * RD, width)


def solution(mesh):
    return jax.shard_map(
        shards,
        mesh=mesh,
        in_specs=(
            P("dom", "slab", None),
            P("dom", None),
            P(None, "slab", None),
            P("slab"),
            P(),
            P(),
            P(),
        ),
        out_specs=(P(("dom", "slab"), None), P(None, "slab")),
        check_vma=False,
    )
```

```python
import functools

import jax
import jax.numpy as jnp
from jax import lax
from jax.experimental import pallas as pl
from jax.experimental.pallas import tpu as pltpu
from jax.sharding import PartitionSpec as P

OB = 128
RD = 256
MB = 2**20
F32 = jnp.float32
BF16 = jnp.bfloat16


def group_block(groups):
    return 16 if groups % 16 == 0 else 8


def spread_columns(blk_ref, cols_ref):
    count = blk_ref.shape[1]
    for j in range(2):
        for at in range(0, count, OB):
            line = blk_ref[j : j + 1, at : at + OB].astype(F32)
            cols_ref[j, at : at + OB, :] = jnp.broadcast_to(line, (OB, OB)).T


def score_kernel(me_ref, noise_ref, x_ref, r_ref, blk_ref, flat_ref, *rest):
    *out_refs, w_ref, acc_ref, perm_ref, cols_ref = rest
    step = pl.program_id(0)
    particles, gb, width = x_ref.shape
    orients = r_ref.shape[0]
    side = 16 * gb

    @pl.when(step == 0)
    def _():
        row = lax.broadcasted_iota(jnp.int32, (side, side), 0)
        col = lax.broadcasted_iota(jnp.int32, (side, side), 1)
        same = ((row // 16) == (col % gb)) & ((row % 16) == (col // gb))
        perm_ref[...] = jnp.where(same, 1.0, 0.0).astype(BF16)
        acc_ref[...] = jnp.zeros_like(acc_ref)
        spread_columns(blk_ref, cols_ref)

    perm = perm_ref[...]

    def regroup(src_ref, dst_ref, scaled, first, number):
        at = pl.multiple_of(first * 16, 16)
        tile = src_ref[pl.ds(at, 16 * number)].reshape(number, side, width)
        wide = jnp.concatenate([tile[t] for t in range(number)], axis=1)
        moved = jnp.dot(perm, wide, preferred_element_type=F32)
        for g in range(gb):
            for t in range(number):
                part = moved[g * 16 : (g + 1) * 16, t * width : (t + 1) * width]
                if scaled:
                    part = part * noise_ref[step * gb + g]
                dst_ref[pl.ds(at + 16 * t, 16), g * width : (g + 1) * width] = part.astype(BF16)

    def tiles(i, carry):
        regroup(r_ref, w_ref, True, i * 4, 4)
        regroup(x_ref, flat_ref, False, i * 4, 4)
        return carry

    def more_tiles(src_ref, dst_ref, scaled):
        def body(i, carry):
            regroup(src_ref, dst_ref, scaled, i, 1)
            return carry

        lax.fori_loop(both * 4, src_ref.shape[0] // 16, body, 0)

    both = min(particles, orients) // 64
    lax.fori_loop(0, both, tiles, 0, unroll=2)
    more_tiles(r_ref, w_ref, True)
    more_tiles(x_ref, flat_ref, False)
    acc_ref[...] += lax.dot_general(
        flat_ref[...], w_ref[...], (((1,), (1,)), ((), ())), preferred_element_type=F32
    )

    @pl.when(step == pl.num_programs(0) - 1)
    def _():
        me = me_ref[0]
        share = particles // len(out_refs)
        for k, out_ref in enumerate(out_refs):
            at = pl.multiple_of((me ^ k) * share, share)
            for j in range(2):
                wanted = cols_ref[j, pl.ds(at, share), :]
                chosen = jnp.zeros((share, OB), F32)
                for b in range(orients // OB):
                    value = acc_ref[pl.ds(at, share), b * OB : (b + 1) * OB]
                    chosen = jnp.where(wanted == b, value, chosen)
                out_ref[:, j * OB : (j + 1) * OB] = chosen


def score_call(me, inv_noise, particles, references, blocks, slab_size):
    count, groups, width = particles.shape
    orients = references.shape[0]
    gb = group_block(groups)
    side = 16 * gb
    share = count // slab_size
    smem = pl.BlockSpec(memory_space=pltpu.SMEM)
    return pl.pallas_call(
        score_kernel,
        grid=(groups // gb,),
        out_shape=[jax.ShapeDtypeStruct((count, groups * width), BF16)]
        + [jax.ShapeDtypeStruct((share, 2 * OB), F32)] * slab_size,
        in_specs=[
            smem,
            smem,
            pl.BlockSpec((count, gb, width), lambda i: (0, i, 0)),
            pl.BlockSpec((orients, gb, width), lambda i: (0, i, 0)),
            pl.BlockSpec((2, count), lambda i: (0, 0)),
        ],
        out_specs=[pl.BlockSpec((count, gb * width), lambda i: (0, i))]
        + [pl.BlockSpec((share, 2 * OB), lambda i: (0, 0))] * slab_size,
        scratch_shapes=[
            pltpu.VMEM((orients, gb * width), BF16),
            pltpu.VMEM((count, orients), F32),
            pltpu.VMEM((side, side), BF16),
            pltpu.VMEM((2, count, OB), F32),
        ],
        compiler_params=pltpu.CompilerParams(vmem_limit_bytes=56 * MB),
        cost_estimate=pl.CostEstimate(
            flops=4 * count * orients * groups * width,
            bytes_accessed=6 * count * groups * width,
            transcendentals=0,
        ),
    )(me, inv_noise, particles, references, blocks)


def softmax_kernel(*refs):
    *parts, out_ref = refs
    total = parts[0][...]
    for part in parts[1:]:
        total = total + part[...]
    highest = jnp.max(total, axis=1, keepdims=True)
    weights = jnp.exp(total - highest)
    out_ref[...] = (weights / jnp.sum(weights, axis=1, keepdims=True)).astype(BF16)


def softmax_call(parts):
    return pl.pallas_call(
        softmax_kernel,
        out_shape=jax.ShapeDtypeStruct(parts[0].shape, BF16),
        compiler_params=pltpu.CompilerParams(vmem_limit_bytes=8 * MB),
    )(*parts)


def plan_kernel(
    place_ref, rowf_ref, pos_ref, addr_ref, item_ref, meta_ref, hot_ref, count_ref, *, owners
):
    _, gb, orients = place_ref.shape
    lanes = addr_ref.shape[2]
    owner = lax.broadcasted_iota(jnp.int32, (owners, 1), 0)
    for g in range(gb):
        hot = jnp.where(place_ref[0, g : g + 1, :] == owner, 1.0, 0.0)
        hot_ref[g * owners : (g + 1) * owners, :] = hot.astype(BF16)
    before = lax.broadcasted_iota(jnp.int32, (orients, orients), 0)
    after = lax.broadcasted_iota(jnp.int32, (orients, orients), 1)
    upto = jnp.where(before <= after, 1.0, 0.0).astype(BF16)
    count_ref[...] = jnp.dot(hot_ref[...], upto, preferred_element_type=F32)

    exact = functools.partial(
        jnp.dot, preferred_element_type=F32, precision=lax.Precision.HIGHEST
    )
    tri = lambda n, lower: jnp.where(
        (lax.broadcasted_iota(jnp.int32, (n, n), 0) > lax.broadcasted_iota(jnp.int32, (n, n), 1))
        == lower,
        1.0,
        0.0,
    )
    below = tri(owners, True)
    row = lax.broadcasted_iota(jnp.int32, (OB, OB), 0)
    col = lax.broadcasted_iota(jnp.int32, (OB, OB), 1)
    earlier = jnp.where(row < col, 1.0, 0.0)
    lane = lax.broadcasted_iota(jnp.int32, (owners, OB), 1)
    sizes = jnp.zeros((owners, OB), F32)
    for g in range(gb):
        size = count_ref[g * owners : (g + 1) * owners, orients - 1 : orients]
        size = jnp.floor((size + 7.0) * 0.125) * 8.0
        sizes = jnp.where(lane == g, size, sizes)
    base = exact(below, sizes)
    ahead = exact(sizes, earlier)
    total = jnp.sum(sizes, axis=1, keepdims=True)
    start = exact(below, jnp.broadcast_to(total, (owners, OB)))[:, :1]
    blocks = jnp.floor((total + (RD - 1.0)) * (1.0 / RD))
    first = exact(below, jnp.broadcast_to(blocks, (owners, OB)))[:, :1]
    owner_f = owner.astype(F32)

    slot = (lax.broadcasted_iota(jnp.int32, (1, lanes), 1) * 8).astype(F32)
    eighth = lax.broadcasted_iota(jnp.int32, (meta_ref.shape[2], 1), 0).astype(F32)
    lane_of = (lax.broadcasted_iota(jnp.int32, (OB, 1), 0) % 8).astype(F32)
    is_last = lax.broadcasted_iota(jnp.int32, (1, lanes), 1) == lanes - 1
    rows = gb * (orients + 7 * owners)
    for g in range(gb):
        low, size = base[:, g : g + 1], sizes[:, g : g + 1]
        hot = hot_ref[g * owners : (g + 1) * owners, :].astype(F32)
        rank = count_ref[g * owners : (g + 1) * owners, :] - 1.0 + low
        pos = jnp.sum(hot * rank, axis=0, keepdims=True)
        pos_ref[0, g : g + 1, :] = pos.astype(jnp.int32)
        block = jnp.floor(pos * 0.125)
        value = rowf_ref[0, g : g + 1, :]
        coarse = value.astype(BF16).astype(F32)
        here = lane_of == pos - 8.0 * block
        spots = jnp.where(eighth == block, 1.0, 0.0).astype(BF16)
        meta = jnp.zeros((meta_ref.shape[2], OB), F32)
        for term in (coarse, value - coarse):
            meta = meta + lax.dot_general(
                spots,
                jnp.where(here, term, 0.0).astype(BF16),
                (((1,), (1,)), ((), ())),
                preferred_element_type=F32,
            )
        meta_ref[0, g] = meta
        inside = (slot >= low) & (slot < low + size)
        goal = jnp.where(inside, start + ahead[:, g : g + 1] - low + slot - rows, 0.0) * 0.125
        goal = jnp.sum(goal, axis=0, keepdims=True) + rows // 8
        used = jnp.sum(size, axis=0, keepdims=True)
        addr_ref[0, g : g + 1, :] = jnp.where(is_last, used, goal).astype(jnp.int32)

    wide = item_ref.shape[2]
    number = lax.broadcasted_iota(jnp.int32, (1, wide), 1).astype(F32)
    inside = (number >= first) & (number < first + blocks)
    done = (number - first) * RD
    pick = lambda value: jnp.sum(jnp.where(inside, value, 0.0), axis=0, keepdims=True)
    item_ref[0, 0:1, :] = pick(jnp.broadcast_to(owner_f, (owners, wide))).astype(jnp.int32)
    item_ref[0, 1:2, :] = pick((start + done) * 0.125).astype(jnp.int32)
    item_ref[0, 2:3, :] = pick(total - done).astype(jnp.int32)
    items = jnp.sum(jnp.broadcast_to(blocks, (owners, wide)), axis=0, keepdims=True)
    item_ref[0, 3:4, :] = items.astype(jnp.int32)


def up_to(value, step):
    return -(-value // step) * step


def sort_sizes(orients, owners):
    slots = orients + 7 * owners
    sure = orients + 144
    blocks = up_to((sure + up_to(max(0, slots - sure), 128)) // 8, 8)
    return slots, sure, blocks


def plan_call(place, rowf, owners):
    steps, gb, orients = place.shape
    slots, _, blocks = sort_sizes(orients, owners)
    lanes = up_to(blocks + 1, 128)
    wide = up_to(owners + gb * slots // RD + 8, 128)
    block = lambda *shape: pl.BlockSpec(
        (1,) + shape, lambda i, n=len(shape): (i,) + (0,) * n
    )
    return pl.pallas_call(
        functools.partial(plan_kernel, owners=owners),
        grid=(steps,),
        out_shape=[
            jax.ShapeDtypeStruct((steps, gb, orients), jnp.int32),
            jax.ShapeDtypeStruct((steps, gb, lanes), jnp.int32),
            jax.ShapeDtypeStruct((steps, 4, wide), jnp.int32),
            jax.ShapeDtypeStruct((steps, gb, blocks, OB), F32),
        ],
        in_specs=[block(gb, orients)] * 2,
        out_specs=[block(gb, orients), block(gb, lanes), block(4, wide), block(gb, blocks, OB)],
        scratch_shapes=[
            pltpu.VMEM((gb * owners, orients), BF16),
            pltpu.VMEM((gb * owners, orients), F32),
        ],
        compiler_params=pltpu.CompilerParams(vmem_limit_bytes=60 * MB),
        cost_estimate=pl.CostEstimate(
            flops=8 * steps * gb * owners * orients * orients,
            bytes_accessed=8 * steps * gb * orients,
            transcendentals=0,
        ),
    )(place, rowf)


def insert_kernel(me_ref, addr_ref, item_ref, x_ref, pos_ref, meta_ref, blk_ref, *rest):
    *post_refs, send_ref, keep_ref = rest[:-9]
    post_t, spread_ref, cols_ref, slice_ref, buf_s, buf_m, volume, stage, sem = rest[-9:]
    step = pl.program_id(0)
    count = x_ref.shape[0]
    orients = post_t.shape[0]
    gb = pos_ref.shape[1]
    width = x_ref.shape[1] // gb
    share = count // len(post_refs)
    lanes = addr_ref.shape[2]
    unroll = 4 if gb % 4 == 0 else 1

    @pl.when(step == 0)
    def _():
        volume[...] = jnp.zeros_like(volume)
        buf_s[...] = jnp.zeros_like(buf_s)
        buf_m[...] = jnp.zeros_like(buf_m)
        me = me_ref[0]
        spread_columns(blk_ref, cols_ref)
        for k, post_ref in enumerate(post_refs):
            at = pl.multiple_of((me ^ k) * share, share)
            post = post_ref[...].astype(F32)
            first = cols_ref[0, pl.ds(at, share), :]
            second = cols_ref[1, pl.ds(at, share), :]
            for b in range(orients // OB):
                spread = jnp.where(
                    first == b, post[:, :OB], jnp.where(second == b, post[:, OB:], 0.0)
                )
                spread_ref[pl.ds(at, share), b * OB : (b + 1) * OB] = spread
        for b in range(orients // OB):
            post_t[b * OB : (b + 1) * OB] = spread_ref[:, b * OB : (b + 1) * OB].T.astype(BF16)

    def some_slices(q, carry):
        span = unroll * width
        at = pl.ds(pl.multiple_of(q * span, span), span)
        value = jnp.dot(post_t[...], x_ref[:, at], preferred_element_type=F32)
        slice_ref[:, at] = value.astype(BF16)
        return carry

    lax.fori_loop(0, gb // unroll, some_slices, 0)

    one, none = jnp.bfloat16(1.0), jnp.bfloat16(0.0)

    def emit(g, base, size):
        pos = pos_ref[0, pl.ds(g, 1), :]
        piece = slice_ref[:, pl.ds(pl.multiple_of(g * width, width), width)]
        parts = []
        for at in range(0, size, 128):
            high = min(128, size - at)
            slot = lax.broadcasted_iota(jnp.int32, (high, orients), 0).astype(F32).astype(BF16)
            near = jnp.clip(pos - (base + at), -1, 128).astype(F32).astype(BF16)
            parts.append(jnp.where(slot == near, one, none))
        order = jnp.concatenate(parts, axis=0)
        rows = jnp.dot(order, piece, preferred_element_type=F32)
        for i in range(size // 8):
            at = addr_ref[0, g, base // 8 + i]
            buf_s[pl.ds(pl.multiple_of(at * 8, 8), 8), :] = rows[8 * i : 8 * i + 8]
            buf_m[pl.ds(at, 1), :] = meta_ref[0, g, pl.ds(base // 8 + i, 1), :]

    slots, sure, _ = sort_sizes(orients, volume.shape[0] // RD)

    def one_group(g, carry):
        emit(g, 0, sure)
        return carry

    lax.fori_loop(0, gb, one_group, 0, unroll=unroll)

    def rest_of_group(g, carry):
        def more(e, c):
            emit(g, sure + e * 128, 128)
            return c

        used = addr_ref[0, g, lanes - 1]
        return lax.fori_loop(0, lax.div(jnp.maximum(used - sure, 0) + 127, 128), more, carry)

    if slots > sure:
        lax.fori_loop(0, gb, rest_of_group, 0)

    bins = lax.broadcasted_iota(jnp.int32, (RD, RD), 0).astype(F32).astype(BF16)
    side = RD // 2
    at_lane = lax.broadcasted_iota(jnp.int32, (side // 8, side), 1) // 8
    own_lane = at_lane == lax.broadcasted_iota(jnp.int32, (side // 8, side), 0)
    line = lax.broadcasted_iota(jnp.int32, (1, RD), 1)
    together = 8

    def some_items(q, carry):
        for u in range(together):
            j = q * together + u
            owner, at, left = item_ref[0, 0, j], item_ref[0, 1, j], item_ref[0, 2, j]
            places = [
                jnp.sum(
                    jnp.where(own_lane, buf_m[pl.ds(at + h * (side // 8), side // 8), :], 0.0),
                    axis=0,
                    keepdims=True,
                )
                for h in range(2)
            ]
            place = jnp.where(line < left, jnp.concatenate(places, axis=1), -9.0)
            whole = jnp.floor(place)
            apart = (bins - whole.astype(BF16)) - (place - whole).astype(BF16)
            weights = jnp.maximum(one - jnp.abs(apart), none)
            values = buf_s[pl.ds(pl.multiple_of(at * 8, 8), RD), :].astype(BF16)
            goal = pl.ds(pl.multiple_of(owner * RD, RD), RD)
            volume[goal, :] += jnp.dot(weights, values, preferred_element_type=F32)
        return carry

    count_items = lax.div(item_ref[0, 3, 0] + together - 1, together)
    lax.fori_loop(0, count_items, some_items, 0)

    @pl.when(step == pl.num_programs(0) - 1)
    def _():
        half = keep_ref.shape[0]
        tile = stage.shape[1]
        copies = []
        number = 0
        for base, out_ref in ((half, send_ref), (0, keep_ref)):
            for at in range(0, half, tile):
                slot = number % 2
                if number >= 2:
                    copies[number - 2].wait()
                stage[slot] = volume[base + at : base + at + tile, :].astype(BF16)
                copy = pltpu.make_async_copy(
                    stage.at[slot], out_ref.at[pl.ds(at, tile)], sem.at[slot]
                )
                copy.start()
                copies.append(copy)
                number += 1
        for copy in copies[-2:]:
            copy.wait()


def insert_block(groups, orients, owners, count, width):
    room = 58 * MB - owners * RD * width * 4 - 6 * MB
    best = 1
    for gb in range(1, groups + 1):
        rows = gb * (orients + 7 * owners) + RD + 8
        need = rows * width * 4 + rows * OB // 2 + 4 * count * gb * width + 2 * orients * gb * width
        if groups % gb == 0 and need <= room:
            best = gb
    return best


def insert_call(me, addr, items, flat, pos, meta, blocks, posts, owners):
    count = flat.shape[0]
    steps, gb, orients = pos.shape
    width = flat.shape[1] // (steps * gb)
    total = owners * RD
    share = posts[0].shape[0]
    rows = gb * (orients + 7 * owners) + RD + 8
    smem = pl.BlockSpec(memory_space=pltpu.SMEM)
    block = lambda shape, **kw: pl.BlockSpec((1,) + shape[1:], lambda i: (i,) + (0,) * (len(shape) - 1), **kw)
    return pl.pallas_call(
        insert_kernel,
        grid=(steps,),
        out_shape=[jax.ShapeDtypeStruct((total // 2, width), BF16)] * 2,
        in_specs=[
            smem,
            block(addr.shape, memory_space=pltpu.SMEM),
            block(items.shape, memory_space=pltpu.SMEM),
            pl.BlockSpec((count, gb * width), lambda i: (0, i)),
            block(pos.shape),
            block(meta.shape),
            pl.BlockSpec((2, count), lambda i: (0, 0)),
        ]
        + [pl.BlockSpec((share, 2 * OB), lambda i: (0, 0))] * len(posts),
        out_specs=[pl.BlockSpec(memory_space=pl.ANY)] * 2,
        scratch_shapes=[
            pltpu.VMEM((orients, count), BF16),
            pltpu.VMEM((count, orients), F32),
            pltpu.VMEM((2, count, OB), F32),
            pltpu.VMEM((orients, gb * width), BF16),
            pltpu.VMEM((rows, width), F32),
            pltpu.VMEM((rows // 8, OB), F32),
            pltpu.VMEM((total, width), F32),
            pltpu.VMEM((2, 512, width), BF16),
            pltpu.SemaphoreType.DMA((2,)),
        ],
        compiler_params=pltpu.CompilerParams(vmem_limit_bytes=62 * MB),
        cost_estimate=pl.CostEstimate(
            flops=8 * count * orients * steps * gb * width,
            bytes_accessed=2 * count * steps * gb * width,
            transcendentals=0,
        ),
    )(me, addr, items, flat, pos, meta, blocks, *posts)


def flip(value, axis, bit):
    size = lax.axis_size(axis)
    return lax.ppermute(value, axis, [(i, i ^ bit) for i in range(size)])


def shards(particles, blocks, references, inv_noise, destination, row_index, fraction):
    groups, width = particles.shape[1:]
    orients = references.shape[0]
    dom_size = lax.axis_size("dom")
    slab_size = lax.axis_size("slab")
    devices = dom_size * slab_size
    dom_pos = lax.axis_index("dom")
    slab_pos = lax.axis_index("slab")
    slab_me = slab_pos.astype(jnp.int32).reshape(1)
    dom_bits = [1 << i for i in range((dom_size - 1).bit_length())]
    slab_bits = [1 << i for i in range((slab_size - 1).bit_length())]

    blocks = blocks.T
    flat, *scores = score_call(slab_me, inv_noise, particles, references, blocks, slab_size)
    gb = insert_block(groups, orients, devices, particles.shape[0], width)
    table = (groups // gb, gb, orients)
    take = lambda array: lax.dynamic_slice_in_dim(array, slab_pos * groups, groups, 0)
    owner = take(destination)
    dom_off = (owner // slab_size) ^ dom_pos
    slab_off = (owner % slab_size) ^ slab_pos
    place = jnp.zeros_like(owner)
    for bit in dom_bits:
        place = place * 2 + jnp.where(dom_off & bit != 0, 1, 0)
    for bit in slab_bits:
        place = place * 2 + jnp.where(slab_off & bit != 0, 1, 0)
    rowf = (take(row_index).astype(F32) + take(fraction)).reshape(table)
    place, own = lax.optimization_barrier((place.reshape(table), scores[0]))
    plan = plan_call(place, rowf, devices)
    own, *plan = lax.optimization_barrier((own, *plan))
    pos, addr, items, meta = plan

    parts = [own] + [flip(scores[k], "slab", k) for k in range(1, slab_size)]
    post = softmax_call(parts)
    posts = [post] + [flip(post, "slab", k) for k in range(1, slab_size)]
    send, keep = insert_call(slab_me, addr, items, flat, pos, meta, blocks, posts, devices)

    def merge(kept, got):
        return kept.astype(F32) + got.astype(F32)

    total = merge(keep, flip(send, "dom", dom_bits[0]))
    rest = dom_bits[1:]
    total = total.reshape((2,) * len(rest) + (slab_size * RD, width))
    halves = []
    for part, order in ((0, rest), (1, rest[::-1])):
        value = total[..., part * OB : (part + 1) * OB]
        axes = list(rest)
        for bit in order:
            axis = axes.index(bit)
            axes.pop(axis)
            kept = lax.index_in_dim(value, 0, axis, keepdims=False)
            sent = lax.index_in_dim(value, 1, axis, keepdims=False)
            value = merge(kept, flip(sent.astype(BF16), "dom", bit))
        halves.append(value)
    value = jnp.concatenate(halves, axis=1)
    for bit in slab_bits:
        near, far = jnp.split(value, 2, axis=0)
        value = merge(near, flip(far.astype(BF16), "slab", bit))
    volume = value

    own = volume.astype(BF16)
    columns = []
    for part, order in ((0, rest), (1, rest[::-1])):
        value = own[:, part * OB : (part + 1) * OB]
        done = []
        for bit in order:
            got = flip(value, "dom", bit)
            axis = len([b for b in done if b > bit])
            done.append(bit)
            mine_low = dom_pos & bit == 0
            value = jnp.where(
                mine_low, jnp.stack([value, got], axis), jnp.stack([got, value], axis)
            )
        columns.append(value)
    value = jnp.concatenate(columns, axis=-1)
    got = flip(value, "dom", dom_bits[0])
    value = jnp.where(
        dom_pos & dom_bits[0] == 0,
        jnp.stack([value, got], len(rest)),
        jnp.stack([got, value], len(rest)),
    )
    return volume, value.reshape(dom_size * RD, width)


def solution(mesh):
    return jax.shard_map(
        shards,
        mesh=mesh,
        in_specs=(
            P("dom", "slab", None),
            P("dom", None),
            P(None, "slab", None),
            P("slab"),
            P(),
            P(),
            P(),
        ),
        out_specs=(P(("dom", "slab"), None), P(None, "slab")),
        check_vma=False,
    )
```

```python
import functools

import jax
import jax.numpy as jnp
from jax import lax
from jax.experimental import pallas as pl
from jax.experimental.pallas import tpu as pltpu
from jax.sharding import PartitionSpec as P

OB = 128
RD = 256
MB = 2**20
F32 = jnp.float32
BF16 = jnp.bfloat16


def group_block(groups):
    return 16 if groups % 16 == 0 else 8


def spread_columns(blk_ref, cols_ref):
    count = blk_ref.shape[1]
    for j in range(2):
        for at in range(0, count, OB):
            line = blk_ref[j : j + 1, at : at + OB].astype(F32)
            cols_ref[j, at : at + OB, :] = jnp.broadcast_to(line, (OB, OB)).T


def score_kernel(me_ref, noise_ref, x_ref, r_ref, blk_ref, flat_ref, *rest):
    *out_refs, w_ref, acc_ref, perm_ref, cols_ref = rest
    step = pl.program_id(0)
    particles, gb, width = x_ref.shape
    orients = r_ref.shape[0]
    side = 16 * gb

    @pl.when(step == 0)
    def _():
        row = lax.broadcasted_iota(jnp.int32, (side, side), 0)
        col = lax.broadcasted_iota(jnp.int32, (side, side), 1)
        same = ((row // 16) == (col % gb)) & ((row % 16) == (col // gb))
        perm_ref[...] = jnp.where(same, 1.0, 0.0).astype(BF16)
        acc_ref[...] = jnp.zeros_like(acc_ref)
        spread_columns(blk_ref, cols_ref)

    perm = perm_ref[...]

    def regroup(src_ref, dst_ref, scaled, first, number):
        at = pl.multiple_of(first * 16, 16)
        tile = src_ref[pl.ds(at, 16 * number)].reshape(number, side, width)
        wide = jnp.concatenate([tile[t] for t in range(number)], axis=1)
        moved = jnp.dot(perm, wide, preferred_element_type=F32)
        for g in range(gb):
            for t in range(number):
                part = moved[g * 16 : (g + 1) * 16, t * width : (t + 1) * width]
                if scaled:
                    part = part * noise_ref[step * gb + g]
                dst_ref[pl.ds(at + 16 * t, 16), g * width : (g + 1) * width] = part.astype(BF16)

    def tiles(i, carry):
        regroup(r_ref, w_ref, True, i * 4, 4)
        regroup(x_ref, flat_ref, False, i * 4, 4)
        return carry

    def more_tiles(src_ref, dst_ref, scaled):
        def body(i, carry):
            regroup(src_ref, dst_ref, scaled, i, 1)
            return carry

        lax.fori_loop(both * 4, src_ref.shape[0] // 16, body, 0)

    both = min(particles, orients) // 64
    lax.fori_loop(0, both, tiles, 0, unroll=2)
    more_tiles(r_ref, w_ref, True)
    more_tiles(x_ref, flat_ref, False)
    acc_ref[...] += lax.dot_general(
        flat_ref[...], w_ref[...], (((1,), (1,)), ((), ())), preferred_element_type=F32
    )

    @pl.when(step == pl.num_programs(0) - 1)
    def _():
        me = me_ref[0]
        share = particles // len(out_refs)
        for k, out_ref in enumerate(out_refs):
            at = pl.multiple_of((me ^ k) * share, share)
            for j in range(2):
                wanted = cols_ref[j, pl.ds(at, share), :]
                chosen = jnp.zeros((share, OB), F32)
                for b in range(orients // OB):
                    value = acc_ref[pl.ds(at, share), b * OB : (b + 1) * OB]
                    chosen = jnp.where(wanted == b, value, chosen)
                out_ref[:, j * OB : (j + 1) * OB] = chosen


def score_call(me, inv_noise, particles, references, blocks, slab_size):
    count, groups, width = particles.shape
    orients = references.shape[0]
    gb = group_block(groups)
    side = 16 * gb
    share = count // slab_size
    smem = pl.BlockSpec(memory_space=pltpu.SMEM)
    return pl.pallas_call(
        score_kernel,
        grid=(groups // gb,),
        out_shape=[jax.ShapeDtypeStruct((count, groups * width), BF16)]
        + [jax.ShapeDtypeStruct((share, 2 * OB), F32)] * slab_size,
        in_specs=[
            smem,
            smem,
            pl.BlockSpec((count, gb, width), lambda i: (0, i, 0)),
            pl.BlockSpec((orients, gb, width), lambda i: (0, i, 0)),
            pl.BlockSpec((2, count), lambda i: (0, 0)),
        ],
        out_specs=[pl.BlockSpec((count, gb * width), lambda i: (0, i))]
        + [pl.BlockSpec((share, 2 * OB), lambda i: (0, 0))] * slab_size,
        scratch_shapes=[
            pltpu.VMEM((orients, gb * width), BF16),
            pltpu.VMEM((count, orients), F32),
            pltpu.VMEM((side, side), BF16),
            pltpu.VMEM((2, count, OB), F32),
        ],
        compiler_params=pltpu.CompilerParams(vmem_limit_bytes=56 * MB),
        cost_estimate=pl.CostEstimate(
            flops=4 * count * orients * groups * width,
            bytes_accessed=6 * count * groups * width,
            transcendentals=0,
        ),
    )(me, inv_noise, particles, references, blocks)


def softmax_kernel(*refs):
    *parts, out_ref = refs
    total = parts[0][...]
    for part in parts[1:]:
        total = total + part[...]
    highest = jnp.max(total, axis=1, keepdims=True)
    weights = jnp.exp(total - highest)
    out_ref[...] = (weights / jnp.sum(weights, axis=1, keepdims=True)).astype(BF16)


def softmax_call(parts):
    return pl.pallas_call(
        softmax_kernel,
        out_shape=jax.ShapeDtypeStruct(parts[0].shape, BF16),
        compiler_params=pltpu.CompilerParams(vmem_limit_bytes=8 * MB),
    )(*parts)


def plan_kernel(
    here_ref, dest_ref, pos_ref, addr_ref, item_ref, place_ref, hot_ref, count_ref, *, sizes
):
    step = pl.program_id(0)
    dom_size, slab_size = sizes
    owners = dom_size * slab_size
    _, units, half = pos_ref.shape
    lanes = addr_ref.shape[2]
    parts = dest_ref.shape[1] // half
    gb = units // parts
    dom_log, slab_log = (dom_size - 1).bit_length(), (slab_size - 1).bit_length()

    @pl.when(step == 0)
    def _():
        off = dest_ref[...] ^ (here_ref[0] * slab_size + here_ref[1])
        place = jnp.zeros_like(off)
        for bit in list(range(slab_log, slab_log + dom_log)) + list(range(slab_log)):
            place = place * 2 + (lax.shift_right_logical(off, bit) & 1)
        place_ref[...] = place

    owner = lax.broadcasted_iota(jnp.int32, (owners, 1), 0)
    for u in range(units):
        g, h = u // parts, u % parts
        line = place_ref[pl.ds(step * gb + g, 1), h * half : (h + 1) * half]
        hot = jnp.where(line == owner, 1.0, 0.0)
        hot_ref[u * owners : (u + 1) * owners, :] = hot.astype(BF16)
    before = lax.broadcasted_iota(jnp.int32, (half, half), 0)
    after = lax.broadcasted_iota(jnp.int32, (half, half), 1)
    upto = jnp.where(before <= after, 1.0, 0.0).astype(BF16)
    count_ref[...] = jnp.dot(hot_ref[...], upto, preferred_element_type=F32)

    exact = functools.partial(
        jnp.dot, preferred_element_type=F32, precision=lax.Precision.HIGHEST
    )
    row = lax.broadcasted_iota(jnp.int32, (owners, owners), 0)
    col = lax.broadcasted_iota(jnp.int32, (owners, owners), 1)
    below = jnp.where(row > col, 1.0, 0.0)
    row = lax.broadcasted_iota(jnp.int32, (OB, OB), 0)
    col = lax.broadcasted_iota(jnp.int32, (OB, OB), 1)
    earlier = jnp.where(row < col, 1.0, 0.0)
    lane = lax.broadcasted_iota(jnp.int32, (owners, OB), 1)
    runs = jnp.zeros((owners, OB), F32)
    for u in range(units):
        size = count_ref[u * owners : (u + 1) * owners, half - 1 : half]
        runs = jnp.where(lane == u, size, runs)
    runs = jnp.floor((runs + 7.0) * 0.125) * 8.0
    base = exact(below, runs)
    ahead = exact(runs, earlier)
    total = jnp.sum(runs, axis=1, keepdims=True)
    start = exact(below, jnp.broadcast_to(total, (owners, OB)))[:, :1]
    blocks = jnp.floor((total + (RD - 1.0)) * (1.0 / RD))
    first = exact(below, jnp.broadcast_to(blocks, (owners, OB)))[:, :1]
    shift = start + ahead - base
    used = jnp.sum(runs, axis=0, keepdims=True)

    slot = (lax.broadcasted_iota(jnp.int32, (1, lanes), 1) * 8).astype(F32)
    is_last = lax.broadcasted_iota(jnp.int32, (1, lanes), 1) == lanes - 1
    rows = units * (half + 7 * owners)
    for u in range(units):
        low, size = base[:, u : u + 1], runs[:, u : u + 1]
        hot = hot_ref[u * owners : (u + 1) * owners, :].astype(F32)
        rank = count_ref[u * owners : (u + 1) * owners, :] + (low - 1.0)
        pos_ref[0, u : u + 1, :] = jnp.sum(hot * rank, axis=0, keepdims=True).astype(jnp.int32)
        inside = (slot >= low) & (slot < low + size)
        goal = jnp.where(inside, shift[:, u : u + 1] + slot - rows, 0.0)
        goal = (jnp.sum(goal, axis=0, keepdims=True) + rows) * 0.125
        addr_ref[0, u : u + 1, :] = jnp.where(is_last, used[:, u : u + 1], goal).astype(jnp.int32)

    wide = item_ref.shape[2]
    number = lax.broadcasted_iota(jnp.int32, (1, wide), 1).astype(F32)
    inside = (number >= first) & (number < first + blocks)
    done = (number - first) * RD
    pick = lambda value: jnp.sum(jnp.where(inside, value, 0.0), axis=0, keepdims=True)
    every = lambda value: jnp.sum(
        jnp.broadcast_to(value, (owners, wide)), axis=0, keepdims=True
    )
    lines = (
        pick(jnp.broadcast_to(owner.astype(F32), (owners, wide))),
        pick((start + done) * 0.125),
        pick(total - done),
        every(blocks),
        every(total * 0.125),
    )
    for i, value in enumerate(lines):
        item_ref[0, i : i + 1, :] = value.astype(jnp.int32)


def meta_kernel(here_ref, index_ref, frac_ref, pos_ref, meta_ref):
    step = pl.program_id(0)
    _, units, half = pos_ref.shape
    parts = index_ref.shape[1] // half
    gb = units // parts
    blocks = meta_ref.shape[2]
    eighth = lax.broadcasted_iota(jnp.int32, (blocks, 1), 0)
    lane_of = lax.broadcasted_iota(jnp.int32, (OB, 1), 0) % 8
    for u in range(units):
        g, h = u // parts, u % parts
        line = pl.ds(step * gb + g, 1)
        span = slice(h * half, (h + 1) * half)
        value = index_ref[line, span].astype(F32) + frac_ref[line, span]
        coarse = value.astype(BF16).astype(F32)
        pos = pos_ref[0, u : u + 1, :]
        block = lax.shift_right_logical(pos, 3)
        here = lane_of == (pos & 7)
        spots = jnp.where(eighth == block, 1.0, 0.0).astype(BF16)
        meta = jnp.zeros((blocks, OB), F32)
        for term in (coarse, value - coarse):
            meta = meta + lax.dot_general(
                spots,
                jnp.where(here, term, 0.0).astype(BF16),
                (((1,), (1,)), ((), ())),
                preferred_element_type=F32,
            )
        meta_ref[0, u] = meta


def up_to(value, step):
    return -(-value // step) * step


def sort_sizes(orients, owners):
    slots = orients + 7 * owners
    sure = orients + 144
    blocks = up_to((sure + up_to(max(0, slots - sure), 128)) // 8, 8)
    return slots, sure, blocks


def planned(shape):
    return pl.BlockSpec((1,) + shape[1:], lambda i, here: (i,) + (0,) * (len(shape) - 1))


def plan_call(here, destination, groups, gb, mesh_sizes):
    orients = destination.shape[1]
    half = min(256, orients)
    owners = mesh_sizes[0] * mesh_sizes[1]
    steps, units = groups // gb, gb * (orients // half)
    slots, _, blocks = sort_sizes(half, owners)
    shapes = [
        (steps, units, half),
        (steps, units, up_to(blocks + 1, 128)),
        (steps, 5, up_to(owners + units * slots // RD + 8, 128)),
    ]
    return pl.pallas_call(
        functools.partial(plan_kernel, sizes=mesh_sizes),
        grid_spec=pltpu.PrefetchScalarGridSpec(
            num_scalar_prefetch=1,
            grid=(steps,),
            in_specs=[pl.BlockSpec((groups, orients), lambda i, here: (here[1], 0))],
            out_specs=[planned(shape) for shape in shapes],
            scratch_shapes=[
                pltpu.VMEM((groups, orients), jnp.int32),
                pltpu.VMEM((units * owners, half), BF16),
                pltpu.VMEM((units * owners, half), F32),
            ],
        ),
        out_shape=[jax.ShapeDtypeStruct(shape, jnp.int32) for shape in shapes],
        compiler_params=pltpu.CompilerParams(vmem_limit_bytes=60 * MB),
        cost_estimate=pl.CostEstimate(
            flops=8 * steps * units * owners * half * half,
            bytes_accessed=8 * groups * orients,
            transcendentals=0,
        ),
    )(here, destination)


def meta_call(here, row_index, fraction, pos, owners):
    steps, units, half = pos.shape
    orients = row_index.shape[1]
    groups = steps * units * half // orients
    blocks = sort_sizes(half, owners)[2]
    shape = (steps, units, blocks, OB)
    table = pl.BlockSpec((groups, orients), lambda i, here: (here[1], 0))
    return pl.pallas_call(
        meta_kernel,
        grid_spec=pltpu.PrefetchScalarGridSpec(
            num_scalar_prefetch=1,
            grid=(steps,),
            in_specs=[table, table, planned(pos.shape)],
            out_specs=planned(shape),
        ),
        out_shape=jax.ShapeDtypeStruct(shape, F32),
        compiler_params=pltpu.CompilerParams(vmem_limit_bytes=60 * MB),
        cost_estimate=pl.CostEstimate(
            flops=8 * steps * units * blocks * half * OB,
            bytes_accessed=8 * steps * units * blocks * OB,
            transcendentals=0,
        ),
    )(here, row_index, fraction, pos)


def insert_kernel(me_ref, addr_ref, item_ref, x_ref, pos_ref, meta_ref, blk_ref, *rest):
    *post_refs, send_ref, keep_ref = rest[:-10]
    post_t, spread_ref, cols_ref, slice_a, slice_b, buf_s, buf_m, volume, stage, sem = rest[-10:]
    step = pl.program_id(0)
    count = x_ref.shape[0]
    orients = post_t.shape[0]
    units, half = pos_ref.shape[1:]
    parts = orients // half
    gb = units // parts
    width = x_ref.shape[1] // gb
    share = count // len(post_refs)
    lanes = addr_ref.shape[2]

    @pl.when(step == 0)
    def _():
        volume[...] = jnp.zeros_like(volume)
        me = me_ref[0]
        spread_columns(blk_ref, cols_ref)
        for k, post_ref in enumerate(post_refs):
            at = pl.multiple_of((me ^ k) * share, share)
            post = post_ref[...].astype(F32)
            first = cols_ref[0, pl.ds(at, share), :]
            second = cols_ref[1, pl.ds(at, share), :]
            for b in range(orients // OB):
                spread = jnp.where(
                    first == b, post[:, :OB], jnp.where(second == b, post[:, OB:], 0.0)
                )
                spread_ref[pl.ds(at, share), b * OB : (b + 1) * OB] = spread
        for b in range(orients // OB):
            post_t[b * OB : (b + 1) * OB] = spread_ref[:, b * OB : (b + 1) * OB].T.astype(BF16)

    tail = pl.ds(pl.multiple_of(item_ref[0, 4, 0] * 8, 8), RD)
    buf_s[tail, :] = jnp.zeros((RD, width), F32)
    one, none = jnp.bfloat16(1.0), jnp.bfloat16(0.0)
    slots, sure, _ = sort_sizes(half, volume.shape[0] // RD)
    per = slice_a.shape[1] // width
    number = gb // per

    def slices(q, dst_ref):
        at = pl.ds(pl.multiple_of(q * (per * width), per * width), per * width)
        value = jnp.dot(post_t[...], x_ref[:, at], preferred_element_type=F32)
        dst_ref[...] = value.astype(BF16)

    def emit(u, piece, base, size):
        pos = pos_ref[0, pl.ds(u, 1), :]
        order = []
        for at in range(0, size, 128):
            high = min(128, size - at)
            slot = lax.broadcasted_iota(jnp.int32, (high, half), 0).astype(F32).astype(BF16)
            near = jnp.clip(pos - (base + at), -1, 128).astype(F32).astype(BF16)
            order.append(jnp.where(slot == near, one, none))
        order = jnp.concatenate(order, axis=0)
        rows = jnp.dot(order, piece, preferred_element_type=F32)
        for i in range(size // 8):
            at = addr_ref[0, u, base // 8 + i]
            buf_s[pl.ds(pl.multiple_of(at * 8, 8), 8), :] = rows[8 * i : 8 * i + 8]
            buf_m[pl.ds(at, 1), :] = meta_ref[0, u, pl.ds(base // 8 + i, 1), :]

    def sort(q, src_ref):
        for g in range(per):
            for h in range(parts):
                piece = src_ref[h * half : (h + 1) * half, g * width : (g + 1) * width]
                emit((q * per + g) * parts + h, piece, 0, sure)

    def rest_of(q, src_ref):
        for g in range(per):
            for h in range(parts):
                u = (q * per + g) * parts + h

                def more(e, c, u=u, g=g, h=h):
                    piece = src_ref[h * half : (h + 1) * half, g * width : (g + 1) * width]
                    emit(u, piece, sure + e * 128, 128)
                    return c

                used = addr_ref[0, u, lanes - 1]
                lax.fori_loop(0, lax.div(jnp.maximum(used - sure, 0) + 127, 128), more, 0)

    def most_used(q):
        most = addr_ref[0, q * per * parts, lanes - 1]
        for u in range(1, per * parts):
            most = jnp.maximum(most, addr_ref[0, q * per * parts + u, lanes - 1])
        return most

    def two(j, carry):
        q = j * 2
        sort(q, slice_a)
        slices(q + 1, slice_b)

        @pl.when(most_used(q) > sure)
        def _():
            rest_of(q, slice_a)

        sort(q + 1, slice_b)
        slices(jnp.minimum(q + 2, number - 1), slice_a)

        @pl.when(most_used(q + 1) > sure)
        def _():
            rest_of(q + 1, slice_b)

        return carry

    slices(0, slice_a)
    lax.fori_loop(0, number // 2, two, 0)
    if number % 2:
        sort(number - 1, slice_a)
        rest_of(number - 1, slice_a)

    bins = lax.broadcasted_iota(jnp.int32, (RD, RD), 0).astype(F32).astype(BF16)
    side = RD // 2
    at_lane = lax.broadcasted_iota(jnp.int32, (side // 8, side), 1) // 8
    own_lane = at_lane == lax.broadcasted_iota(jnp.int32, (side // 8, side), 0)
    line = lax.broadcasted_iota(jnp.int32, (1, RD), 1)
    together = 8

    def some_items(q, carry):
        for u in range(together):
            j = q * together + u
            owner, at, left = item_ref[0, 0, j], item_ref[0, 1, j], item_ref[0, 2, j]
            places = [
                jnp.sum(
                    jnp.where(own_lane, buf_m[pl.ds(at + h * (side // 8), side // 8), :], 0.0),
                    axis=0,
                    keepdims=True,
                )
                for h in range(2)
            ]
            place = jnp.where(line < left, jnp.concatenate(places, axis=1), -9.0)
            whole = jnp.floor(place)
            apart = (bins - whole.astype(BF16)) - (place - whole).astype(BF16)
            weights = jnp.maximum(one - jnp.abs(apart), none)
            values = buf_s[pl.ds(pl.multiple_of(at * 8, 8), RD), :].astype(BF16)
            goal = pl.ds(pl.multiple_of(owner * RD, RD), RD)
            volume[goal, :] += jnp.dot(weights, values, preferred_element_type=F32)
        return carry

    count_items = lax.div(item_ref[0, 3, 0] + together - 1, together)
    lax.fori_loop(0, count_items, some_items, 0)

    @pl.when(step == pl.num_programs(0) - 1)
    def _():
        half = keep_ref.shape[0]
        tile = stage.shape[1]
        copies = []
        number = 0
        for base, out_ref in ((half, send_ref), (0, keep_ref)):
            for at in range(0, half, tile):
                slot = number % 2
                if number >= 2:
                    copies[number - 2].wait()
                stage[slot] = volume[base + at : base + at + tile, :].astype(BF16)
                copy = pltpu.make_async_copy(
                    stage.at[slot], out_ref.at[pl.ds(at, tile)], sem.at[slot]
                )
                copy.start()
                copies.append(copy)
                number += 1
        for copy in copies[-2:]:
            copy.wait()


def group_pair(gb):
    return 2 if gb % 4 == 0 else 1


def insert_block(groups, orients, owners, count, width):
    half = min(256, orients)
    slots, _, blocks = sort_sizes(half, owners)
    room = 52 * MB - owners * RD * width * 4
    best = 1
    for gb in range(1, groups + 1):
        units = gb * (orients // half)
        rows = units * slots + RD + 8
        need = rows * (width * 4 + OB // 2) + 4 * count * gb * width + units * blocks * OB * 8
        if groups % gb == 0 and need <= room:
            best = gb
    return best


def insert_call(me, addr, items, flat, pos, meta, blocks, posts, orients, owners):
    count, length = flat.shape
    steps, units, half = pos.shape
    gb = units * half // orients
    width = length // (steps * gb)
    total = owners * RD
    share = posts[0].shape[0]
    rows = units * sort_sizes(half, owners)[0] + RD + 8
    smem = pl.BlockSpec(memory_space=pltpu.SMEM)
    block = lambda shape, **kw: pl.BlockSpec(
        (1,) + shape[1:], lambda i: (i,) + (0,) * (len(shape) - 1), **kw
    )
    return pl.pallas_call(
        insert_kernel,
        grid=(steps,),
        out_shape=[jax.ShapeDtypeStruct((total // 2, width), BF16)] * 2,
        in_specs=[
            smem,
            block(addr.shape, memory_space=pltpu.SMEM),
            block(items.shape, memory_space=pltpu.SMEM),
            pl.BlockSpec((count, gb * width), lambda i: (0, i)),
            block(pos.shape),
            block(meta.shape),
            pl.BlockSpec((2, count), lambda i: (0, 0)),
        ]
        + [pl.BlockSpec((share, 2 * OB), lambda i: (0, 0))] * len(posts),
        out_specs=[pl.BlockSpec(memory_space=pl.ANY)] * 2,
        scratch_shapes=[
            pltpu.VMEM((orients, count), BF16),
            pltpu.VMEM((count, orients), F32),
            pltpu.VMEM((2, count, OB), F32),
            pltpu.VMEM((orients, group_pair(gb) * width), BF16),
            pltpu.VMEM((orients, group_pair(gb) * width), BF16),
            pltpu.VMEM((rows, width), F32),
            pltpu.VMEM((rows // 8, OB), F32),
            pltpu.VMEM((total, width), F32),
            pltpu.VMEM((2, 512, width), BF16),
            pltpu.SemaphoreType.DMA((2,)),
        ],
        compiler_params=pltpu.CompilerParams(vmem_limit_bytes=62 * MB),
        cost_estimate=pl.CostEstimate(
            flops=8 * count * orients * length,
            bytes_accessed=2 * count * length,
            transcendentals=0,
        ),
    )(me, addr, items, flat, pos, meta, blocks, *posts)


def flip(value, axis, bit):
    size = lax.axis_size(axis)
    return lax.ppermute(value, axis, [(i, i ^ bit) for i in range(size)])


def shards(particles, blocks, references, inv_noise, destination, row_index, fraction):
    groups, width = particles.shape[1:]
    orients = references.shape[0]
    dom_size = lax.axis_size("dom")
    slab_size = lax.axis_size("slab")
    devices = dom_size * slab_size
    dom_pos = lax.axis_index("dom")
    slab_pos = lax.axis_index("slab")
    here = jnp.stack([dom_pos, slab_pos]).astype(jnp.int32)
    slab_me = here[1:]
    dom_bits = [1 << i for i in range((dom_size - 1).bit_length())]
    slab_bits = [1 << i for i in range((slab_size - 1).bit_length())]

    blocks = blocks.T
    flat, *scores = score_call(slab_me, inv_noise, particles, references, blocks, slab_size)
    gb = insert_block(groups, orients, devices, particles.shape[0], width)
    here, own = lax.optimization_barrier((here, scores[0]))
    plan = plan_call(here, destination, groups, gb, (dom_size, slab_size))
    own, *plan = lax.optimization_barrier((own, *plan))
    pos, addr, items = plan
    parts = [own] + [flip(scores[k], "slab", k) for k in range(1, slab_size)]
    post = softmax_call(parts)
    post, pos = lax.optimization_barrier((post, pos))
    meta = meta_call(here, row_index, fraction, pos, devices)
    posts = [post] + [flip(post, "slab", k) for k in range(1, slab_size)]
    send, keep = insert_call(
        slab_me, addr, items, flat, pos, meta, blocks, posts, orients, devices
    )

    def merge(kept, got):
        return kept.astype(F32) + got.astype(F32)

    total = merge(keep, flip(send, "dom", dom_bits[0]))
    rest = dom_bits[1:]
    total = total.reshape((2,) * len(rest) + (slab_size * RD, width))
    halves = []
    for part, order in ((0, rest), (1, rest[::-1])):
        value = total[..., part * OB : (part + 1) * OB]
        axes = list(rest)
        for bit in order:
            axis = axes.index(bit)
            axes.pop(axis)
            kept = lax.index_in_dim(value, 0, axis, keepdims=False)
            sent = lax.index_in_dim(value, 1, axis, keepdims=False)
            value = merge(kept, flip(sent.astype(BF16), "dom", bit))
        halves.append(value)
    value = jnp.concatenate(halves, axis=1)
    for bit in slab_bits:
        near, far = jnp.split(value, 2, axis=0)
        value = merge(near, flip(far.astype(BF16), "slab", bit))
    volume = value

    own = volume.astype(BF16)
    columns = []
    for part, order in ((0, rest), (1, rest[::-1])):
        value = own[:, part * OB : (part + 1) * OB]
        done = []
        for bit in order:
            got = flip(value, "dom", bit)
            axis = len([b for b in done if b > bit])
            done.append(bit)
            mine_low = dom_pos & bit == 0
            value = jnp.where(
                mine_low, jnp.stack([value, got], axis), jnp.stack([got, value], axis)
            )
        columns.append(value)
    value = jnp.concatenate(columns, axis=-1)
    got = flip(value, "dom", dom_bits[0])
    value = jnp.where(
        dom_pos & dom_bits[0] == 0,
        jnp.stack([value, got], len(rest)),
        jnp.stack([got, value], len(rest)),
    )
    return volume, value.reshape(dom_size * RD, width)


def solution(mesh):
    return jax.shard_map(
        shards,
        mesh=mesh,
        in_specs=(
            P("dom", "slab", None),
            P("dom", None),
            P(None, "slab", None),
            P("slab"),
            P(),
            P(),
            P(),
        ),
        out_specs=(P(("dom", "slab"), None), P(None, "slab")),
        check_vma=False,
    )
```

```python
import functools

import jax
import jax.numpy as jnp
from jax import lax
from jax.experimental import pallas as pl
from jax.experimental.pallas import tpu as pltpu
from jax.sharding import PartitionSpec as P

OB = 128
RD = 256
MB = 2**20
F32 = jnp.float32
BF16 = jnp.bfloat16


def group_block(groups):
    return 16 if groups % 16 == 0 else 8


def spread_columns(blk_ref, cols_ref):
    count = blk_ref.shape[1]
    for j in range(2):
        for at in range(0, count, OB):
            line = blk_ref[j : j + 1, at : at + OB].astype(F32)
            cols_ref[j, at : at + OB, :] = jnp.broadcast_to(line, (OB, OB)).T


def score_kernel(me_ref, noise_ref, x_ref, r_ref, blk_ref, flat_ref, *rest):
    *out_refs, w_ref, acc_ref, perm_ref, cols_ref = rest
    step = pl.program_id(0)
    particles, gb, width = x_ref.shape
    orients = r_ref.shape[0]
    side = 16 * gb

    @pl.when(step == 0)
    def _():
        row = lax.broadcasted_iota(jnp.int32, (side, side), 0)
        col = lax.broadcasted_iota(jnp.int32, (side, side), 1)
        same = ((row // 16) == (col % gb)) & ((row % 16) == (col // gb))
        perm_ref[...] = jnp.where(same, 1.0, 0.0).astype(BF16)
        acc_ref[...] = jnp.zeros_like(acc_ref)
        spread_columns(blk_ref, cols_ref)

    perm = perm_ref[...]

    def regroup(src_ref, dst_ref, scaled, first, number):
        at = pl.multiple_of(first * 16, 16)
        if not scaled:
            for t in range(number):
                turned = jnp.swapaxes(src_ref[pl.ds(at + 16 * t, 16)], 0, 1)
                for g in range(gb):
                    dst_ref[pl.ds(at + 16 * t, 16), g * width : (g + 1) * width] = turned[g]
            return
        tile = src_ref[pl.ds(at, 16 * number)].reshape(number, side, width)
        wide = jnp.concatenate([tile[t] for t in range(number)], axis=1)
        moved = jnp.dot(perm, wide, preferred_element_type=F32)
        for g in range(gb):
            for t in range(number):
                part = moved[g * 16 : (g + 1) * 16, t * width : (t + 1) * width]
                if scaled:
                    part = part * noise_ref[step * gb + g]
                dst_ref[pl.ds(at + 16 * t, 16), g * width : (g + 1) * width] = part.astype(BF16)

    def tiles(i, carry):
        regroup(r_ref, w_ref, True, i * 4, 4)
        regroup(x_ref, flat_ref, False, i * 4, 4)
        return carry

    def more_tiles(src_ref, dst_ref, scaled):
        def body(i, carry):
            regroup(src_ref, dst_ref, scaled, i, 1)
            return carry

        lax.fori_loop(both * 4, src_ref.shape[0] // 16, body, 0)

    both = min(particles, orients) // 64
    lax.fori_loop(0, both, tiles, 0, unroll=2)
    more_tiles(r_ref, w_ref, True)
    more_tiles(x_ref, flat_ref, False)
    acc_ref[...] += lax.dot_general(
        flat_ref[...], w_ref[...], (((1,), (1,)), ((), ())), preferred_element_type=F32
    )

    @pl.when(step == pl.num_programs(0) - 1)
    def _():
        me = me_ref[0]
        share = particles // len(out_refs)
        for k, out_ref in enumerate(out_refs):
            at = pl.multiple_of((me ^ k) * share, share)
            for j in range(2):
                wanted = cols_ref[j, pl.ds(at, share), :]
                chosen = jnp.zeros((share, OB), F32)
                for b in range(orients // OB):
                    value = acc_ref[pl.ds(at, share), b * OB : (b + 1) * OB]
                    chosen = jnp.where(wanted == b, value, chosen)
                out_ref[:, j * OB : (j + 1) * OB] = chosen


def score_call(me, inv_noise, particles, references, blocks, slab_size):
    count, groups, width = particles.shape
    orients = references.shape[0]
    gb = group_block(groups)
    side = 16 * gb
    share = count // slab_size
    smem = pl.BlockSpec(memory_space=pltpu.SMEM)
    return pl.pallas_call(
        score_kernel,
        grid=(groups // gb,),
        out_shape=[jax.ShapeDtypeStruct((count, groups * width), BF16)]
        + [jax.ShapeDtypeStruct((share, 2 * OB), F32)] * slab_size,
        in_specs=[
            smem,
            smem,
            pl.BlockSpec((count, gb, width), lambda i: (0, i, 0)),
            pl.BlockSpec((orients, gb, width), lambda i: (0, i, 0)),
            pl.BlockSpec((2, count), lambda i: (0, 0)),
        ],
        out_specs=[pl.BlockSpec((count, gb * width), lambda i: (0, i))]
        + [pl.BlockSpec((share, 2 * OB), lambda i: (0, 0))] * slab_size,
        scratch_shapes=[
            pltpu.VMEM((orients, gb * width), BF16),
            pltpu.VMEM((count, orients), F32),
            pltpu.VMEM((side, side), BF16),
            pltpu.VMEM((2, count, OB), F32),
        ],
        compiler_params=pltpu.CompilerParams(vmem_limit_bytes=56 * MB),
        cost_estimate=pl.CostEstimate(
            flops=4 * count * orients * groups * width,
            bytes_accessed=6 * count * groups * width,
            transcendentals=0,
        ),
    )(me, inv_noise, particles, references, blocks)


def softmax_kernel(*refs):
    *parts, out_ref = refs
    total = parts[0][...]
    for part in parts[1:]:
        total = total + part[...]
    highest = jnp.max(total, axis=1, keepdims=True)
    weights = jnp.exp(total - highest)
    out_ref[...] = (weights / jnp.sum(weights, axis=1, keepdims=True)).astype(BF16)


def softmax_call(parts):
    return pl.pallas_call(
        softmax_kernel,
        out_shape=jax.ShapeDtypeStruct(parts[0].shape, BF16),
        compiler_params=pltpu.CompilerParams(vmem_limit_bytes=8 * MB),
    )(*parts)


def plan_kernel(
    here_ref, dest_ref, pos_ref, addr_ref, item_ref, place_ref, hot_ref, count_ref, *, sizes
):
    step = pl.program_id(0)
    dom_size, slab_size = sizes
    owners = dom_size * slab_size
    _, units, half = pos_ref.shape
    lanes = addr_ref.shape[2]
    parts = dest_ref.shape[1] // half
    gb = units // parts
    dom_log, slab_log = (dom_size - 1).bit_length(), (slab_size - 1).bit_length()

    @pl.when(step == 0)
    def _():
        off = dest_ref[...] ^ (here_ref[0] * slab_size + here_ref[1])
        place = jnp.zeros_like(off)
        for bit in list(range(slab_log, slab_log + dom_log)) + list(range(slab_log)):
            place = place * 2 + (lax.shift_right_logical(off, bit) & 1)
        place_ref[...] = place

    owner = lax.broadcasted_iota(jnp.int32, (owners, 1), 0)
    for u in range(units):
        g, h = u // parts, u % parts
        line = place_ref[pl.ds(step * gb + g, 1), h * half : (h + 1) * half]
        hot = jnp.where(line == owner, 1.0, 0.0)
        hot_ref[u * owners : (u + 1) * owners, :] = hot.astype(BF16)
    before = lax.broadcasted_iota(jnp.int32, (half, half), 0)
    after = lax.broadcasted_iota(jnp.int32, (half, half), 1)
    upto = jnp.where(before <= after, 1.0, 0.0).astype(BF16)
    count_ref[...] = jnp.dot(hot_ref[...], upto, preferred_element_type=F32)

    exact = functools.partial(
        jnp.dot, preferred_element_type=F32, precision=lax.Precision.HIGHEST
    )
    row = lax.broadcasted_iota(jnp.int32, (owners, owners), 0)
    col = lax.broadcasted_iota(jnp.int32, (owners, owners), 1)
    below = jnp.where(row > col, 1.0, 0.0)
    row = lax.broadcasted_iota(jnp.int32, (OB, OB), 0)
    col = lax.broadcasted_iota(jnp.int32, (OB, OB), 1)
    earlier = jnp.where(row < col, 1.0, 0.0)
    lane = lax.broadcasted_iota(jnp.int32, (owners, OB), 1)
    runs = jnp.zeros((owners, OB), F32)
    for u in range(units):
        size = count_ref[u * owners : (u + 1) * owners, half - 1 : half]
        runs = jnp.where(lane == u, size, runs)
    runs = jnp.floor((runs + 7.0) * 0.125) * 8.0
    base = exact(below, runs)
    ahead = exact(runs, earlier)
    total = jnp.sum(runs, axis=1, keepdims=True)
    start = exact(below, jnp.broadcast_to(total, (owners, OB)))[:, :1]
    blocks = jnp.floor((total + (2 * RD - 1.0)) * (0.5 / RD))
    first = exact(below, jnp.broadcast_to(blocks, (owners, OB)))[:, :1]
    shift = start + ahead - base
    used = jnp.sum(runs, axis=0, keepdims=True)

    slot = (lax.broadcasted_iota(jnp.int32, (1, lanes), 1) * 8).astype(F32)
    is_last = lax.broadcasted_iota(jnp.int32, (1, lanes), 1) == lanes - 1
    rows = units * (half + 7 * owners)
    for u in range(units):
        low, size = base[:, u : u + 1], runs[:, u : u + 1]
        hot = hot_ref[u * owners : (u + 1) * owners, :].astype(F32)
        rank = count_ref[u * owners : (u + 1) * owners, :] + (low - 1.0)
        pos_ref[0, u : u + 1, :] = jnp.sum(hot * rank, axis=0, keepdims=True).astype(jnp.int32)
        inside = (slot >= low) & (slot < low + size)
        goal = jnp.where(inside, shift[:, u : u + 1] + slot - rows, 0.0)
        goal = (jnp.sum(goal, axis=0, keepdims=True) + rows) * 0.125
        addr_ref[0, u : u + 1, :] = jnp.where(is_last, used[:, u : u + 1], goal).astype(jnp.int32)

    wide = item_ref.shape[2]
    number = lax.broadcasted_iota(jnp.int32, (1, wide), 1).astype(F32)
    inside = (number >= first) & (number < first + blocks)
    done = (number - first) * (2 * RD)
    pick = lambda value: jnp.sum(jnp.where(inside, value, 0.0), axis=0, keepdims=True)
    every = lambda value: jnp.sum(
        jnp.broadcast_to(value, (owners, wide)), axis=0, keepdims=True
    )
    lines = (
        pick(jnp.broadcast_to(owner.astype(F32), (owners, wide))),
        pick((start + done) * 0.125),
        pick(total - done),
        every(blocks),
        every(total * 0.125),
    )
    for i, value in enumerate(lines):
        item_ref[0, i : i + 1, :] = value.astype(jnp.int32)


def meta_kernel(here_ref, index_ref, frac_ref, pos_ref, addr_ref, table_ref, meta_ref):
    step = pl.program_id(0)
    _, units, half = pos_ref.shape
    parts = index_ref.shape[1] // half
    gb = units // parts
    blocks = meta_ref.shape[1]
    low = lambda value: value.astype(F32).astype(BF16)
    eighth = low(lax.broadcasted_iota(jnp.int32, (blocks, half), 0))
    lane_of = low(lax.broadcasted_iota(jnp.int32, (OB, half), 0) % 8)
    one, none = jnp.bfloat16(1.0), jnp.bfloat16(0.0)
    for u in range(units):
        g, h = u // parts, u % parts
        line = pl.ds(step * gb + g, 1)
        span = slice(h * half, (h + 1) * half)
        pos = pos_ref[0, u : u + 1, :]
        here = lane_of == low(pos & 7)
        spots = jnp.where(eighth == low(lax.shift_right_logical(pos, 3)), one, none)
        terms = [
            jnp.where(here, low(index_ref[line, span]), none),
            jnp.where(here, low(frac_ref[line, span]), none),
        ]
        meta_ref[u] = lax.dot_general(
            jnp.concatenate([spots, spots], axis=1),
            jnp.concatenate(terms, axis=1),
            (((1,), (1,)), ((), ())),
            preferred_element_type=F32,
        )

    def move(u, carry):
        for i in range(blocks):
            table_ref[0, pl.ds(addr_ref[0, u, i], 1), :] = meta_ref[u, i : i + 1, :]
        return carry

    lax.fori_loop(0, units, move, 0)


def up_to(value, step):
    return -(-value // step) * step


def sort_sizes(orients, owners):
    slots = orients + 7 * owners
    sure = orients + 144
    blocks = up_to((sure + up_to(max(0, slots - sure), 128)) // 8, 8)
    return slots, sure, blocks


def planned(shape):
    return pl.BlockSpec((1,) + shape[1:], lambda i, here: (i,) + (0,) * (len(shape) - 1))


def plan_call(here, destination, groups, gb, mesh_sizes):
    orients = destination.shape[1]
    half = min(256, orients)
    owners = mesh_sizes[0] * mesh_sizes[1]
    steps, units = groups // gb, gb * (orients // half)
    slots, _, blocks = sort_sizes(half, owners)
    shapes = [
        (steps, units, half),
        (steps, units, up_to(blocks + 1, 128)),
        (steps, 5, up_to(owners + units * slots // RD + 8, 128)),
    ]
    return pl.pallas_call(
        functools.partial(plan_kernel, sizes=mesh_sizes),
        grid_spec=pltpu.PrefetchScalarGridSpec(
            num_scalar_prefetch=1,
            grid=(steps,),
            in_specs=[pl.BlockSpec((groups, orients), lambda i, here: (here[1], 0))],
            out_specs=[planned(shape) for shape in shapes],
            scratch_shapes=[
                pltpu.VMEM((groups, orients), jnp.int32),
                pltpu.VMEM((units * owners, half), BF16),
                pltpu.VMEM((units * owners, half), F32),
            ],
        ),
        out_shape=[jax.ShapeDtypeStruct(shape, jnp.int32) for shape in shapes],
        compiler_params=pltpu.CompilerParams(vmem_limit_bytes=60 * MB),
        cost_estimate=pl.CostEstimate(
            flops=8 * steps * units * owners * half * half,
            bytes_accessed=8 * groups * orients,
            transcendentals=0,
        ),
    )(here, destination)


def table_rows(units, half, owners):
    return up_to((units * sort_sizes(half, owners)[0] + 2 * RD + 8) // 8, 8)


def meta_call(here, row_index, fraction, pos, addr, owners):
    steps, units, half = pos.shape
    orients = row_index.shape[1]
    groups = steps * units * half // orients
    blocks = sort_sizes(half, owners)[2]
    shape = (steps, table_rows(units, half, owners), OB)
    table = pl.BlockSpec((groups, orients), lambda i, here: (here[1], 0))
    return pl.pallas_call(
        meta_kernel,
        grid_spec=pltpu.PrefetchScalarGridSpec(
            num_scalar_prefetch=1,
            grid=(steps,),
            in_specs=[
                table,
                table,
                planned(pos.shape),
                pl.BlockSpec(
                    (1,) + addr.shape[1:], lambda i, here: (i, 0, 0), memory_space=pltpu.SMEM
                ),
            ],
            out_specs=planned(shape),
            scratch_shapes=[pltpu.VMEM((units, blocks, OB), F32)],
        ),
        out_shape=jax.ShapeDtypeStruct(shape, F32),
        compiler_params=pltpu.CompilerParams(vmem_limit_bytes=60 * MB),
        cost_estimate=pl.CostEstimate(
            flops=8 * steps * units * blocks * half * OB,
            bytes_accessed=8 * steps * units * blocks * OB,
            transcendentals=0,
        ),
    )(here, row_index, fraction, pos, addr)


def insert_kernel(me_ref, addr_ref, item_ref, x_ref, pos_ref, meta_ref, blk_ref, *rest):
    *post_refs, send_ref, keep_ref = rest[:-9]
    post_t, spread_ref, cols_ref, slice_a, slice_b, buf_s, volume, stage, sem = rest[-9:]
    step = pl.program_id(0)
    count = x_ref.shape[0]
    orients = post_t.shape[0]
    units, half = pos_ref.shape[1:]
    parts = orients // half
    gb = units // parts
    width = x_ref.shape[1] // gb
    share = count // len(post_refs)
    lanes = addr_ref.shape[2]

    @pl.when(step == 0)
    def _():
        volume[...] = jnp.zeros_like(volume)
        me = me_ref[0]
        spread_columns(blk_ref, cols_ref)
        for k, post_ref in enumerate(post_refs):
            at = pl.multiple_of((me ^ k) * share, share)
            post = post_ref[...].astype(F32)
            first = cols_ref[0, pl.ds(at, share), :]
            second = cols_ref[1, pl.ds(at, share), :]
            for b in range(orients // OB):
                spread = jnp.where(
                    first == b, post[:, :OB], jnp.where(second == b, post[:, OB:], 0.0)
                )
                spread_ref[pl.ds(at, share), b * OB : (b + 1) * OB] = spread
        for b in range(orients // OB):
            post_t[b * OB : (b + 1) * OB] = spread_ref[:, b * OB : (b + 1) * OB].T.astype(BF16)

    tail = pl.ds(pl.multiple_of(item_ref[0, 4, 0] * 8, 8), 2 * RD)
    buf_s[tail, :] = jnp.zeros((2 * RD, width), F32)
    one, none = jnp.bfloat16(1.0), jnp.bfloat16(0.0)
    slots, sure, _ = sort_sizes(half, volume.shape[0] // RD)
    per = slice_a.shape[1] // width
    number = gb // per

    def slices(q, dst_ref):
        at = pl.ds(pl.multiple_of(q * (per * width), per * width), per * width)
        value = jnp.dot(post_t[...], x_ref[:, at], preferred_element_type=F32)
        dst_ref[...] = value.astype(BF16)

    def emit(u, piece, base, size):
        pos = pos_ref[0, pl.ds(u, 1), :]
        order = []
        for at in range(0, size, 128):
            high = min(128, size - at)
            slot = lax.broadcasted_iota(jnp.int32, (high, half), 0).astype(F32).astype(BF16)
            near = jnp.clip(pos - (base + at), -1, 128).astype(F32).astype(BF16)
            order.append(jnp.where(slot == near, one, none))
        order = jnp.concatenate(order, axis=0)
        rows = jnp.dot(order, piece, preferred_element_type=F32)
        for i in range(size // 8):
            at = addr_ref[0, u, base // 8 + i]
            buf_s[pl.ds(pl.multiple_of(at * 8, 8), 8), :] = rows[8 * i : 8 * i + 8]

    def sort(q, src_ref):
        for g in range(per):
            for h in range(parts):
                piece = src_ref[h * half : (h + 1) * half, g * width : (g + 1) * width]
                emit((q * per + g) * parts + h, piece, 0, sure)

    def rest_of(q, src_ref):
        for g in range(per):
            for h in range(parts):
                u = (q * per + g) * parts + h

                def more(e, c, u=u, g=g, h=h):
                    piece = src_ref[h * half : (h + 1) * half, g * width : (g + 1) * width]
                    emit(u, piece, sure + e * 128, 128)
                    return c

                used = addr_ref[0, u, lanes - 1]
                lax.fori_loop(0, lax.div(jnp.maximum(used - sure, 0) + 127, 128), more, 0)

    def most_used(q):
        most = addr_ref[0, q * per * parts, lanes - 1]
        for u in range(1, per * parts):
            most = jnp.maximum(most, addr_ref[0, q * per * parts + u, lanes - 1])
        return most

    def two(j, carry):
        q = j * 2
        sort(q, slice_a)
        slices(q + 1, slice_b)

        @pl.when(most_used(q) > sure)
        def _():
            rest_of(q, slice_a)

        sort(q + 1, slice_b)
        slices(jnp.minimum(q + 2, number - 1), slice_a)

        @pl.when(most_used(q + 1) > sure)
        def _():
            rest_of(q + 1, slice_b)

        return carry

    slices(0, slice_a)
    lax.fori_loop(0, number // 2, two, 0)
    if number % 2:
        sort(number - 1, slice_a)
        rest_of(number - 1, slice_a)

    bins = lax.broadcasted_iota(jnp.int32, (RD, 2 * RD), 0).astype(F32).astype(BF16)
    side = RD // 2
    at_lane = lax.broadcasted_iota(jnp.int32, (side // 8, side), 1) // 8
    own_lane = at_lane == lax.broadcasted_iota(jnp.int32, (side // 8, side), 0)
    line = lax.broadcasted_iota(jnp.int32, (1, 2 * RD), 1)
    together = 4

    def some_items(q, carry):
        for u in range(together):
            j = q * together + u
            owner, at, left = item_ref[0, 0, j], item_ref[0, 1, j], item_ref[0, 2, j]
            places = [
                jnp.sum(
                    jnp.where(own_lane, meta_ref[0, pl.ds(at + h * (side // 8), side // 8), :], 0.0),
                    axis=0,
                    keepdims=True,
                )
                for h in range(4)
            ]
            place = jnp.where(line < left, jnp.concatenate(places, axis=1), -9.0)
            whole = jnp.floor(place)
            apart = (bins - whole.astype(BF16)) - (place - whole).astype(BF16)
            weights = jnp.maximum(one - jnp.abs(apart), none)
            values = buf_s[pl.ds(pl.multiple_of(at * 8, 8), 2 * RD), :].astype(BF16)
            goal = pl.ds(pl.multiple_of(owner * RD, RD), RD)
            volume[goal, :] += jnp.dot(weights, values, preferred_element_type=F32)
        return carry

    count_items = lax.div(item_ref[0, 3, 0] + together - 1, together)
    lax.fori_loop(0, count_items, some_items, 0)

    @pl.when(step == pl.num_programs(0) - 1)
    def _():
        half = keep_ref.shape[0]
        tile = stage.shape[1]
        copies = []
        number = 0
        for base, out_ref in ((half, send_ref), (0, keep_ref)):
            for at in range(0, half, tile):
                slot = number % 2
                if number >= 2:
                    copies[number - 2].wait()
                stage[slot] = volume[base + at : base + at + tile, :].astype(BF16)
                copy = pltpu.make_async_copy(
                    stage.at[slot], out_ref.at[pl.ds(at, tile)], sem.at[slot]
                )
                copy.start()
                copies.append(copy)
                number += 1
        for copy in copies[-2:]:
            copy.wait()


def group_pair(gb):
    return 2 if gb % 4 == 0 else 1


def insert_block(groups, orients, owners, count, width):
    half = min(256, orients)
    slots, _, blocks = sort_sizes(half, owners)
    room = 52 * MB - owners * RD * width * 4
    best = 1
    for gb in range(1, groups + 1):
        units = gb * (orients // half)
        rows = units * slots + 2 * RD + 8
        need = rows * (width * 4 + OB) + 4 * count * gb * width
        if groups % gb == 0 and need <= room:
            best = gb
    return best


def insert_call(me, addr, items, flat, pos, meta, blocks, posts, orients, owners):
    count, length = flat.shape
    steps, units, half = pos.shape
    gb = units * half // orients
    width = length // (steps * gb)
    total = owners * RD
    share = posts[0].shape[0]
    rows = units * sort_sizes(half, owners)[0] + 2 * RD + 8
    smem = pl.BlockSpec(memory_space=pltpu.SMEM)
    block = lambda shape, **kw: pl.BlockSpec(
        (1,) + shape[1:], lambda i: (i,) + (0,) * (len(shape) - 1), **kw
    )
    return pl.pallas_call(
        insert_kernel,
        grid=(steps,),
        out_shape=[jax.ShapeDtypeStruct((total // 2, width), BF16)] * 2,
        in_specs=[
            smem,
            block(addr.shape, memory_space=pltpu.SMEM),
            block(items.shape, memory_space=pltpu.SMEM),
            pl.BlockSpec((count, gb * width), lambda i: (0, i)),
            block(pos.shape),
            block(meta.shape),
            pl.BlockSpec((2, count), lambda i: (0, 0)),
        ]
        + [pl.BlockSpec((share, 2 * OB), lambda i: (0, 0))] * len(posts),
        out_specs=[pl.BlockSpec(memory_space=pl.ANY)] * 2,
        scratch_shapes=[
            pltpu.VMEM((orients, count), BF16),
            pltpu.VMEM((count, orients), F32),
            pltpu.VMEM((2, count, OB), F32),
            pltpu.VMEM((orients, group_pair(gb) * width), BF16),
            pltpu.VMEM((orients, group_pair(gb) * width), BF16),
            pltpu.VMEM((rows, width), F32),
            pltpu.VMEM((total, width), F32),
            pltpu.VMEM((2, 512, width), BF16),
            pltpu.SemaphoreType.DMA((2,)),
        ],
        compiler_params=pltpu.CompilerParams(vmem_limit_bytes=62 * MB),
        cost_estimate=pl.CostEstimate(
            flops=8 * count * orients * length,
            bytes_accessed=2 * count * length,
            transcendentals=0,
        ),
    )(me, addr, items, flat, pos, meta, blocks, *posts)


def flip(value, axis, bit):
    size = lax.axis_size(axis)
    return lax.ppermute(value, axis, [(i, i ^ bit) for i in range(size)])


def shards(particles, blocks, references, inv_noise, destination, row_index, fraction):
    groups, width = particles.shape[1:]
    orients = references.shape[0]
    dom_size = lax.axis_size("dom")
    slab_size = lax.axis_size("slab")
    devices = dom_size * slab_size
    dom_pos = lax.axis_index("dom")
    slab_pos = lax.axis_index("slab")
    here = jnp.stack([dom_pos, slab_pos]).astype(jnp.int32)
    slab_me = here[1:]
    dom_bits = [1 << i for i in range((dom_size - 1).bit_length())]
    slab_bits = [1 << i for i in range((slab_size - 1).bit_length())]

    blocks = blocks.T
    flat, *scores = score_call(slab_me, inv_noise, particles, references, blocks, slab_size)
    gb = insert_block(groups, orients, devices, particles.shape[0], width)
    here, own = lax.optimization_barrier((here, scores[0]))
    plan = plan_call(here, destination, groups, gb, (dom_size, slab_size))
    own, *plan = lax.optimization_barrier((own, *plan))
    pos, addr, items = plan
    parts = [own] + [flip(scores[k], "slab", k) for k in range(1, slab_size)]
    post = softmax_call(parts)
    post, pos = lax.optimization_barrier((post, pos))
    meta = meta_call(here, row_index, fraction, pos, addr, devices)
    posts = [post] + [flip(post, "slab", k) for k in range(1, slab_size)]
    send, keep = insert_call(
        slab_me, addr, items, flat, pos, meta, blocks, posts, orients, devices
    )

    def added(terms):
        return functools.reduce(jnp.add, [term.astype(F32) for term in terms])

    def halve(terms, axis_name, axis, bit):
        size = terms[0].shape[axis] // 2
        pick = lambda term, at: lax.slice_in_dim(term, at, at + size, axis=axis)
        sent = added([pick(term, size) for term in terms]).astype(BF16)
        return [pick(term, 0) for term in terms] + [flip(sent, axis_name, bit)]

    terms = [keep, flip(send, "dom", dom_bits[0])]
    rest = dom_bits[1:]
    terms = [term.reshape((2,) * len(rest) + (slab_size * RD, width)) for term in terms]
    columns = [[term[..., part * OB : (part + 1) * OB] for term in terms] for part in range(2)]
    for stage in range(len(rest)):
        for part in range(2):
            axis = stage if part == 0 else len(rest) - 1 - stage
            columns[part] = halve(columns[part], "dom", axis, rest[axis])
    columns = [[term.reshape(slab_size * RD, OB) for term in terms] for terms in columns]
    terms = [jnp.concatenate(pair, axis=1) for pair in zip(*columns)]
    for bit in slab_bits:
        terms = halve(terms, "slab", 0, bit)
    volume = added(terms)

    own = volume.astype(BF16)
    plane = [own] + [flip(own, "dom", 2 * k) for k in range(1, dom_size // 2)]
    chip = dom_pos // 2
    placed = []
    for k in range(dom_size // 2):
        value = plane[0]
        for j in range(1, dom_size // 2):
            value = jnp.where(chip ^ j == k, plane[j], value)
        placed.append(value)
    value = jnp.stack(placed)
    got = flip(value, "dom", dom_bits[0])
    value = jnp.where(
        dom_pos & dom_bits[0] == 0,
        jnp.stack([value, got], 1),
        jnp.stack([got, value], 1),
    )
    return volume, value.reshape(dom_size * RD, width)


def solution(mesh):
    return jax.shard_map(
        shards,
        mesh=mesh,
        in_specs=(
            P("dom", "slab", None),
            P("dom", None),
            P(None, "slab", None),
            P("slab"),
            P(),
            P(),
            P(),
        ),
        out_specs=(P(("dom", "slab"), None), P(None, "slab")),
        check_vma=False,
    )
```

```python
import functools

import jax
import jax.numpy as jnp
from jax import lax
from jax.experimental import pallas as pl
from jax.experimental.pallas import tpu as pltpu
from jax.sharding import PartitionSpec as P

OB = 128
RD = 256
MB = 2**20
OUT_SLOTS = 8
OUT_TILE = 1024
F32 = jnp.float32
BF16 = jnp.bfloat16


def group_block(groups):
    return 16 if groups % 16 == 0 else 8


def spread_columns(blk_ref, cols_ref):
    count = blk_ref.shape[1]
    for j in range(2):
        for at in range(0, count, OB):
            line = blk_ref[j : j + 1, at : at + OB].astype(F32)
            cols_ref[j, at : at + OB, :] = jnp.broadcast_to(line, (OB, OB)).T


def score_kernel(me_ref, noise_ref, x_ref, r_ref, blk_ref, flat_ref, *rest):
    *out_refs, w_ref, acc_ref, perm_ref, cols_ref = rest
    step = pl.program_id(0)
    particles, gb, width = x_ref.shape
    orients = r_ref.shape[0]
    side = 16 * gb

    @pl.when(step == 0)
    def _():
        row = lax.broadcasted_iota(jnp.int32, (side, side), 0)
        col = lax.broadcasted_iota(jnp.int32, (side, side), 1)
        same = ((row // 16) == (col % gb)) & ((row % 16) == (col // gb))
        perm_ref[...] = jnp.where(same, 1.0, 0.0).astype(BF16)
        acc_ref[...] = jnp.zeros_like(acc_ref)
        spread_columns(blk_ref, cols_ref)

    perm = perm_ref[...]

    def regroup(jobs):
        at = [pl.multiple_of(first * 16, 16) for _, _, _, first in jobs]
        wide = [job[0][pl.ds(a, 16)].reshape(side, width) for job, a in zip(jobs, at)]
        moved = jnp.dot(perm, jnp.concatenate(wide, axis=1), preferred_element_type=F32)
        for g in range(gb):
            for t, (_, dst_ref, scaled, _) in enumerate(jobs):
                part = moved[g * 16 : (g + 1) * 16, t * width : (t + 1) * width]
                if scaled:
                    part = part * noise_ref[step * gb + g]
                dst_ref[pl.ds(at[t], 16), g * width : (g + 1) * width] = part.astype(BF16)

    def turn(src_ref, dst_ref, first):
        at = pl.ds(pl.multiple_of(first * 16, 16), 16)
        turned = jnp.swapaxes(src_ref[at], 0, 1)
        for g in range(gb):
            dst_ref[at, g * width : (g + 1) * width] = turned[g]

    def tiles(i, carry):
        jobs = [(r_ref, w_ref, True, i * 4 + t) for t in range(4)]
        regroup(jobs + [(x_ref, flat_ref, False, i * 4)])
        for t in range(1, 4):
            turn(x_ref, flat_ref, i * 4 + t)
        return carry

    def more_tiles(src_ref, dst_ref, scaled):
        def body(i, carry):
            regroup([(src_ref, dst_ref, scaled, i)])
            return carry

        lax.fori_loop(both * 4, src_ref.shape[0] // 16, body, 0)

    both = min(particles, orients) // 64
    lax.fori_loop(0, both, tiles, 0, unroll=2)
    more_tiles(r_ref, w_ref, True)
    more_tiles(x_ref, flat_ref, False)
    acc_ref[...] += lax.dot_general(
        flat_ref[...], w_ref[...], (((1,), (1,)), ((), ())), preferred_element_type=F32
    )

    @pl.when(step == pl.num_programs(0) - 1)
    def _():
        me = me_ref[0]
        share = particles // len(out_refs)
        for k, out_ref in enumerate(out_refs):
            at = pl.multiple_of((me ^ k) * share, share)
            for j in range(2):
                wanted = cols_ref[j, pl.ds(at, share), :]
                chosen = jnp.zeros((share, OB), F32)
                for b in range(orients // OB):
                    value = acc_ref[pl.ds(at, share), b * OB : (b + 1) * OB]
                    chosen = jnp.where(wanted == b, value, chosen)
                out_ref[:, j * OB : (j + 1) * OB] = chosen


def score_call(me, inv_noise, particles, references, blocks, slab_size):
    count, groups, width = particles.shape
    orients = references.shape[0]
    gb = group_block(groups)
    side = 16 * gb
    share = count // slab_size
    smem = pl.BlockSpec(memory_space=pltpu.SMEM)
    return pl.pallas_call(
        score_kernel,
        grid=(groups // gb,),
        out_shape=[jax.ShapeDtypeStruct((count, groups * width), BF16)]
        + [jax.ShapeDtypeStruct((share, 2 * OB), F32)] * slab_size,
        in_specs=[
            smem,
            smem,
            pl.BlockSpec((count, gb, width), lambda i: (0, i, 0)),
            pl.BlockSpec((orients, gb, width), lambda i: (0, i, 0)),
            pl.BlockSpec((2, count), lambda i: (0, 0)),
        ],
        out_specs=[pl.BlockSpec((count, gb * width), lambda i: (0, i))]
        + [pl.BlockSpec((share, 2 * OB), lambda i: (0, 0))] * slab_size,
        scratch_shapes=[
            pltpu.VMEM((orients, gb * width), BF16),
            pltpu.VMEM((count, orients), F32),
            pltpu.VMEM((side, side), BF16),
            pltpu.VMEM((2, count, OB), F32),
        ],
        compiler_params=pltpu.CompilerParams(vmem_limit_bytes=56 * MB),
        cost_estimate=pl.CostEstimate(
            flops=4 * count * orients * groups * width,
            bytes_accessed=6 * count * groups * width,
            transcendentals=0,
        ),
    )(me, inv_noise, particles, references, blocks)


def softmax_kernel(*refs):
    *parts, out_ref = refs
    total = parts[0][...]
    for part in parts[1:]:
        total = total + part[...]
    highest = jnp.max(total, axis=1, keepdims=True)
    weights = jnp.exp(total - highest)
    out_ref[...] = (weights / jnp.sum(weights, axis=1, keepdims=True)).astype(BF16)


def softmax_call(parts):
    return pl.pallas_call(
        softmax_kernel,
        out_shape=jax.ShapeDtypeStruct(parts[0].shape, BF16),
        compiler_params=pltpu.CompilerParams(vmem_limit_bytes=8 * MB),
    )(*parts)


def plan_kernel(
    here_ref, dest_ref, pos_ref, addr_ref, item_ref, place_ref, hot_ref, count_ref, *, sizes
):
    step = pl.program_id(0)
    dom_size, slab_size = sizes
    owners = dom_size * slab_size
    _, units, half = pos_ref.shape
    lanes = addr_ref.shape[2]
    parts = dest_ref.shape[1] // half
    gb = units // parts
    dom_log, slab_log = (dom_size - 1).bit_length(), (slab_size - 1).bit_length()

    @pl.when(step == 0)
    def _():
        off = dest_ref[...] ^ (here_ref[0] * slab_size + here_ref[1])
        place = jnp.zeros_like(off)
        for bit in list(range(slab_log, slab_log + dom_log)) + list(range(slab_log)):
            place = place * 2 + (lax.shift_right_logical(off, bit) & 1)
        place_ref[...] = place

    owner = lax.broadcasted_iota(jnp.int32, (owners, 1), 0)
    for u in range(units):
        g, h = u // parts, u % parts
        line = place_ref[pl.ds(step * gb + g, 1), h * half : (h + 1) * half]
        hot = jnp.where(line == owner, 1.0, 0.0)
        hot_ref[u * owners : (u + 1) * owners, :] = hot.astype(BF16)
    before = lax.broadcasted_iota(jnp.int32, (half, half), 0)
    after = lax.broadcasted_iota(jnp.int32, (half, half), 1)
    upto = jnp.where(before <= after, 1.0, 0.0).astype(BF16)
    count_ref[...] = jnp.dot(hot_ref[...], upto, preferred_element_type=F32)

    exact = functools.partial(
        jnp.dot, preferred_element_type=F32, precision=lax.Precision.HIGHEST
    )
    row = lax.broadcasted_iota(jnp.int32, (owners, owners), 0)
    col = lax.broadcasted_iota(jnp.int32, (owners, owners), 1)
    below = jnp.where(row > col, 1.0, 0.0)
    row = lax.broadcasted_iota(jnp.int32, (OB, OB), 0)
    col = lax.broadcasted_iota(jnp.int32, (OB, OB), 1)
    earlier = jnp.where(row < col, 1.0, 0.0)
    lane = lax.broadcasted_iota(jnp.int32, (owners, OB), 1)
    runs = jnp.zeros((owners, OB), F32)
    for u in range(units):
        size = count_ref[u * owners : (u + 1) * owners, half - 1 : half]
        runs = jnp.where(lane == u, size, runs)
    runs = jnp.floor((runs + 7.0) * 0.125) * 8.0
    base = exact(below, runs)
    ahead = exact(runs, earlier)
    total = jnp.sum(runs, axis=1, keepdims=True)
    start = exact(below, jnp.broadcast_to(total, (owners, OB)))[:, :1]
    blocks = jnp.floor((total + (2 * RD - 1.0)) * (0.5 / RD))
    first = exact(below, jnp.broadcast_to(blocks, (owners, OB)))[:, :1]
    shift = start + ahead - base
    used = jnp.sum(runs, axis=0, keepdims=True)

    slot = (lax.broadcasted_iota(jnp.int32, (1, lanes), 1) * 8).astype(F32)
    is_last = lax.broadcasted_iota(jnp.int32, (1, lanes), 1) == lanes - 1
    rows = units * (half + 7 * owners)
    for u in range(units):
        low, size = base[:, u : u + 1], runs[:, u : u + 1]
        hot = hot_ref[u * owners : (u + 1) * owners, :].astype(F32)
        rank = count_ref[u * owners : (u + 1) * owners, :] + (low - 1.0)
        pos_ref[0, u : u + 1, :] = jnp.sum(hot * rank, axis=0, keepdims=True).astype(jnp.int32)
        inside = (slot >= low) & (slot < low + size)
        goal = jnp.where(inside, shift[:, u : u + 1] + slot - rows, 0.0)
        goal = (jnp.sum(goal, axis=0, keepdims=True) + rows) * 0.125
        addr_ref[0, u : u + 1, :] = jnp.where(is_last, used[:, u : u + 1], goal).astype(jnp.int32)

    wide = item_ref.shape[2]
    number = lax.broadcasted_iota(jnp.int32, (1, wide), 1).astype(F32)
    inside = (number >= first) & (number < first + blocks)
    done = (number - first) * (2 * RD)
    pick = lambda value: jnp.sum(jnp.where(inside, value, 0.0), axis=0, keepdims=True)
    every = lambda value: jnp.sum(
        jnp.broadcast_to(value, (owners, wide)), axis=0, keepdims=True
    )
    lines = (
        pick(jnp.broadcast_to(owner.astype(F32), (owners, wide))),
        pick((start + done) * 0.125),
        pick(total - done),
        every(blocks),
        every(total * 0.125),
    )
    for i, value in enumerate(lines):
        item_ref[0, i : i + 1, :] = value.astype(jnp.int32)


def meta_kernel(here_ref, index_ref, frac_ref, pos_ref, meta_ref):
    step = pl.program_id(0)
    _, units, half = pos_ref.shape
    parts = index_ref.shape[1] // half
    gb = units // parts
    blocks = meta_ref.shape[2]
    low = lambda value: value.astype(F32).astype(BF16)
    eighth = low(lax.broadcasted_iota(jnp.int32, (blocks, half), 0))
    lane_of = low(lax.broadcasted_iota(jnp.int32, (OB, half), 0) % 8)
    one, none = jnp.bfloat16(1.0), jnp.bfloat16(0.0)
    for u in range(units):
        g, h = u // parts, u % parts
        line = pl.ds(step * gb + g, 1)
        span = slice(h * half, (h + 1) * half)
        pos = pos_ref[0, u : u + 1, :]
        here = lane_of == low(pos & 7)
        spots = jnp.where(eighth == low(lax.shift_right_logical(pos, 3)), one, none)
        terms = [
            jnp.where(here, low(index_ref[line, span]), none),
            jnp.where(here, low(frac_ref[line, span]), none),
        ]
        meta_ref[0, u] = lax.dot_general(
            jnp.concatenate([spots, spots], axis=1),
            jnp.concatenate(terms, axis=1),
            (((1,), (1,)), ((), ())),
            preferred_element_type=F32,
        )


def up_to(value, step):
    return -(-value // step) * step


def sort_sizes(orients, owners):
    slots = orients + 7 * owners
    sure = orients + 144
    blocks = up_to((sure + up_to(max(0, slots - sure), 128)) // 8, 8)
    return slots, sure, blocks


def planned(shape):
    return pl.BlockSpec((1,) + shape[1:], lambda i, here: (i,) + (0,) * (len(shape) - 1))


def plan_call(here, destination, groups, gb, mesh_sizes):
    orients = destination.shape[1]
    half = min(256, orients)
    owners = mesh_sizes[0] * mesh_sizes[1]
    steps, units = groups // gb, gb * (orients // half)
    slots, _, blocks = sort_sizes(half, owners)
    shapes = [
        (steps, units, half),
        (steps, units, up_to(blocks + 1, 128)),
        (steps, 5, up_to(owners + units * slots // RD + 8, 128)),
    ]
    return pl.pallas_call(
        functools.partial(plan_kernel, sizes=mesh_sizes),
        grid_spec=pltpu.PrefetchScalarGridSpec(
            num_scalar_prefetch=1,
            grid=(steps,),
            in_specs=[pl.BlockSpec((groups, orients), lambda i, here: (here[1], 0))],
            out_specs=[planned(shape) for shape in shapes],
            scratch_shapes=[
                pltpu.VMEM((groups, orients), jnp.int32),
                pltpu.VMEM((units * owners, half), BF16),
                pltpu.VMEM((units * owners, half), F32),
            ],
        ),
        out_shape=[jax.ShapeDtypeStruct(shape, jnp.int32) for shape in shapes],
        compiler_params=pltpu.CompilerParams(vmem_limit_bytes=60 * MB),
        cost_estimate=pl.CostEstimate(
            flops=8 * steps * units * owners * half * half,
            bytes_accessed=8 * groups * orients,
            transcendentals=0,
        ),
    )(here, destination)


def meta_call(here, row_index, fraction, pos, owners):
    steps, units, half = pos.shape
    orients = row_index.shape[1]
    groups = steps * units * half // orients
    blocks = sort_sizes(half, owners)[2]
    shape = (steps, units, blocks, OB)
    table = pl.BlockSpec((groups, orients), lambda i, here: (here[1], 0))
    return pl.pallas_call(
        meta_kernel,
        grid_spec=pltpu.PrefetchScalarGridSpec(
            num_scalar_prefetch=1,
            grid=(steps,),
            in_specs=[table, table, planned(pos.shape)],
            out_specs=planned(shape),
        ),
        out_shape=jax.ShapeDtypeStruct(shape, F32),
        compiler_params=pltpu.CompilerParams(vmem_limit_bytes=60 * MB),
        cost_estimate=pl.CostEstimate(
            flops=8 * steps * units * blocks * half * OB,
            bytes_accessed=8 * steps * units * blocks * OB,
            transcendentals=0,
        ),
    )(here, row_index, fraction, pos)


def insert_kernel(me_ref, addr_ref, item_ref, x_ref, pos_ref, meta_ref, blk_ref, *rest):
    *post_refs, send_ref, keep_ref = rest[:-10]
    post_t, spread_ref, cols_ref, slice_a, slice_b, buf_s, buf_m, volume, stage, sem = rest[-10:]
    step = pl.program_id(0)
    count = x_ref.shape[0]
    orients = post_t.shape[0]
    units, half = pos_ref.shape[1:]
    parts = orients // half
    gb = units // parts
    width = x_ref.shape[1] // gb
    share = count // len(post_refs)
    lanes = addr_ref.shape[2]

    @pl.when(step == 0)
    def _():
        volume[...] = jnp.zeros_like(volume)
        me = me_ref[0]
        spread_columns(blk_ref, cols_ref)
        for k, post_ref in enumerate(post_refs):
            at = pl.multiple_of((me ^ k) * share, share)
            post = post_ref[...].astype(F32)
            first = cols_ref[0, pl.ds(at, share), :]
            second = cols_ref[1, pl.ds(at, share), :]
            for b in range(orients // OB):
                spread = jnp.where(
                    first == b, post[:, :OB], jnp.where(second == b, post[:, OB:], 0.0)
                )
                spread_ref[pl.ds(at, share), b * OB : (b + 1) * OB] = spread
        for b in range(orients // OB):
            post_t[b * OB : (b + 1) * OB] = spread_ref[:, b * OB : (b + 1) * OB].T.astype(BF16)

    tail = pl.ds(pl.multiple_of(item_ref[0, 4, 0] * 8, 8), 2 * RD)
    buf_s[tail, :] = jnp.zeros((2 * RD, width), F32)
    one, none = jnp.bfloat16(1.0), jnp.bfloat16(0.0)
    slots, sure, _ = sort_sizes(half, volume.shape[0] // RD)
    per = slice_a.shape[1] // width
    number = gb // per

    def slices(q, dst_ref):
        at = pl.ds(pl.multiple_of(q * (per * width), per * width), per * width)
        value = jnp.dot(post_t[...], x_ref[:, at], preferred_element_type=F32)
        dst_ref[...] = value.astype(BF16)

    def emit(u, piece, base, size):
        pos = pos_ref[0, pl.ds(u, 1), :]
        order = []
        for at in range(0, size, 128):
            high = min(128, size - at)
            slot = lax.broadcasted_iota(jnp.int32, (high, half), 0).astype(F32).astype(BF16)
            near = jnp.clip(pos - (base + at), -1, 128).astype(F32).astype(BF16)
            order.append(jnp.where(slot == near, one, none))
        order = jnp.concatenate(order, axis=0)
        rows = jnp.dot(order, piece, preferred_element_type=F32)
        for i in range(size // 8):
            at = addr_ref[0, u, base // 8 + i]
            buf_s[pl.ds(pl.multiple_of(at * 8, 8), 8), :] = rows[8 * i : 8 * i + 8]
            buf_m[pl.ds(at, 1), :] = meta_ref[0, u, pl.ds(base // 8 + i, 1), :]

    def sort(q, src_ref):
        for g in range(per):
            for h in range(parts):
                piece = src_ref[h * half : (h + 1) * half, g * width : (g + 1) * width]
                emit((q * per + g) * parts + h, piece, 0, sure)

    def rest_of(q, src_ref):
        for g in range(per):
            for h in range(parts):
                u = (q * per + g) * parts + h

                def more(e, c, u=u, g=g, h=h):
                    piece = src_ref[h * half : (h + 1) * half, g * width : (g + 1) * width]
                    emit(u, piece, sure + e * 128, 128)
                    return c

                used = addr_ref[0, u, lanes - 1]
                lax.fori_loop(0, lax.div(jnp.maximum(used - sure, 0) + 127, 128), more, 0)

    def most_used(q):
        most = addr_ref[0, q * per * parts, lanes - 1]
        for u in range(1, per * parts):
            most = jnp.maximum(most, addr_ref[0, q * per * parts + u, lanes - 1])
        return most

    def two(j, carry):
        q = j * 2
        sort(q, slice_a)
        slices(q + 1, slice_b)

        @pl.when(most_used(q) > sure)
        def _():
            rest_of(q, slice_a)

        sort(q + 1, slice_b)
        slices(jnp.minimum(q + 2, number - 1), slice_a)

        @pl.when(most_used(q + 1) > sure)
        def _():
            rest_of(q + 1, slice_b)

        return carry

    slices(0, slice_a)
    lax.fori_loop(0, number // 2, two, 0)
    if number % 2:
        sort(number - 1, slice_a)
        rest_of(number - 1, slice_a)

    bins = lax.broadcasted_iota(jnp.int32, (RD, 2 * RD), 0).astype(F32).astype(BF16)
    side = RD // 2
    at_lane = lax.broadcasted_iota(jnp.int32, (side // 8, side), 1) // 8
    own_lane = at_lane == lax.broadcasted_iota(jnp.int32, (side // 8, side), 0)
    line = lax.broadcasted_iota(jnp.int32, (1, 2 * RD), 1)
    together = 4

    def some_items(q, carry):
        for u in range(together):
            j = q * together + u
            owner, at, left = item_ref[0, 0, j], item_ref[0, 1, j], item_ref[0, 2, j]
            places = [
                jnp.sum(
                    jnp.where(own_lane, buf_m[pl.ds(at + h * (side // 8), side // 8), :], 0.0),
                    axis=0,
                    keepdims=True,
                )
                for h in range(4)
            ]
            place = jnp.where(line < left, jnp.concatenate(places, axis=1), -9.0)
            whole = jnp.floor(place)
            apart = (bins - whole.astype(BF16)) - (place - whole).astype(BF16)
            weights = jnp.maximum(one - jnp.abs(apart), none)
            values = buf_s[pl.ds(pl.multiple_of(at * 8, 8), 2 * RD), :].astype(BF16)
            goal = pl.ds(pl.multiple_of(owner * RD, RD), RD)
            volume[goal, :] += jnp.dot(weights, values, preferred_element_type=F32)
        return carry

    count_items = lax.div(item_ref[0, 3, 0] + together - 1, together)
    lax.fori_loop(0, count_items, some_items, 0)

    @pl.when(step == pl.num_programs(0) - 1)
    def _():
        side_rows = keep_ref.shape[1]
        slots_out, _, tile, _ = stage.shape
        copies = []
        for base, out_ref in ((side_rows, send_ref), (0, keep_ref)):
            for at in range(0, side_rows, tile):
                slot = len(copies) % slots_out
                if len(copies) >= slots_out:
                    copies[len(copies) - slots_out].wait()
                value = volume[base + at : base + at + tile, :].astype(BF16)
                for c in range(2):
                    stage[slot, c] = value[:, c * OB : (c + 1) * OB]
                copy = pltpu.make_async_copy(
                    stage.at[slot], out_ref.at[:, pl.ds(at, tile)], sem.at[slot]
                )
                copy.start()
                copies.append(copy)
        for copy in copies[-slots_out:]:
            copy.wait()


def group_pair(gb):
    return 2 if gb % 4 == 0 else 1


def insert_block(groups, orients, owners, count, width):
    half = min(256, orients)
    slots, _, blocks = sort_sizes(half, owners)
    room = 50 * MB - owners * RD * width * 4
    best = 1
    for gb in range(1, groups + 1):
        units = gb * (orients // half)
        rows = units * slots + 2 * RD + 8
        need = rows * (width * 4 + OB // 2) + 4 * count * gb * width + units * blocks * OB * 8
        if groups % gb == 0 and need <= room:
            best = gb
    return best


def insert_call(me, addr, items, flat, pos, meta, blocks, posts, orients, owners):
    count, length = flat.shape
    steps, units, half = pos.shape
    gb = units * half // orients
    width = length // (steps * gb)
    total = owners * RD
    share = posts[0].shape[0]
    rows = units * sort_sizes(half, owners)[0] + 2 * RD + 8
    smem = pl.BlockSpec(memory_space=pltpu.SMEM)
    block = lambda shape, **kw: pl.BlockSpec(
        (1,) + shape[1:], lambda i: (i,) + (0,) * (len(shape) - 1), **kw
    )
    return pl.pallas_call(
        insert_kernel,
        grid=(steps,),
        out_shape=[jax.ShapeDtypeStruct((2, total // 2, OB), BF16)] * 2,
        in_specs=[
            smem,
            block(addr.shape, memory_space=pltpu.SMEM),
            block(items.shape, memory_space=pltpu.SMEM),
            pl.BlockSpec((count, gb * width), lambda i: (0, i)),
            block(pos.shape),
            block(meta.shape),
            pl.BlockSpec((2, count), lambda i: (0, 0)),
        ]
        + [pl.BlockSpec((share, 2 * OB), lambda i: (0, 0))] * len(posts),
        out_specs=[pl.BlockSpec(memory_space=pl.ANY)] * 2,
        scratch_shapes=[
            pltpu.VMEM((orients, count), BF16),
            pltpu.VMEM((count, orients), F32),
            pltpu.VMEM((2, count, OB), F32),
            pltpu.VMEM((orients, group_pair(gb) * width), BF16),
            pltpu.VMEM((orients, group_pair(gb) * width), BF16),
            pltpu.VMEM((rows, width), F32),
            pltpu.VMEM((rows // 8, OB), F32),
            pltpu.VMEM((total, width), F32),
            pltpu.VMEM((OUT_SLOTS, 2, OUT_TILE, OB), BF16),
            pltpu.SemaphoreType.DMA((OUT_SLOTS,)),
        ],
        compiler_params=pltpu.CompilerParams(vmem_limit_bytes=62 * MB),
        cost_estimate=pl.CostEstimate(
            flops=8 * count * orients * length,
            bytes_accessed=2 * count * length,
            transcendentals=0,
        ),
    )(me, addr, items, flat, pos, meta, blocks, *posts)


def flip(value, axis, bit):
    size = lax.axis_size(axis)
    return lax.ppermute(value, axis, [(i, i ^ bit) for i in range(size)])


def shards(particles, blocks, references, inv_noise, destination, row_index, fraction):
    groups, width = particles.shape[1:]
    orients = references.shape[0]
    dom_size = lax.axis_size("dom")
    slab_size = lax.axis_size("slab")
    devices = dom_size * slab_size
    dom_pos = lax.axis_index("dom")
    slab_pos = lax.axis_index("slab")
    here = jnp.stack([dom_pos, slab_pos]).astype(jnp.int32)
    slab_me = here[1:]
    dom_bits = [1 << i for i in range((dom_size - 1).bit_length())]
    slab_bits = [1 << i for i in range((slab_size - 1).bit_length())]

    blocks = blocks.T
    flat, *scores = score_call(slab_me, inv_noise, particles, references, blocks, slab_size)
    gb = insert_block(groups, orients, devices, particles.shape[0], width)
    here, own = lax.optimization_barrier((here, scores[0]))
    plan = plan_call(here, destination, groups, gb, (dom_size, slab_size))
    own, *plan = lax.optimization_barrier((own, *plan))
    pos, addr, items = plan
    parts = [own] + [flip(scores[k], "slab", k) for k in range(1, slab_size)]
    post = softmax_call(parts)
    post, pos = lax.optimization_barrier((post, pos))
    meta = meta_call(here, row_index, fraction, pos, devices)
    posts = [post] + [flip(post, "slab", k) for k in range(1, slab_size)]
    send, keep = insert_call(
        slab_me, addr, items, flat, pos, meta, blocks, posts, orients, devices
    )

    def added(terms):
        return functools.reduce(jnp.add, [term.astype(F32) for term in terms])

    def halve(terms, axis_name, axis, bit):
        size = terms[0].shape[axis] // 2
        pick = lambda term, at: lax.slice_in_dim(term, at, at + size, axis=axis)
        sent = added([pick(term, size) for term in terms]).astype(BF16)
        return [pick(term, 0) for term in terms] + [flip(sent, axis_name, bit)]

    terms = [keep, flip(send, "dom", dom_bits[0])]
    rest = dom_bits[1:]
    columns = []
    for part in range(2):
        columns.append(
            [term[part].reshape((2,) * len(rest) + (slab_size * RD, OB)) for term in terms]
        )
    for stage in range(len(rest)):
        for part in range(2):
            axis = stage if part == 0 else len(rest) - 1 - stage
            columns[part] = halve(columns[part], "dom", axis, rest[axis])
    terms = [jnp.stack([t.reshape(slab_size * RD, OB) for t in pair]) for pair in zip(*columns)]
    for bit in slab_bits:
        terms = halve(terms, "slab", 1, bit)
    volume = jnp.concatenate([added([term[part] for term in terms]) for part in range(2)], axis=1)

    own = volume.astype(BF16)
    plane = [own] + [flip(own, "dom", 2 * k) for k in range(1, dom_size // 2)]
    chip = dom_pos // 2
    placed = []
    for k in range(dom_size // 2):
        value = plane[0]
        for j in range(1, dom_size // 2):
            value = jnp.where(chip ^ j == k, plane[j], value)
        placed.append(value)
    value = jnp.stack(placed)
    got = flip(value, "dom", dom_bits[0])
    value = jnp.where(
        dom_pos & dom_bits[0] == 0,
        jnp.stack([value, got], 1),
        jnp.stack([got, value], 1),
    )
    return volume, value.reshape(dom_size * RD, width)


def solution(mesh):
    return jax.shard_map(
        shards,
        mesh=mesh,
        in_specs=(
            P("dom", "slab", None),
            P("dom", None),
            P(None, "slab", None),
            P("slab"),
            P(),
            P(),
            P(),
        ),
        out_specs=(P(("dom", "slab"), None), P(None, "slab")),
        check_vma=False,
    )
```

```python
import functools

import jax
import jax.numpy as jnp
from jax import lax
from jax.experimental import pallas as pl
from jax.experimental.pallas import tpu as pltpu
from jax.sharding import PartitionSpec as P

OB = 128
RD = 256
MB = 2**20
OUT_SLOTS = 4
OUT_TILE = 1024
F32 = jnp.float32
BF16 = jnp.bfloat16


def group_block(groups):
    return 16 if groups % 16 == 0 else 8


def spread_columns(blk_ref, cols_ref):
    count = blk_ref.shape[1]
    for j in range(2):
        for at in range(0, count, OB):
            line = blk_ref[j : j + 1, at : at + OB].astype(F32)
            cols_ref[j, at : at + OB, :] = jnp.broadcast_to(line, (OB, OB)).T


def score_kernel(me_ref, noise_ref, x_ref, r_ref, blk_ref, flat_ref, *rest):
    *out_refs, w_ref, acc_ref, perm_ref, cols_ref = rest
    step = pl.program_id(0)
    particles, gb, width = x_ref.shape
    orients = r_ref.shape[0]
    side = 16 * gb

    @pl.when(step == 0)
    def _():
        row = lax.broadcasted_iota(jnp.int32, (side, side), 0)
        col = lax.broadcasted_iota(jnp.int32, (side, side), 1)
        same = ((row // 16) == (col % gb)) & ((row % 16) == (col // gb))
        perm_ref[...] = jnp.where(same, 1.0, 0.0).astype(BF16)
        acc_ref[...] = jnp.zeros_like(acc_ref)
        spread_columns(blk_ref, cols_ref)

    perm = perm_ref[...]

    def regroup(jobs):
        at = [pl.multiple_of(first * 16, 16) for _, _, _, first in jobs]
        wide = [job[0][pl.ds(a, 16)].reshape(side, width) for job, a in zip(jobs, at)]
        moved = jnp.dot(perm, jnp.concatenate(wide, axis=1), preferred_element_type=F32)
        for g in range(gb):
            for t, (_, dst_ref, scaled, _) in enumerate(jobs):
                part = moved[g * 16 : (g + 1) * 16, t * width : (t + 1) * width]
                if scaled:
                    part = part * noise_ref[step * gb + g]
                dst_ref[pl.ds(at[t], 16), g * width : (g + 1) * width] = part.astype(BF16)

    def turn(src_ref, dst_ref, first):
        at = pl.ds(pl.multiple_of(first * 16, 16), 16)
        turned = jnp.swapaxes(src_ref[at], 0, 1)
        for g in range(gb):
            dst_ref[at, g * width : (g + 1) * width] = turned[g]

    def tiles(i, carry):
        jobs = [(r_ref, w_ref, True, i * 4 + t) for t in range(4)]
        regroup(jobs + [(x_ref, flat_ref, False, i * 4)])
        for t in range(1, 4):
            turn(x_ref, flat_ref, i * 4 + t)
        return carry

    def more_tiles(src_ref, dst_ref, scaled):
        def body(i, carry):
            regroup([(src_ref, dst_ref, scaled, i)])
            return carry

        lax.fori_loop(both * 4, src_ref.shape[0] // 16, body, 0)

    both = min(particles, orients) // 64
    lax.fori_loop(0, both, tiles, 0, unroll=2)
    more_tiles(r_ref, w_ref, True)
    more_tiles(x_ref, flat_ref, False)
    acc_ref[...] += lax.dot_general(
        flat_ref[...], w_ref[...], (((1,), (1,)), ((), ())), preferred_element_type=F32
    )

    @pl.when(step == pl.num_programs(0) - 1)
    def _():
        me = me_ref[0]
        share = particles // len(out_refs)
        for k, out_ref in enumerate(out_refs):
            at = pl.multiple_of((me ^ k) * share, share)
            for j in range(2):
                wanted = cols_ref[j, pl.ds(at, share), :]
                chosen = jnp.zeros((share, OB), F32)
                for b in range(orients // OB):
                    value = acc_ref[pl.ds(at, share), b * OB : (b + 1) * OB]
                    chosen = jnp.where(wanted == b, value, chosen)
                out_ref[:, j * OB : (j + 1) * OB] = chosen


def score_call(me, inv_noise, particles, references, blocks, slab_size):
    count, groups, width = particles.shape
    orients = references.shape[0]
    gb = group_block(groups)
    side = 16 * gb
    share = count // slab_size
    smem = pl.BlockSpec(memory_space=pltpu.SMEM)
    return pl.pallas_call(
        score_kernel,
        grid=(groups // gb,),
        out_shape=[jax.ShapeDtypeStruct((count, groups * width), BF16)]
        + [jax.ShapeDtypeStruct((share, 2 * OB), F32)] * slab_size,
        in_specs=[
            smem,
            smem,
            pl.BlockSpec((count, gb, width), lambda i: (0, i, 0)),
            pl.BlockSpec((orients, gb, width), lambda i: (0, i, 0)),
            pl.BlockSpec((2, count), lambda i: (0, 0)),
        ],
        out_specs=[pl.BlockSpec((count, gb * width), lambda i: (0, i))]
        + [pl.BlockSpec((share, 2 * OB), lambda i: (0, 0))] * slab_size,
        scratch_shapes=[
            pltpu.VMEM((orients, gb * width), BF16),
            pltpu.VMEM((count, orients), F32),
            pltpu.VMEM((side, side), BF16),
            pltpu.VMEM((2, count, OB), F32),
        ],
        compiler_params=pltpu.CompilerParams(vmem_limit_bytes=32 * MB),
        cost_estimate=pl.CostEstimate(
            flops=4 * count * orients * groups * width,
            bytes_accessed=6 * count * groups * width,
            transcendentals=0,
        ),
    )(me, inv_noise, particles, references, blocks)


def softmax_kernel(*refs):
    *parts, out_ref = refs
    total = parts[0][...]
    for part in parts[1:]:
        total = total + part[...]
    highest = jnp.max(total, axis=1, keepdims=True)
    weights = jnp.exp(total - highest)
    out_ref[...] = (weights / jnp.sum(weights, axis=1, keepdims=True)).astype(BF16)


def softmax_call(parts):
    return pl.pallas_call(
        softmax_kernel,
        out_shape=jax.ShapeDtypeStruct(parts[0].shape, BF16),
        compiler_params=pltpu.CompilerParams(vmem_limit_bytes=8 * MB),
    )(*parts)


def plan_kernel(
    here_ref, dest_ref, pos_ref, addr_ref, item_ref, place_ref, hot_ref, count_ref, *, sizes
):
    step = pl.program_id(0)
    dom_size, slab_size = sizes
    owners = dom_size * slab_size
    _, units, half = pos_ref.shape
    lanes = addr_ref.shape[2]
    parts = dest_ref.shape[1] // half
    gb = units // parts
    dom_log, slab_log = (dom_size - 1).bit_length(), (slab_size - 1).bit_length()

    @pl.when(step == 0)
    def _():
        off = dest_ref[...] ^ (here_ref[0] * slab_size + here_ref[1])
        place = jnp.zeros_like(off)
        for bit in list(range(slab_log, slab_log + dom_log)) + list(range(slab_log)):
            place = place * 2 + (lax.shift_right_logical(off, bit) & 1)
        place_ref[...] = place

    owner = lax.broadcasted_iota(jnp.int32, (owners, 1), 0)
    for u in range(units):
        g, h = u // parts, u % parts
        line = place_ref[pl.ds(step * gb + g, 1), h * half : (h + 1) * half]
        hot = jnp.where(line == owner, 1.0, 0.0)
        hot_ref[u * owners : (u + 1) * owners, :] = hot.astype(BF16)
    before = lax.broadcasted_iota(jnp.int32, (half, half), 0)
    after = lax.broadcasted_iota(jnp.int32, (half, half), 1)
    upto = jnp.where(before <= after, 1.0, 0.0).astype(BF16)
    count_ref[...] = jnp.dot(hot_ref[...], upto, preferred_element_type=F32)

    exact = functools.partial(
        jnp.dot, preferred_element_type=F32, precision=lax.Precision.HIGHEST
    )
    row = lax.broadcasted_iota(jnp.int32, (owners, owners), 0)
    col = lax.broadcasted_iota(jnp.int32, (owners, owners), 1)
    below = jnp.where(row > col, 1.0, 0.0)
    row = lax.broadcasted_iota(jnp.int32, (OB, OB), 0)
    col = lax.broadcasted_iota(jnp.int32, (OB, OB), 1)
    earlier = jnp.where(row < col, 1.0, 0.0)
    lane = lax.broadcasted_iota(jnp.int32, (owners, OB), 1)
    runs = jnp.zeros((owners, OB), F32)
    for u in range(units):
        size = count_ref[u * owners : (u + 1) * owners, half - 1 : half]
        runs = jnp.where(lane == u, size, runs)
    runs = jnp.floor((runs + 7.0) * 0.125) * 8.0
    base = exact(below, runs)
    ahead = exact(runs, earlier)
    total = jnp.sum(runs, axis=1, keepdims=True)
    start = exact(below, jnp.broadcast_to(total, (owners, OB)))[:, :1]
    blocks = jnp.floor((total + (RD - 1.0)) * (1.0 / RD))
    first = exact(below, jnp.broadcast_to(blocks, (owners, OB)))[:, :1]
    shift = start + ahead - base
    used = jnp.sum(runs, axis=0, keepdims=True)

    slot = (lax.broadcasted_iota(jnp.int32, (1, lanes), 1) * 8).astype(F32)
    is_last = lax.broadcasted_iota(jnp.int32, (1, lanes), 1) == lanes - 1
    rows = units * (half + 7 * owners)
    for u in range(units):
        low, size = base[:, u : u + 1], runs[:, u : u + 1]
        hot = hot_ref[u * owners : (u + 1) * owners, :].astype(F32)
        rank = count_ref[u * owners : (u + 1) * owners, :] + (low - 1.0)
        pos_ref[0, u : u + 1, :] = jnp.sum(hot * rank, axis=0, keepdims=True).astype(jnp.int32)
        inside = (slot >= low) & (slot < low + size)
        goal = jnp.where(inside, shift[:, u : u + 1] + slot - rows, 0.0)
        goal = (jnp.sum(goal, axis=0, keepdims=True) + rows) * 0.125
        addr_ref[0, u : u + 1, :] = jnp.where(is_last, used[:, u : u + 1], goal).astype(jnp.int32)

    wide = item_ref.shape[2]
    number = lax.broadcasted_iota(jnp.int32, (1, wide), 1).astype(F32)
    inside = (number >= first) & (number < first + blocks)
    done = (number - first) * RD
    pick = lambda value: jnp.sum(jnp.where(inside, value, 0.0), axis=0, keepdims=True)
    every = lambda value: jnp.sum(
        jnp.broadcast_to(value, (owners, wide)), axis=0, keepdims=True
    )
    lines = (
        pick(jnp.broadcast_to(owner.astype(F32), (owners, wide))),
        pick((start + done) * 0.125),
        pick(total - done),
        every(blocks),
        every(total * 0.125),
    )
    for i, value in enumerate(lines):
        item_ref[0, i : i + 1, :] = value.astype(jnp.int32)


def meta_kernel(here_ref, index_ref, frac_ref, pos_ref, meta_ref):
    step = pl.program_id(0)
    _, units, half = pos_ref.shape
    parts = index_ref.shape[1] // half
    gb = units // parts
    blocks = meta_ref.shape[2]
    low = lambda value: value.astype(F32).astype(BF16)
    eighth = low(lax.broadcasted_iota(jnp.int32, (blocks, half), 0))
    lane_of = low(lax.broadcasted_iota(jnp.int32, (OB, half), 0) % 8)
    one, none = jnp.bfloat16(1.0), jnp.bfloat16(0.0)
    for u in range(units):
        g, h = u // parts, u % parts
        line = pl.ds(step * gb + g, 1)
        span = slice(h * half, (h + 1) * half)
        pos = pos_ref[0, u : u + 1, :]
        here = lane_of == low(pos & 7)
        spots = jnp.where(eighth == low(lax.shift_right_logical(pos, 3)), one, none)
        terms = [
            jnp.where(here, low(index_ref[line, span]), none),
            jnp.where(here, low(frac_ref[line, span]), none),
        ]
        meta_ref[0, u] = lax.dot_general(
            jnp.concatenate([spots, spots], axis=1),
            jnp.concatenate(terms, axis=1),
            (((1,), (1,)), ((), ())),
            preferred_element_type=F32,
        )


def up_to(value, step):
    return -(-value // step) * step


def sort_sizes(orients, owners):
    slots = orients + 7 * owners
    sure = orients + 144
    blocks = up_to((sure + up_to(max(0, slots - sure), 128)) // 8, 8)
    return slots, sure, blocks


def planned(shape):
    return pl.BlockSpec((1,) + shape[1:], lambda i, here: (i,) + (0,) * (len(shape) - 1))


def plan_call(here, destination, groups, gb, mesh_sizes):
    orients = destination.shape[1]
    half = min(256, orients)
    owners = mesh_sizes[0] * mesh_sizes[1]
    steps, units = groups // gb, gb * (orients // half)
    slots, _, blocks = sort_sizes(half, owners)
    shapes = [
        (steps, units, half),
        (steps, units, up_to(blocks + 1, 128)),
        (steps, 5, up_to(owners + units * slots // RD + 8, 128)),
    ]
    return pl.pallas_call(
        functools.partial(plan_kernel, sizes=mesh_sizes),
        grid_spec=pltpu.PrefetchScalarGridSpec(
            num_scalar_prefetch=1,
            grid=(steps,),
            in_specs=[pl.BlockSpec((groups, orients), lambda i, here: (here[1], 0))],
            out_specs=[planned(shape) for shape in shapes],
            scratch_shapes=[
                pltpu.VMEM((groups, orients), jnp.int32),
                pltpu.VMEM((units * owners, half), BF16),
                pltpu.VMEM((units * owners, half), F32),
            ],
        ),
        out_shape=[jax.ShapeDtypeStruct(shape, jnp.int32) for shape in shapes],
        compiler_params=pltpu.CompilerParams(vmem_limit_bytes=16 * MB),
        cost_estimate=pl.CostEstimate(
            flops=8 * steps * units * owners * half * half,
            bytes_accessed=8 * groups * orients,
            transcendentals=0,
        ),
    )(here, destination)


def meta_call(here, row_index, fraction, pos, owners):
    steps, units, half = pos.shape
    orients = row_index.shape[1]
    groups = steps * units * half // orients
    blocks = sort_sizes(half, owners)[2]
    shape = (steps, units, blocks, OB)
    table = pl.BlockSpec((groups, orients), lambda i, here: (here[1], 0))
    return pl.pallas_call(
        meta_kernel,
        grid_spec=pltpu.PrefetchScalarGridSpec(
            num_scalar_prefetch=1,
            grid=(steps,),
            in_specs=[table, table, planned(pos.shape)],
            out_specs=planned(shape),
        ),
        out_shape=jax.ShapeDtypeStruct(shape, F32),
        compiler_params=pltpu.CompilerParams(vmem_limit_bytes=16 * MB),
        cost_estimate=pl.CostEstimate(
            flops=8 * steps * units * blocks * half * OB,
            bytes_accessed=8 * steps * units * blocks * OB,
            transcendentals=0,
        ),
    )(here, row_index, fraction, pos)


def insert_kernel(me_ref, addr_ref, item_ref, x_ref, pos_ref, meta_ref, blk_ref, *rest):
    *post_refs, send_ref, keep_ref = rest[:-10]
    post_t, spread_ref, cols_ref, slice_a, slice_b, buf_s, buf_m, volume, stage, sem = rest[-10:]
    step = pl.program_id(0)
    count = x_ref.shape[0]
    orients = post_t.shape[0]
    units, half = pos_ref.shape[1:]
    parts = orients // half
    gb = units // parts
    width = x_ref.shape[1] // gb
    share = count // len(post_refs)
    lanes = addr_ref.shape[2]

    @pl.when(step == 0)
    def _():
        volume[...] = jnp.zeros_like(volume)
        me = me_ref[0]
        spread_columns(blk_ref, cols_ref)
        for k, post_ref in enumerate(post_refs):
            at = pl.multiple_of((me ^ k) * share, share)
            post = post_ref[...].astype(F32)
            first = cols_ref[0, pl.ds(at, share), :]
            second = cols_ref[1, pl.ds(at, share), :]
            for b in range(orients // OB):
                spread = jnp.where(
                    first == b, post[:, :OB], jnp.where(second == b, post[:, OB:], 0.0)
                )
                spread_ref[pl.ds(at, share), b * OB : (b + 1) * OB] = spread
        for b in range(orients // OB):
            post_t[b * OB : (b + 1) * OB] = spread_ref[:, b * OB : (b + 1) * OB].T.astype(BF16)

    tail = pl.ds(pl.multiple_of(item_ref[0, 4, 0] * 8, 8), RD)
    buf_s[tail, :] = jnp.zeros((RD, width), F32)
    one, none = jnp.bfloat16(1.0), jnp.bfloat16(0.0)
    slots, sure, _ = sort_sizes(half, volume.shape[0] // RD)
    per = slice_a.shape[1] // width
    number = gb // per

    def slices(q, dst_ref):
        at = pl.ds(pl.multiple_of(q * (per * width), per * width), per * width)
        value = jnp.dot(post_t[...], x_ref[:, at], preferred_element_type=F32)
        dst_ref[...] = value.astype(BF16)

    def emit(u, piece, base, size):
        pos = pos_ref[0, pl.ds(u, 1), :]
        order = []
        for at in range(0, size, 128):
            high = min(128, size - at)
            slot = lax.broadcasted_iota(jnp.int32, (high, half), 0).astype(F32).astype(BF16)
            near = jnp.clip(pos - (base + at), -1, 128).astype(F32).astype(BF16)
            order.append(jnp.where(slot == near, one, none))
        order = jnp.concatenate(order, axis=0)
        rows = jnp.dot(order, piece, preferred_element_type=F32)
        for i in range(size // 8):
            at = addr_ref[0, u, base // 8 + i]
            buf_s[pl.ds(pl.multiple_of(at * 8, 8), 8), :] = rows[8 * i : 8 * i + 8]
            buf_m[pl.ds(at, 1), :] = meta_ref[0, u, pl.ds(base // 8 + i, 1), :]

    def sort(q, src_ref):
        for g in range(per):
            for h in range(parts):
                piece = src_ref[h * half : (h + 1) * half, g * width : (g + 1) * width]
                emit((q * per + g) * parts + h, piece, 0, sure)

    def rest_of(q, src_ref):
        for g in range(per):
            for h in range(parts):
                u = (q * per + g) * parts + h

                def more(e, c, u=u, g=g, h=h):
                    piece = src_ref[h * half : (h + 1) * half, g * width : (g + 1) * width]
                    emit(u, piece, sure + e * 128, 128)
                    return c

                used = addr_ref[0, u, lanes - 1]
                lax.fori_loop(0, lax.div(jnp.maximum(used - sure, 0) + 127, 128), more, 0)

    def most_used(q):
        most = addr_ref[0, q * per * parts, lanes - 1]
        for u in range(1, per * parts):
            most = jnp.maximum(most, addr_ref[0, q * per * parts + u, lanes - 1])
        return most

    def two(j, carry):
        q = j * 2
        sort(q, slice_a)
        slices(q + 1, slice_b)

        @pl.when(most_used(q) > sure)
        def _():
            rest_of(q, slice_a)

        sort(q + 1, slice_b)
        slices(jnp.minimum(q + 2, number - 1), slice_a)

        @pl.when(most_used(q + 1) > sure)
        def _():
            rest_of(q + 1, slice_b)

        return carry

    slices(0, slice_a)
    lax.fori_loop(0, number // 2, two, 0)
    if number % 2:
        sort(number - 1, slice_a)
        rest_of(number - 1, slice_a)

    bins = lax.broadcasted_iota(jnp.int32, (RD, RD), 0).astype(F32).astype(BF16)
    side = RD // 2
    at_lane = lax.broadcasted_iota(jnp.int32, (side // 8, side), 1) // 8
    own_lane = at_lane == lax.broadcasted_iota(jnp.int32, (side // 8, side), 0)
    line = lax.broadcasted_iota(jnp.int32, (1, RD), 1)
    together = 8

    def some_items(q, carry):
        for u in range(together):
            j = q * together + u
            owner, at, left = item_ref[0, 0, j], item_ref[0, 1, j], item_ref[0, 2, j]
            places = [
                jnp.sum(
                    jnp.where(own_lane, buf_m[pl.ds(at + h * (side // 8), side // 8), :], 0.0),
                    axis=0,
                    keepdims=True,
                )
                for h in range(2)
            ]
            place = jnp.where(line < left, jnp.concatenate(places, axis=1), -9.0)
            whole = jnp.floor(place)
            apart = (bins - whole.astype(BF16)) - (place - whole).astype(BF16)
            weights = jnp.maximum(one - jnp.abs(apart), none)
            values = buf_s[pl.ds(pl.multiple_of(at * 8, 8), RD), :].astype(BF16)
            goal = pl.ds(pl.multiple_of(owner * RD, RD), RD)
            volume[goal, :] += jnp.dot(weights, values, preferred_element_type=F32)
        return carry

    count_items = lax.div(item_ref[0, 3, 0] + together - 1, together)
    lax.fori_loop(0, count_items, some_items, 0)

    @pl.when(step == pl.num_programs(0) - 1)
    def _():
        side_rows = keep_ref.shape[1]
        slots_out, _, tile, _ = stage.shape
        copies = []
        for base, out_ref in ((side_rows, send_ref), (0, keep_ref)):
            for at in range(0, side_rows, tile):
                slot = len(copies) % slots_out
                if len(copies) >= slots_out:
                    copies[len(copies) - slots_out].wait()
                value = volume[base + at : base + at + tile, :].astype(BF16)
                for c in range(2):
                    stage[slot, c] = value[:, c * OB : (c + 1) * OB]
                copy = pltpu.make_async_copy(
                    stage.at[slot], out_ref.at[:, pl.ds(at, tile)], sem.at[slot]
                )
                copy.start()
                copies.append(copy)
        for copy in copies[-slots_out:]:
            copy.wait()


def group_pair(gb):
    return 2 if gb % 2 == 0 else 1


def insert_block(groups, orients, owners, count, width):
    half = min(256, orients)
    slots, _, blocks = sort_sizes(half, owners)
    room = max(27 * MB - owners * RD * width * 4, 18 * MB)
    best = 1
    for gb in range(1, groups + 1):
        units = gb * (orients // half)
        rows = units * slots + RD + 8
        need = rows * (width * 4 + OB // 2) + 4 * count * gb * width + units * blocks * OB * 8
        if groups % gb == 0 and need <= room:
            best = gb
    return best


def insert_call(me, addr, items, flat, pos, meta, blocks, posts, orients, owners):
    count, length = flat.shape
    steps, units, half = pos.shape
    gb = units * half // orients
    width = length // (steps * gb)
    total = owners * RD
    share = posts[0].shape[0]
    rows = units * sort_sizes(half, owners)[0] + RD + 8
    limit = total * width * 4 // MB + 26
    smem = pl.BlockSpec(memory_space=pltpu.SMEM)
    block = lambda shape, **kw: pl.BlockSpec(
        (1,) + shape[1:], lambda i: (i,) + (0,) * (len(shape) - 1), **kw
    )
    return pl.pallas_call(
        insert_kernel,
        grid=(steps,),
        out_shape=[jax.ShapeDtypeStruct((2, total // 2, OB), BF16)] * 2,
        in_specs=[
            smem,
            block(addr.shape, memory_space=pltpu.SMEM),
            block(items.shape, memory_space=pltpu.SMEM),
            pl.BlockSpec((count, gb * width), lambda i: (0, i)),
            block(pos.shape),
            block(meta.shape),
            pl.BlockSpec((2, count), lambda i: (0, 0)),
        ]
        + [pl.BlockSpec((share, 2 * OB), lambda i: (0, 0))] * len(posts),
        out_specs=[pl.BlockSpec(memory_space=pl.ANY)] * 2,
        scratch_shapes=[
            pltpu.VMEM((orients, count), BF16),
            pltpu.VMEM((count, orients), F32),
            pltpu.VMEM((2, count, OB), F32),
            pltpu.VMEM((orients, group_pair(gb) * width), BF16),
            pltpu.VMEM((orients, group_pair(gb) * width), BF16),
            pltpu.VMEM((rows, width), F32),
            pltpu.VMEM((rows // 8, OB), F32),
            pltpu.VMEM((total, width), F32),
            pltpu.VMEM((OUT_SLOTS, 2, OUT_TILE, OB), BF16),
            pltpu.SemaphoreType.DMA((OUT_SLOTS,)),
        ],
        compiler_params=pltpu.CompilerParams(vmem_limit_bytes=max(34, limit) * MB),
        cost_estimate=pl.CostEstimate(
            flops=8 * count * orients * length,
            bytes_accessed=2 * count * length,
            transcendentals=0,
        ),
    )(me, addr, items, flat, pos, meta, blocks, *posts)


def flip(value, axis, bit):
    size = lax.axis_size(axis)
    return lax.ppermute(value, axis, [(i, i ^ bit) for i in range(size)])


def shards(particles, blocks, references, inv_noise, destination, row_index, fraction):
    groups, width = particles.shape[1:]
    orients = references.shape[0]
    dom_size = lax.axis_size("dom")
    slab_size = lax.axis_size("slab")
    devices = dom_size * slab_size
    dom_pos = lax.axis_index("dom")
    slab_pos = lax.axis_index("slab")
    here = jnp.stack([dom_pos, slab_pos]).astype(jnp.int32)
    slab_me = here[1:]
    dom_bits = [1 << i for i in range((dom_size - 1).bit_length())]
    slab_bits = [1 << i for i in range((slab_size - 1).bit_length())]

    blocks = blocks.T
    flat, *scores = score_call(slab_me, inv_noise, particles, references, blocks, slab_size)
    gb = insert_block(groups, orients, devices, particles.shape[0], width)
    here, own = lax.optimization_barrier((here, scores[0]))
    plan = plan_call(here, destination, groups, gb, (dom_size, slab_size))
    own, *plan = lax.optimization_barrier((own, *plan))
    pos, addr, items = plan
    parts = [own] + [flip(scores[k], "slab", k) for k in range(1, slab_size)]
    post = softmax_call(parts)
    post, pos = lax.optimization_barrier((post, pos))
    meta = meta_call(here, row_index, fraction, pos, devices)
    posts = [post] + [flip(post, "slab", k) for k in range(1, slab_size)]
    send, keep = insert_call(
        slab_me, addr, items, flat, pos, meta, blocks, posts, orients, devices
    )

    def added(terms):
        return functools.reduce(jnp.add, [term.astype(F32) for term in terms])

    def halve(terms, axis_name, axis, bit):
        size = terms[0].shape[axis] // 2
        pick = lambda term, at: lax.slice_in_dim(term, at, at + size, axis=axis)
        sent = added([pick(term, size) for term in terms]).astype(BF16)
        return [pick(term, 0) for term in terms] + [flip(sent, axis_name, bit)]

    terms = [keep, flip(send, "dom", dom_bits[0])]
    rest = dom_bits[1:]
    columns = []
    for part in range(2):
        columns.append(
            [term[part].reshape((2,) * len(rest) + (slab_size * RD, OB)) for term in terms]
        )
    for stage in range(len(rest)):
        for part in range(2):
            axis = stage if part == 0 else len(rest) - 1 - stage
            columns[part] = halve(columns[part], "dom", axis, rest[axis])
    terms = [jnp.stack([t.reshape(slab_size * RD, OB) for t in pair]) for pair in zip(*columns)]
    for bit in slab_bits:
        terms = halve(terms, "slab", 1, bit)
    volume = jnp.concatenate([added([term[part] for term in terms]) for part in range(2)], axis=1)

    own = volume.astype(BF16)
    plane = [own] + [flip(own, "dom", 2 * k) for k in range(1, dom_size // 2)]
    chip = dom_pos // 2
    placed = []
    for k in range(dom_size // 2):
        value = plane[0]
        for j in range(1, dom_size // 2):
            value = jnp.where(chip ^ j == k, plane[j], value)
        placed.append(value)
    value = jnp.stack(placed)
    got = flip(value, "dom", dom_bits[0])
    value = jnp.where(
        dom_pos & dom_bits[0] == 0,
        jnp.stack([value, got], 1),
        jnp.stack([got, value], 1),
    )
    return volume, value.reshape(dom_size * RD, width)


def solution(mesh):
    return jax.shard_map(
        shards,
        mesh=mesh,
        in_specs=(
            P("dom", "slab", None),
            P("dom", None),
            P(None, "slab", None),
            P("slab"),
            P(),
            P(),
            P(),
        ),
        out_specs=(P(("dom", "slab"), None), P(None, "slab")),
        check_vma=False,
    )
```

```python
import functools

import jax
import jax.numpy as jnp
from jax import lax
from jax.experimental import pallas as pl
from jax.experimental.pallas import tpu as pltpu
from jax.sharding import PartitionSpec as P

OB = 128
RD = 256
MB = 2**20
OUT_SLOTS = 4
OUT_TILE = 1024
F32 = jnp.float32
BF16 = jnp.bfloat16


def group_block(groups):
    return 16 if groups % 16 == 0 else 8


def spread_columns(blk_ref, cols_ref):
    count = blk_ref.shape[1]
    for j in range(2):
        for at in range(0, count, OB):
            line = blk_ref[j : j + 1, at : at + OB].astype(F32)
            cols_ref[j, at : at + OB, :] = jnp.broadcast_to(line, (OB, OB)).T


def score_kernel(here_ref, noise_ref, x_ref, r_ref, blk_ref, keep_ref, send_ref, *rest):
    *out_refs, w_ref, acc_ref, perm_ref, cols_ref = rest
    step = pl.program_id(0)
    particles, gb, width = x_ref.shape
    orients = r_ref.shape[0]
    side = 16 * gb
    core = here_ref[0] & 1

    @pl.when(step == 0)
    def _():
        row = lax.broadcasted_iota(jnp.int32, (side, side), 0)
        col = lax.broadcasted_iota(jnp.int32, (side, side), 1)
        same = ((row // 16) == (col % gb)) & ((row % 16) == (col // gb))
        perm_ref[...] = jnp.where(same, 1.0, 0.0).astype(BF16)
        acc_ref[...] = jnp.zeros_like(acc_ref)
        spread_columns(blk_ref, cols_ref)

    perm = perm_ref[...]

    per = gb // 2
    weighted = (w_ref.at[0], w_ref.at[1])

    def regroup(jobs):
        at = [pl.multiple_of(first * 16, 16) for _, _, _, first in jobs]
        wide = [job[0][pl.ds(a, 16)].reshape(side, width) for job, a in zip(jobs, at)]
        moved = jnp.dot(perm, jnp.concatenate(wide, axis=1), preferred_element_type=F32)
        for g in range(gb):
            lanes = slice(g % per * width, (g % per + 1) * width)
            for t, (_, halves, scaled, _) in enumerate(jobs):
                part = moved[g * 16 : (g + 1) * 16, t * width : (t + 1) * width]
                if scaled:
                    part = part * noise_ref[step * gb + g]
                halves[g // per][pl.ds(at[t], 16), lanes] = part.astype(BF16)

    def turn(src_ref, halves, first):
        at = pl.ds(pl.multiple_of(first * 16, 16), 16)
        turned = jnp.swapaxes(src_ref[at], 0, 1)
        for g in range(gb):
            halves[g // per][at, g % per * width : (g % per + 1) * width] = turned[g]

    both = min(particles, orients) // 64

    def all_tiles(halves):
        def tiles(i, carry):
            jobs = [(r_ref, weighted, True, i * 4 + t) for t in range(4)]
            regroup(jobs + [(x_ref, halves, False, i * 4)])
            for t in range(1, 4):
                turn(x_ref, halves, i * 4 + t)
            return carry

        def more_tiles(src_ref, goal, scaled):
            def body(i, carry):
                regroup([(src_ref, goal, scaled, i)])
                return carry

            lax.fori_loop(both * 4, src_ref.shape[0] // 16, body, 0)

        lax.fori_loop(0, both, tiles, 0, unroll=2)
        more_tiles(r_ref, weighted, True)
        more_tiles(x_ref, halves, False)

    @pl.when(core == 0)
    def _():
        all_tiles((keep_ref, send_ref))

    @pl.when(core == 1)
    def _():
        all_tiles((send_ref, keep_ref))

    for half_ref, which in ((keep_ref, core), (send_ref, 1 - core)):
        acc_ref[...] += lax.dot_general(
            half_ref[...], w_ref[which], (((1,), (1,)), ((), ())), preferred_element_type=F32
        )

    @pl.when(step == pl.num_programs(0) - 1)
    def _():
        me = here_ref[1]
        share = particles // len(out_refs)
        for k, out_ref in enumerate(out_refs):
            at = pl.multiple_of((me ^ k) * share, share)
            for j in range(2):
                wanted = cols_ref[j, pl.ds(at, share), :]
                chosen = jnp.zeros((share, OB), F32)
                for b in range(orients // OB):
                    value = acc_ref[pl.ds(at, share), b * OB : (b + 1) * OB]
                    chosen = jnp.where(wanted == b, value, chosen)
                out_ref[:, j * OB : (j + 1) * OB] = chosen


def score_call(here, inv_noise, particles, references, blocks, slab_size):
    count, groups, width = particles.shape
    orients = references.shape[0]
    gb = group_block(groups)
    side = 16 * gb
    share = count // slab_size
    smem = pl.BlockSpec(memory_space=pltpu.SMEM)
    return pl.pallas_call(
        score_kernel,
        grid=(groups // gb,),
        out_shape=[jax.ShapeDtypeStruct((count, groups // 2 * width), BF16)] * 2
        + [jax.ShapeDtypeStruct((share, 2 * OB), F32)] * slab_size,
        in_specs=[
            smem,
            smem,
            pl.BlockSpec((count, gb, width), lambda i: (0, i, 0)),
            pl.BlockSpec((orients, gb, width), lambda i: (0, i, 0)),
            pl.BlockSpec((2, count), lambda i: (0, 0)),
        ],
        out_specs=[pl.BlockSpec((count, gb // 2 * width), lambda i: (0, i))] * 2
        + [pl.BlockSpec((share, 2 * OB), lambda i: (0, 0))] * slab_size,
        scratch_shapes=[
            pltpu.VMEM((2, orients, gb // 2 * width), BF16),
            pltpu.VMEM((count, orients), F32),
            pltpu.VMEM((side, side), BF16),
            pltpu.VMEM((2, count, OB), F32),
        ],
        compiler_params=pltpu.CompilerParams(vmem_limit_bytes=56 * MB),
        cost_estimate=pl.CostEstimate(
            flops=4 * count * orients * groups * width,
            bytes_accessed=6 * count * groups * width,
            transcendentals=0,
        ),
    )(here, inv_noise, particles, references, blocks)


def softmax_kernel(*refs):
    *parts, out_ref = refs
    total = parts[0][...]
    for part in parts[1:]:
        total = total + part[...]
    highest = jnp.max(total, axis=1, keepdims=True)
    weights = jnp.exp(total - highest)
    out_ref[...] = (weights / jnp.sum(weights, axis=1, keepdims=True)).astype(BF16)


def softmax_call(parts):
    return pl.pallas_call(
        softmax_kernel,
        out_shape=jax.ShapeDtypeStruct(parts[0].shape, BF16),
        compiler_params=pltpu.CompilerParams(vmem_limit_bytes=8 * MB),
    )(*parts)


def own_row(here_ref, local, per):
    return lax.div(local, per) * (2 * per) + (here_ref[0] & 1) * per + lax.rem(local, per)


def plan_kernel(
    here_ref, dest_ref, pos_ref, addr_ref, item_ref, place_ref, hot_ref, count_ref, *, sizes, per
):
    step = pl.program_id(0)
    dom_size, slab_size = sizes
    owners = dom_size * slab_size
    _, units, half = pos_ref.shape
    lanes = addr_ref.shape[2]
    parts = dest_ref.shape[1] // half
    gb = units // parts
    dom_log, slab_log = (dom_size - 1).bit_length(), (slab_size - 1).bit_length()

    @pl.when(step == 0)
    def _():
        off = dest_ref[...] ^ (here_ref[0] * slab_size + here_ref[1])
        place = jnp.zeros_like(off)
        for bit in list(range(slab_log, slab_log + dom_log)) + list(range(slab_log)):
            place = place * 2 + (lax.shift_right_logical(off, bit) & 1)
        place_ref[...] = place

    owner = lax.broadcasted_iota(jnp.int32, (owners, 1), 0)
    for u in range(units):
        g, h = u // parts, u % parts
        at = pl.ds(own_row(here_ref, step * gb + g, per), 1)
        line = place_ref[at, h * half : (h + 1) * half]
        hot = jnp.where(line == owner, 1.0, 0.0)
        hot_ref[u * owners : (u + 1) * owners, :] = hot.astype(BF16)
    before = lax.broadcasted_iota(jnp.int32, (half, half), 0)
    after = lax.broadcasted_iota(jnp.int32, (half, half), 1)
    upto = jnp.where(before <= after, 1.0, 0.0).astype(BF16)
    count_ref[...] = jnp.dot(hot_ref[...], upto, preferred_element_type=F32)

    exact = functools.partial(
        jnp.dot, preferred_element_type=F32, precision=lax.Precision.HIGHEST
    )
    row = lax.broadcasted_iota(jnp.int32, (owners, owners), 0)
    col = lax.broadcasted_iota(jnp.int32, (owners, owners), 1)
    below = jnp.where(row > col, 1.0, 0.0)
    row = lax.broadcasted_iota(jnp.int32, (OB, OB), 0)
    col = lax.broadcasted_iota(jnp.int32, (OB, OB), 1)
    earlier = jnp.where(row < col, 1.0, 0.0)
    lane = lax.broadcasted_iota(jnp.int32, (owners, OB), 1)
    runs = jnp.zeros((owners, OB), F32)
    for u in range(units):
        size = count_ref[u * owners : (u + 1) * owners, half - 1 : half]
        runs = jnp.where(lane == u, size, runs)
    runs = jnp.floor((runs + 7.0) * 0.125) * 8.0
    base = exact(below, runs)
    ahead = exact(runs, earlier)
    total = jnp.sum(runs, axis=1, keepdims=True)
    start = exact(below, jnp.broadcast_to(total, (owners, OB)))[:, :1]
    blocks = jnp.floor((total + (RD - 1.0)) * (1.0 / RD))
    first = exact(below, jnp.broadcast_to(blocks, (owners, OB)))[:, :1]
    shift = start + ahead - base
    used = jnp.sum(runs, axis=0, keepdims=True)

    slot = (lax.broadcasted_iota(jnp.int32, (1, lanes), 1) * 8).astype(F32)
    is_last = lax.broadcasted_iota(jnp.int32, (1, lanes), 1) == lanes - 1
    rows = units * (half + 7 * owners)
    for u in range(units):
        low, size = base[:, u : u + 1], runs[:, u : u + 1]
        hot = hot_ref[u * owners : (u + 1) * owners, :].astype(F32)
        rank = count_ref[u * owners : (u + 1) * owners, :] + (low - 1.0)
        pos_ref[0, u : u + 1, :] = jnp.sum(hot * rank, axis=0, keepdims=True).astype(jnp.int32)
        inside = (slot >= low) & (slot < low + size)
        goal = jnp.where(inside, shift[:, u : u + 1] + slot - rows, 0.0)
        goal = (jnp.sum(goal, axis=0, keepdims=True) + rows) * 0.125
        addr_ref[0, u : u + 1, :] = jnp.where(is_last, used[:, u : u + 1], goal).astype(jnp.int32)

    wide = item_ref.shape[2]
    number = lax.broadcasted_iota(jnp.int32, (1, wide), 1).astype(F32)
    inside = (number >= first) & (number < first + blocks)
    done = (number - first) * RD
    pick = lambda value: jnp.sum(jnp.where(inside, value, 0.0), axis=0, keepdims=True)
    every = lambda value: jnp.sum(
        jnp.broadcast_to(value, (owners, wide)), axis=0, keepdims=True
    )
    lines = (
        pick(jnp.broadcast_to(owner.astype(F32), (owners, wide))),
        pick((start + done) * 0.125),
        pick(total - done),
        every(blocks),
        every(total * 0.125),
    )
    for i, value in enumerate(lines):
        item_ref[0, i : i + 1, :] = value.astype(jnp.int32)


def meta_kernel(here_ref, index_ref, frac_ref, pos_ref, meta_ref, *, per):
    step = pl.program_id(0)
    _, units, half = pos_ref.shape
    parts = index_ref.shape[1] // half
    gb = units // parts
    blocks = meta_ref.shape[2]
    low = lambda value: value.astype(F32).astype(BF16)
    eighth = low(lax.broadcasted_iota(jnp.int32, (blocks, half), 0))
    lane_of = low(lax.broadcasted_iota(jnp.int32, (OB, half), 0) % 8)
    one, none = jnp.bfloat16(1.0), jnp.bfloat16(0.0)
    for u in range(units):
        g, h = u // parts, u % parts
        line = pl.ds(own_row(here_ref, step * gb + g, per), 1)
        span = slice(h * half, (h + 1) * half)
        pos = pos_ref[0, u : u + 1, :]
        here = lane_of == low(pos & 7)
        spots = jnp.where(eighth == low(lax.shift_right_logical(pos, 3)), one, none)
        terms = [
            jnp.where(here, low(index_ref[line, span]), none),
            jnp.where(here, low(frac_ref[line, span]), none),
        ]
        meta_ref[0, u] = lax.dot_general(
            jnp.concatenate([spots, spots], axis=1),
            jnp.concatenate(terms, axis=1),
            (((1,), (1,)), ((), ())),
            preferred_element_type=F32,
        )


def up_to(value, step):
    return -(-value // step) * step


def sort_sizes(orients, owners):
    slots = orients + 7 * owners
    sure = orients + 144
    blocks = up_to((sure + up_to(max(0, slots - sure), 128)) // 8, 8)
    return slots, sure, blocks


def planned(shape):
    return pl.BlockSpec((1,) + shape[1:], lambda i, here: (i,) + (0,) * (len(shape) - 1))


def plan_call(here, destination, groups, gb, mesh_sizes):
    orients = destination.shape[1]
    half = min(256, orients)
    owners = mesh_sizes[0] * mesh_sizes[1]
    steps, units = groups // 2 // gb, gb * (orients // half)
    slots, _, blocks = sort_sizes(half, owners)
    shapes = [
        (steps, units, half),
        (steps, units, up_to(blocks + 1, 128)),
        (steps, 5, up_to(owners + units * slots // RD + 8, 128)),
    ]
    return pl.pallas_call(
        functools.partial(plan_kernel, sizes=mesh_sizes, per=group_block(groups) // 2),
        grid_spec=pltpu.PrefetchScalarGridSpec(
            num_scalar_prefetch=1,
            grid=(steps,),
            in_specs=[pl.BlockSpec((groups, orients), lambda i, here: (here[1], 0))],
            out_specs=[planned(shape) for shape in shapes],
            scratch_shapes=[
                pltpu.VMEM((groups, orients), jnp.int32),
                pltpu.VMEM((units * owners, half), BF16),
                pltpu.VMEM((units * owners, half), F32),
            ],
        ),
        out_shape=[jax.ShapeDtypeStruct(shape, jnp.int32) for shape in shapes],
        compiler_params=pltpu.CompilerParams(vmem_limit_bytes=60 * MB),
        cost_estimate=pl.CostEstimate(
            flops=8 * steps * units * owners * half * half,
            bytes_accessed=8 * groups * orients,
            transcendentals=0,
        ),
    )(here, destination)


def meta_call(here, row_index, fraction, pos, owners):
    steps, units, half = pos.shape
    orients = row_index.shape[1]
    groups = 2 * steps * units * half // orients
    blocks = sort_sizes(half, owners)[2]
    shape = (steps, units, blocks, OB)
    table = pl.BlockSpec((groups, orients), lambda i, here: (here[1], 0))
    return pl.pallas_call(
        functools.partial(meta_kernel, per=group_block(groups) // 2),
        grid_spec=pltpu.PrefetchScalarGridSpec(
            num_scalar_prefetch=1,
            grid=(steps,),
            in_specs=[table, table, planned(pos.shape)],
            out_specs=planned(shape),
        ),
        out_shape=jax.ShapeDtypeStruct(shape, F32),
        compiler_params=pltpu.CompilerParams(vmem_limit_bytes=16 * MB),
        cost_estimate=pl.CostEstimate(
            flops=8 * steps * units * blocks * half * OB,
            bytes_accessed=8 * steps * units * blocks * OB,
            transcendentals=0,
        ),
    )(here, row_index, fraction, pos)


def insert_kernel(
    me_ref, addr_ref, item_ref, x_ref, y_ref, pos_ref, meta_ref, blk_ref, more_blk_ref, *rest
):
    *post_refs, more_ref, send_ref, keep_ref = rest[:-10]
    post_t, spread_ref, cols_ref, slice_a, slice_b, buf_s, buf_m, volume, stage, sem = rest[-10:]
    step = pl.program_id(0)
    count = x_ref.shape[0]
    orients = post_t.shape[1]
    units, half = pos_ref.shape[1:]
    parts = orients // half
    gb = units // parts
    width = x_ref.shape[1] // gb
    share = count // len(post_refs)
    lanes = addr_ref.shape[2]

    @pl.when(step == 0)
    def _():
        volume[...] = jnp.zeros_like(volume)
        me = me_ref[0]
        others = [more_ref.at[k] for k in range(len(post_refs))]
        for who, (lists, pieces) in enumerate(((blk_ref, post_refs), (more_blk_ref, others))):
            spread_columns(lists, cols_ref)
            for k, post_ref in enumerate(pieces):
                at = pl.multiple_of((me ^ k) * share, share)
                post = post_ref[...].astype(F32)
                first = cols_ref[0, pl.ds(at, share), :]
                second = cols_ref[1, pl.ds(at, share), :]
                for b in range(orients // OB):
                    spread = jnp.where(
                        first == b, post[:, :OB], jnp.where(second == b, post[:, OB:], 0.0)
                    )
                    spread_ref[pl.ds(at, share), b * OB : (b + 1) * OB] = spread
            for b in range(orients // OB):
                rows = slice(b * OB, (b + 1) * OB)
                post_t[who, rows] = spread_ref[:, rows].T.astype(BF16)

    tail = pl.ds(pl.multiple_of(item_ref[0, 4, 0] * 8, 8), RD)
    buf_s[tail, :] = jnp.zeros((RD, width), F32)
    one, none = jnp.bfloat16(1.0), jnp.bfloat16(0.0)
    slots, sure, _ = sort_sizes(half, volume.shape[0] // RD)
    per = slice_a.shape[1] // width
    number = gb // per

    def slices(q, dst_ref):
        at = pl.ds(pl.multiple_of(q * (per * width), per * width), per * width)
        value = jnp.dot(post_t[0], x_ref[:, at], preferred_element_type=F32)
        value = value + jnp.dot(post_t[1], y_ref[:, at], preferred_element_type=F32)
        dst_ref[...] = value.astype(BF16)

    def emit(u, piece, base, size):
        pos = pos_ref[0, pl.ds(u, 1), :]
        order = []
        for at in range(0, size, 128):
            high = min(128, size - at)
            slot = lax.broadcasted_iota(jnp.int32, (high, half), 0).astype(F32).astype(BF16)
            near = jnp.clip(pos - (base + at), -1, 128).astype(F32).astype(BF16)
            order.append(jnp.where(slot == near, one, none))
        order = jnp.concatenate(order, axis=0)
        rows = jnp.dot(order, piece, preferred_element_type=F32)
        for i in range(size // 8):
            at = addr_ref[0, u, base // 8 + i]
            buf_s[pl.ds(pl.multiple_of(at * 8, 8), 8), :] = rows[8 * i : 8 * i + 8]
            buf_m[pl.ds(at, 1), :] = meta_ref[0, u, pl.ds(base // 8 + i, 1), :]

    def sort(q, src_ref):
        for g in range(per):
            for h in range(parts):
                piece = src_ref[h * half : (h + 1) * half, g * width : (g + 1) * width]
                emit((q * per + g) * parts + h, piece, 0, sure)

    def rest_of(q, src_ref):
        for g in range(per):
            for h in range(parts):
                u = (q * per + g) * parts + h

                def more(e, c, u=u, g=g, h=h):
                    piece = src_ref[h * half : (h + 1) * half, g * width : (g + 1) * width]
                    emit(u, piece, sure + e * 128, 128)
                    return c

                used = addr_ref[0, u, lanes - 1]
                lax.fori_loop(0, lax.div(jnp.maximum(used - sure, 0) + 127, 128), more, 0)

    def most_used(q):
        most = addr_ref[0, q * per * parts, lanes - 1]
        for u in range(1, per * parts):
            most = jnp.maximum(most, addr_ref[0, q * per * parts + u, lanes - 1])
        return most

    def two(j, carry):
        q = j * 2
        sort(q, slice_a)
        slices(q + 1, slice_b)

        @pl.when(most_used(q) > sure)
        def _():
            rest_of(q, slice_a)

        sort(q + 1, slice_b)
        slices(jnp.minimum(q + 2, number - 1), slice_a)

        @pl.when(most_used(q + 1) > sure)
        def _():
            rest_of(q + 1, slice_b)

        return carry

    slices(0, slice_a)
    lax.fori_loop(0, number // 2, two, 0)
    if number % 2:
        sort(number - 1, slice_a)
        rest_of(number - 1, slice_a)

    bins = lax.broadcasted_iota(jnp.int32, (RD, RD), 0).astype(F32).astype(BF16)
    side = RD // 2
    at_lane = lax.broadcasted_iota(jnp.int32, (side // 8, side), 1) // 8
    own_lane = at_lane == lax.broadcasted_iota(jnp.int32, (side // 8, side), 0)
    line = lax.broadcasted_iota(jnp.int32, (1, RD), 1)
    together = 8

    def some_items(q, carry):
        for u in range(together):
            j = q * together + u
            owner, at, left = item_ref[0, 0, j], item_ref[0, 1, j], item_ref[0, 2, j]
            places = [
                jnp.sum(
                    jnp.where(own_lane, buf_m[pl.ds(at + h * (side // 8), side // 8), :], 0.0),
                    axis=0,
                    keepdims=True,
                )
                for h in range(2)
            ]
            place = jnp.where(line < left, jnp.concatenate(places, axis=1), -9.0)
            whole = jnp.floor(place)
            apart = (bins - whole.astype(BF16)) - (place - whole).astype(BF16)
            weights = jnp.maximum(one - jnp.abs(apart), none)
            values = buf_s[pl.ds(pl.multiple_of(at * 8, 8), RD), :].astype(BF16)
            goal = pl.ds(pl.multiple_of(owner * RD, RD), RD)
            volume[goal, :] += jnp.dot(weights, values, preferred_element_type=F32)
        return carry

    count_items = lax.div(item_ref[0, 3, 0] + together - 1, together)
    lax.fori_loop(0, count_items, some_items, 0)

    @pl.when(step == pl.num_programs(0) - 1)
    def _():
        side_rows = keep_ref.shape[1]
        slots_out, _, tile, _ = stage.shape
        copies = []
        for base, out_ref in ((side_rows, send_ref), (0, keep_ref)):
            for at in range(0, side_rows, tile):
                slot = len(copies) % slots_out
                if len(copies) >= slots_out:
                    copies[len(copies) - slots_out].wait()
                value = volume[base + at : base + at + tile, :].astype(BF16)
                for c in range(2):
                    stage[slot, c] = value[:, c * OB : (c + 1) * OB]
                copy = pltpu.make_async_copy(
                    stage.at[slot], out_ref.at[:, pl.ds(at, tile)], sem.at[slot]
                )
                copy.start()
                copies.append(copy)
        for copy in copies[-slots_out:]:
            copy.wait()


def group_pair(gb):
    return 2 if gb % 2 == 0 else 1


def insert_block(groups, orients, owners, count, width):
    half = min(256, orients)
    slots, _, blocks = sort_sizes(half, owners)
    room = max(32 * MB - owners * RD * width * 4, 18 * MB)
    best = 1
    for gb in range(1, groups + 1):
        units = gb * (orients // half)
        rows = units * slots + RD + 8
        need = rows * (width * 4 + OB // 2) + 8 * count * gb * width + units * blocks * OB * 8
        if groups % gb == 0 and need <= room:
            best = gb
    return best


def insert_call(me, addr, items, flats, pos, meta, blocks, posts, more, orients, owners):
    count, length = flats[0].shape
    steps, units, half = pos.shape
    gb = units * half // orients
    width = length // (steps * gb)
    total = owners * RD
    share = posts[0].shape[0]
    rows = units * sort_sizes(half, owners)[0] + RD + 8
    limit = total * width * 4 // MB + 30
    smem = pl.BlockSpec(memory_space=pltpu.SMEM)
    block = lambda shape, **kw: pl.BlockSpec(
        (1,) + shape[1:], lambda i: (i,) + (0,) * (len(shape) - 1), **kw
    )
    return pl.pallas_call(
        insert_kernel,
        grid=(steps,),
        out_shape=[jax.ShapeDtypeStruct((2, total // 2, OB), BF16)] * 2,
        in_specs=[
            smem,
            block(addr.shape, memory_space=pltpu.SMEM),
            block(items.shape, memory_space=pltpu.SMEM),
            pl.BlockSpec((count, gb * width), lambda i: (0, i)),
            pl.BlockSpec((count, gb * width), lambda i: (0, i)),
            block(pos.shape),
            block(meta.shape),
            pl.BlockSpec((2, count), lambda i: (0, 0)),
            pl.BlockSpec((2, count), lambda i: (0, 0)),
        ]
        + [pl.BlockSpec((share, 2 * OB), lambda i: (0, 0))] * len(posts)
        + [pl.BlockSpec(more.shape, lambda i: (0, 0, 0))],
        out_specs=[pl.BlockSpec(memory_space=pl.ANY)] * 2,
        scratch_shapes=[
            pltpu.VMEM((2, orients, count), BF16),
            pltpu.VMEM((count, orients), F32),
            pltpu.VMEM((2, count, OB), F32),
            pltpu.VMEM((orients, group_pair(gb) * width), BF16),
            pltpu.VMEM((orients, group_pair(gb) * width), BF16),
            pltpu.VMEM((rows, width), F32),
            pltpu.VMEM((rows // 8, OB), F32),
            pltpu.VMEM((total, width), F32),
            pltpu.VMEM((OUT_SLOTS, 2, OUT_TILE, OB), BF16),
            pltpu.SemaphoreType.DMA((OUT_SLOTS,)),
        ],
        compiler_params=pltpu.CompilerParams(vmem_limit_bytes=limit * MB),
        cost_estimate=pl.CostEstimate(
            flops=8 * count * orients * length,
            bytes_accessed=2 * count * length,
            transcendentals=0,
        ),
    )(me, addr, items, *flats, pos, meta, *blocks, *posts, more)


def flip(value, axis, bit):
    size = lax.axis_size(axis)
    return lax.ppermute(value, axis, [(i, i ^ bit) for i in range(size)])


def shards(particles, blocks, references, inv_noise, destination, row_index, fraction):
    groups, width = particles.shape[1:]
    orients = references.shape[0]
    dom_size = lax.axis_size("dom")
    slab_size = lax.axis_size("slab")
    devices = dom_size * slab_size
    dom_pos = lax.axis_index("dom")
    slab_pos = lax.axis_index("slab")
    here = jnp.stack([dom_pos, slab_pos]).astype(jnp.int32)
    slab_me = here[1:]
    dom_bits = [1 << i for i in range((dom_size - 1).bit_length())]
    slab_bits = [1 << i for i in range((slab_size - 1).bit_length())]

    blocks = blocks.T
    kept, sent, *scores = score_call(here, inv_noise, particles, references, blocks, slab_size)
    gb = insert_block(groups // 2, orients, devices, particles.shape[0], width)
    here, own = lax.optimization_barrier((here, scores[0]))
    plan = plan_call(here, destination, groups, gb, (dom_size, slab_size))
    own, *plan = lax.optimization_barrier((own, *plan))
    pos, addr, items = plan
    parts = [own] + [flip(scores[k], "slab", k) for k in range(1, slab_size)]
    flats = [kept, flip(sent, "dom", dom_bits[0])]
    post = softmax_call(parts)
    post, pos = lax.optimization_barrier((post, pos))
    meta = meta_call(here, row_index, fraction, pos, devices)
    posts = [post] + [flip(post, "slab", k) for k in range(1, slab_size)]
    more = flip(jnp.stack(posts), "dom", dom_bits[0])
    lists = [blocks, flip(blocks, "dom", dom_bits[0])]
    send, keep = insert_call(
        slab_me, addr, items, flats, pos, meta, lists, posts, more, orients, devices
    )

    def added(terms):
        return functools.reduce(jnp.add, [term.astype(F32) for term in terms])

    def halve(terms, axis_name, axis, bit):
        size = terms[0].shape[axis] // 2
        pick = lambda term, at: lax.slice_in_dim(term, at, at + size, axis=axis)
        sent = added([pick(term, size) for term in terms]).astype(BF16)
        return [pick(term, 0) for term in terms] + [flip(sent, axis_name, bit)]

    terms = [keep, flip(send, "dom", dom_bits[0])]
    rest = dom_bits[1:]
    columns = []
    for part in range(2):
        columns.append(
            [term[part].reshape((2,) * len(rest) + (slab_size * RD, OB)) for term in terms]
        )
    for stage in range(len(rest)):
        for part in range(2):
            axis = stage if part == 0 else len(rest) - 1 - stage
            columns[part] = halve(columns[part], "dom", axis, rest[axis])
    terms = [jnp.stack([t.reshape(slab_size * RD, OB) for t in pair]) for pair in zip(*columns)]
    for bit in slab_bits:
        terms = halve(terms, "slab", 1, bit)
    volume = jnp.concatenate([added([term[part] for term in terms]) for part in range(2)], axis=1)

    own = volume.astype(BF16)
    plane = [own] + [flip(own, "dom", 2 * k) for k in range(1, dom_size // 2)]
    chip = dom_pos // 2
    placed = []
    for k in range(dom_size // 2):
        value = plane[0]
        for j in range(1, dom_size // 2):
            value = jnp.where(chip ^ j == k, plane[j], value)
        placed.append(value)
    value = jnp.stack(placed)
    got = flip(value, "dom", dom_bits[0])
    value = jnp.where(
        dom_pos & dom_bits[0] == 0,
        jnp.stack([value, got], 1),
        jnp.stack([got, value], 1),
    )
    return volume, value.reshape(dom_size * RD, width)


def solution(mesh):
    return jax.shard_map(
        shards,
        mesh=mesh,
        in_specs=(
            P("dom", "slab", None),
            P("dom", None),
            P(None, "slab", None),
            P("slab"),
            P(),
            P(),
            P(),
        ),
        out_specs=(P(("dom", "slab"), None), P(None, "slab")),
        check_vma=False,
    )
```

```python
import functools

import jax
import jax.numpy as jnp
from jax import lax
from jax.experimental import pallas as pl
from jax.experimental.pallas import tpu as pltpu
from jax.sharding import PartitionSpec as P

OB = 128
RD = 256
MB = 2**20
OUT_SLOTS = 4
OUT_TILE = 1024
F32 = jnp.float32
BF16 = jnp.bfloat16


def group_block(groups):
    return 16 if groups % 16 == 0 else 8


def spread_columns(blk_ref, cols_ref):
    count = blk_ref.shape[1]
    for j in range(2):
        for at in range(0, count, OB):
            line = blk_ref[j : j + 1, at : at + OB].astype(F32)
            cols_ref[j, at : at + OB, :] = jnp.broadcast_to(line, (OB, OB)).T


def score_kernel(here_ref, noise_ref, x_ref, r_ref, blk_ref, keep_ref, send_ref, *rest):
    out_refs = rest[:-8]
    flat_a, flat_b, w_a, w_b, acc_ref, perm_ref, cols_ref, sem = rest[-8:]
    step = pl.program_id(0)
    steps = pl.num_programs(0) - 1
    particles, gb, width = x_ref.shape
    orients = r_ref.shape[0]
    side = 16 * gb
    per = gb // 2
    core = here_ref[0] & 1
    rounds = 4

    def copies(flat_ref, slot, at_step, swap):
        lanes = pl.ds(pl.multiple_of(at_step * (per * width), per * width), per * width)
        goals = (send_ref, keep_ref) if swap else (keep_ref, send_ref)
        return [
            pltpu.make_async_copy(flat_ref.at[h], goals[h].at[:, lanes], sem.at[slot, h])
            for h in range(2)
        ]

    def send_out(flat_ref, slot):
        for which in range(2):

            @pl.when(core == which)
            def _(which=which):
                for copy in copies(flat_ref, slot, step, which == 1):
                    copy.start()

    def wait_out(flat_ref, slot):
        for copy in copies(flat_ref, slot, 0, False):
            copy.wait()

    def regroup(jobs):
        at = [pl.multiple_of(first * 16, 16) for _, _, _, first in jobs]
        wide = [job[0][pl.ds(a, 16)].reshape(side, width) for job, a in zip(jobs, at)]
        moved = jnp.dot(perm_ref[...], jnp.concatenate(wide, axis=1), preferred_element_type=F32)
        for g in range(gb):
            lanes = slice(g % per * width, (g % per + 1) * width)
            for t, (_, goal_ref, scaled, _) in enumerate(jobs):
                part = moved[g * 16 : (g + 1) * 16, t * width : (t + 1) * width]
                if scaled:
                    part = part * noise_ref[step * gb + g]
                goal_ref[g // per, pl.ds(at[t], 16), lanes] = part.astype(BF16)

    def turn(src_ref, goal_ref, first):
        at = pl.ds(pl.multiple_of(first * 16, 16), 16)
        turned = jnp.swapaxes(src_ref[at], 0, 1)
        for g in range(gb):
            goal_ref[g // per, at, g % per * width : (g % per + 1) * width] = turned[g]

    def tiles(i, flat_ref, w_ref):
        ours, theirs = orients // 16 // rounds, particles // 16 // rounds
        jobs = [(r_ref, w_ref, True, i * ours + t) for t in range(ours)]
        for t in range(0, theirs, 4):
            jobs.append((x_ref, flat_ref, False, i * theirs + t))
        for at in range(0, len(jobs), 5):
            regroup(jobs[at : at + 5])
        for t in range(theirs):
            if t % 4:
                turn(x_ref, flat_ref, i * theirs + t)

    def product(left, right):
        acc_ref[...] += lax.dot_general(
            left, right, (((1,), (1,)), ((), ())), preferred_element_type=F32
        )

    def both(i, flat_ref, w_ref, last_flat, last_w):
        span = 2 * per * width // rounds
        at = pl.ds(pl.multiple_of(lax.rem(i, rounds // 2) * span, span), span)
        h = lax.div(i, rounds // 2)
        product(last_flat[h, :, at], last_w[h, :, at])
        tiles(i, flat_ref, w_ref)

    def loop(body, *refs):
        lax.fori_loop(0, rounds, lambda i, c: (body(i, *refs), c)[1], 0)

    @pl.when(step == 0)
    def _():
        row = lax.broadcasted_iota(jnp.int32, (side, side), 0)
        col = lax.broadcasted_iota(jnp.int32, (side, side), 1)
        same = ((row // 16) == (col % gb)) & ((row % 16) == (col // gb))
        perm_ref[...] = jnp.where(same, 1.0, 0.0).astype(BF16)
        acc_ref[...] = jnp.zeros_like(acc_ref)
        spread_columns(blk_ref, cols_ref)
        loop(tiles, flat_a, w_a)
        send_out(flat_a, 0)

    inner = (step > 0) & (step < steps)

    @pl.when(inner & (lax.rem(step, 2) == 1))
    def _():
        @pl.when(step > 1)
        def _():
            wait_out(flat_b, 1)

        loop(both, flat_b, w_b, flat_a, w_a)
        send_out(flat_b, 1)

    @pl.when(inner & (lax.rem(step, 2) == 0))
    def _():
        wait_out(flat_a, 0)
        loop(both, flat_a, w_a, flat_b, w_b)
        send_out(flat_a, 0)

    def finish(last_flat, last_w):
        for h in range(2):
            product(last_flat[h], last_w[h])
        me = here_ref[1]
        share = particles // len(out_refs)
        for k, out_ref in enumerate(out_refs):
            at = pl.multiple_of((me ^ k) * share, share)
            for j in range(2):
                wanted = cols_ref[j, pl.ds(at, share), :]
                chosen = jnp.zeros((share, OB), F32)
                for b in range(orients // OB):
                    value = acc_ref[pl.ds(at, share), b * OB : (b + 1) * OB]
                    chosen = jnp.where(wanted == b, value, chosen)
                out_ref[:, j * OB : (j + 1) * OB] = chosen
        wait_out(flat_a, 0)

        @pl.when(steps > 1)
        def _():
            wait_out(flat_b, 1)

    @pl.when((step == steps) & (lax.rem(step, 2) == 1))
    def _():
        finish(flat_a, w_a)

    @pl.when((step == steps) & (lax.rem(step, 2) == 0))
    def _():
        finish(flat_b, w_b)


def score_call(here, inv_noise, particles, references, blocks, slab_size):
    count, groups, width = particles.shape
    orients = references.shape[0]
    gb = group_block(groups)
    side = 16 * gb
    share = count // slab_size
    smem = pl.BlockSpec(memory_space=pltpu.SMEM)
    steps = groups // gb
    return pl.pallas_call(
        score_kernel,
        grid=(steps + 1,),
        out_shape=[jax.ShapeDtypeStruct((count, groups // 2 * width), BF16)] * 2
        + [jax.ShapeDtypeStruct((share, 2 * OB), F32)] * slab_size,
        in_specs=[
            smem,
            smem,
            pl.BlockSpec((count, gb, width), lambda i: (0, jnp.minimum(i, steps - 1), 0)),
            pl.BlockSpec((orients, gb, width), lambda i: (0, jnp.minimum(i, steps - 1), 0)),
            pl.BlockSpec((2, count), lambda i: (0, 0)),
        ],
        out_specs=[pl.BlockSpec(memory_space=pl.ANY)] * 2
        + [pl.BlockSpec((share, 2 * OB), lambda i: (0, 0))] * slab_size,
        scratch_shapes=[
            pltpu.VMEM((2, count, gb // 2 * width), BF16),
            pltpu.VMEM((2, count, gb // 2 * width), BF16),
            pltpu.VMEM((2, orients, gb // 2 * width), BF16),
            pltpu.VMEM((2, orients, gb // 2 * width), BF16),
            pltpu.VMEM((count, orients), F32),
            pltpu.VMEM((side, side), BF16),
            pltpu.VMEM((2, count, OB), F32),
            pltpu.SemaphoreType.DMA((2, 2)),
        ],
        compiler_params=pltpu.CompilerParams(vmem_limit_bytes=56 * MB),
        cost_estimate=pl.CostEstimate(
            flops=4 * count * orients * groups * width,
            bytes_accessed=6 * count * groups * width,
            transcendentals=0,
        ),
    )(here, inv_noise, particles, references, blocks)


def softmax_kernel(*refs):
    *parts, out_ref = refs
    total = parts[0][...]
    for part in parts[1:]:
        total = total + part[...]
    highest = jnp.max(total, axis=1, keepdims=True)
    weights = jnp.exp(total - highest)
    out_ref[...] = (weights / jnp.sum(weights, axis=1, keepdims=True)).astype(BF16)


def softmax_call(parts):
    return pl.pallas_call(
        softmax_kernel,
        out_shape=jax.ShapeDtypeStruct(parts[0].shape, BF16),
        compiler_params=pltpu.CompilerParams(vmem_limit_bytes=8 * MB),
    )(*parts)


def own_row(here_ref, local, per):
    return lax.div(local, per) * (2 * per) + (here_ref[0] & 1) * per + lax.rem(local, per)


def plan_kernel(
    here_ref, dest_ref, pos_ref, addr_ref, item_ref, place_ref, hot_ref, count_ref, *, sizes, per
):
    step = pl.program_id(0)
    dom_size, slab_size = sizes
    owners = dom_size * slab_size
    _, units, half = pos_ref.shape
    lanes = addr_ref.shape[2]
    parts = dest_ref.shape[1] // half
    gb = units // parts
    dom_log, slab_log = (dom_size - 1).bit_length(), (slab_size - 1).bit_length()

    @pl.when(step == 0)
    def _():
        off = dest_ref[...] ^ (here_ref[0] * slab_size + here_ref[1])
        place = jnp.zeros_like(off)
        for bit in list(range(slab_log, slab_log + dom_log)) + list(range(slab_log)):
            place = place * 2 + (lax.shift_right_logical(off, bit) & 1)
        place_ref[...] = place

    owner = lax.broadcasted_iota(jnp.int32, (owners, 1), 0)
    for u in range(units):
        g, h = u // parts, u % parts
        at = pl.ds(own_row(here_ref, step * gb + g, per), 1)
        line = place_ref[at, h * half : (h + 1) * half]
        hot = jnp.where(line == owner, 1.0, 0.0)
        hot_ref[u * owners : (u + 1) * owners, :] = hot.astype(BF16)
    before = lax.broadcasted_iota(jnp.int32, (half, half), 0)
    after = lax.broadcasted_iota(jnp.int32, (half, half), 1)
    upto = jnp.where(before <= after, 1.0, 0.0).astype(BF16)
    count_ref[...] = jnp.dot(hot_ref[...], upto, preferred_element_type=F32)

    exact = functools.partial(
        jnp.dot, preferred_element_type=F32, precision=lax.Precision.HIGHEST
    )
    row = lax.broadcasted_iota(jnp.int32, (owners, owners), 0)
    col = lax.broadcasted_iota(jnp.int32, (owners, owners), 1)
    below = jnp.where(row > col, 1.0, 0.0)
    row = lax.broadcasted_iota(jnp.int32, (OB, OB), 0)
    col = lax.broadcasted_iota(jnp.int32, (OB, OB), 1)
    earlier = jnp.where(row < col, 1.0, 0.0)
    lane = lax.broadcasted_iota(jnp.int32, (owners, OB), 1)
    runs = jnp.zeros((owners, OB), F32)
    for u in range(units):
        size = count_ref[u * owners : (u + 1) * owners, half - 1 : half]
        runs = jnp.where(lane == u, size, runs)
    runs = jnp.floor((runs + 7.0) * 0.125) * 8.0
    base = exact(below, runs)
    ahead = exact(runs, earlier)
    total = jnp.sum(runs, axis=1, keepdims=True)
    start = exact(below, jnp.broadcast_to(total, (owners, OB)))[:, :1]
    blocks = jnp.floor((total + (RD - 1.0)) * (1.0 / RD))
    first = exact(below, jnp.broadcast_to(blocks, (owners, OB)))[:, :1]
    shift = start + ahead - base
    used = jnp.sum(runs, axis=0, keepdims=True)

    slot = (lax.broadcasted_iota(jnp.int32, (1, lanes), 1) * 8).astype(F32)
    is_last = lax.broadcasted_iota(jnp.int32, (1, lanes), 1) == lanes - 1
    rows = units * (half + 7 * owners)
    for u in range(units):
        low, size = base[:, u : u + 1], runs[:, u : u + 1]
        hot = hot_ref[u * owners : (u + 1) * owners, :].astype(F32)
        rank = count_ref[u * owners : (u + 1) * owners, :] + (low - 1.0)
        pos_ref[0, u : u + 1, :] = jnp.sum(hot * rank, axis=0, keepdims=True).astype(jnp.int32)
        inside = (slot >= low) & (slot < low + size)
        goal = jnp.where(inside, shift[:, u : u + 1] + slot - rows, 0.0)
        goal = (jnp.sum(goal, axis=0, keepdims=True) + rows) * 0.125
        addr_ref[0, u : u + 1, :] = jnp.where(is_last, used[:, u : u + 1], goal).astype(jnp.int32)

    wide = item_ref.shape[2]
    number = lax.broadcasted_iota(jnp.int32, (1, wide), 1).astype(F32)
    inside = (number >= first) & (number < first + blocks)
    done = (number - first) * RD
    pick = lambda value: jnp.sum(jnp.where(inside, value, 0.0), axis=0, keepdims=True)
    every = lambda value: jnp.sum(
        jnp.broadcast_to(value, (owners, wide)), axis=0, keepdims=True
    )
    lines = (
        pick(jnp.broadcast_to(owner.astype(F32), (owners, wide))),
        pick((start + done) * 0.125),
        pick(total - done),
        every(blocks),
        every(total * 0.125),
    )
    for i, value in enumerate(lines):
        item_ref[0, i : i + 1, :] = value.astype(jnp.int32)


def meta_kernel(here_ref, index_ref, frac_ref, pos_ref, meta_ref, *, per):
    step = pl.program_id(0)
    _, units, half = pos_ref.shape
    parts = index_ref.shape[1] // half
    gb = units // parts
    blocks = meta_ref.shape[2]
    low = lambda value: value.astype(F32).astype(BF16)
    eighth = low(lax.broadcasted_iota(jnp.int32, (blocks, half), 0))
    lane_of = low(lax.broadcasted_iota(jnp.int32, (OB, half), 0) % 8)
    one, none = jnp.bfloat16(1.0), jnp.bfloat16(0.0)
    for u in range(units):
        g, h = u // parts, u % parts
        line = pl.ds(own_row(here_ref, step * gb + g, per), 1)
        span = slice(h * half, (h + 1) * half)
        pos = pos_ref[0, u : u + 1, :]
        here = lane_of == low(pos & 7)
        spots = jnp.where(eighth == low(lax.shift_right_logical(pos, 3)), one, none)
        terms = [
            jnp.where(here, low(index_ref[line, span]), none),
            jnp.where(here, low(frac_ref[line, span]), none),
        ]
        meta_ref[0, u] = lax.dot_general(
            jnp.concatenate([spots, spots], axis=1),
            jnp.concatenate(terms, axis=1),
            (((1,), (1,)), ((), ())),
            preferred_element_type=F32,
        )


def up_to(value, step):
    return -(-value // step) * step


def sort_sizes(orients, owners):
    slots = orients + 7 * owners
    sure = orients + 144
    blocks = up_to((sure + up_to(max(0, slots - sure), 128)) // 8, 8)
    return slots, sure, blocks


def planned(shape):
    return pl.BlockSpec((1,) + shape[1:], lambda i, here: (i,) + (0,) * (len(shape) - 1))


def plan_call(here, destination, groups, gb, mesh_sizes):
    orients = destination.shape[1]
    half = min(256, orients)
    owners = mesh_sizes[0] * mesh_sizes[1]
    steps, units = groups // 2 // gb, gb * (orients // half)
    slots, _, blocks = sort_sizes(half, owners)
    shapes = [
        (steps, units, half),
        (steps, units, up_to(blocks + 1, 128)),
        (steps, 5, up_to(owners + units * slots // RD + 8, 128)),
    ]
    return pl.pallas_call(
        functools.partial(plan_kernel, sizes=mesh_sizes, per=group_block(groups) // 2),
        grid_spec=pltpu.PrefetchScalarGridSpec(
            num_scalar_prefetch=1,
            grid=(steps,),
            in_specs=[pl.BlockSpec((groups, orients), lambda i, here: (here[1], 0))],
            out_specs=[planned(shape) for shape in shapes],
            scratch_shapes=[
                pltpu.VMEM((groups, orients), jnp.int32),
                pltpu.VMEM((units * owners, half), BF16),
                pltpu.VMEM((units * owners, half), F32),
            ],
        ),
        out_shape=[jax.ShapeDtypeStruct(shape, jnp.int32) for shape in shapes],
        compiler_params=pltpu.CompilerParams(vmem_limit_bytes=55 * MB),
        cost_estimate=pl.CostEstimate(
            flops=8 * steps * units * owners * half * half,
            bytes_accessed=8 * groups * orients,
            transcendentals=0,
        ),
    )(here, destination)


def meta_call(here, row_index, fraction, pos, owners):
    steps, units, half = pos.shape
    orients = row_index.shape[1]
    groups = 2 * steps * units * half // orients
    blocks = sort_sizes(half, owners)[2]
    shape = (steps, units, blocks, OB)
    table = pl.BlockSpec((groups, orients), lambda i, here: (here[1], 0))
    return pl.pallas_call(
        functools.partial(meta_kernel, per=group_block(groups) // 2),
        grid_spec=pltpu.PrefetchScalarGridSpec(
            num_scalar_prefetch=1,
            grid=(steps,),
            in_specs=[table, table, planned(pos.shape)],
            out_specs=planned(shape),
        ),
        out_shape=jax.ShapeDtypeStruct(shape, F32),
        compiler_params=pltpu.CompilerParams(vmem_limit_bytes=16 * MB),
        cost_estimate=pl.CostEstimate(
            flops=8 * steps * units * blocks * half * OB,
            bytes_accessed=8 * steps * units * blocks * OB,
            transcendentals=0,
        ),
    )(here, row_index, fraction, pos)


def insert_kernel(
    me_ref, addr_ref, item_ref, x_ref, y_ref, pos_ref, meta_ref, blk_ref, more_blk_ref, *rest
):
    *post_refs, more_ref, send_ref, keep_ref = rest[:-10]
    post_t, spread_ref, cols_ref, slice_a, slice_b, buf_s, buf_m, volume, stage, sem = rest[-10:]
    step = pl.program_id(0)
    count = x_ref.shape[0]
    orients = post_t.shape[0]
    units, half = pos_ref.shape[1:]
    parts = orients // half
    gb = units // parts
    width = x_ref.shape[1] // gb
    share = count // len(post_refs)
    lanes = addr_ref.shape[2]

    @pl.when(step == 0)
    def _():
        volume[...] = jnp.zeros_like(volume)
        me = me_ref[0]
        others = [more_ref.at[k] for k in range(len(post_refs))]
        for who, (lists, pieces) in enumerate(((blk_ref, post_refs), (more_blk_ref, others))):
            spread_columns(lists, cols_ref)
            for k, post_ref in enumerate(pieces):
                at = pl.multiple_of((me ^ k) * share, share)
                post = post_ref[...].astype(F32)
                first = cols_ref[0, pl.ds(at, share), :]
                second = cols_ref[1, pl.ds(at, share), :]
                for b in range(orients // OB):
                    spread = jnp.where(
                        first == b, post[:, :OB], jnp.where(second == b, post[:, OB:], 0.0)
                    )
                    spread_ref[pl.ds(at, share), b * OB : (b + 1) * OB] = spread
            for b in range(orients // OB):
                rows = slice(b * OB, (b + 1) * OB)
                post_t[rows, who * count : (who + 1) * count] = spread_ref[:, rows].T.astype(BF16)

    tail = pl.ds(pl.multiple_of(item_ref[0, 4, 0] * 8, 8), RD)
    buf_s[tail, :] = jnp.zeros((RD, width), F32)
    one, none = jnp.bfloat16(1.0), jnp.bfloat16(0.0)
    slots, sure, _ = sort_sizes(half, volume.shape[0] // RD)
    per = slice_a.shape[1] // width
    number = gb // per

    def slices(q, dst_ref):
        at = pl.ds(pl.multiple_of(q * (per * width), per * width), per * width)
        images = jnp.concatenate([x_ref[:, at], y_ref[:, at]], axis=0)
        value = jnp.dot(post_t[...], images, preferred_element_type=F32)
        dst_ref[...] = value.astype(BF16)

    def emit(u, piece, base, size):
        pos = pos_ref[0, pl.ds(u, 1), :]
        order = []
        for at in range(0, size, 128):
            high = min(128, size - at)
            slot = lax.broadcasted_iota(jnp.int32, (high, half), 0).astype(F32).astype(BF16)
            near = jnp.clip(pos - (base + at), -1, 128).astype(F32).astype(BF16)
            order.append(jnp.where(slot == near, one, none))
        order = jnp.concatenate(order, axis=0)
        rows = jnp.dot(order, piece, preferred_element_type=F32)
        for i in range(size // 8):
            at = addr_ref[0, u, base // 8 + i]
            buf_s[pl.ds(pl.multiple_of(at * 8, 8), 8), :] = rows[8 * i : 8 * i + 8]
            buf_m[pl.ds(at, 1), :] = meta_ref[0, u, pl.ds(base // 8 + i, 1), :]

    def sort(q, src_ref):
        for g in range(per):
            for h in range(parts):
                piece = src_ref[h * half : (h + 1) * half, g * width : (g + 1) * width]
                emit((q * per + g) * parts + h, piece, 0, sure)

    def rest_of(q, src_ref):
        for g in range(per):
            for h in range(parts):
                u = (q * per + g) * parts + h

                def more(e, c, u=u, g=g, h=h):
                    piece = src_ref[h * half : (h + 1) * half, g * width : (g + 1) * width]
                    emit(u, piece, sure + e * 128, 128)
                    return c

                used = addr_ref[0, u, lanes - 1]
                lax.fori_loop(0, lax.div(jnp.maximum(used - sure, 0) + 127, 128), more, 0)

    def most_used(q):
        most = addr_ref[0, q * per * parts, lanes - 1]
        for u in range(1, per * parts):
            most = jnp.maximum(most, addr_ref[0, q * per * parts + u, lanes - 1])
        return most

    def two(j, carry):
        q = j * 2
        sort(q, slice_a)
        slices(q + 1, slice_b)

        @pl.when(most_used(q) > sure)
        def _():
            rest_of(q, slice_a)

        sort(q + 1, slice_b)
        slices(jnp.minimum(q + 2, number - 1), slice_a)

        @pl.when(most_used(q + 1) > sure)
        def _():
            rest_of(q + 1, slice_b)

        return carry

    slices(0, slice_a)
    lax.fori_loop(0, number // 2, two, 0)
    if number % 2:
        sort(number - 1, slice_a)
        rest_of(number - 1, slice_a)

    bins = lax.broadcasted_iota(jnp.int32, (RD, RD), 0).astype(F32).astype(BF16)
    side = RD // 2
    at_lane = lax.broadcasted_iota(jnp.int32, (side // 8, side), 1) // 8
    own_lane = at_lane == lax.broadcasted_iota(jnp.int32, (side // 8, side), 0)
    line = lax.broadcasted_iota(jnp.int32, (1, RD), 1)
    together = 8

    def some_items(q, carry):
        for u in range(together):
            j = q * together + u
            owner, at, left = item_ref[0, 0, j], item_ref[0, 1, j], item_ref[0, 2, j]
            places = [
                jnp.sum(
                    jnp.where(own_lane, buf_m[pl.ds(at + h * (side // 8), side // 8), :], 0.0),
                    axis=0,
                    keepdims=True,
                )
                for h in range(2)
            ]
            place = jnp.where(line < left, jnp.concatenate(places, axis=1), -9.0)
            whole = jnp.floor(place)
            apart = (bins - whole.astype(BF16)) - (place - whole).astype(BF16)
            weights = jnp.maximum(one - jnp.abs(apart), none)
            values = buf_s[pl.ds(pl.multiple_of(at * 8, 8), RD), :].astype(BF16)
            goal = pl.ds(pl.multiple_of(owner * RD, RD), RD)
            volume[goal, :] += jnp.dot(weights, values, preferred_element_type=F32)
        return carry

    count_items = lax.div(item_ref[0, 3, 0] + together - 1, together)
    lax.fori_loop(0, count_items, some_items, 0)

    @pl.when(step == pl.num_programs(0) - 1)
    def _():
        side_rows = keep_ref.shape[1]
        slots_out, _, tile, _ = stage.shape
        copies = []
        for base, out_ref in ((side_rows, send_ref), (0, keep_ref)):
            for at in range(0, side_rows, tile):
                slot = len(copies) % slots_out
                if len(copies) >= slots_out:
                    copies[len(copies) - slots_out].wait()
                value = volume[base + at : base + at + tile, :].astype(BF16)
                for c in range(2):
                    stage[slot, c] = value[:, c * OB : (c + 1) * OB]
                copy = pltpu.make_async_copy(
                    stage.at[slot], out_ref.at[:, pl.ds(at, tile)], sem.at[slot]
                )
                copy.start()
                copies.append(copy)
        for copy in copies[-slots_out:]:
            copy.wait()


def group_pair(gb):
    return 2 if gb % 2 == 0 else 1


def insert_block(groups, orients, owners, count, width):
    half = min(256, orients)
    slots, _, blocks = sort_sizes(half, owners)
    room = max(32 * MB - owners * RD * width * 4, 18 * MB)
    best = 1
    for gb in range(1, groups + 1):
        units = gb * (orients // half)
        rows = units * slots + RD + 8
        need = rows * (width * 4 + OB // 2) + 8 * count * gb * width + units * blocks * OB * 8
        if groups % gb == 0 and need <= room:
            best = gb
    return best


def insert_call(me, addr, items, flats, pos, meta, blocks, posts, more, orients, owners):
    count, length = flats[0].shape
    steps, units, half = pos.shape
    gb = units * half // orients
    width = length // (steps * gb)
    total = owners * RD
    share = posts[0].shape[0]
    rows = units * sort_sizes(half, owners)[0] + RD + 8
    limit = total * width * 4 // MB + 30
    smem = pl.BlockSpec(memory_space=pltpu.SMEM)
    block = lambda shape, **kw: pl.BlockSpec(
        (1,) + shape[1:], lambda i: (i,) + (0,) * (len(shape) - 1), **kw
    )
    return pl.pallas_call(
        insert_kernel,
        grid=(steps,),
        out_shape=[jax.ShapeDtypeStruct((2, total // 2, OB), BF16)] * 2,
        in_specs=[
            smem,
            block(addr.shape, memory_space=pltpu.SMEM),
            block(items.shape, memory_space=pltpu.SMEM),
            pl.BlockSpec((count, gb * width), lambda i: (0, i)),
            pl.BlockSpec((count, gb * width), lambda i: (0, i)),
            block(pos.shape),
            block(meta.shape),
            pl.BlockSpec((2, count), lambda i: (0, 0)),
            pl.BlockSpec((2, count), lambda i: (0, 0)),
        ]
        + [pl.BlockSpec((share, 2 * OB), lambda i: (0, 0))] * len(posts)
        + [pl.BlockSpec(more.shape, lambda i: (0, 0, 0))],
        out_specs=[pl.BlockSpec(memory_space=pl.ANY)] * 2,
        scratch_shapes=[
            pltpu.VMEM((orients, 2 * count), BF16),
            pltpu.VMEM((count, orients), F32),
            pltpu.VMEM((2, count, OB), F32),
            pltpu.VMEM((orients, group_pair(gb) * width), BF16),
            pltpu.VMEM((orients, group_pair(gb) * width), BF16),
            pltpu.VMEM((rows, width), F32),
            pltpu.VMEM((rows // 8, OB), F32),
            pltpu.VMEM((total, width), F32),
            pltpu.VMEM((OUT_SLOTS, 2, OUT_TILE, OB), BF16),
            pltpu.SemaphoreType.DMA((OUT_SLOTS,)),
        ],
        compiler_params=pltpu.CompilerParams(vmem_limit_bytes=limit * MB),
        cost_estimate=pl.CostEstimate(
            flops=8 * count * orients * length,
            bytes_accessed=2 * count * length,
            transcendentals=0,
        ),
    )(me, addr, items, *flats, pos, meta, *blocks, *posts, more)


def flip(value, axis, bit):
    size = lax.axis_size(axis)
    return lax.ppermute(value, axis, [(i, i ^ bit) for i in range(size)])


def shards(particles, blocks, references, inv_noise, destination, row_index, fraction):
    groups, width = particles.shape[1:]
    orients = references.shape[0]
    dom_size = lax.axis_size("dom")
    slab_size = lax.axis_size("slab")
    devices = dom_size * slab_size
    dom_pos = lax.axis_index("dom")
    slab_pos = lax.axis_index("slab")
    here = jnp.stack([dom_pos, slab_pos]).astype(jnp.int32)
    slab_me = here[1:]
    dom_bits = [1 << i for i in range((dom_size - 1).bit_length())]
    slab_bits = [1 << i for i in range((slab_size - 1).bit_length())]

    blocks = blocks.T
    kept, sent, *scores = score_call(here, inv_noise, particles, references, blocks, slab_size)
    gb = insert_block(groups // 2, orients, devices, particles.shape[0], width)
    here, own = lax.optimization_barrier((here, scores[0]))
    plan = plan_call(here, destination, groups, gb, (dom_size, slab_size))
    own, *plan = lax.optimization_barrier((own, *plan))
    pos, addr, items = plan
    parts = [own] + [flip(scores[k], "slab", k) for k in range(1, slab_size)]
    flats = [kept, flip(sent, "dom", dom_bits[0])]
    post = softmax_call(parts)
    more_blocks = flip(blocks, "dom", dom_bits[0])
    post, more_blocks, later = lax.optimization_barrier((post, more_blocks, here))
    meta = meta_call(later, row_index, fraction, pos, devices)
    posts = [post] + [flip(post, "slab", k) for k in range(1, slab_size)]
    pile, meta = lax.optimization_barrier((jnp.stack(posts), meta))
    more = flip(pile, "dom", dom_bits[0])
    lists = [blocks, more_blocks]
    send, keep = insert_call(
        slab_me, addr, items, flats, pos, meta, lists, posts, more, orients, devices
    )

    def added(terms):
        return functools.reduce(jnp.add, [term.astype(F32) for term in terms])

    def halve(terms, axis_name, axis, bit):
        size = terms[0].shape[axis] // 2
        pick = lambda term, at: lax.slice_in_dim(term, at, at + size, axis=axis)
        sent = added([pick(term, size) for term in terms]).astype(BF16)
        return [pick(term, 0) for term in terms] + [flip(sent, axis_name, bit)]

    terms = [keep, flip(send, "dom", dom_bits[0])]
    rest = dom_bits[1:]
    columns = []
    for part in range(2):
        columns.append(
            [term[part].reshape((2,) * len(rest) + (slab_size * RD, OB)) for term in terms]
        )
    for stage in range(len(rest)):
        for part in range(2):
            axis = stage if part == 0 else len(rest) - 1 - stage
            columns[part] = halve(columns[part], "dom", axis, rest[axis])
    terms = [jnp.stack([t.reshape(slab_size * RD, OB) for t in pair]) for pair in zip(*columns)]
    for bit in slab_bits:
        terms = halve(terms, "slab", 1, bit)
    volume = jnp.concatenate([added([term[part] for term in terms]) for part in range(2)], axis=1)

    own = volume.astype(BF16)
    plane = [own] + [flip(own, "dom", 2 * k) for k in range(1, dom_size // 2)]
    chip = dom_pos // 2
    placed = []
    for k in range(dom_size // 2):
        value = plane[0]
        for j in range(1, dom_size // 2):
            value = jnp.where(chip ^ j == k, plane[j], value)
        placed.append(value)
    value = jnp.stack(placed)
    got = flip(value, "dom", dom_bits[0])
    value = jnp.where(
        dom_pos & dom_bits[0] == 0,
        jnp.stack([value, got], 1),
        jnp.stack([got, value], 1),
    )
    return volume, value.reshape(dom_size * RD, width)


def solution(mesh):
    return jax.shard_map(
        shards,
        mesh=mesh,
        in_specs=(
            P("dom", "slab", None),
            P("dom", None),
            P(None, "slab", None),
            P("slab"),
            P(),
            P(),
            P(),
        ),
        out_specs=(P(("dom", "slab"), None), P(None, "slab")),
        check_vma=False,
    )
```

```python
import functools

import jax
import jax.numpy as jnp
from jax import lax
from jax.experimental import pallas as pl
from jax.experimental.pallas import tpu as pltpu
from jax.sharding import PartitionSpec as P

OB = 128
RD = 256
MB = 2**20
OUT_SLOTS = 4
STREAMS = 4
OUT_TILE = 1024
F32 = jnp.float32
BF16 = jnp.bfloat16


def group_block(groups):
    return 16 if groups % 16 == 0 else 8


def spread_columns(blk_ref, cols_ref):
    count = blk_ref.shape[1]
    for j in range(2):
        for at in range(0, count, OB):
            line = blk_ref[j : j + 1, at : at + OB].astype(F32)
            cols_ref[j, at : at + OB, :] = jnp.broadcast_to(line, (OB, OB)).T


def score_kernel(here_ref, noise_ref, blk_ref, *rest):
    x_refs, r_refs = rest[:STREAMS], rest[STREAMS : 2 * STREAMS]
    keep_ref, send_ref = rest[2 * STREAMS : 2 * STREAMS + 2]
    out_refs = rest[2 * STREAMS + 2 : -8]
    flat_a, flat_b, w_a, w_b, acc_ref, perm_ref, cols_ref, sem = rest[-8:]
    step = pl.program_id(0)
    steps = pl.num_programs(0) - 1
    gb, width = x_refs[0].shape[1:]
    particles, orients = acc_ref.shape
    side = 16 * gb
    per = gb // 2
    core = here_ref[0] & 1
    rounds = 4

    def copies(flat_ref, slot, at_step, swap):
        lanes = pl.ds(pl.multiple_of(at_step * (per * width), per * width), per * width)
        goals = (send_ref, keep_ref) if swap else (keep_ref, send_ref)
        return [
            pltpu.make_async_copy(flat_ref.at[h], goals[h].at[:, lanes], sem.at[slot, h])
            for h in range(2)
        ]

    def send_out(flat_ref, slot):
        for which in range(2):

            @pl.when(core == which)
            def _(which=which):
                for copy in copies(flat_ref, slot, step, which == 1):
                    copy.start()

    def wait_out(flat_ref, slot):
        for copy in copies(flat_ref, slot, 0, False):
            copy.wait()

    def regroup(jobs):
        wide = [ref[pl.ds(first * 16, 16)].reshape(side, width) for ref, first, *_ in jobs]
        moved = jnp.dot(perm_ref[...], jnp.concatenate(wide, axis=1), preferred_element_type=F32)
        for g in range(gb):
            lanes = slice(g % per * width, (g % per + 1) * width)
            for t, (_, first, base, goal_ref, scaled) in enumerate(jobs):
                part = moved[g * 16 : (g + 1) * 16, t * width : (t + 1) * width]
                if scaled:
                    part = part * noise_ref[step * gb + g]
                at = pl.ds(pl.multiple_of(base + first * 16, 16), 16)
                goal_ref[g // per, at, lanes] = part.astype(BF16)

    def turn(src_ref, first, base, goal_ref):
        turned = jnp.swapaxes(src_ref[pl.ds(first * 16, 16)], 0, 1)
        at = pl.ds(pl.multiple_of(base + first * 16, 16), 16)
        for g in range(gb):
            goal_ref[g // per, at, g % per * width : (g % per + 1) * width] = turned[g]

    def tiles(i, flat_ref, w_ref):
        jobs, turns = [], []
        for s in range(STREAMS):
            rows = orients // STREAMS
            for t in range(rows // 16 // rounds):
                jobs.append((r_refs[s], i * (rows // 16 // rounds) + t, s * rows, w_ref, True))
            rows = particles // STREAMS
            for t in range(rows // 16 // rounds):
                job = (x_refs[s], i * (rows // 16 // rounds) + t, s * rows, flat_ref)
                if (s * (rows // 16 // rounds) + t) % 4:
                    turns.append(job)
                else:
                    jobs.append(job + (False,))
        for at in range(0, len(jobs), 5):
            regroup(jobs[at : at + 5])
        for job in turns:
            turn(*job)

    def product(left, right):
        acc_ref[...] += lax.dot_general(
            left, right, (((1,), (1,)), ((), ())), preferred_element_type=F32
        )

    def both(i, flat_ref, w_ref, last_flat, last_w):
        span = 2 * per * width // rounds
        at = pl.ds(pl.multiple_of(lax.rem(i, rounds // 2) * span, span), span)
        h = lax.div(i, rounds // 2)
        product(last_flat[h, :, at], last_w[h, :, at])
        tiles(i, flat_ref, w_ref)

    def loop(body, *refs):
        lax.fori_loop(0, rounds, lambda i, c: (body(i, *refs), c)[1], 0)

    @pl.when(step == 0)
    def _():
        row = lax.broadcasted_iota(jnp.int32, (side, side), 0)
        col = lax.broadcasted_iota(jnp.int32, (side, side), 1)
        same = ((row // 16) == (col % gb)) & ((row % 16) == (col // gb))
        perm_ref[...] = jnp.where(same, 1.0, 0.0).astype(BF16)
        acc_ref[...] = jnp.zeros_like(acc_ref)
        spread_columns(blk_ref, cols_ref)
        loop(tiles, flat_a, w_a)
        send_out(flat_a, 0)

    inner = (step > 0) & (step < steps)

    @pl.when(inner & (lax.rem(step, 2) == 1))
    def _():
        @pl.when(step > 1)
        def _():
            wait_out(flat_b, 1)

        loop(both, flat_b, w_b, flat_a, w_a)
        send_out(flat_b, 1)

    @pl.when(inner & (lax.rem(step, 2) == 0))
    def _():
        wait_out(flat_a, 0)
        loop(both, flat_a, w_a, flat_b, w_b)
        send_out(flat_a, 0)

    def finish(last_flat, last_w):
        for h in range(2):
            product(last_flat[h], last_w[h])
        me = here_ref[1]
        share = particles // len(out_refs)
        for k, out_ref in enumerate(out_refs):
            at = pl.multiple_of((me ^ k) * share, share)
            for j in range(2):
                wanted = cols_ref[j, pl.ds(at, share), :]
                chosen = jnp.zeros((share, OB), F32)
                for b in range(orients // OB):
                    value = acc_ref[pl.ds(at, share), b * OB : (b + 1) * OB]
                    chosen = jnp.where(wanted == b, value, chosen)
                out_ref[:, j * OB : (j + 1) * OB] = chosen
        wait_out(flat_a, 0)

        @pl.when(steps > 1)
        def _():
            wait_out(flat_b, 1)

    @pl.when((step == steps) & (lax.rem(step, 2) == 1))
    def _():
        finish(flat_a, w_a)

    @pl.when((step == steps) & (lax.rem(step, 2) == 0))
    def _():
        finish(flat_b, w_b)


def score_call(here, inv_noise, particles, references, blocks, slab_size):
    count, groups, width = particles.shape
    orients = references.shape[0]
    gb = group_block(groups)
    side = 16 * gb
    share = count // slab_size
    smem = pl.BlockSpec(memory_space=pltpu.SMEM)
    steps = groups // gb
    return pl.pallas_call(
        score_kernel,
        grid=(steps + 1,),
        out_shape=[jax.ShapeDtypeStruct((count, groups // 2 * width), BF16)] * 2
        + [jax.ShapeDtypeStruct((share, 2 * OB), F32)] * slab_size,
        in_specs=[
            smem,
            smem,
            pl.BlockSpec((2, count), lambda i: (0, 0)),
        ]
        + [
            pl.BlockSpec(
                (rows // STREAMS, gb, width), lambda i, s=s: (s, jnp.minimum(i, steps - 1), 0)
            )
            for rows in (count, orients)
            for s in range(STREAMS)
        ],
        out_specs=[pl.BlockSpec(memory_space=pl.ANY)] * 2
        + [pl.BlockSpec((share, 2 * OB), lambda i: (0, 0))] * slab_size,
        scratch_shapes=[
            pltpu.VMEM((2, count, gb // 2 * width), BF16),
            pltpu.VMEM((2, count, gb // 2 * width), BF16),
            pltpu.VMEM((2, orients, gb // 2 * width), BF16),
            pltpu.VMEM((2, orients, gb // 2 * width), BF16),
            pltpu.VMEM((count, orients), F32),
            pltpu.VMEM((side, side), BF16),
            pltpu.VMEM((2, count, OB), F32),
            pltpu.SemaphoreType.DMA((2, 2)),
        ],
        compiler_params=pltpu.CompilerParams(vmem_limit_bytes=56 * MB),
        cost_estimate=pl.CostEstimate(
            flops=4 * count * orients * groups * width,
            bytes_accessed=6 * count * groups * width,
            transcendentals=0,
        ),
    )(here, inv_noise, blocks, *[particles] * STREAMS, *[references] * STREAMS)


def softmax_kernel(*refs):
    *parts, out_ref = refs
    total = parts[0][...]
    for part in parts[1:]:
        total = total + part[...]
    highest = jnp.max(total, axis=1, keepdims=True)
    weights = jnp.exp(total - highest)
    out_ref[...] = (weights / jnp.sum(weights, axis=1, keepdims=True)).astype(BF16)


def softmax_call(parts):
    return pl.pallas_call(
        softmax_kernel,
        out_shape=jax.ShapeDtypeStruct(parts[0].shape, BF16),
        compiler_params=pltpu.CompilerParams(vmem_limit_bytes=8 * MB),
    )(*parts)


def own_row(here_ref, local, per):
    return lax.div(local, per) * (2 * per) + (here_ref[0] & 1) * per + lax.rem(local, per)


def plan_kernel(
    here_ref, dest_ref, pos_ref, addr_ref, item_ref, place_ref, hot_ref, count_ref, *, sizes, per
):
    step = pl.program_id(0)
    dom_size, slab_size = sizes
    owners = dom_size * slab_size
    _, units, half = pos_ref.shape
    lanes = addr_ref.shape[2]
    parts = dest_ref.shape[1] // half
    gb = units // parts
    dom_log, slab_log = (dom_size - 1).bit_length(), (slab_size - 1).bit_length()

    @pl.when(step == 0)
    def _():
        off = dest_ref[...] ^ (here_ref[0] * slab_size + here_ref[1])
        place = jnp.zeros_like(off)
        for bit in list(range(slab_log, slab_log + dom_log)) + list(range(slab_log)):
            place = place * 2 + (lax.shift_right_logical(off, bit) & 1)
        place_ref[...] = place

    owner = lax.broadcasted_iota(jnp.int32, (owners, 1), 0)
    for u in range(units):
        g, h = u // parts, u % parts
        at = pl.ds(own_row(here_ref, step * gb + g, per), 1)
        line = place_ref[at, h * half : (h + 1) * half]
        hot = jnp.where(line == owner, 1.0, 0.0)
        hot_ref[u * owners : (u + 1) * owners, :] = hot.astype(BF16)
    before = lax.broadcasted_iota(jnp.int32, (half, half), 0)
    after = lax.broadcasted_iota(jnp.int32, (half, half), 1)
    upto = jnp.where(before <= after, 1.0, 0.0).astype(BF16)
    count_ref[...] = jnp.dot(hot_ref[...], upto, preferred_element_type=F32)

    exact = functools.partial(
        jnp.dot, preferred_element_type=F32, precision=lax.Precision.HIGHEST
    )
    row = lax.broadcasted_iota(jnp.int32, (owners, owners), 0)
    col = lax.broadcasted_iota(jnp.int32, (owners, owners), 1)
    below = jnp.where(row > col, 1.0, 0.0)
    row = lax.broadcasted_iota(jnp.int32, (OB, OB), 0)
    col = lax.broadcasted_iota(jnp.int32, (OB, OB), 1)
    earlier = jnp.where(row < col, 1.0, 0.0)
    lane = lax.broadcasted_iota(jnp.int32, (owners, OB), 1)
    runs = jnp.zeros((owners, OB), F32)
    for u in range(units):
        size = count_ref[u * owners : (u + 1) * owners, half - 1 : half]
        runs = jnp.where(lane == u, size, runs)
    runs = jnp.floor((runs + 7.0) * 0.125) * 8.0
    base = exact(below, runs)
    ahead = exact(runs, earlier)
    total = jnp.sum(runs, axis=1, keepdims=True)
    start = exact(below, jnp.broadcast_to(total, (owners, OB)))[:, :1]
    blocks = jnp.floor((total + (RD - 1.0)) * (1.0 / RD))
    first = exact(below, jnp.broadcast_to(blocks, (owners, OB)))[:, :1]
    shift = start + ahead - base
    used = jnp.sum(runs, axis=0, keepdims=True)

    slot = (lax.broadcasted_iota(jnp.int32, (1, lanes), 1) * 8).astype(F32)
    is_last = lax.broadcasted_iota(jnp.int32, (1, lanes), 1) == lanes - 1
    rows = units * (half + 7 * owners)
    for u in range(units):
        low, size = base[:, u : u + 1], runs[:, u : u + 1]
        hot = hot_ref[u * owners : (u + 1) * owners, :].astype(F32)
        rank = count_ref[u * owners : (u + 1) * owners, :] + (low - 1.0)
        pos_ref[0, u : u + 1, :] = jnp.sum(hot * rank, axis=0, keepdims=True).astype(jnp.int32)
        inside = (slot >= low) & (slot < low + size)
        goal = jnp.where(inside, shift[:, u : u + 1] + slot - rows, 0.0)
        goal = (jnp.sum(goal, axis=0, keepdims=True) + rows) * 0.125
        addr_ref[0, u : u + 1, :] = jnp.where(is_last, used[:, u : u + 1], goal).astype(jnp.int32)

    wide = item_ref.shape[2]
    number = lax.broadcasted_iota(jnp.int32, (1, wide), 1).astype(F32)
    inside = (number >= first) & (number < first + blocks)
    done = (number - first) * RD
    pick = lambda value: jnp.sum(jnp.where(inside, value, 0.0), axis=0, keepdims=True)
    every = lambda value: jnp.sum(
        jnp.broadcast_to(value, (owners, wide)), axis=0, keepdims=True
    )
    lines = (
        pick(jnp.broadcast_to(owner.astype(F32), (owners, wide))),
        pick((start + done) * 0.125),
        pick(total - done),
        every(blocks),
        every(total * 0.125),
    )
    for i, value in enumerate(lines):
        item_ref[0, i : i + 1, :] = value.astype(jnp.int32)


def meta_kernel(here_ref, index_ref, frac_ref, pos_ref, meta_ref, *, per):
    step = pl.program_id(0)
    _, units, half = pos_ref.shape
    parts = index_ref.shape[1] // half
    gb = units // parts
    blocks = meta_ref.shape[2]
    low = lambda value: value.astype(F32).astype(BF16)
    eighth = low(lax.broadcasted_iota(jnp.int32, (blocks, half), 0))
    lane_of = low(lax.broadcasted_iota(jnp.int32, (OB, half), 0) % 8)
    one, none = jnp.bfloat16(1.0), jnp.bfloat16(0.0)
    for u in range(units):
        g, h = u // parts, u % parts
        line = pl.ds(own_row(here_ref, step * gb + g, per), 1)
        span = slice(h * half, (h + 1) * half)
        pos = pos_ref[0, u : u + 1, :]
        here = lane_of == low(pos & 7)
        spots = jnp.where(eighth == low(lax.shift_right_logical(pos, 3)), one, none)
        terms = [
            jnp.where(here, low(index_ref[line, span]), none),
            jnp.where(here, low(frac_ref[line, span]), none),
        ]
        meta_ref[0, u] = lax.dot_general(
            jnp.concatenate([spots, spots], axis=1),
            jnp.concatenate(terms, axis=1),
            (((1,), (1,)), ((), ())),
            preferred_element_type=F32,
        )


def up_to(value, step):
    return -(-value // step) * step


def sort_sizes(orients, owners):
    slots = orients + 7 * owners
    sure = orients + 144
    blocks = up_to((sure + up_to(max(0, slots - sure), 128)) // 8, 8)
    return slots, sure, blocks


def planned(shape):
    return pl.BlockSpec((1,) + shape[1:], lambda i, here: (i,) + (0,) * (len(shape) - 1))


def plan_call(here, destination, groups, gb, mesh_sizes):
    orients = destination.shape[1]
    half = min(256, orients)
    owners = mesh_sizes[0] * mesh_sizes[1]
    steps, units = groups // 2 // gb, gb * (orients // half)
    slots, _, blocks = sort_sizes(half, owners)
    shapes = [
        (steps, units, half),
        (steps, units, up_to(blocks + 1, 128)),
        (steps, 5, up_to(owners + units * slots // RD + 8, 128)),
    ]
    return pl.pallas_call(
        functools.partial(plan_kernel, sizes=mesh_sizes, per=group_block(groups) // 2),
        grid_spec=pltpu.PrefetchScalarGridSpec(
            num_scalar_prefetch=1,
            grid=(steps,),
            in_specs=[pl.BlockSpec((groups, orients), lambda i, here: (here[1], 0))],
            out_specs=[planned(shape) for shape in shapes],
            scratch_shapes=[
                pltpu.VMEM((groups, orients), jnp.int32),
                pltpu.VMEM((units * owners, half), BF16),
                pltpu.VMEM((units * owners, half), F32),
            ],
        ),
        out_shape=[jax.ShapeDtypeStruct(shape, jnp.int32) for shape in shapes],
        compiler_params=pltpu.CompilerParams(vmem_limit_bytes=55 * MB),
        cost_estimate=pl.CostEstimate(
            flops=8 * steps * units * owners * half * half,
            bytes_accessed=8 * groups * orients,
            transcendentals=0,
        ),
    )(here, destination)


def meta_call(here, row_index, fraction, pos, owners):
    steps, units, half = pos.shape
    orients = row_index.shape[1]
    groups = 2 * steps * units * half // orients
    blocks = sort_sizes(half, owners)[2]
    shape = (steps, units, blocks, OB)
    table = pl.BlockSpec((groups, orients), lambda i, here: (here[1], 0))
    return pl.pallas_call(
        functools.partial(meta_kernel, per=group_block(groups) // 2),
        grid_spec=pltpu.PrefetchScalarGridSpec(
            num_scalar_prefetch=1,
            grid=(steps,),
            in_specs=[table, table, planned(pos.shape)],
            out_specs=planned(shape),
        ),
        out_shape=jax.ShapeDtypeStruct(shape, F32),
        compiler_params=pltpu.CompilerParams(vmem_limit_bytes=16 * MB),
        cost_estimate=pl.CostEstimate(
            flops=8 * steps * units * blocks * half * OB,
            bytes_accessed=8 * steps * units * blocks * OB,
            transcendentals=0,
        ),
    )(here, row_index, fraction, pos)


def insert_kernel(
    me_ref, addr_ref, item_ref, x_ref, y_ref, pos_ref, meta_ref, blk_ref, more_blk_ref, *rest
):
    *post_refs, more_ref, send_ref, keep_ref = rest[:-10]
    post_t, spread_ref, cols_ref, slice_a, slice_b, buf_s, buf_m, volume, stage, sem = rest[-10:]
    step = pl.program_id(0)
    count = x_ref.shape[0]
    orients = post_t.shape[0]
    units, half = pos_ref.shape[1:]
    parts = orients // half
    gb = units // parts
    width = x_ref.shape[1] // gb
    share = count // len(post_refs)
    lanes = addr_ref.shape[2]

    @pl.when(step == 0)
    def _():
        volume[...] = jnp.zeros_like(volume)
        me = me_ref[0]
        others = [more_ref.at[k] for k in range(len(post_refs))]
        for who, (lists, pieces) in enumerate(((blk_ref, post_refs), (more_blk_ref, others))):
            spread_columns(lists, cols_ref)
            for k, post_ref in enumerate(pieces):
                at = pl.multiple_of((me ^ k) * share, share)
                post = post_ref[...].astype(F32)
                first = cols_ref[0, pl.ds(at, share), :]
                second = cols_ref[1, pl.ds(at, share), :]
                for b in range(orients // OB):
                    spread = jnp.where(
                        first == b, post[:, :OB], jnp.where(second == b, post[:, OB:], 0.0)
                    )
                    spread_ref[pl.ds(at, share), b * OB : (b + 1) * OB] = spread
            for b in range(orients // OB):
                rows = slice(b * OB, (b + 1) * OB)
                post_t[rows, who * count : (who + 1) * count] = spread_ref[:, rows].T.astype(BF16)

    tail = pl.ds(pl.multiple_of(item_ref[0, 4, 0] * 8, 8), RD)
    buf_s[tail, :] = jnp.zeros((RD, width), F32)
    one, none = jnp.bfloat16(1.0), jnp.bfloat16(0.0)
    slots, sure, _ = sort_sizes(half, volume.shape[0] // RD)
    per = slice_a.shape[1] // width
    number = gb // per

    def slices(q, dst_ref):
        at = pl.ds(pl.multiple_of(q * (per * width), per * width), per * width)
        images = jnp.concatenate([x_ref[:, at], y_ref[:, at]], axis=0)
        value = jnp.dot(post_t[...], images, preferred_element_type=F32)
        dst_ref[...] = value.astype(BF16)

    def emit(u, piece, base, size):
        pos = pos_ref[0, pl.ds(u, 1), :]
        order = []
        for at in range(0, size, 128):
            high = min(128, size - at)
            slot = lax.broadcasted_iota(jnp.int32, (high, half), 0).astype(F32).astype(BF16)
            near = jnp.clip(pos - (base + at), -1, 128).astype(F32).astype(BF16)
            order.append(jnp.where(slot == near, one, none))
        order = jnp.concatenate(order, axis=0)
        rows = jnp.dot(order, piece, preferred_element_type=F32)
        for i in range(size // 8):
            at = addr_ref[0, u, base // 8 + i]
            buf_s[pl.ds(pl.multiple_of(at * 8, 8), 8), :] = rows[8 * i : 8 * i + 8]
            buf_m[pl.ds(at, 1), :] = meta_ref[0, u, pl.ds(base // 8 + i, 1), :]

    def sort(q, src_ref):
        for g in range(per):
            for h in range(parts):
                piece = src_ref[h * half : (h + 1) * half, g * width : (g + 1) * width]
                emit((q * per + g) * parts + h, piece, 0, sure)

    def rest_of(q, src_ref):
        for g in range(per):
            for h in range(parts):
                u = (q * per + g) * parts + h

                def more(e, c, u=u, g=g, h=h):
                    piece = src_ref[h * half : (h + 1) * half, g * width : (g + 1) * width]
                    emit(u, piece, sure + e * 128, 128)
                    return c

                used = addr_ref[0, u, lanes - 1]
                lax.fori_loop(0, lax.div(jnp.maximum(used - sure, 0) + 127, 128), more, 0)

    def most_used(q):
        most = addr_ref[0, q * per * parts, lanes - 1]
        for u in range(1, per * parts):
            most = jnp.maximum(most, addr_ref[0, q * per * parts + u, lanes - 1])
        return most

    def two(j, carry):
        q = j * 2
        sort(q, slice_a)
        slices(q + 1, slice_b)

        @pl.when(most_used(q) > sure)
        def _():
            rest_of(q, slice_a)

        sort(q + 1, slice_b)
        slices(jnp.minimum(q + 2, number - 1), slice_a)

        @pl.when(most_used(q + 1) > sure)
        def _():
            rest_of(q + 1, slice_b)

        return carry

    slices(0, slice_a)
    lax.fori_loop(0, number // 2, two, 0)
    if number % 2:
        sort(number - 1, slice_a)
        rest_of(number - 1, slice_a)

    bins = lax.broadcasted_iota(jnp.int32, (RD, RD), 0).astype(F32).astype(BF16)
    side = RD // 2
    at_lane = lax.broadcasted_iota(jnp.int32, (side // 8, side), 1) // 8
    own_lane = at_lane == lax.broadcasted_iota(jnp.int32, (side // 8, side), 0)
    line = lax.broadcasted_iota(jnp.int32, (1, RD), 1)
    together = 8

    def some_items(q, carry):
        for u in range(together):
            j = q * together + u
            owner, at, left = item_ref[0, 0, j], item_ref[0, 1, j], item_ref[0, 2, j]
            places = [
                jnp.sum(
                    jnp.where(own_lane, buf_m[pl.ds(at + h * (side // 8), side // 8), :], 0.0),
                    axis=0,
                    keepdims=True,
                )
                for h in range(2)
            ]
            place = jnp.where(line < left, jnp.concatenate(places, axis=1), -9.0)
            whole = jnp.floor(place)
            apart = (bins - whole.astype(BF16)) - (place - whole).astype(BF16)
            weights = jnp.maximum(one - jnp.abs(apart), none)
            values = buf_s[pl.ds(pl.multiple_of(at * 8, 8), RD), :].astype(BF16)
            goal = pl.ds(pl.multiple_of(owner * RD, RD), RD)
            volume[goal, :] += jnp.dot(weights, values, preferred_element_type=F32)
        return carry

    count_items = lax.div(item_ref[0, 3, 0] + together - 1, together)
    lax.fori_loop(0, count_items, some_items, 0)

    @pl.when(step == pl.num_programs(0) - 1)
    def _():
        side_rows = keep_ref.shape[1]
        slots_out, _, tile, _ = stage.shape
        copies = []
        for base, out_ref in ((side_rows, send_ref), (0, keep_ref)):
            for at in range(0, side_rows, tile):
                slot = len(copies) % slots_out
                if len(copies) >= slots_out:
                    copies[len(copies) - slots_out].wait()
                value = volume[base + at : base + at + tile, :].astype(BF16)
                for c in range(2):
                    stage[slot, c] = value[:, c * OB : (c + 1) * OB]
                copy = pltpu.make_async_copy(
                    stage.at[slot], out_ref.at[:, pl.ds(at, tile)], sem.at[slot]
                )
                copy.start()
                copies.append(copy)
        for copy in copies[-slots_out:]:
            copy.wait()


def group_pair(gb):
    return 2 if gb % 2 == 0 else 1


def insert_block(groups, orients, owners, count, width):
    half = min(256, orients)
    slots, _, blocks = sort_sizes(half, owners)
    room = max(32 * MB - owners * RD * width * 4, 18 * MB)
    best = 1
    for gb in range(1, groups + 1):
        units = gb * (orients // half)
        rows = units * slots + RD + 8
        need = rows * (width * 4 + OB // 2) + 8 * count * gb * width + units * blocks * OB * 8
        if groups % gb == 0 and need <= room:
            best = gb
    return best


def insert_call(me, addr, items, flats, pos, meta, blocks, posts, more, orients, owners):
    count, length = flats[0].shape
    steps, units, half = pos.shape
    gb = units * half // orients
    width = length // (steps * gb)
    total = owners * RD
    share = posts[0].shape[0]
    rows = units * sort_sizes(half, owners)[0] + RD + 8
    limit = total * width * 4 // MB + 30
    smem = pl.BlockSpec(memory_space=pltpu.SMEM)
    block = lambda shape, **kw: pl.BlockSpec(
        (1,) + shape[1:], lambda i: (i,) + (0,) * (len(shape) - 1), **kw
    )
    return pl.pallas_call(
        insert_kernel,
        grid=(steps,),
        out_shape=[jax.ShapeDtypeStruct((2, total // 2, OB), BF16)] * 2,
        in_specs=[
            smem,
            block(addr.shape, memory_space=pltpu.SMEM),
            block(items.shape, memory_space=pltpu.SMEM),
            pl.BlockSpec((count, gb * width), lambda i: (0, i)),
            pl.BlockSpec((count, gb * width), lambda i: (0, i)),
            block(pos.shape),
            block(meta.shape),
            pl.BlockSpec((2, count), lambda i: (0, 0)),
            pl.BlockSpec((2, count), lambda i: (0, 0)),
        ]
        + [pl.BlockSpec((share, 2 * OB), lambda i: (0, 0))] * len(posts)
        + [pl.BlockSpec(more.shape, lambda i: (0, 0, 0))],
        out_specs=[pl.BlockSpec(memory_space=pl.ANY)] * 2,
        scratch_shapes=[
            pltpu.VMEM((orients, 2 * count), BF16),
            pltpu.VMEM((count, orients), F32),
            pltpu.VMEM((2, count, OB), F32),
            pltpu.VMEM((orients, group_pair(gb) * width), BF16),
            pltpu.VMEM((orients, group_pair(gb) * width), BF16),
            pltpu.VMEM((rows, width), F32),
            pltpu.VMEM((rows // 8, OB), F32),
            pltpu.VMEM((total, width), F32),
            pltpu.VMEM((OUT_SLOTS, 2, OUT_TILE, OB), BF16),
            pltpu.SemaphoreType.DMA((OUT_SLOTS,)),
        ],
        compiler_params=pltpu.CompilerParams(vmem_limit_bytes=limit * MB),
        cost_estimate=pl.CostEstimate(
            flops=8 * count * orients * length,
            bytes_accessed=2 * count * length,
            transcendentals=0,
        ),
    )(me, addr, items, *flats, pos, meta, *blocks, *posts, more)


def flip(value, axis, bit):
    size = lax.axis_size(axis)
    return lax.ppermute(value, axis, [(i, i ^ bit) for i in range(size)])


def shards(particles, blocks, references, inv_noise, destination, row_index, fraction):
    groups, width = particles.shape[1:]
    orients = references.shape[0]
    dom_size = lax.axis_size("dom")
    slab_size = lax.axis_size("slab")
    devices = dom_size * slab_size
    dom_pos = lax.axis_index("dom")
    slab_pos = lax.axis_index("slab")
    here = jnp.stack([dom_pos, slab_pos]).astype(jnp.int32)
    slab_me = here[1:]
    dom_bits = [1 << i for i in range((dom_size - 1).bit_length())]
    slab_bits = [1 << i for i in range((slab_size - 1).bit_length())]

    blocks = blocks.T
    kept, sent, *scores = score_call(here, inv_noise, particles, references, blocks, slab_size)
    gb = insert_block(groups // 2, orients, devices, particles.shape[0], width)
    here, own = lax.optimization_barrier((here, scores[0]))
    plan = plan_call(here, destination, groups, gb, (dom_size, slab_size))
    own, *plan = lax.optimization_barrier((own, *plan))
    pos, addr, items = plan
    parts = [own] + [flip(scores[k], "slab", k) for k in range(1, slab_size)]
    flats = [kept, flip(sent, "dom", dom_bits[0])]
    post = softmax_call(parts)
    more_blocks = flip(blocks, "dom", dom_bits[0])
    post, more_blocks, later = lax.optimization_barrier((post, more_blocks, here))
    meta = meta_call(later, row_index, fraction, pos, devices)
    posts = [post] + [flip(post, "slab", k) for k in range(1, slab_size)]
    pile, meta = lax.optimization_barrier((jnp.stack(posts), meta))
    more = flip(pile, "dom", dom_bits[0])
    lists = [blocks, more_blocks]
    send, keep = insert_call(
        slab_me, addr, items, flats, pos, meta, lists, posts, more, orients, devices
    )

    def added(terms):
        return functools.reduce(jnp.add, [term.astype(F32) for term in terms])

    def halve(terms, axis_name, axis, bit):
        size = terms[0].shape[axis] // 2
        pick = lambda term, at: lax.slice_in_dim(term, at, at + size, axis=axis)
        sent = added([pick(term, size) for term in terms]).astype(BF16)
        return [pick(term, 0) for term in terms] + [flip(sent, axis_name, bit)]

    terms = [keep, flip(send, "dom", dom_bits[0])]
    rest = dom_bits[1:]
    columns = []
    for part in range(2):
        columns.append(
            [term[part].reshape((2,) * len(rest) + (slab_size * RD, OB)) for term in terms]
        )
    for stage in range(len(rest)):
        for part in range(2):
            axis = stage if part == 0 else len(rest) - 1 - stage
            columns[part] = halve(columns[part], "dom", axis, rest[axis])
    terms = [jnp.stack([t.reshape(slab_size * RD, OB) for t in pair]) for pair in zip(*columns)]
    for bit in slab_bits:
        terms = halve(terms, "slab", 1, bit)
    volume = jnp.concatenate([added([term[part] for term in terms]) for part in range(2)], axis=1)

    own = volume.astype(BF16)
    plane = [own] + [flip(own, "dom", 2 * k) for k in range(1, dom_size // 2)]
    chip = dom_pos // 2
    placed = []
    for k in range(dom_size // 2):
        value = plane[0]
        for j in range(1, dom_size // 2):
            value = jnp.where(chip ^ j == k, plane[j], value)
        placed.append(value)
    value = jnp.stack(placed)
    got = flip(value, "dom", dom_bits[0])
    value = jnp.where(
        dom_pos & dom_bits[0] == 0,
        jnp.stack([value, got], 1),
        jnp.stack([got, value], 1),
    )
    return volume, value.reshape(dom_size * RD, width)


def solution(mesh):
    return jax.shard_map(
        shards,
        mesh=mesh,
        in_specs=(
            P("dom", "slab", None),
            P("dom", None),
            P(None, "slab", None),
            P("slab"),
            P(),
            P(),
            P(),
        ),
        out_specs=(P(("dom", "slab"), None), P(None, "slab")),
        check_vma=False,
    )
```

```python
import functools

import jax
import jax.numpy as jnp
from jax import lax
from jax.experimental import pallas as pl
from jax.experimental.pallas import tpu as pltpu
from jax.sharding import PartitionSpec as P

OB = 128
RD = 256
MB = 2**20
OUT_SLOTS = 4
STREAMS = 4
OUT_TILE = 1024
F32 = jnp.float32
BF16 = jnp.bfloat16


def group_block(groups):
    return 16 if groups % 16 == 0 else 8


def spread_columns(blk_ref, cols_ref):
    count = blk_ref.shape[1]
    for j in range(2):
        for at in range(0, count, OB):
            line = blk_ref[j : j + 1, at : at + OB].astype(F32)
            cols_ref[j, at : at + OB, :] = jnp.broadcast_to(line, (OB, OB)).T


def score_kernel(here_ref, noise_ref, blk_ref, *rest):
    x_refs, r_refs = rest[:STREAMS], rest[STREAMS : 2 * STREAMS]
    keep_ref, send_ref = rest[2 * STREAMS : 2 * STREAMS + 2]
    out_ref = rest[2 * STREAMS + 2]
    flat_a, flat_b, w_a, w_b, acc_ref, perm_ref, cols_ref, sem = rest[-8:]
    step = pl.program_id(0)
    steps = pl.num_programs(0) - 1
    gb, width = x_refs[0].shape[1:]
    particles, orients = acc_ref.shape
    side = 16 * gb
    per = gb // 2
    core = here_ref[0] & 1
    rounds = 4

    def copies(flat_ref, slot, at_step, swap):
        lanes = pl.ds(pl.multiple_of(at_step * (per * width), per * width), per * width)
        goals = (send_ref, keep_ref) if swap else (keep_ref, send_ref)
        return [
            pltpu.make_async_copy(flat_ref.at[h], goals[h].at[:, lanes], sem.at[slot, h])
            for h in range(2)
        ]

    def send_out(flat_ref, slot):
        for which in range(2):

            @pl.when(core == which)
            def _(which=which):
                for copy in copies(flat_ref, slot, step, which == 1):
                    copy.start()

    def wait_out(flat_ref, slot):
        for copy in copies(flat_ref, slot, 0, False):
            copy.wait()

    def regroup(jobs):
        wide = [ref[pl.ds(first * 16, 16)].reshape(side, width) for ref, first, *_ in jobs]
        moved = jnp.dot(perm_ref[...], jnp.concatenate(wide, axis=1), preferred_element_type=F32)
        for g in range(gb):
            lanes = slice(g % per * width, (g % per + 1) * width)
            for t, (_, first, base, goal_ref, scaled) in enumerate(jobs):
                part = moved[g * 16 : (g + 1) * 16, t * width : (t + 1) * width]
                if scaled:
                    part = part * noise_ref[step * gb + g]
                at = pl.ds(pl.multiple_of(base + first * 16, 16), 16)
                goal_ref[g // per, at, lanes] = part.astype(BF16)

    def turn(src_ref, first, base, goal_ref):
        turned = jnp.swapaxes(src_ref[pl.ds(first * 16, 16)], 0, 1)
        at = pl.ds(pl.multiple_of(base + first * 16, 16), 16)
        for g in range(gb):
            goal_ref[g // per, at, g % per * width : (g % per + 1) * width] = turned[g]

    def tiles(i, flat_ref, w_ref):
        jobs, turns = [], []
        for s in range(STREAMS):
            rows = orients // STREAMS
            for t in range(rows // 16 // rounds):
                jobs.append((r_refs[s], i * (rows // 16 // rounds) + t, s * rows, w_ref, True))
            rows = particles // STREAMS
            for t in range(rows // 16 // rounds):
                job = (x_refs[s], i * (rows // 16 // rounds) + t, s * rows, flat_ref)
                if (s * (rows // 16 // rounds) + t) % 4:
                    turns.append(job)
                else:
                    jobs.append(job + (False,))
        for at in range(0, len(jobs), 5):
            regroup(jobs[at : at + 5])
        for job in turns:
            turn(*job)

    def product(left, right):
        acc_ref[...] += lax.dot_general(
            left, right, (((1,), (1,)), ((), ())), preferred_element_type=F32
        )

    def both(i, flat_ref, w_ref, last_flat, last_w):
        span = 2 * per * width // rounds
        at = pl.ds(pl.multiple_of(lax.rem(i, rounds // 2) * span, span), span)
        h = lax.div(i, rounds // 2)
        product(last_flat[h, :, at], last_w[h, :, at])
        tiles(i, flat_ref, w_ref)

    def loop(body, *refs):
        lax.fori_loop(0, rounds, lambda i, c: (body(i, *refs), c)[1], 0)

    @pl.when(step == 0)
    def _():
        row = lax.broadcasted_iota(jnp.int32, (side, side), 0)
        col = lax.broadcasted_iota(jnp.int32, (side, side), 1)
        same = ((row // 16) == (col % gb)) & ((row % 16) == (col // gb))
        perm_ref[...] = jnp.where(same, 1.0, 0.0).astype(BF16)
        acc_ref[...] = jnp.zeros_like(acc_ref)
        spread_columns(blk_ref, cols_ref)
        loop(tiles, flat_a, w_a)
        send_out(flat_a, 0)

    inner = (step > 0) & (step < steps)

    @pl.when(inner & (lax.rem(step, 2) == 1))
    def _():
        @pl.when(step > 1)
        def _():
            wait_out(flat_b, 1)

        loop(both, flat_b, w_b, flat_a, w_a)
        send_out(flat_b, 1)

    @pl.when(inner & (lax.rem(step, 2) == 0))
    def _():
        wait_out(flat_a, 0)
        loop(both, flat_a, w_a, flat_b, w_b)
        send_out(flat_a, 0)

    def finish(last_flat, last_w):
        for h in range(2):
            product(last_flat[h], last_w[h])
        share = out_ref.shape[1]
        for k in range(out_ref.shape[0]):
            rows = slice(k * share, (k + 1) * share)
            for j in range(2):
                wanted = cols_ref[j, rows, :]
                chosen = jnp.zeros((share, OB), F32)
                for b in range(orients // OB):
                    value = acc_ref[rows, b * OB : (b + 1) * OB]
                    chosen = jnp.where(wanted == b, value, chosen)
                out_ref[k, :, j * OB : (j + 1) * OB] = chosen
        wait_out(flat_a, 0)

        @pl.when(steps > 1)
        def _():
            wait_out(flat_b, 1)

    @pl.when((step == steps) & (lax.rem(step, 2) == 1))
    def _():
        finish(flat_a, w_a)

    @pl.when((step == steps) & (lax.rem(step, 2) == 0))
    def _():
        finish(flat_b, w_b)


def score_call(here, inv_noise, particles, references, blocks, slab_size):
    count, groups, width = particles.shape
    orients = references.shape[0]
    gb = group_block(groups)
    side = 16 * gb
    share = count // slab_size
    smem = pl.BlockSpec(memory_space=pltpu.SMEM)
    steps = groups // gb
    return pl.pallas_call(
        score_kernel,
        grid=(steps + 1,),
        out_shape=[jax.ShapeDtypeStruct((count, groups // 2 * width), BF16)] * 2
        + [jax.ShapeDtypeStruct((slab_size, share, 2 * OB), F32)],
        in_specs=[
            smem,
            smem,
            pl.BlockSpec((2, count), lambda i: (0, 0)),
        ]
        + [
            pl.BlockSpec(
                (rows // STREAMS, gb, width), lambda i, s=s: (s, jnp.minimum(i, steps - 1), 0)
            )
            for rows in (count, orients)
            for s in range(STREAMS)
        ],
        out_specs=[pl.BlockSpec(memory_space=pl.ANY)] * 2
        + [pl.BlockSpec((slab_size, share, 2 * OB), lambda i: (0, 0, 0))],
        scratch_shapes=[
            pltpu.VMEM((2, count, gb // 2 * width), BF16),
            pltpu.VMEM((2, count, gb // 2 * width), BF16),
            pltpu.VMEM((2, orients, gb // 2 * width), BF16),
            pltpu.VMEM((2, orients, gb // 2 * width), BF16),
            pltpu.VMEM((count, orients), F32),
            pltpu.VMEM((side, side), BF16),
            pltpu.VMEM((2, count, OB), F32),
            pltpu.SemaphoreType.DMA((2, 2)),
        ],
        compiler_params=pltpu.CompilerParams(vmem_limit_bytes=56 * MB),
        cost_estimate=pl.CostEstimate(
            flops=4 * count * orients * groups * width,
            bytes_accessed=6 * count * groups * width,
            transcendentals=0,
        ),
    )(here, inv_noise, blocks, *[particles] * STREAMS, *[references] * STREAMS)


def softmax_kernel(parts_ref, out_ref):
    total = parts_ref[0]
    for k in range(1, parts_ref.shape[0]):
        total = total + parts_ref[k]
    highest = jnp.max(total, axis=1, keepdims=True)
    weights = jnp.exp(total - highest)
    post = (weights / jnp.sum(weights, axis=1, keepdims=True)).astype(BF16)
    for k in range(out_ref.shape[0]):
        out_ref[k] = post


def softmax_call(parts):
    return pl.pallas_call(
        softmax_kernel,
        out_shape=jax.ShapeDtypeStruct(parts.shape, BF16),
        compiler_params=pltpu.CompilerParams(vmem_limit_bytes=8 * MB),
    )(parts)


def own_row(here_ref, local, per):
    return lax.div(local, per) * (2 * per) + (here_ref[0] & 1) * per + lax.rem(local, per)


def plan_kernel(
    here_ref, dest_ref, pos_ref, addr_ref, item_ref, place_ref, hot_ref, count_ref, *, sizes, per
):
    step = pl.program_id(0)
    dom_size, slab_size = sizes
    owners = dom_size * slab_size
    _, units, half = pos_ref.shape
    lanes = addr_ref.shape[2]
    parts = dest_ref.shape[1] // half
    gb = units // parts
    dom_log, slab_log = (dom_size - 1).bit_length(), (slab_size - 1).bit_length()

    @pl.when(step == 0)
    def _():
        off = dest_ref[...] ^ (here_ref[0] * slab_size)
        place = jnp.zeros_like(off)
        for bit in list(range(slab_log, slab_log + dom_log)) + list(range(slab_log))[::-1]:
            place = place * 2 + (lax.shift_right_logical(off, bit) & 1)
        place_ref[...] = place

    owner = lax.broadcasted_iota(jnp.int32, (owners, 1), 0)
    for u in range(units):
        g, h = u // parts, u % parts
        at = pl.ds(own_row(here_ref, step * gb + g, per), 1)
        line = place_ref[at, h * half : (h + 1) * half]
        hot = jnp.where(line == owner, 1.0, 0.0)
        hot_ref[u * owners : (u + 1) * owners, :] = hot.astype(BF16)
    before = lax.broadcasted_iota(jnp.int32, (half, half), 0)
    after = lax.broadcasted_iota(jnp.int32, (half, half), 1)
    upto = jnp.where(before <= after, 1.0, 0.0).astype(BF16)
    count_ref[...] = jnp.dot(hot_ref[...], upto, preferred_element_type=F32)

    exact = functools.partial(
        jnp.dot, preferred_element_type=F32, precision=lax.Precision.HIGHEST
    )
    row = lax.broadcasted_iota(jnp.int32, (owners, owners), 0)
    col = lax.broadcasted_iota(jnp.int32, (owners, owners), 1)
    below = jnp.where(row > col, 1.0, 0.0)
    row = lax.broadcasted_iota(jnp.int32, (OB, OB), 0)
    col = lax.broadcasted_iota(jnp.int32, (OB, OB), 1)
    earlier = jnp.where(row < col, 1.0, 0.0)
    lane = lax.broadcasted_iota(jnp.int32, (owners, OB), 1)
    runs = jnp.zeros((owners, OB), F32)
    for u in range(units):
        size = count_ref[u * owners : (u + 1) * owners, half - 1 : half]
        runs = jnp.where(lane == u, size, runs)
    runs = jnp.floor((runs + 7.0) * 0.125) * 8.0
    base = exact(below, runs)
    ahead = exact(runs, earlier)
    total = jnp.sum(runs, axis=1, keepdims=True)
    start = exact(below, jnp.broadcast_to(total, (owners, OB)))[:, :1]
    blocks = jnp.floor((total + (RD - 1.0)) * (1.0 / RD))
    first = exact(below, jnp.broadcast_to(blocks, (owners, OB)))[:, :1]
    shift = start + ahead - base
    used = jnp.sum(runs, axis=0, keepdims=True)

    slot = (lax.broadcasted_iota(jnp.int32, (1, lanes), 1) * 8).astype(F32)
    is_last = lax.broadcasted_iota(jnp.int32, (1, lanes), 1) == lanes - 1
    rows = units * (half + 7 * owners)
    for u in range(units):
        low, size = base[:, u : u + 1], runs[:, u : u + 1]
        hot = hot_ref[u * owners : (u + 1) * owners, :].astype(F32)
        rank = count_ref[u * owners : (u + 1) * owners, :] + (low - 1.0)
        pos_ref[0, u : u + 1, :] = jnp.sum(hot * rank, axis=0, keepdims=True).astype(jnp.int32)
        inside = (slot >= low) & (slot < low + size)
        goal = jnp.where(inside, shift[:, u : u + 1] + slot - rows, 0.0)
        goal = (jnp.sum(goal, axis=0, keepdims=True) + rows) * 0.125
        addr_ref[0, u : u + 1, :] = jnp.where(is_last, used[:, u : u + 1], goal).astype(jnp.int32)

    wide = item_ref.shape[2]
    number = lax.broadcasted_iota(jnp.int32, (1, wide), 1).astype(F32)
    inside = (number >= first) & (number < first + blocks)
    done = (number - first) * RD
    pick = lambda value: jnp.sum(jnp.where(inside, value, 0.0), axis=0, keepdims=True)
    every = lambda value: jnp.sum(
        jnp.broadcast_to(value, (owners, wide)), axis=0, keepdims=True
    )
    lines = (
        pick(jnp.broadcast_to(owner.astype(F32), (owners, wide))),
        pick((start + done) * 0.125),
        pick(total - done),
        every(blocks),
        every(total * 0.125),
    )
    for i, value in enumerate(lines):
        item_ref[0, i : i + 1, :] = value.astype(jnp.int32)


def meta_kernel(here_ref, index_ref, frac_ref, pos_ref, meta_ref, *, per):
    step = pl.program_id(0)
    _, units, half = pos_ref.shape
    parts = index_ref.shape[1] // half
    gb = units // parts
    blocks = meta_ref.shape[2]
    low = lambda value: value.astype(F32).astype(BF16)
    eighth = low(lax.broadcasted_iota(jnp.int32, (blocks, half), 0))
    lane_of = low(lax.broadcasted_iota(jnp.int32, (OB, half), 0) % 8)
    one, none = jnp.bfloat16(1.0), jnp.bfloat16(0.0)
    for u in range(units):
        g, h = u // parts, u % parts
        line = pl.ds(own_row(here_ref, step * gb + g, per), 1)
        span = slice(h * half, (h + 1) * half)
        pos = pos_ref[0, u : u + 1, :]
        here = lane_of == low(pos & 7)
        spots = jnp.where(eighth == low(lax.shift_right_logical(pos, 3)), one, none)
        terms = [
            jnp.where(here, low(index_ref[line, span]), none),
            jnp.where(here, low(frac_ref[line, span]), none),
        ]
        meta_ref[0, u] = lax.dot_general(
            jnp.concatenate([spots, spots], axis=1),
            jnp.concatenate(terms, axis=1),
            (((1,), (1,)), ((), ())),
            preferred_element_type=F32,
        )


def up_to(value, step):
    return -(-value // step) * step


def sort_sizes(orients, owners):
    slots = orients + 7 * owners
    sure = orients + 144
    blocks = up_to((sure + up_to(max(0, slots - sure), 128)) // 8, 8)
    return slots, sure, blocks


def planned(shape):
    return pl.BlockSpec((1,) + shape[1:], lambda i, here: (i,) + (0,) * (len(shape) - 1))


def plan_call(here, destination, groups, gb, mesh_sizes):
    orients = destination.shape[1]
    half = min(256, orients)
    owners = mesh_sizes[0] * mesh_sizes[1]
    steps, units = groups // 2 // gb, gb * (orients // half)
    slots, _, blocks = sort_sizes(half, owners)
    shapes = [
        (steps, units, half),
        (steps, units, up_to(blocks + 1, 128)),
        (steps, 5, up_to(owners + units * slots // RD + 8, 128)),
    ]
    return pl.pallas_call(
        functools.partial(plan_kernel, sizes=mesh_sizes, per=group_block(groups) // 2),
        grid_spec=pltpu.PrefetchScalarGridSpec(
            num_scalar_prefetch=1,
            grid=(steps,),
            in_specs=[pl.BlockSpec((groups, orients), lambda i, here: (here[1], 0))],
            out_specs=[planned(shape) for shape in shapes],
            scratch_shapes=[
                pltpu.VMEM((groups, orients), jnp.int32),
                pltpu.VMEM((units * owners, half), BF16),
                pltpu.VMEM((units * owners, half), F32),
            ],
        ),
        out_shape=[jax.ShapeDtypeStruct(shape, jnp.int32) for shape in shapes],
        compiler_params=pltpu.CompilerParams(vmem_limit_bytes=55 * MB),
        cost_estimate=pl.CostEstimate(
            flops=8 * steps * units * owners * half * half,
            bytes_accessed=8 * groups * orients,
            transcendentals=0,
        ),
    )(here, destination)


def meta_call(here, row_index, fraction, pos, owners):
    steps, units, half = pos.shape
    orients = row_index.shape[1]
    groups = 2 * steps * units * half // orients
    blocks = sort_sizes(half, owners)[2]
    shape = (steps, units, blocks, OB)
    table = pl.BlockSpec((groups, orients), lambda i, here: (here[1], 0))
    return pl.pallas_call(
        functools.partial(meta_kernel, per=group_block(groups) // 2),
        grid_spec=pltpu.PrefetchScalarGridSpec(
            num_scalar_prefetch=1,
            grid=(steps,),
            in_specs=[table, table, planned(pos.shape)],
            out_specs=planned(shape),
        ),
        out_shape=jax.ShapeDtypeStruct(shape, F32),
        compiler_params=pltpu.CompilerParams(vmem_limit_bytes=16 * MB),
        cost_estimate=pl.CostEstimate(
            flops=8 * steps * units * blocks * half * OB,
            bytes_accessed=8 * steps * units * blocks * OB,
            transcendentals=0,
        ),
    )(here, row_index, fraction, pos)


def insert_kernel(
    addr_ref, item_ref, x_ref, y_ref, pos_ref, meta_ref, blk_ref, more_blk_ref, *rest
):
    post_ref, more_ref, send_ref, keep_ref = rest[:-10]
    post_t, spread_ref, cols_ref, slice_a, slice_b, buf_s, buf_m, volume, stage, sem = rest[-10:]
    step = pl.program_id(0)
    count = x_ref.shape[0]
    orients = post_t.shape[0]
    units, half = pos_ref.shape[1:]
    parts = orients // half
    gb = units // parts
    width = x_ref.shape[1] // gb
    share = post_ref.shape[1]
    lanes = addr_ref.shape[2]

    @pl.when(step == 0)
    def _():
        volume[...] = jnp.zeros_like(volume)
        for who, (lists, pieces) in enumerate(((blk_ref, post_ref), (more_blk_ref, more_ref))):
            spread_columns(lists, cols_ref)
            for k in range(pieces.shape[0]):
                at = slice(k * share, (k + 1) * share)
                post = pieces[k].astype(F32)
                first = cols_ref[0, at, :]
                second = cols_ref[1, at, :]
                for b in range(orients // OB):
                    spread = jnp.where(
                        first == b, post[:, :OB], jnp.where(second == b, post[:, OB:], 0.0)
                    )
                    spread_ref[at, b * OB : (b + 1) * OB] = spread
            for b in range(orients // OB):
                rows = slice(b * OB, (b + 1) * OB)
                post_t[rows, who * count : (who + 1) * count] = spread_ref[:, rows].T.astype(BF16)

    tail = pl.ds(pl.multiple_of(item_ref[0, 4, 0] * 8, 8), RD)
    buf_s[tail, :] = jnp.zeros((RD, width), F32)
    one, none = jnp.bfloat16(1.0), jnp.bfloat16(0.0)
    slots, sure, _ = sort_sizes(half, volume.shape[0] // RD)
    per = slice_a.shape[1] // width
    number = gb // per

    def slices(q, dst_ref):
        at = pl.ds(pl.multiple_of(q * (per * width), per * width), per * width)
        images = jnp.concatenate([x_ref[:, at], y_ref[:, at]], axis=0)
        value = jnp.dot(post_t[...], images, preferred_element_type=F32)
        dst_ref[...] = value.astype(BF16)

    def emit(u, piece, base, size):
        pos = pos_ref[0, pl.ds(u, 1), :]
        order = []
        for at in range(0, size, 128):
            high = min(128, size - at)
            slot = lax.broadcasted_iota(jnp.int32, (high, half), 0).astype(F32).astype(BF16)
            near = jnp.clip(pos - (base + at), -1, 128).astype(F32).astype(BF16)
            order.append(jnp.where(slot == near, one, none))
        order = jnp.concatenate(order, axis=0)
        rows = jnp.dot(order, piece, preferred_element_type=F32)
        for i in range(size // 8):
            at = addr_ref[0, u, base // 8 + i]
            buf_s[pl.ds(pl.multiple_of(at * 8, 8), 8), :] = rows[8 * i : 8 * i + 8]
            buf_m[pl.ds(at, 1), :] = meta_ref[0, u, pl.ds(base // 8 + i, 1), :]

    def sort(q, src_ref):
        for g in range(per):
            for h in range(parts):
                piece = src_ref[h * half : (h + 1) * half, g * width : (g + 1) * width]
                emit((q * per + g) * parts + h, piece, 0, sure)

    def rest_of(q, src_ref):
        for g in range(per):
            for h in range(parts):
                u = (q * per + g) * parts + h

                def more(e, c, u=u, g=g, h=h):
                    piece = src_ref[h * half : (h + 1) * half, g * width : (g + 1) * width]
                    emit(u, piece, sure + e * 128, 128)
                    return c

                used = addr_ref[0, u, lanes - 1]
                lax.fori_loop(0, lax.div(jnp.maximum(used - sure, 0) + 127, 128), more, 0)

    def most_used(q):
        most = addr_ref[0, q * per * parts, lanes - 1]
        for u in range(1, per * parts):
            most = jnp.maximum(most, addr_ref[0, q * per * parts + u, lanes - 1])
        return most

    def two(j, carry):
        q = j * 2
        sort(q, slice_a)
        slices(q + 1, slice_b)

        @pl.when(most_used(q) > sure)
        def _():
            rest_of(q, slice_a)

        sort(q + 1, slice_b)
        slices(jnp.minimum(q + 2, number - 1), slice_a)

        @pl.when(most_used(q + 1) > sure)
        def _():
            rest_of(q + 1, slice_b)

        return carry

    slices(0, slice_a)
    lax.fori_loop(0, number // 2, two, 0)
    if number % 2:
        sort(number - 1, slice_a)
        rest_of(number - 1, slice_a)

    bins = lax.broadcasted_iota(jnp.int32, (RD, RD), 0).astype(F32).astype(BF16)
    side = RD // 2
    at_lane = lax.broadcasted_iota(jnp.int32, (side // 8, side), 1) // 8
    own_lane = at_lane == lax.broadcasted_iota(jnp.int32, (side // 8, side), 0)
    line = lax.broadcasted_iota(jnp.int32, (1, RD), 1)
    together = 8

    def some_items(q, carry):
        for u in range(together):
            j = q * together + u
            owner, at, left = item_ref[0, 0, j], item_ref[0, 1, j], item_ref[0, 2, j]
            places = [
                jnp.sum(
                    jnp.where(own_lane, buf_m[pl.ds(at + h * (side // 8), side // 8), :], 0.0),
                    axis=0,
                    keepdims=True,
                )
                for h in range(2)
            ]
            place = jnp.where(line < left, jnp.concatenate(places, axis=1), -9.0)
            whole = jnp.floor(place)
            apart = (bins - whole.astype(BF16)) - (place - whole).astype(BF16)
            weights = jnp.maximum(one - jnp.abs(apart), none)
            values = buf_s[pl.ds(pl.multiple_of(at * 8, 8), RD), :].astype(BF16)
            goal = pl.ds(pl.multiple_of(owner * RD, RD), RD)
            volume[goal, :] += jnp.dot(weights, values, preferred_element_type=F32)
        return carry

    count_items = lax.div(item_ref[0, 3, 0] + together - 1, together)
    lax.fori_loop(0, count_items, some_items, 0)

    @pl.when(step == pl.num_programs(0) - 1)
    def _():
        side_rows = keep_ref.shape[1]
        slots_out, _, tile, _ = stage.shape
        copies = []
        for base, out_ref in ((side_rows, send_ref), (0, keep_ref)):
            for at in range(0, side_rows, tile):
                slot = len(copies) % slots_out
                if len(copies) >= slots_out:
                    copies[len(copies) - slots_out].wait()
                value = volume[base + at : base + at + tile, :].astype(BF16)
                for c in range(2):
                    stage[slot, c] = value[:, c * OB : (c + 1) * OB]
                copy = pltpu.make_async_copy(
                    stage.at[slot], out_ref.at[:, pl.ds(at, tile)], sem.at[slot]
                )
                copy.start()
                copies.append(copy)
        for copy in copies[-slots_out:]:
            copy.wait()


def group_pair(gb):
    return 2 if gb % 2 == 0 else 1


def insert_block(groups, orients, owners, count, width):
    half = min(256, orients)
    slots, _, blocks = sort_sizes(half, owners)
    room = max(32 * MB - owners * RD * width * 4, 18 * MB)
    best = 1
    for gb in range(1, groups + 1):
        units = gb * (orients // half)
        rows = units * slots + RD + 8
        need = rows * (width * 4 + OB // 2) + 8 * count * gb * width + units * blocks * OB * 8
        if groups % gb == 0 and need <= room:
            best = gb
    return best


def insert_call(addr, items, flats, pos, meta, blocks, posts, orients, owners):
    count, length = flats[0].shape
    steps, units, half = pos.shape
    gb = units * half // orients
    width = length // (steps * gb)
    total = owners * RD
    rows = units * sort_sizes(half, owners)[0] + RD + 8
    limit = total * width * 4 // MB + 30
    block = lambda shape, **kw: pl.BlockSpec(
        (1,) + shape[1:], lambda i: (i,) + (0,) * (len(shape) - 1), **kw
    )
    return pl.pallas_call(
        insert_kernel,
        grid=(steps,),
        out_shape=[jax.ShapeDtypeStruct((2, total // 2, OB), BF16)] * 2,
        in_specs=[
            block(addr.shape, memory_space=pltpu.SMEM),
            block(items.shape, memory_space=pltpu.SMEM),
            pl.BlockSpec((count, gb * width), lambda i: (0, i)),
            pl.BlockSpec((count, gb * width), lambda i: (0, i)),
            block(pos.shape),
            block(meta.shape),
            pl.BlockSpec((2, count), lambda i: (0, 0)),
            pl.BlockSpec((2, count), lambda i: (0, 0)),
        ]
        + [pl.BlockSpec(posts[0].shape, lambda i: (0, 0, 0))] * 2,
        out_specs=[pl.BlockSpec(memory_space=pl.ANY)] * 2,
        scratch_shapes=[
            pltpu.VMEM((orients, 2 * count), BF16),
            pltpu.VMEM((count, orients), F32),
            pltpu.VMEM((2, count, OB), F32),
            pltpu.VMEM((orients, group_pair(gb) * width), BF16),
            pltpu.VMEM((orients, group_pair(gb) * width), BF16),
            pltpu.VMEM((rows, width), F32),
            pltpu.VMEM((rows // 8, OB), F32),
            pltpu.VMEM((total, width), F32),
            pltpu.VMEM((OUT_SLOTS, 2, OUT_TILE, OB), BF16),
            pltpu.SemaphoreType.DMA((OUT_SLOTS,)),
        ],
        compiler_params=pltpu.CompilerParams(vmem_limit_bytes=limit * MB),
        cost_estimate=pl.CostEstimate(
            flops=8 * count * orients * length,
            bytes_accessed=2 * count * length,
            transcendentals=0,
        ),
    )(addr, items, *flats, pos, meta, *blocks, *posts)


def flip(value, axis, bit):
    size = lax.axis_size(axis)
    return lax.ppermute(value, axis, [(i, i ^ bit) for i in range(size)])


def shards(particles, blocks, references, inv_noise, destination, row_index, fraction):
    groups, width = particles.shape[1:]
    orients = references.shape[0]
    dom_size = lax.axis_size("dom")
    slab_size = lax.axis_size("slab")
    devices = dom_size * slab_size
    dom_pos = lax.axis_index("dom")
    slab_pos = lax.axis_index("slab")
    here = jnp.stack([dom_pos, slab_pos]).astype(jnp.int32)
    dom_bits = [1 << i for i in range((dom_size - 1).bit_length())]
    swap = lambda value, axis: lax.all_to_all(value, "slab", axis, axis, tiled=True)

    blocks = blocks.T
    kept, sent, scores = score_call(here, inv_noise, particles, references, blocks, slab_size)
    gb = insert_block(groups // 2, orients, devices, particles.shape[0], width)
    here, scores, sent = lax.optimization_barrier((here, scores, sent))
    plan = plan_call(here, destination, groups, gb, (dom_size, slab_size))
    flats = [kept, flip(sent, "dom", dom_bits[0])]
    more_blocks = flip(blocks, "dom", dom_bits[0])
    parts = swap(scores, 0)
    parts, more_blocks, later, *plan = lax.optimization_barrier(
        (parts, more_blocks, here, *plan)
    )
    pos, addr, items = plan
    meta = meta_call(later, row_index, fraction, pos, devices)
    post = swap(softmax_call(parts), 0)
    post, meta = lax.optimization_barrier((post, meta))
    posts = [post, flip(post, "dom", dom_bits[0])]
    lists = [blocks, more_blocks]
    send, keep = insert_call(addr, items, flats, pos, meta, lists, posts, orients, devices)

    def added(terms):
        return functools.reduce(jnp.add, [term.astype(F32) for term in terms])

    def halve(terms, axis_name, axis, bit):
        size = terms[0].shape[axis] // 2
        pick = lambda term, at: lax.slice_in_dim(term, at, at + size, axis=axis)
        sent = added([pick(term, size) for term in terms]).astype(BF16)
        return [pick(term, 0) for term in terms] + [flip(sent, axis_name, bit)]

    terms = [keep, flip(send, "dom", dom_bits[0])]
    rest = dom_bits[1:]
    columns = []
    for part in range(2):
        columns.append(
            [term[part].reshape((2,) * len(rest) + (slab_size * RD, OB)) for term in terms]
        )
    for stage in range(len(rest)):
        for part in range(2):
            axis = stage if part == 0 else len(rest) - 1 - stage
            columns[part] = halve(columns[part], "dom", axis, rest[axis])
    terms = [jnp.stack([t.reshape(slab_size * RD, OB) for t in pair]) for pair in zip(*columns)]
    pieces = added(terms).astype(BF16).reshape(2, slab_size, RD, OB)
    pieces = swap(pieces, 1)
    volume = jnp.concatenate(
        [added([pieces[part, k] for k in range(slab_size)]) for part in range(2)], axis=1
    )

    own = volume.astype(BF16)
    plane = [own] + [flip(own, "dom", 2 * k) for k in range(1, dom_size // 2)]
    chip = dom_pos // 2
    placed = []
    for k in range(dom_size // 2):
        value = plane[0]
        for j in range(1, dom_size // 2):
            value = jnp.where(chip ^ j == k, plane[j], value)
        placed.append(value)
    value = jnp.stack(placed)
    got = flip(value, "dom", dom_bits[0])
    value = jnp.where(
        dom_pos & dom_bits[0] == 0,
        jnp.stack([value, got], 1),
        jnp.stack([got, value], 1),
    )
    return volume, value.reshape(dom_size * RD, width)


def solution(mesh):
    return jax.shard_map(
        shards,
        mesh=mesh,
        in_specs=(
            P("dom", "slab", None),
            P("dom", None),
            P(None, "slab", None),
            P("slab"),
            P(),
            P(),
            P(),
        ),
        out_specs=(P(("dom", "slab"), None), P(None, "slab")),
        check_vma=False,
    )
```

```python
import functools

import jax
import jax.numpy as jnp
from jax import lax
from jax.experimental import pallas as pl
from jax.experimental.pallas import tpu as pltpu
from jax.sharding import PartitionSpec as P

OB = 128
RD = 256
MB = 2**20
OUT_SLOTS = 4
STREAMS = 4
OUT_TILE = 1024
F32 = jnp.float32
BF16 = jnp.bfloat16


def group_block(groups):
    return 16 if groups % 16 == 0 else 8


def spread_columns(blk_ref, cols_ref):
    count = blk_ref.shape[1]
    for j in range(2):
        for at in range(0, count, OB):
            line = blk_ref[j : j + 1, at : at + OB].astype(F32)
            cols_ref[j, at : at + OB, :] = jnp.broadcast_to(line, (OB, OB)).T


def score_kernel(here_ref, noise_ref, blk_ref, *rest):
    x_refs, r_refs = rest[:STREAMS], rest[STREAMS : 2 * STREAMS]
    keep_ref, send_ref = rest[2 * STREAMS : 2 * STREAMS + 2]
    out_refs = rest[2 * STREAMS + 2 : -8]
    flat_a, flat_b, w_a, w_b, acc_ref, perm_ref, cols_ref, sem = rest[-8:]
    step = pl.program_id(0)
    steps = pl.num_programs(0) - 1
    gb, width = x_refs[0].shape[1:]
    particles, orients = acc_ref.shape
    side = 16 * gb
    per = gb // 2
    slabs = len(out_refs)
    core = lax.div(here_ref[0], slabs) & 1
    rounds = 4

    def copies(flat_ref, slot, at_step, swap):
        lanes = pl.ds(pl.multiple_of(at_step * (per * width), per * width), per * width)
        goals = (send_ref, keep_ref) if swap else (keep_ref, send_ref)
        return [
            pltpu.make_async_copy(flat_ref.at[h], goals[h].at[:, lanes], sem.at[slot, h])
            for h in range(2)
        ]

    def send_out(flat_ref, slot):
        for which in range(2):

            @pl.when(core == which)
            def _(which=which):
                for copy in copies(flat_ref, slot, step, which == 1):
                    copy.start()

    def wait_out(flat_ref, slot):
        for copy in copies(flat_ref, slot, 0, False):
            copy.wait()

    def regroup(jobs):
        wide = [ref[pl.ds(first * 16, 16)].reshape(side, width) for ref, first, *_ in jobs]
        moved = jnp.dot(perm_ref[...], jnp.concatenate(wide, axis=1), preferred_element_type=F32)
        for g in range(gb):
            lanes = slice(g % per * width, (g % per + 1) * width)
            for t, (_, first, base, goal_ref, scaled) in enumerate(jobs):
                part = moved[g * 16 : (g + 1) * 16, t * width : (t + 1) * width]
                if scaled:
                    part = part * noise_ref[step * gb + g]
                at = pl.ds(pl.multiple_of(base + first * 16, 16), 16)
                goal_ref[g // per, at, lanes] = part.astype(BF16)

    def turn(src_ref, first, base, goal_ref):
        turned = jnp.swapaxes(src_ref[pl.ds(first * 16, 16)], 0, 1)
        at = pl.ds(pl.multiple_of(base + first * 16, 16), 16)
        for g in range(gb):
            goal_ref[g // per, at, g % per * width : (g % per + 1) * width] = turned[g]

    def tiles(i, flat_ref, w_ref):
        jobs, turns = [], []
        for s in range(STREAMS):
            rows = orients // STREAMS
            for t in range(rows // 16 // rounds):
                jobs.append((r_refs[s], i * (rows // 16 // rounds) + t, s * rows, w_ref, True))
            rows = particles // STREAMS
            for t in range(rows // 16 // rounds):
                job = (x_refs[s], i * (rows // 16 // rounds) + t, s * rows, flat_ref)
                if (s * (rows // 16 // rounds) + t) % 2:
                    turns.append(job)
                else:
                    jobs.append(job + (False,))
        for at in range(0, len(jobs), 6):
            regroup(jobs[at : at + 6])
        for job in turns:
            turn(*job)

    def product(left, right):
        acc_ref[...] += lax.dot_general(
            left, right, (((1,), (1,)), ((), ())), preferred_element_type=F32
        )

    def both(i, flat_ref, w_ref, last_flat, last_w):
        span = 2 * per * width // rounds
        at = pl.ds(pl.multiple_of(lax.rem(i, rounds // 2) * span, span), span)
        h = lax.div(i, rounds // 2)
        product(last_flat[h, :, at], last_w[h, :, at])
        tiles(i, flat_ref, w_ref)

    def loop(body, *refs):
        lax.fori_loop(0, rounds, lambda i, c: (body(i, *refs), c)[1], 0)

    @pl.when(step == 0)
    def _():
        row = lax.broadcasted_iota(jnp.int32, (side, side), 0)
        col = lax.broadcasted_iota(jnp.int32, (side, side), 1)
        same = ((row // 16) == (col % gb)) & ((row % 16) == (col // gb))
        perm_ref[...] = jnp.where(same, 1.0, 0.0).astype(BF16)
        acc_ref[...] = jnp.zeros_like(acc_ref)
        spread_columns(blk_ref, cols_ref)
        loop(tiles, flat_a, w_a)
        send_out(flat_a, 0)

    inner = (step > 0) & (step < steps)

    @pl.when(inner & (lax.rem(step, 2) == 1))
    def _():
        @pl.when(step > 1)
        def _():
            wait_out(flat_b, 1)

        loop(both, flat_b, w_b, flat_a, w_a)
        send_out(flat_b, 1)

    @pl.when(inner & (lax.rem(step, 2) == 0))
    def _():
        wait_out(flat_a, 0)
        loop(both, flat_a, w_a, flat_b, w_b)
        send_out(flat_a, 0)

    def finish(last_flat, last_w):
        for h in range(2):
            product(last_flat[h], last_w[h])
        me = lax.rem(here_ref[0], slabs)
        share = particles // len(out_refs)
        for k, out_ref in enumerate(out_refs):
            at = pl.multiple_of((me ^ k) * share, share)
            for j in range(2):
                wanted = cols_ref[j, pl.ds(at, share), :]
                chosen = jnp.zeros((share, OB), F32)
                for b in range(orients // OB):
                    value = acc_ref[pl.ds(at, share), b * OB : (b + 1) * OB]
                    chosen = jnp.where(wanted == b, value, chosen)
                out_ref[:, j * OB : (j + 1) * OB] = chosen
        wait_out(flat_a, 0)

        @pl.when(steps > 1)
        def _():
            wait_out(flat_b, 1)

    @pl.when((step == steps) & (lax.rem(step, 2) == 1))
    def _():
        finish(flat_a, w_a)

    @pl.when((step == steps) & (lax.rem(step, 2) == 0))
    def _():
        finish(flat_b, w_b)


def score_call(here, inv_noise, particles, references, blocks, slab_size):
    count, groups, width = particles.shape
    orients = references.shape[0]
    gb = group_block(groups)
    side = 16 * gb
    share = count // slab_size
    smem = pl.BlockSpec(memory_space=pltpu.SMEM)
    steps = groups // gb
    return pl.pallas_call(
        score_kernel,
        grid=(steps + 1,),
        out_shape=[jax.ShapeDtypeStruct((count, groups // 2 * width), BF16)] * 2
        + [jax.ShapeDtypeStruct((share, 2 * OB), F32)] * slab_size,
        in_specs=[
            smem,
            smem,
            pl.BlockSpec((2, count), lambda i: (0, 0)),
        ]
        + [
            pl.BlockSpec(
                (rows // STREAMS, gb, width), lambda i, s=s: (s, jnp.minimum(i, steps - 1), 0)
            )
            for rows in (count, orients)
            for s in range(STREAMS)
        ],
        out_specs=[pl.BlockSpec(memory_space=pl.ANY)] * 2
        + [pl.BlockSpec((share, 2 * OB), lambda i: (0, 0))] * slab_size,
        scratch_shapes=[
            pltpu.VMEM((2, count, gb // 2 * width), BF16),
            pltpu.VMEM((2, count, gb // 2 * width), BF16),
            pltpu.VMEM((2, orients, gb // 2 * width), BF16),
            pltpu.VMEM((2, orients, gb // 2 * width), BF16),
            pltpu.VMEM((count, orients), F32),
            pltpu.VMEM((side, side), BF16),
            pltpu.VMEM((2, count, OB), F32),
            pltpu.SemaphoreType.DMA((2, 2)),
        ],
        compiler_params=pltpu.CompilerParams(vmem_limit_bytes=56 * MB),
        cost_estimate=pl.CostEstimate(
            flops=4 * count * orients * groups * width,
            bytes_accessed=6 * count * groups * width,
            transcendentals=0,
        ),
    )(here, inv_noise, blocks, *[particles] * STREAMS, *[references] * STREAMS)


def softmax_kernel(*refs):
    *parts, out_ref = refs
    total = parts[0][...]
    for part in parts[1:]:
        total = total + part[...]
    highest = jnp.max(total, axis=1, keepdims=True)
    weights = jnp.exp(total - highest)
    out_ref[...] = (weights / jnp.sum(weights, axis=1, keepdims=True)).astype(BF16)


def softmax_call(parts):
    return pl.pallas_call(
        softmax_kernel,
        out_shape=jax.ShapeDtypeStruct(parts[0].shape, BF16),
        compiler_params=pltpu.CompilerParams(vmem_limit_bytes=8 * MB),
    )(*parts)


def own_row(here_ref, local, per, slabs):
    core = lax.div(here_ref[0], slabs) & 1
    return lax.div(local, per) * (2 * per) + core * per + lax.rem(local, per)


def plan_kernel(
    here_ref, dest_ref, pos_ref, addr_ref, item_ref, place_ref, hot_ref, count_ref, *, sizes, per
):
    step = pl.program_id(0)
    dom_size, slab_size = sizes
    owners = dom_size * slab_size
    _, units, half = pos_ref.shape
    lanes = addr_ref.shape[2]
    parts = dest_ref.shape[1] // half
    gb = units // parts
    dom_log, slab_log = (dom_size - 1).bit_length(), (slab_size - 1).bit_length()

    @pl.when(step == 0)
    def _():
        off = dest_ref[...] ^ here_ref[0]
        place = jnp.zeros_like(off)
        for bit in list(range(slab_log, slab_log + dom_log)) + list(range(slab_log)):
            place = place * 2 + (lax.shift_right_logical(off, bit) & 1)
        place_ref[...] = place

    owner = lax.broadcasted_iota(jnp.int32, (owners, 1), 0)
    for u in range(units):
        g, h = u // parts, u % parts
        at = pl.ds(own_row(here_ref, step * gb + g, per, slab_size), 1)
        line = place_ref[at, h * half : (h + 1) * half]
        hot = jnp.where(line == owner, 1.0, 0.0)
        hot_ref[u * owners : (u + 1) * owners, :] = hot.astype(BF16)
    before = lax.broadcasted_iota(jnp.int32, (half, half), 0)
    after = lax.broadcasted_iota(jnp.int32, (half, half), 1)
    upto = jnp.where(before <= after, 1.0, 0.0).astype(BF16)
    count_ref[...] = jnp.dot(hot_ref[...], upto, preferred_element_type=F32)

    exact = functools.partial(
        jnp.dot, preferred_element_type=F32, precision=lax.Precision.HIGHEST
    )
    row = lax.broadcasted_iota(jnp.int32, (owners, owners), 0)
    col = lax.broadcasted_iota(jnp.int32, (owners, owners), 1)
    below = jnp.where(row > col, 1.0, 0.0)
    row = lax.broadcasted_iota(jnp.int32, (OB, OB), 0)
    col = lax.broadcasted_iota(jnp.int32, (OB, OB), 1)
    earlier = jnp.where(row < col, 1.0, 0.0)
    lane = lax.broadcasted_iota(jnp.int32, (owners, OB), 1)
    runs = jnp.zeros((owners, OB), F32)
    for u in range(units):
        size = count_ref[u * owners : (u + 1) * owners, half - 1 : half]
        runs = jnp.where(lane == u, size, runs)
    runs = jnp.floor((runs + 7.0) * 0.125) * 8.0
    base = exact(below, runs)
    ahead = exact(runs, earlier)
    total = jnp.sum(runs, axis=1, keepdims=True)
    start = exact(below, jnp.broadcast_to(total, (owners, OB)))[:, :1]
    blocks = jnp.floor((total + (RD - 1.0)) * (1.0 / RD))
    first = exact(below, jnp.broadcast_to(blocks, (owners, OB)))[:, :1]
    shift = start + ahead - base
    used = jnp.sum(runs, axis=0, keepdims=True)

    slot = (lax.broadcasted_iota(jnp.int32, (1, lanes), 1) * 8).astype(F32)
    is_last = lax.broadcasted_iota(jnp.int32, (1, lanes), 1) == lanes - 1
    rows = units * (half + 7 * owners)
    for u in range(units):
        low, size = base[:, u : u + 1], runs[:, u : u + 1]
        hot = hot_ref[u * owners : (u + 1) * owners, :].astype(F32)
        rank = count_ref[u * owners : (u + 1) * owners, :] + (low - 1.0)
        pos_ref[0, u : u + 1, :] = jnp.sum(hot * rank, axis=0, keepdims=True).astype(jnp.int32)
        inside = (slot >= low) & (slot < low + size)
        goal = jnp.where(inside, shift[:, u : u + 1] + slot - rows, 0.0)
        goal = (jnp.sum(goal, axis=0, keepdims=True) + rows) * 0.125
        addr_ref[0, u : u + 1, :] = jnp.where(is_last, used[:, u : u + 1], goal).astype(jnp.int32)

    wide = item_ref.shape[2]
    number = lax.broadcasted_iota(jnp.int32, (1, wide), 1).astype(F32)
    inside = (number >= first) & (number < first + blocks)
    done = (number - first) * RD
    pick = lambda value: jnp.sum(jnp.where(inside, value, 0.0), axis=0, keepdims=True)
    every = lambda value: jnp.sum(
        jnp.broadcast_to(value, (owners, wide)), axis=0, keepdims=True
    )
    lines = (
        pick(jnp.broadcast_to(owner.astype(F32), (owners, wide))),
        pick((start + done) * 0.125),
        pick(total - done),
        every(blocks),
        every(total * 0.125),
    )
    for i, value in enumerate(lines):
        item_ref[0, i : i + 1, :] = value.astype(jnp.int32)


def meta_kernel(here_ref, index_ref, frac_ref, pos_ref, meta_ref, *, per, slabs):
    step = pl.program_id(0)
    _, units, half = pos_ref.shape
    parts = index_ref.shape[1] // half
    gb = units // parts
    blocks = meta_ref.shape[2]
    low = lambda value: value.astype(F32).astype(BF16)
    eighth = low(lax.broadcasted_iota(jnp.int32, (blocks, half), 0))
    lane_of = low(lax.broadcasted_iota(jnp.int32, (OB, half), 0) % 8)
    one, none = jnp.bfloat16(1.0), jnp.bfloat16(0.0)
    for u in range(units):
        g, h = u // parts, u % parts
        line = pl.ds(own_row(here_ref, step * gb + g, per, slabs), 1)
        span = slice(h * half, (h + 1) * half)
        pos = pos_ref[0, u : u + 1, :]
        here = lane_of == low(pos & 7)
        spots = jnp.where(eighth == low(lax.shift_right_logical(pos, 3)), one, none)
        terms = [
            jnp.where(here, low(index_ref[line, span]), none),
            jnp.where(here, low(frac_ref[line, span]), none),
        ]
        meta_ref[0, u] = lax.dot_general(
            jnp.concatenate([spots, spots], axis=1),
            jnp.concatenate(terms, axis=1),
            (((1,), (1,)), ((), ())),
            preferred_element_type=F32,
        )


def up_to(value, step):
    return -(-value // step) * step


def sort_sizes(orients, owners):
    slots = orients + 7 * owners
    sure = orients + 144
    blocks = up_to((sure + up_to(max(0, slots - sure), 128)) // 8, 8)
    return slots, sure, blocks


def planned(shape):
    return pl.BlockSpec((1,) + shape[1:], lambda i, here: (i,) + (0,) * (len(shape) - 1))


def plan_call(here, destination, groups, gb, mesh_sizes):
    orients = destination.shape[1]
    half = min(256, orients)
    owners = mesh_sizes[0] * mesh_sizes[1]
    steps, units = groups // 2 // gb, gb * (orients // half)
    slots, _, blocks = sort_sizes(half, owners)
    shapes = [
        (steps, units, half),
        (steps, units, up_to(blocks + 1, 128)),
        (steps, 5, up_to(owners + units * slots // RD + 8, 128)),
    ]
    return pl.pallas_call(
        functools.partial(plan_kernel, sizes=mesh_sizes, per=group_block(groups) // 2),
        grid_spec=pltpu.PrefetchScalarGridSpec(
            num_scalar_prefetch=1,
            grid=(steps,),
            in_specs=[
                pl.BlockSpec(
                    (groups, orients), lambda i, here: (lax.rem(here[0], mesh_sizes[1]), 0)
                )
            ],
            out_specs=[planned(shape) for shape in shapes],
            scratch_shapes=[
                pltpu.VMEM((groups, orients), jnp.int32),
                pltpu.VMEM((units * owners, half), BF16),
                pltpu.VMEM((units * owners, half), F32),
            ],
        ),
        out_shape=[jax.ShapeDtypeStruct(shape, jnp.int32) for shape in shapes],
        compiler_params=pltpu.CompilerParams(vmem_limit_bytes=55 * MB),
        cost_estimate=pl.CostEstimate(
            flops=8 * steps * units * owners * half * half,
            bytes_accessed=8 * groups * orients,
            transcendentals=0,
        ),
    )(here, destination)


def meta_call(here, row_index, fraction, pos, owners, slabs):
    steps, units, half = pos.shape
    orients = row_index.shape[1]
    groups = 2 * steps * units * half // orients
    blocks = sort_sizes(half, owners)[2]
    shape = (steps, units, blocks, OB)
    table = pl.BlockSpec((groups, orients), lambda i, here: (lax.rem(here[0], slabs), 0))
    return pl.pallas_call(
        functools.partial(meta_kernel, per=group_block(groups) // 2, slabs=slabs),
        grid_spec=pltpu.PrefetchScalarGridSpec(
            num_scalar_prefetch=1,
            grid=(steps,),
            in_specs=[table, table, planned(pos.shape)],
            out_specs=planned(shape),
        ),
        out_shape=jax.ShapeDtypeStruct(shape, F32),
        compiler_params=pltpu.CompilerParams(vmem_limit_bytes=16 * MB),
        cost_estimate=pl.CostEstimate(
            flops=8 * steps * units * blocks * half * OB,
            bytes_accessed=8 * steps * units * blocks * OB,
            transcendentals=0,
        ),
    )(here, row_index, fraction, pos)


def insert_kernel(
    addr_ref, item_ref, x_ref, y_ref, pos_ref, meta_ref, blk_ref, more_blk_ref, *rest
):
    post_ref, more_ref, send_ref, keep_ref = rest[:-8]
    post_t, slice_a, slice_b, buf_s, buf_m, volume, stage, sem = rest[-8:]
    step = pl.program_id(0)
    count = x_ref.shape[0]
    orients = post_t.shape[0]
    units, half = pos_ref.shape[1:]
    parts = orients // half
    gb = units // parts
    width = x_ref.shape[1] // gb
    share = post_ref.shape[1]
    lanes = addr_ref.shape[2]

    @pl.when(step == 0)
    def _():
        volume[...] = jnp.zeros_like(volume)
        for who, (lists, pieces) in enumerate(((blk_ref, post_ref), (more_blk_ref, more_ref))):
            for k in range(pieces.shape[0]):
                lanes = slice(k * share, (k + 1) * share)
                turned = pieces[k].astype(F32).T
                for b in range(orients // OB):
                    value = jnp.where(
                        lists[0:1, lanes] == b,
                        turned[:OB],
                        jnp.where(lists[1:2, lanes] == b, turned[OB:], 0.0),
                    )
                    at = slice(who * count + k * share, who * count + (k + 1) * share)
                    post_t[b * OB : (b + 1) * OB, at] = value.astype(BF16)

    tail = pl.ds(pl.multiple_of(item_ref[0, 4, 0] * 8, 8), RD)
    buf_s[tail, :] = jnp.zeros((RD, width), F32)
    one, none = jnp.bfloat16(1.0), jnp.bfloat16(0.0)
    slots, sure, _ = sort_sizes(half, volume.shape[0] // RD)
    per = slice_a.shape[1] // width
    number = gb // per

    def slices(q, dst_ref):
        at = pl.ds(pl.multiple_of(q * (per * width), per * width), per * width)
        images = jnp.concatenate([x_ref[:, at], y_ref[:, at]], axis=0)
        value = jnp.dot(post_t[...], images, preferred_element_type=F32)
        dst_ref[...] = value.astype(BF16)

    def emit(u, piece, base, size):
        pos = pos_ref[0, pl.ds(u, 1), :]
        order = []
        for at in range(0, size, 128):
            high = min(128, size - at)
            slot = lax.broadcasted_iota(jnp.int32, (high, half), 0).astype(F32).astype(BF16)
            near = jnp.clip(pos - (base + at), -1, 128).astype(F32).astype(BF16)
            order.append(jnp.where(slot == near, one, none))
        order = jnp.concatenate(order, axis=0)
        rows = jnp.dot(order, piece, preferred_element_type=F32)
        for i in range(size // 8):
            at = addr_ref[0, u, base // 8 + i]
            buf_s[pl.ds(pl.multiple_of(at * 8, 8), 8), :] = rows[8 * i : 8 * i + 8]
            buf_m[pl.ds(at, 1), :] = meta_ref[0, u, pl.ds(base // 8 + i, 1), :]

    def sort(q, src_ref):
        for g in range(per):
            for h in range(parts):
                piece = src_ref[h * half : (h + 1) * half, g * width : (g + 1) * width]
                emit((q * per + g) * parts + h, piece, 0, sure)

    def rest_of(q, src_ref):
        for g in range(per):
            for h in range(parts):
                u = (q * per + g) * parts + h

                def more(e, c, u=u, g=g, h=h):
                    piece = src_ref[h * half : (h + 1) * half, g * width : (g + 1) * width]
                    emit(u, piece, sure + e * 128, 128)
                    return c

                used = addr_ref[0, u, lanes - 1]
                lax.fori_loop(0, lax.div(jnp.maximum(used - sure, 0) + 127, 128), more, 0)

    def most_used(q):
        most = addr_ref[0, q * per * parts, lanes - 1]
        for u in range(1, per * parts):
            most = jnp.maximum(most, addr_ref[0, q * per * parts + u, lanes - 1])
        return most

    def two(j, carry):
        q = j * 2
        sort(q, slice_a)
        slices(q + 1, slice_b)

        @pl.when(most_used(q) > sure)
        def _():
            rest_of(q, slice_a)

        sort(q + 1, slice_b)
        slices(jnp.minimum(q + 2, number - 1), slice_a)

        @pl.when(most_used(q + 1) > sure)
        def _():
            rest_of(q + 1, slice_b)

        return carry

    slices(0, slice_a)
    lax.fori_loop(0, number // 2, two, 0)
    if number % 2:
        sort(number - 1, slice_a)
        rest_of(number - 1, slice_a)

    bins = lax.broadcasted_iota(jnp.int32, (RD, RD), 0).astype(F32).astype(BF16)
    side = RD // 2
    at_lane = lax.broadcasted_iota(jnp.int32, (side // 8, side), 1) // 8
    own_lane = at_lane == lax.broadcasted_iota(jnp.int32, (side // 8, side), 0)
    line = lax.broadcasted_iota(jnp.int32, (1, RD), 1)
    together = 8

    def some_items(q, carry):
        for u in range(together):
            j = q * together + u
            owner, at, left = item_ref[0, 0, j], item_ref[0, 1, j], item_ref[0, 2, j]
            places = [
                jnp.sum(
                    jnp.where(own_lane, buf_m[pl.ds(at + h * (side // 8), side // 8), :], 0.0),
                    axis=0,
                    keepdims=True,
                )
                for h in range(2)
            ]
            place = jnp.where(line < left, jnp.concatenate(places, axis=1), -9.0)
            whole = jnp.floor(place)
            apart = (bins - whole.astype(BF16)) - (place - whole).astype(BF16)
            weights = jnp.maximum(one - jnp.abs(apart), none)
            values = buf_s[pl.ds(pl.multiple_of(at * 8, 8), RD), :].astype(BF16)
            goal = pl.ds(pl.multiple_of(owner * RD, RD), RD)
            volume[goal, :] += jnp.dot(weights, values, preferred_element_type=F32)
        return carry

    count_items = lax.div(item_ref[0, 3, 0] + together - 1, together)
    lax.fori_loop(0, count_items, some_items, 0)

    @pl.when(step == pl.num_programs(0) - 1)
    def _():
        side_rows = keep_ref.shape[1]
        slots_out, _, tile, _ = stage.shape
        copies = []
        for base, out_ref in ((side_rows, send_ref), (0, keep_ref)):
            for at in range(0, side_rows, tile):
                slot = len(copies) % slots_out
                if len(copies) >= slots_out:
                    copies[len(copies) - slots_out].wait()
                value = volume[base + at : base + at + tile, :].astype(BF16)
                for c in range(2):
                    stage[slot, c] = value[:, c * OB : (c + 1) * OB]
                copy = pltpu.make_async_copy(
                    stage.at[slot], out_ref.at[:, pl.ds(at, tile)], sem.at[slot]
                )
                copy.start()
                copies.append(copy)
        for copy in copies[-slots_out:]:
            copy.wait()


def group_pair(gb):
    return 2 if gb % 2 == 0 else 1


def insert_block(groups, orients, owners, count, width):
    half = min(256, orients)
    slots, _, blocks = sort_sizes(half, owners)
    room = max(32 * MB - owners * RD * width * 4, 18 * MB)
    best = 1
    for gb in range(1, groups + 1):
        units = gb * (orients // half)
        rows = units * slots + RD + 8
        need = rows * (width * 4 + OB // 2) + 8 * count * gb * width + units * blocks * OB * 8
        if groups % gb == 0 and need <= room:
            best = gb
    return best


def insert_call(addr, items, flats, pos, meta, blocks, posts, orients, owners):
    count, length = flats[0].shape
    steps, units, half = pos.shape
    gb = units * half // orients
    width = length // (steps * gb)
    total = owners * RD
    rows = units * sort_sizes(half, owners)[0] + RD + 8
    limit = total * width * 4 // MB + 30
    block = lambda shape, **kw: pl.BlockSpec(
        (1,) + shape[1:], lambda i: (i,) + (0,) * (len(shape) - 1), **kw
    )
    return pl.pallas_call(
        insert_kernel,
        grid=(steps,),
        out_shape=[jax.ShapeDtypeStruct((2, total // 2, OB), BF16)] * 2,
        in_specs=[
            block(addr.shape, memory_space=pltpu.SMEM),
            block(items.shape, memory_space=pltpu.SMEM),
            pl.BlockSpec((count, gb * width), lambda i: (0, i)),
            pl.BlockSpec((count, gb * width), lambda i: (0, i)),
            block(pos.shape),
            block(meta.shape),
            pl.BlockSpec((2, count), lambda i: (0, 0)),
            pl.BlockSpec((2, count), lambda i: (0, 0)),
        ]
        + [pl.BlockSpec(posts[0].shape, lambda i: (0, 0, 0))] * 2,
        out_specs=[pl.BlockSpec(memory_space=pl.ANY)] * 2,
        scratch_shapes=[
            pltpu.VMEM((orients, 2 * count), BF16),
            pltpu.VMEM((orients, group_pair(gb) * width), BF16),
            pltpu.VMEM((orients, group_pair(gb) * width), BF16),
            pltpu.VMEM((rows, width), F32),
            pltpu.VMEM((rows // 8, OB), F32),
            pltpu.VMEM((total, width), F32),
            pltpu.VMEM((OUT_SLOTS, 2, OUT_TILE, OB), BF16),
            pltpu.SemaphoreType.DMA((OUT_SLOTS,)),
        ],
        compiler_params=pltpu.CompilerParams(vmem_limit_bytes=limit * MB),
        cost_estimate=pl.CostEstimate(
            flops=8 * count * orients * length,
            bytes_accessed=2 * count * length,
            transcendentals=0,
        ),
    )(addr, items, *flats, pos, meta, *blocks, *posts)


def flip(value, axis, bit):
    size = lax.axis_size(axis)
    return lax.ppermute(value, axis, [(i, i ^ bit) for i in range(size)])


def shards(particles, blocks, references, inv_noise, destination, row_index, fraction):
    groups, width = particles.shape[1:]
    orients = references.shape[0]
    dom_size = lax.axis_size("dom")
    slab_size = lax.axis_size("slab")
    devices = dom_size * slab_size
    dom_pos = lax.axis_index("dom")
    slab_pos = lax.axis_index("slab")
    here = lax.axis_index(("dom", "slab")).astype(jnp.int32).reshape(1)
    dom_bits = [1 << i for i in range((dom_size - 1).bit_length())]
    slab_bits = [1 << i for i in range((slab_size - 1).bit_length())]

    blocks = blocks.T
    kept, sent, *scores = score_call(here, inv_noise, particles, references, blocks, slab_size)
    gb = insert_block(groups // 2, orients, devices, particles.shape[0], width)
    here, own = lax.optimization_barrier((here, scores[0]))
    plan = plan_call(here, destination, groups, gb, (dom_size, slab_size))
    own, *plan = lax.optimization_barrier((own, *plan))
    pos, addr, items = plan
    parts = [own] + [flip(scores[k], "slab", k) for k in range(1, slab_size)]
    flats = [kept, flip(sent, "dom", dom_bits[0])]
    post = softmax_call(parts)
    more_blocks = flip(blocks, "dom", dom_bits[0])
    post, more_blocks, later = lax.optimization_barrier((post, more_blocks, here))
    meta = meta_call(later, row_index, fraction, pos, devices, slab_size)
    posts = [post] + [flip(post, "slab", k) for k in range(1, slab_size)]
    ordered = []
    for k in range(slab_size):
        value = posts[0]
        for j in range(1, slab_size):
            value = jnp.where(slab_pos ^ j == k, posts[j], value)
        ordered.append(value)
    pile, meta = lax.optimization_barrier((jnp.stack(ordered), meta))
    posts = [pile, flip(pile, "dom", dom_bits[0])]
    lists = [blocks, more_blocks]
    send, keep = insert_call(addr, items, flats, pos, meta, lists, posts, orients, devices)

    def added(terms):
        return functools.reduce(jnp.add, [term.astype(F32) for term in terms])

    def halve(terms, axis_name, axis, bit):
        size = terms[0].shape[axis] // 2
        pick = lambda term, at: lax.slice_in_dim(term, at, at + size, axis=axis)
        sent = added([pick(term, size) for term in terms]).astype(BF16)
        return [pick(term, 0) for term in terms] + [flip(sent, axis_name, bit)]

    terms = [keep, flip(send, "dom", dom_bits[0])]
    rest = dom_bits[1:]
    columns = []
    for part in range(2):
        columns.append(
            [term[part].reshape((2,) * len(rest) + (slab_size * RD, OB)) for term in terms]
        )
    for stage in range(len(rest)):
        for part in range(2):
            axis = stage if part == 0 else len(rest) - 1 - stage
            columns[part] = halve(columns[part], "dom", axis, rest[axis])
    terms = [jnp.stack([t.reshape(slab_size * RD, OB) for t in pair]) for pair in zip(*columns)]
    for bit in slab_bits:
        terms = halve(terms, "slab", 1, bit)
    volume = jnp.concatenate([added([term[part] for term in terms]) for part in range(2)], axis=1)

    own = volume.astype(BF16)
    plane = [own] + [flip(own, "dom", 2 * k) for k in range(1, dom_size // 2)]
    chip = dom_pos // 2
    placed = []
    for k in range(dom_size // 2):
        value = plane[0]
        for j in range(1, dom_size // 2):
            value = jnp.where(chip ^ j == k, plane[j], value)
        placed.append(value)
    value = jnp.stack(placed)
    got = flip(value, "dom", dom_bits[0])
    value = jnp.where(
        dom_pos & dom_bits[0] == 0,
        jnp.stack([value, got], 1),
        jnp.stack([got, value], 1),
    )
    return volume, value.reshape(dom_size * RD, width)


def solution(mesh):
    return jax.shard_map(
        shards,
        mesh=mesh,
        in_specs=(
            P("dom", "slab", None),
            P("dom", None),
            P(None, "slab", None),
            P("slab"),
            P(),
            P(),
            P(),
        ),
        out_specs=(P(("dom", "slab"), None), P(None, "slab")),
        check_vma=False,
    )
```

```python
import functools

import jax
import jax.numpy as jnp
from jax import lax
from jax.experimental import pallas as pl
from jax.experimental.pallas import tpu as pltpu
from jax.sharding import PartitionSpec as P

OB = 128
RD = 256
MB = 2**20
OUT_SLOTS = 4
STREAMS = 4
OUT_TILE = 1024
F32 = jnp.float32
BF16 = jnp.bfloat16


def group_block(groups):
    return 16 if groups % 16 == 0 else 8


def spread_columns(blk_ref, cols_ref):
    count = blk_ref.shape[1]
    for j in range(2):
        for at in range(0, count, OB):
            line = blk_ref[j : j + 1, at : at + OB].astype(F32)
            cols_ref[j, at : at + OB, :] = jnp.broadcast_to(line, (OB, OB)).T


def score_kernel(here_ref, noise_ref, blk_ref, *rest):
    x_refs, r_refs = rest[:STREAMS], rest[STREAMS : 2 * STREAMS]
    keep_ref, send_ref = rest[2 * STREAMS : 2 * STREAMS + 2]
    out_refs = rest[2 * STREAMS + 2 : -8]
    flat_a, flat_b, w_a, w_b, acc_ref, perm_ref, cols_ref, sem = rest[-8:]
    step = pl.program_id(0)
    steps = pl.num_programs(0) - 1
    gb, width = x_refs[0].shape[1:]
    particles, orients = acc_ref.shape
    side = 16 * gb
    per = gb // 2
    slabs = len(out_refs)
    core = lax.div(here_ref[0], slabs) & 1
    rounds = 4

    def copies(flat_ref, slot, at_step, swap):
        lanes = pl.ds(pl.multiple_of(at_step * (per * width), per * width), per * width)
        goals = (send_ref, keep_ref) if swap else (keep_ref, send_ref)
        return [
            pltpu.make_async_copy(flat_ref.at[h], goals[h].at[:, lanes], sem.at[slot, h])
            for h in range(2)
        ]

    def send_out(flat_ref, slot):
        for which in range(2):

            @pl.when(core == which)
            def _(which=which):
                for copy in copies(flat_ref, slot, step, which == 1):
                    copy.start()

    def wait_out(flat_ref, slot):
        for copy in copies(flat_ref, slot, 0, False):
            copy.wait()

    def regroup(jobs):
        wide = [ref[pl.ds(first * 16, 16)].reshape(side, width) for ref, first, *_ in jobs]
        moved = jnp.dot(perm_ref[...], jnp.concatenate(wide, axis=1), preferred_element_type=F32)
        for g in range(gb):
            lanes = slice(g % per * width, (g % per + 1) * width)
            for t, (_, first, base, goal_ref, scaled) in enumerate(jobs):
                part = moved[g * 16 : (g + 1) * 16, t * width : (t + 1) * width]
                if scaled:
                    part = part * noise_ref[step * gb + g]
                at = pl.ds(pl.multiple_of(base + first * 16, 16), 16)
                goal_ref[g // per, at, lanes] = part.astype(BF16)

    def turn(src_ref, first, base, goal_ref, scaled):
        turned = jnp.swapaxes(src_ref[pl.ds(first * 16, 16)], 0, 1)
        at = pl.ds(pl.multiple_of(base + first * 16, 16), 16)
        for g in range(gb):
            part = turned[g]
            if scaled:
                part = (part.astype(F32) * noise_ref[step * gb + g]).astype(BF16)
            goal_ref[g // per, at, g % per * width : (g % per + 1) * width] = part

    def tiles(i, flat_ref, w_ref):
        jobs, turns = [], []
        for s in range(STREAMS):
            rows = orients // STREAMS
            for t in range(rows // 16 // rounds):
                job = (r_refs[s], i * (rows // 16 // rounds) + t, s * rows, w_ref, True)
                (turns if t % 2 else jobs).append(job)
            rows = particles // STREAMS
            for t in range(rows // 16 // rounds):
                job = (x_refs[s], i * (rows // 16 // rounds) + t, s * rows, flat_ref, False)
                turns.append(job)
        regroup(jobs)
        for job in turns:
            turn(*job)

    def product(left, right):
        acc_ref[...] += lax.dot_general(
            left, right, (((1,), (1,)), ((), ())), preferred_element_type=F32
        )

    def both(i, flat_ref, w_ref, last_flat, last_w):
        span = 2 * per * width // rounds
        at = pl.ds(pl.multiple_of(lax.rem(i, rounds // 2) * span, span), span)
        h = lax.div(i, rounds // 2)
        product(last_flat[h, :, at], last_w[h, :, at])
        tiles(i, flat_ref, w_ref)

    def loop(body, *refs):
        lax.fori_loop(0, rounds, lambda i, c: (body(i, *refs), c)[1], 0)

    @pl.when(step == 0)
    def _():
        row = lax.broadcasted_iota(jnp.int32, (side, side), 0)
        col = lax.broadcasted_iota(jnp.int32, (side, side), 1)
        same = ((row // 16) == (col % gb)) & ((row % 16) == (col // gb))
        perm_ref[...] = jnp.where(same, 1.0, 0.0).astype(BF16)
        acc_ref[...] = jnp.zeros_like(acc_ref)
        spread_columns(blk_ref, cols_ref)
        loop(tiles, flat_a, w_a)
        send_out(flat_a, 0)

    inner = (step > 0) & (step < steps)

    @pl.when(inner & (lax.rem(step, 2) == 1))
    def _():
        @pl.when(step > 1)
        def _():
            wait_out(flat_b, 1)

        loop(both, flat_b, w_b, flat_a, w_a)
        send_out(flat_b, 1)

    @pl.when(inner & (lax.rem(step, 2) == 0))
    def _():
        wait_out(flat_a, 0)
        loop(both, flat_a, w_a, flat_b, w_b)
        send_out(flat_a, 0)

    def finish(last_flat, last_w):
        for h in range(2):
            product(last_flat[h], last_w[h])
        me = lax.rem(here_ref[0], slabs)
        share = particles // len(out_refs)
        for k, out_ref in enumerate(out_refs):
            at = pl.multiple_of((me ^ k) * share, share)
            for j in range(2):
                wanted = cols_ref[j, pl.ds(at, share), :]
                chosen = jnp.zeros((share, OB), F32)
                for b in range(orients // OB):
                    value = acc_ref[pl.ds(at, share), b * OB : (b + 1) * OB]
                    chosen = jnp.where(wanted == b, value, chosen)
                out_ref[:, j * OB : (j + 1) * OB] = chosen
        wait_out(flat_a, 0)

        @pl.when(steps > 1)
        def _():
            wait_out(flat_b, 1)

    @pl.when((step == steps) & (lax.rem(step, 2) == 1))
    def _():
        finish(flat_a, w_a)

    @pl.when((step == steps) & (lax.rem(step, 2) == 0))
    def _():
        finish(flat_b, w_b)


def score_call(here, inv_noise, particles, references, blocks, slab_size):
    count, groups, width = particles.shape
    orients = references.shape[0]
    gb = group_block(groups)
    side = 16 * gb
    share = count // slab_size
    smem = pl.BlockSpec(memory_space=pltpu.SMEM)
    steps = groups // gb
    return pl.pallas_call(
        score_kernel,
        grid=(steps + 1,),
        out_shape=[jax.ShapeDtypeStruct((count, groups // 2 * width), BF16)] * 2
        + [jax.ShapeDtypeStruct((share, 2 * OB), F32)] * slab_size,
        in_specs=[
            smem,
            smem,
            pl.BlockSpec((2, count), lambda i: (0, 0)),
        ]
        + [
            pl.BlockSpec(
                (rows // STREAMS, gb, width), lambda i, s=s: (s, jnp.minimum(i, steps - 1), 0)
            )
            for rows in (count, orients)
            for s in range(STREAMS)
        ],
        out_specs=[pl.BlockSpec(memory_space=pl.ANY)] * 2
        + [pl.BlockSpec((share, 2 * OB), lambda i: (0, 0))] * slab_size,
        scratch_shapes=[
            pltpu.VMEM((2, count, gb // 2 * width), BF16),
            pltpu.VMEM((2, count, gb // 2 * width), BF16),
            pltpu.VMEM((2, orients, gb // 2 * width), BF16),
            pltpu.VMEM((2, orients, gb // 2 * width), BF16),
            pltpu.VMEM((count, orients), F32),
            pltpu.VMEM((side, side), BF16),
            pltpu.VMEM((2, count, OB), F32),
            pltpu.SemaphoreType.DMA((2, 2)),
        ],
        compiler_params=pltpu.CompilerParams(vmem_limit_bytes=56 * MB),
        cost_estimate=pl.CostEstimate(
            flops=4 * count * orients * groups * width,
            bytes_accessed=6 * count * groups * width,
            transcendentals=0,
        ),
    )(here, inv_noise, blocks, *[particles] * STREAMS, *[references] * STREAMS)


def softmax_kernel(*refs):
    *parts, out_ref = refs
    total = parts[0][...]
    for part in parts[1:]:
        total = total + part[...]
    highest = jnp.max(total, axis=1, keepdims=True)
    weights = jnp.exp(total - highest)
    out_ref[...] = (weights / jnp.sum(weights, axis=1, keepdims=True)).astype(BF16)


def softmax_call(parts):
    return pl.pallas_call(
        softmax_kernel,
        out_shape=jax.ShapeDtypeStruct(parts[0].shape, BF16),
        compiler_params=pltpu.CompilerParams(vmem_limit_bytes=8 * MB),
    )(*parts)


def own_row(here_ref, local, per, slabs):
    core = lax.div(here_ref[0], slabs) & 1
    return lax.div(local, per) * (2 * per) + core * per + lax.rem(local, per)


def plan_kernel(
    here_ref, dest_ref, pos_ref, addr_ref, item_ref, place_ref, hot_ref, count_ref, *, sizes, per
):
    step = pl.program_id(0)
    dom_size, slab_size = sizes
    owners = dom_size * slab_size
    _, units, half = pos_ref.shape
    lanes = addr_ref.shape[2]
    parts = dest_ref.shape[1] // half
    gb = units // parts
    dom_log, slab_log = (dom_size - 1).bit_length(), (slab_size - 1).bit_length()

    @pl.when(step == 0)
    def _():
        off = dest_ref[...] ^ here_ref[0]
        place = jnp.zeros_like(off)
        for bit in list(range(slab_log, slab_log + dom_log)) + list(range(slab_log)):
            place = place * 2 + (lax.shift_right_logical(off, bit) & 1)
        place_ref[...] = place

    owner = lax.broadcasted_iota(jnp.int32, (owners, 1), 0)
    for u in range(units):
        g, h = u // parts, u % parts
        at = pl.ds(own_row(here_ref, step * gb + g, per, slab_size), 1)
        line = place_ref[at, h * half : (h + 1) * half]
        hot = jnp.where(line == owner, 1.0, 0.0)
        hot_ref[u * owners : (u + 1) * owners, :] = hot.astype(BF16)
    before = lax.broadcasted_iota(jnp.int32, (half, half), 0)
    after = lax.broadcasted_iota(jnp.int32, (half, half), 1)
    upto = jnp.where(before <= after, 1.0, 0.0).astype(BF16)
    count_ref[...] = jnp.dot(hot_ref[...], upto, preferred_element_type=F32)

    exact = functools.partial(
        jnp.dot, preferred_element_type=F32, precision=lax.Precision.HIGHEST
    )
    row = lax.broadcasted_iota(jnp.int32, (owners, owners), 0)
    col = lax.broadcasted_iota(jnp.int32, (owners, owners), 1)
    below = jnp.where(row > col, 1.0, 0.0)
    row = lax.broadcasted_iota(jnp.int32, (OB, OB), 0)
    col = lax.broadcasted_iota(jnp.int32, (OB, OB), 1)
    earlier = jnp.where(row < col, 1.0, 0.0)
    lane = lax.broadcasted_iota(jnp.int32, (owners, OB), 1)
    runs = jnp.zeros((owners, OB), F32)
    for u in range(units):
        size = count_ref[u * owners : (u + 1) * owners, half - 1 : half]
        runs = jnp.where(lane == u, size, runs)
    runs = jnp.floor((runs + 7.0) * 0.125) * 8.0
    base = exact(below, runs)
    ahead = exact(runs, earlier)
    total = jnp.sum(runs, axis=1, keepdims=True)
    start = exact(below, jnp.broadcast_to(total, (owners, OB)))[:, :1]
    blocks = jnp.floor((total + (RD - 1.0)) * (1.0 / RD))
    first = exact(below, jnp.broadcast_to(blocks, (owners, OB)))[:, :1]
    shift = start + ahead - base
    used = jnp.sum(runs, axis=0, keepdims=True)

    slot = (lax.broadcasted_iota(jnp.int32, (1, lanes), 1) * 8).astype(F32)
    is_last = lax.broadcasted_iota(jnp.int32, (1, lanes), 1) == lanes - 1
    rows = units * (half + 7 * owners)
    for u in range(units):
        low, size = base[:, u : u + 1], runs[:, u : u + 1]
        hot = hot_ref[u * owners : (u + 1) * owners, :].astype(F32)
        rank = count_ref[u * owners : (u + 1) * owners, :] + (low - 1.0)
        pos_ref[0, u : u + 1, :] = jnp.sum(hot * rank, axis=0, keepdims=True).astype(jnp.int32)
        inside = (slot >= low) & (slot < low + size)
        goal = jnp.where(inside, shift[:, u : u + 1] + slot - rows, 0.0)
        goal = (jnp.sum(goal, axis=0, keepdims=True) + rows) * 0.125
        addr_ref[0, u : u + 1, :] = jnp.where(is_last, used[:, u : u + 1], goal).astype(jnp.int32)

    wide = item_ref.shape[2]
    number = lax.broadcasted_iota(jnp.int32, (1, wide), 1).astype(F32)
    inside = (number >= first) & (number < first + blocks)
    done = (number - first) * RD
    pick = lambda value: jnp.sum(jnp.where(inside, value, 0.0), axis=0, keepdims=True)
    every = lambda value: jnp.sum(
        jnp.broadcast_to(value, (owners, wide)), axis=0, keepdims=True
    )
    lines = (
        pick(jnp.broadcast_to(owner.astype(F32), (owners, wide))),
        pick((start + done) * 0.125),
        pick(total - done),
        every(blocks),
        every(total * 0.125),
    )
    for i, value in enumerate(lines):
        item_ref[0, i : i + 1, :] = value.astype(jnp.int32)


def meta_kernel(here_ref, index_ref, frac_ref, pos_ref, meta_ref, *, per, slabs):
    step = pl.program_id(0)
    _, units, half = pos_ref.shape
    parts = index_ref.shape[1] // half
    gb = units // parts
    blocks = meta_ref.shape[2]
    low = lambda value: value.astype(F32).astype(BF16)
    eighth = low(lax.broadcasted_iota(jnp.int32, (blocks, half), 0))
    lane_of = low(lax.broadcasted_iota(jnp.int32, (OB, half), 0) % 8)
    one, none = jnp.bfloat16(1.0), jnp.bfloat16(0.0)
    for u in range(units):
        g, h = u // parts, u % parts
        line = pl.ds(own_row(here_ref, step * gb + g, per, slabs), 1)
        span = slice(h * half, (h + 1) * half)
        pos = pos_ref[0, u : u + 1, :]
        here = lane_of == low(pos & 7)
        spots = jnp.where(eighth == low(lax.shift_right_logical(pos, 3)), one, none)
        terms = [
            jnp.where(here, low(index_ref[line, span]), none),
            jnp.where(here, low(frac_ref[line, span]), none),
        ]
        meta_ref[0, u] = lax.dot_general(
            jnp.concatenate([spots, spots], axis=1),
            jnp.concatenate(terms, axis=1),
            (((1,), (1,)), ((), ())),
            preferred_element_type=F32,
        )


def up_to(value, step):
    return -(-value // step) * step


def sort_sizes(orients, owners):
    slots = orients + 7 * owners
    sure = orients + 144
    blocks = up_to((sure + up_to(max(0, slots - sure), 128)) // 8, 8)
    return slots, sure, blocks


def planned(shape):
    return pl.BlockSpec((1,) + shape[1:], lambda i, here: (i,) + (0,) * (len(shape) - 1))


def plan_call(here, destination, groups, gb, mesh_sizes):
    orients = destination.shape[1]
    half = min(256, orients)
    owners = mesh_sizes[0] * mesh_sizes[1]
    steps, units = groups // 2 // gb, gb * (orients // half)
    slots, _, blocks = sort_sizes(half, owners)
    shapes = [
        (steps, units, half),
        (steps, units, up_to(blocks + 1, 128)),
        (steps, 5, up_to(owners + units * slots // RD + 8, 128)),
    ]
    return pl.pallas_call(
        functools.partial(plan_kernel, sizes=mesh_sizes, per=group_block(groups) // 2),
        grid_spec=pltpu.PrefetchScalarGridSpec(
            num_scalar_prefetch=1,
            grid=(steps,),
            in_specs=[
                pl.BlockSpec(
                    (groups, orients), lambda i, here: (lax.rem(here[0], mesh_sizes[1]), 0)
                )
            ],
            out_specs=[planned(shape) for shape in shapes],
            scratch_shapes=[
                pltpu.VMEM((groups, orients), jnp.int32),
                pltpu.VMEM((units * owners, half), BF16),
                pltpu.VMEM((units * owners, half), F32),
            ],
        ),
        out_shape=[jax.ShapeDtypeStruct(shape, jnp.int32) for shape in shapes],
        compiler_params=pltpu.CompilerParams(vmem_limit_bytes=55 * MB),
        cost_estimate=pl.CostEstimate(
            flops=8 * steps * units * owners * half * half,
            bytes_accessed=8 * groups * orients,
            transcendentals=0,
        ),
    )(here, destination)


def meta_call(here, row_index, fraction, pos, owners, slabs):
    steps, units, half = pos.shape
    orients = row_index.shape[1]
    groups = 2 * steps * units * half // orients
    blocks = sort_sizes(half, owners)[2]
    shape = (steps, units, blocks, OB)
    table = pl.BlockSpec((groups, orients), lambda i, here: (lax.rem(here[0], slabs), 0))
    return pl.pallas_call(
        functools.partial(meta_kernel, per=group_block(groups) // 2, slabs=slabs),
        grid_spec=pltpu.PrefetchScalarGridSpec(
            num_scalar_prefetch=1,
            grid=(steps,),
            in_specs=[table, table, planned(pos.shape)],
            out_specs=planned(shape),
        ),
        out_shape=jax.ShapeDtypeStruct(shape, F32),
        compiler_params=pltpu.CompilerParams(vmem_limit_bytes=16 * MB),
        cost_estimate=pl.CostEstimate(
            flops=8 * steps * units * blocks * half * OB,
            bytes_accessed=8 * steps * units * blocks * OB,
            transcendentals=0,
        ),
    )(here, row_index, fraction, pos)


def insert_kernel(
    addr_ref, item_ref, x_ref, y_ref, pos_ref, meta_ref, blk_ref, more_blk_ref, *rest
):
    post_ref, more_ref, send_ref, keep_ref = rest[:-8]
    post_t, slice_a, slice_b, buf_s, buf_m, volume, stage, sem = rest[-8:]
    step = pl.program_id(0)
    count = x_ref.shape[0]
    orients = post_t.shape[0]
    units, half = pos_ref.shape[1:]
    parts = orients // half
    gb = units // parts
    width = x_ref.shape[1] // gb
    share = post_ref.shape[1]
    lanes = addr_ref.shape[2]

    @pl.when(step == 0)
    def _():
        volume[...] = jnp.zeros_like(volume)
        for who, (lists, pieces) in enumerate(((blk_ref, post_ref), (more_blk_ref, more_ref))):
            for k in range(pieces.shape[0]):
                lanes = slice(k * share, (k + 1) * share)
                turned = pieces[k].astype(F32).T
                for b in range(orients // OB):
                    value = jnp.where(
                        lists[0:1, lanes] == b,
                        turned[:OB],
                        jnp.where(lists[1:2, lanes] == b, turned[OB:], 0.0),
                    )
                    at = slice(who * count + k * share, who * count + (k + 1) * share)
                    post_t[b * OB : (b + 1) * OB, at] = value.astype(BF16)

    tail = pl.ds(pl.multiple_of(item_ref[0, 4, 0] * 8, 8), RD)
    buf_s[tail, :] = jnp.zeros((RD, width), F32)
    one, none = jnp.bfloat16(1.0), jnp.bfloat16(0.0)
    slots, sure, _ = sort_sizes(half, volume.shape[0] // RD)
    per = slice_a.shape[1] // width
    number = gb // per

    def slices(q, dst_ref):
        at = pl.ds(pl.multiple_of(q * (per * width), per * width), per * width)
        images = jnp.concatenate([x_ref[:, at], y_ref[:, at]], axis=0)
        value = jnp.dot(post_t[...], images, preferred_element_type=F32)
        dst_ref[...] = value.astype(BF16)

    def emit(u, piece, base, size):
        pos = pos_ref[0, pl.ds(u, 1), :]
        order = []
        for at in range(0, size, 128):
            high = min(128, size - at)
            slot = lax.broadcasted_iota(jnp.int32, (high, half), 0).astype(F32).astype(BF16)
            near = jnp.clip(pos - (base + at), -1, 128).astype(F32).astype(BF16)
            order.append(jnp.where(slot == near, one, none))
        order = jnp.concatenate(order, axis=0)
        rows = jnp.dot(order, piece, preferred_element_type=F32)
        for i in range(size // 8):
            at = addr_ref[0, u, base // 8 + i]
            buf_s[pl.ds(pl.multiple_of(at * 8, 8), 8), :] = rows[8 * i : 8 * i + 8]
            buf_m[pl.ds(at, 1), :] = meta_ref[0, u, pl.ds(base // 8 + i, 1), :]

    def sort(q, src_ref):
        for g in range(per):
            for h in range(parts):
                piece = src_ref[h * half : (h + 1) * half, g * width : (g + 1) * width]
                emit((q * per + g) * parts + h, piece, 0, sure)

    def rest_of(q, src_ref):
        for g in range(per):
            for h in range(parts):
                u = (q * per + g) * parts + h

                def more(e, c, u=u, g=g, h=h):
                    piece = src_ref[h * half : (h + 1) * half, g * width : (g + 1) * width]
                    emit(u, piece, sure + e * 128, 128)
                    return c

                used = addr_ref[0, u, lanes - 1]
                lax.fori_loop(0, lax.div(jnp.maximum(used - sure, 0) + 127, 128), more, 0)

    def most_used(q):
        most = addr_ref[0, q * per * parts, lanes - 1]
        for u in range(1, per * parts):
            most = jnp.maximum(most, addr_ref[0, q * per * parts + u, lanes - 1])
        return most

    def two(j, carry):
        q = j * 2
        sort(q, slice_a)
        slices(q + 1, slice_b)

        @pl.when(most_used(q) > sure)
        def _():
            rest_of(q, slice_a)

        sort(q + 1, slice_b)
        slices(jnp.minimum(q + 2, number - 1), slice_a)

        @pl.when(most_used(q + 1) > sure)
        def _():
            rest_of(q + 1, slice_b)

        return carry

    slices(0, slice_a)
    lax.fori_loop(0, number // 2, two, 0)
    if number % 2:
        sort(number - 1, slice_a)
        rest_of(number - 1, slice_a)

    bins = lax.broadcasted_iota(jnp.int32, (RD, RD), 0).astype(F32).astype(BF16)
    side = RD // 2
    at_lane = lax.broadcasted_iota(jnp.int32, (side // 8, side), 1) // 8
    own_lane = at_lane == lax.broadcasted_iota(jnp.int32, (side // 8, side), 0)
    line = lax.broadcasted_iota(jnp.int32, (1, RD), 1)
    together = 8

    def some_items(q, carry):
        for u in range(together):
            j = q * together + u
            owner, at, left = item_ref[0, 0, j], item_ref[0, 1, j], item_ref[0, 2, j]
            places = [
                jnp.sum(
                    jnp.where(own_lane, buf_m[pl.ds(at + h * (side // 8), side // 8), :], 0.0),
                    axis=0,
                    keepdims=True,
                )
                for h in range(2)
            ]
            place = jnp.where(line < left, jnp.concatenate(places, axis=1), -9.0)
            whole = jnp.floor(place)
            apart = (bins - whole.astype(BF16)) - (place - whole).astype(BF16)
            weights = jnp.maximum(one - jnp.abs(apart), none)
            values = buf_s[pl.ds(pl.multiple_of(at * 8, 8), RD), :].astype(BF16)
            goal = pl.ds(pl.multiple_of(owner * RD, RD), RD)
            volume[goal, :] += jnp.dot(weights, values, preferred_element_type=F32)
        return carry

    count_items = lax.div(item_ref[0, 3, 0] + together - 1, together)
    lax.fori_loop(0, count_items, some_items, 0)

    @pl.when(step == pl.num_programs(0) - 1)
    def _():
        side_rows = keep_ref.shape[1]
        slots_out, _, tile, _ = stage.shape
        copies = []
        for base, out_ref in ((side_rows, send_ref), (0, keep_ref)):
            for at in range(0, side_rows, tile):
                slot = len(copies) % slots_out
                if len(copies) >= slots_out:
                    copies[len(copies) - slots_out].wait()
                value = volume[base + at : base + at + tile, :].astype(BF16)
                for c in range(2):
                    stage[slot, c] = value[:, c * OB : (c + 1) * OB]
                copy = pltpu.make_async_copy(
                    stage.at[slot], out_ref.at[:, pl.ds(at, tile)], sem.at[slot]
                )
                copy.start()
                copies.append(copy)
        for copy in copies[-slots_out:]:
            copy.wait()


def group_pair(gb):
    return 2 if gb % 2 == 0 else 1


def insert_block(groups, orients, owners, count, width):
    half = min(256, orients)
    slots, _, blocks = sort_sizes(half, owners)
    room = max(32 * MB - owners * RD * width * 4, 18 * MB)
    best = 1
    for gb in range(1, groups + 1):
        units = gb * (orients // half)
        rows = units * slots + RD + 8
        need = rows * (width * 4 + OB // 2) + 8 * count * gb * width + units * blocks * OB * 8
        if groups % gb == 0 and need <= room:
            best = gb
    return best


def insert_call(addr, items, flats, pos, meta, blocks, posts, orients, owners):
    count, length = flats[0].shape
    steps, units, half = pos.shape
    gb = units * half // orients
    width = length // (steps * gb)
    total = owners * RD
    rows = units * sort_sizes(half, owners)[0] + RD + 8
    limit = total * width * 4 // MB + 30
    block = lambda shape, **kw: pl.BlockSpec(
        (1,) + shape[1:], lambda i: (i,) + (0,) * (len(shape) - 1), **kw
    )
    return pl.pallas_call(
        insert_kernel,
        grid=(steps,),
        out_shape=[jax.ShapeDtypeStruct((2, total // 2, OB), BF16)] * 2,
        in_specs=[
            block(addr.shape, memory_space=pltpu.SMEM),
            block(items.shape, memory_space=pltpu.SMEM),
            pl.BlockSpec((count, gb * width), lambda i: (0, i)),
            pl.BlockSpec((count, gb * width), lambda i: (0, i)),
            block(pos.shape),
            block(meta.shape),
            pl.BlockSpec((2, count), lambda i: (0, 0)),
            pl.BlockSpec((2, count), lambda i: (0, 0)),
        ]
        + [pl.BlockSpec(posts[0].shape, lambda i: (0, 0, 0))] * 2,
        out_specs=[pl.BlockSpec(memory_space=pl.ANY)] * 2,
        scratch_shapes=[
            pltpu.VMEM((orients, 2 * count), BF16),
            pltpu.VMEM((orients, group_pair(gb) * width), BF16),
            pltpu.VMEM((orients, group_pair(gb) * width), BF16),
            pltpu.VMEM((rows, width), F32),
            pltpu.VMEM((rows // 8, OB), F32),
            pltpu.VMEM((total, width), F32),
            pltpu.VMEM((OUT_SLOTS, 2, OUT_TILE, OB), BF16),
            pltpu.SemaphoreType.DMA((OUT_SLOTS,)),
        ],
        compiler_params=pltpu.CompilerParams(vmem_limit_bytes=limit * MB),
        cost_estimate=pl.CostEstimate(
            flops=8 * count * orients * length,
            bytes_accessed=2 * count * length,
            transcendentals=0,
        ),
    )(addr, items, *flats, pos, meta, *blocks, *posts)


def flip(value, axis, bit):
    size = lax.axis_size(axis)
    return lax.ppermute(value, axis, [(i, i ^ bit) for i in range(size)])


def shards(particles, blocks, references, inv_noise, destination, row_index, fraction):
    groups, width = particles.shape[1:]
    orients = references.shape[0]
    dom_size = lax.axis_size("dom")
    slab_size = lax.axis_size("slab")
    devices = dom_size * slab_size
    dom_pos = lax.axis_index("dom")
    slab_pos = lax.axis_index("slab")
    here = lax.axis_index(("dom", "slab")).astype(jnp.int32).reshape(1)
    dom_bits = [1 << i for i in range((dom_size - 1).bit_length())]
    slab_bits = [1 << i for i in range((slab_size - 1).bit_length())]

    blocks = blocks.T
    kept, sent, *scores = score_call(here, inv_noise, particles, references, blocks, slab_size)
    gb = insert_block(groups // 2, orients, devices, particles.shape[0], width)
    here, own = lax.optimization_barrier((here, scores[0]))
    plan = plan_call(here, destination, groups, gb, (dom_size, slab_size))
    own, *plan = lax.optimization_barrier((own, *plan))
    pos, addr, items = plan
    parts = [own] + [flip(scores[k], "slab", k) for k in range(1, slab_size)]
    flats = [kept, flip(sent, "dom", dom_bits[0])]
    post = softmax_call(parts)
    more_blocks = flip(blocks, "dom", dom_bits[0])
    post, more_blocks, later = lax.optimization_barrier((post, more_blocks, here))
    meta = meta_call(later, row_index, fraction, pos, devices, slab_size)
    posts = [post] + [flip(post, "slab", k) for k in range(1, slab_size)]
    ordered = []
    for k in range(slab_size):
        value = posts[0]
        for j in range(1, slab_size):
            value = jnp.where(slab_pos ^ j == k, posts[j], value)
        ordered.append(value)
    pile, meta = lax.optimization_barrier((jnp.stack(ordered), meta))
    posts = [pile, flip(pile, "dom", dom_bits[0])]
    lists = [blocks, more_blocks]
    send, keep = insert_call(addr, items, flats, pos, meta, lists, posts, orients, devices)

    def added(terms):
        return functools.reduce(jnp.add, [term.astype(F32) for term in terms])

    def halve(terms, axis_name, axis, bit):
        size = terms[0].shape[axis] // 2
        pick = lambda term, at: lax.slice_in_dim(term, at, at + size, axis=axis)
        sent = added([pick(term, size) for term in terms]).astype(BF16)
        return [pick(term, 0) for term in terms] + [flip(sent, axis_name, bit)]

    terms = [keep, flip(send, "dom", dom_bits[0])]
    rest = dom_bits[1:]
    columns = []
    for part in range(2):
        columns.append(
            [term[part].reshape((2,) * len(rest) + (slab_size * RD, OB)) for term in terms]
        )
    for stage in range(len(rest)):
        for part in range(2):
            axis = stage if part == 0 else len(rest) - 1 - stage
            columns[part] = halve(columns[part], "dom", axis, rest[axis])
    terms = [jnp.stack([t.reshape(slab_size * RD, OB) for t in pair]) for pair in zip(*columns)]
    for bit in slab_bits:
        terms = halve(terms, "slab", 1, bit)
    volume = jnp.concatenate([added([term[part] for term in terms]) for part in range(2)], axis=1)

    own = volume.astype(BF16)
    plane = [own] + [flip(own, "dom", 2 * k) for k in range(1, dom_size // 2)]
    chip = dom_pos // 2
    placed = []
    for k in range(dom_size // 2):
        value = plane[0]
        for j in range(1, dom_size // 2):
            value = jnp.where(chip ^ j == k, plane[j], value)
        placed.append(value)
    value = jnp.stack(placed)
    got = flip(value, "dom", dom_bits[0])
    value = jnp.where(
        dom_pos & dom_bits[0] == 0,
        jnp.stack([value, got], 1),
        jnp.stack([got, value], 1),
    )
    return volume, value.reshape(dom_size * RD, width)


def solution(mesh):
    return jax.shard_map(
        shards,
        mesh=mesh,
        in_specs=(
            P("dom", "slab", None),
            P("dom", None),
            P(None, "slab", None),
            P("slab"),
            P(),
            P(),
            P(),
        ),
        out_specs=(P(("dom", "slab"), None), P(None, "slab")),
        check_vma=False,
    )
```

```python
import functools

import jax
import jax.numpy as jnp
from jax import lax
from jax.experimental import pallas as pl
from jax.experimental.pallas import tpu as pltpu
from jax.sharding import PartitionSpec as P

OB = 128
RD = 256
MB = 2**20
OUT_SLOTS = 4
STREAMS = 4
OUT_TILE = 1024
F32 = jnp.float32
BF16 = jnp.bfloat16


def group_block(groups):
    return 16 if groups % 16 == 0 else 8


def spread_columns(blk_ref, cols_ref):
    count = blk_ref.shape[1]
    for j in range(2):
        for at in range(0, count, OB):
            line = blk_ref[j : j + 1, at : at + OB].astype(F32)
            cols_ref[j, at : at + OB, :] = jnp.broadcast_to(line, (OB, OB)).T


def score_kernel(here_ref, noise_ref, blk_ref, *rest):
    x_refs, r_refs = rest[:STREAMS], rest[STREAMS : 2 * STREAMS]
    keep_ref, send_ref = rest[2 * STREAMS : 2 * STREAMS + 2]
    out_refs = rest[2 * STREAMS + 2 : -8]
    flat_a, flat_b, w_a, w_b, acc_ref, perm_ref, cols_ref, sem = rest[-8:]
    step = pl.program_id(0)
    steps = pl.num_programs(0) - 1
    gb, width = x_refs[0].shape[1:]
    particles, orients = acc_ref.shape
    side = 16 * gb
    per = gb // 2
    slabs = len(out_refs)
    core = lax.div(here_ref[0], slabs) & 1
    rounds = 4

    def copies(flat_ref, slot, at_step, swap):
        lanes = pl.ds(pl.multiple_of(at_step * (per * width), per * width), per * width)
        goals = (send_ref, keep_ref) if swap else (keep_ref, send_ref)
        return [
            pltpu.make_async_copy(flat_ref.at[h], goals[h].at[:, lanes], sem.at[slot, h])
            for h in range(2)
        ]

    def send_out(flat_ref, slot):
        for which in range(2):

            @pl.when(core == which)
            def _(which=which):
                for copy in copies(flat_ref, slot, step, which == 1):
                    copy.start()

    def wait_out(flat_ref, slot):
        for copy in copies(flat_ref, slot, 0, False):
            copy.wait()

    def regroup(jobs):
        wide = [ref[pl.ds(first * 16, 16)].reshape(side, width) for ref, first, *_ in jobs]
        moved = jnp.dot(perm_ref[...], jnp.concatenate(wide, axis=1), preferred_element_type=F32)
        for g in range(gb):
            lanes = slice(g % per * width, (g % per + 1) * width)
            for t, (_, first, base, goal_ref) in enumerate(jobs):
                part = moved[g * 16 : (g + 1) * 16, t * width : (t + 1) * width]
                part = part * noise_ref[step * gb + g]
                at = pl.ds(pl.multiple_of(base + first * 16, 16), 16)
                goal_ref[g // per, at, lanes] = part.astype(BF16)

    def turn(src_ref, first, base, goal_ref):
        turned = jnp.swapaxes(src_ref[pl.ds(first * 16, 16)], 0, 1)
        at = pl.ds(pl.multiple_of(base + first * 16, 16), 16)
        for g in range(gb):
            goal_ref[g // per, at, g % per * width : (g % per + 1) * width] = turned[g]

    def tiles(i, flat_ref, w_ref):
        jobs, turns = [], []
        for s in range(STREAMS):
            rows = orients // STREAMS
            for t in range(rows // 16 // rounds):
                jobs.append((r_refs[s], i * (rows // 16 // rounds) + t, s * rows, w_ref))
            rows = particles // STREAMS
            for t in range(rows // 16 // rounds):
                turns.append((x_refs[s], i * (rows // 16 // rounds) + t, s * rows, flat_ref))
        for at in range(0, len(jobs), 4):
            regroup(jobs[at : at + 4])
        for job in turns:
            turn(*job)

    def product(left, right):
        acc_ref[...] += lax.dot_general(
            left, right, (((1,), (1,)), ((), ())), preferred_element_type=F32
        )

    def both(i, flat_ref, w_ref, last_flat, last_w):
        span = 2 * per * width // rounds
        at = pl.ds(pl.multiple_of(lax.rem(i, rounds // 2) * span, span), span)
        h = lax.div(i, rounds // 2)
        product(last_flat[h, :, at], last_w[h, :, at])
        tiles(i, flat_ref, w_ref)

    def loop(body, *refs):
        lax.fori_loop(0, rounds, lambda i, c: (body(i, *refs), c)[1], 0)

    @pl.when(step == 0)
    def _():
        row = lax.broadcasted_iota(jnp.int32, (side, side), 0)
        col = lax.broadcasted_iota(jnp.int32, (side, side), 1)
        same = ((row // 16) == (col % gb)) & ((row % 16) == (col // gb))
        perm_ref[...] = jnp.where(same, 1.0, 0.0).astype(BF16)
        acc_ref[...] = jnp.zeros_like(acc_ref)
        spread_columns(blk_ref, cols_ref)
        loop(tiles, flat_a, w_a)
        send_out(flat_a, 0)

    inner = (step > 0) & (step < steps)

    @pl.when(inner & (lax.rem(step, 2) == 1))
    def _():
        @pl.when(step > 1)
        def _():
            wait_out(flat_b, 1)

        loop(both, flat_b, w_b, flat_a, w_a)
        send_out(flat_b, 1)

    @pl.when(inner & (lax.rem(step, 2) == 0))
    def _():
        wait_out(flat_a, 0)
        loop(both, flat_a, w_a, flat_b, w_b)
        send_out(flat_a, 0)

    def finish(last_flat, last_w):
        for h in range(2):
            product(last_flat[h], last_w[h])
        me = lax.rem(here_ref[0], slabs)
        share = particles // len(out_refs)
        for k, out_ref in enumerate(out_refs):
            at = pl.multiple_of((me ^ k) * share, share)
            for j in range(2):
                wanted = cols_ref[j, pl.ds(at, share), :]
                chosen = jnp.zeros((share, OB), F32)
                for b in range(orients // OB):
                    value = acc_ref[pl.ds(at, share), b * OB : (b + 1) * OB]
                    chosen = jnp.where(wanted == b, value, chosen)
                out_ref[:, j * OB : (j + 1) * OB] = chosen
        wait_out(flat_a, 0)

        @pl.when(steps > 1)
        def _():
            wait_out(flat_b, 1)

    @pl.when((step == steps) & (lax.rem(step, 2) == 1))
    def _():
        finish(flat_a, w_a)

    @pl.when((step == steps) & (lax.rem(step, 2) == 0))
    def _():
        finish(flat_b, w_b)


def score_call(here, inv_noise, particles, references, blocks, slab_size):
    count, groups, width = particles.shape
    orients = references.shape[0]
    gb = group_block(groups)
    side = 16 * gb
    share = count // slab_size
    smem = pl.BlockSpec(memory_space=pltpu.SMEM)
    steps = groups // gb
    return pl.pallas_call(
        score_kernel,
        grid=(steps + 1,),
        out_shape=[jax.ShapeDtypeStruct((count, groups // 2 * width), BF16)] * 2
        + [jax.ShapeDtypeStruct((share, 2 * OB), F32)] * slab_size,
        in_specs=[
            smem,
            smem,
            pl.BlockSpec((2, count), lambda i: (0, 0)),
        ]
        + [
            pl.BlockSpec(
                (rows // STREAMS, gb, width), lambda i, s=s: (s, jnp.minimum(i, steps - 1), 0)
            )
            for rows in (count, orients)
            for s in range(STREAMS)
        ],
        out_specs=[pl.BlockSpec(memory_space=pl.ANY)] * 2
        + [pl.BlockSpec((share, 2 * OB), lambda i: (0, 0))] * slab_size,
        scratch_shapes=[
            pltpu.VMEM((2, count, gb // 2 * width), BF16),
            pltpu.VMEM((2, count, gb // 2 * width), BF16),
            pltpu.VMEM((2, orients, gb // 2 * width), BF16),
            pltpu.VMEM((2, orients, gb // 2 * width), BF16),
            pltpu.VMEM((count, orients), F32),
            pltpu.VMEM((side, side), BF16),
            pltpu.VMEM((2, count, OB), F32),
            pltpu.SemaphoreType.DMA((2, 2)),
        ],
        compiler_params=pltpu.CompilerParams(vmem_limit_bytes=56 * MB),
        cost_estimate=pl.CostEstimate(
            flops=4 * count * orients * groups * width,
            bytes_accessed=6 * count * groups * width,
            transcendentals=0,
        ),
    )(here, inv_noise, blocks, *[particles] * STREAMS, *[references] * STREAMS)


def softmax_kernel(*refs):
    *parts, out_ref = refs
    total = parts[0][...]
    for part in parts[1:]:
        total = total + part[...]
    highest = jnp.max(total, axis=1, keepdims=True)
    weights = jnp.exp(total - highest)
    out_ref[...] = (weights / jnp.sum(weights, axis=1, keepdims=True)).astype(BF16)


def softmax_call(parts):
    return pl.pallas_call(
        softmax_kernel,
        out_shape=jax.ShapeDtypeStruct(parts[0].shape, BF16),
        compiler_params=pltpu.CompilerParams(vmem_limit_bytes=8 * MB),
    )(*parts)


def own_row(here_ref, local, per, slabs):
    core = lax.div(here_ref[0], slabs) & 1
    return lax.div(local, per) * (2 * per) + core * per + lax.rem(local, per)


def plan_kernel(
    here_ref, dest_ref, pos_ref, addr_ref, item_ref, place_ref, hot_ref, count_ref, *, sizes, per
):
    step = pl.program_id(0)
    dom_size, slab_size = sizes
    owners = dom_size * slab_size
    _, units, half = pos_ref.shape
    lanes = addr_ref.shape[2]
    parts = dest_ref.shape[1] // half
    gb = units // parts
    dom_log, slab_log = (dom_size - 1).bit_length(), (slab_size - 1).bit_length()

    @pl.when(step == 0)
    def _():
        off = dest_ref[...] ^ here_ref[0]
        place = jnp.zeros_like(off)
        for bit in list(range(slab_log, slab_log + dom_log)) + list(range(slab_log)):
            place = place * 2 + (lax.shift_right_logical(off, bit) & 1)
        place_ref[...] = place

    owner = lax.broadcasted_iota(jnp.int32, (owners, 1), 0)
    for u in range(units):
        g, h = u // parts, u % parts
        at = pl.ds(own_row(here_ref, step * gb + g, per, slab_size), 1)
        line = place_ref[at, h * half : (h + 1) * half]
        hot = jnp.where(line == owner, 1.0, 0.0)
        hot_ref[u * owners : (u + 1) * owners, :] = hot.astype(BF16)
    before = lax.broadcasted_iota(jnp.int32, (half, half), 0)
    after = lax.broadcasted_iota(jnp.int32, (half, half), 1)
    upto = jnp.where(before <= after, 1.0, 0.0).astype(BF16)
    count_ref[...] = jnp.dot(hot_ref[...], upto, preferred_element_type=F32)

    exact = functools.partial(
        jnp.dot, preferred_element_type=F32, precision=lax.Precision.HIGHEST
    )
    row = lax.broadcasted_iota(jnp.int32, (owners, owners), 0)
    col = lax.broadcasted_iota(jnp.int32, (owners, owners), 1)
    below = jnp.where(row > col, 1.0, 0.0)
    row = lax.broadcasted_iota(jnp.int32, (OB, OB), 0)
    col = lax.broadcasted_iota(jnp.int32, (OB, OB), 1)
    earlier = jnp.where(row < col, 1.0, 0.0)
    lane = lax.broadcasted_iota(jnp.int32, (owners, OB), 1)
    runs = jnp.zeros((owners, OB), F32)
    for u in range(units):
        size = count_ref[u * owners : (u + 1) * owners, half - 1 : half]
        runs = jnp.where(lane == u, size, runs)
    runs = jnp.floor((runs + 7.0) * 0.125) * 8.0
    base = exact(below, runs)
    ahead = exact(runs, earlier)
    total = jnp.sum(runs, axis=1, keepdims=True)
    start = exact(below, jnp.broadcast_to(total, (owners, OB)))[:, :1]
    blocks = jnp.floor((total + (RD - 1.0)) * (1.0 / RD))
    first = exact(below, jnp.broadcast_to(blocks, (owners, OB)))[:, :1]
    shift = start + ahead - base
    used = jnp.sum(runs, axis=0, keepdims=True)

    slot = (lax.broadcasted_iota(jnp.int32, (1, lanes), 1) * 8).astype(F32)
    is_last = lax.broadcasted_iota(jnp.int32, (1, lanes), 1) == lanes - 1
    rows = units * (half + 7 * owners)
    for u in range(units):
        low, size = base[:, u : u + 1], runs[:, u : u + 1]
        hot = hot_ref[u * owners : (u + 1) * owners, :].astype(F32)
        rank = count_ref[u * owners : (u + 1) * owners, :] + (low - 1.0)
        pos_ref[0, u : u + 1, :] = jnp.sum(hot * rank, axis=0, keepdims=True).astype(jnp.int32)
        inside = (slot >= low) & (slot < low + size)
        goal = jnp.where(inside, shift[:, u : u + 1] + slot - rows, 0.0)
        goal = (jnp.sum(goal, axis=0, keepdims=True) + rows) * 0.125
        addr_ref[0, u : u + 1, :] = jnp.where(is_last, used[:, u : u + 1], goal).astype(jnp.int32)

    wide = item_ref.shape[2]
    number = lax.broadcasted_iota(jnp.int32, (1, wide), 1).astype(F32)
    inside = (number >= first) & (number < first + blocks)
    done = (number - first) * RD
    pick = lambda value: jnp.sum(jnp.where(inside, value, 0.0), axis=0, keepdims=True)
    every = lambda value: jnp.sum(
        jnp.broadcast_to(value, (owners, wide)), axis=0, keepdims=True
    )
    lines = (
        pick(jnp.broadcast_to(owner.astype(F32), (owners, wide))),
        pick((start + done) * 0.125),
        pick(total - done),
        every(blocks),
        every(total * 0.125),
    )
    for i, value in enumerate(lines):
        item_ref[0, i : i + 1, :] = value.astype(jnp.int32)


def meta_kernel(here_ref, index_ref, frac_ref, pos_ref, meta_ref, *, per, slabs):
    step = pl.program_id(0)
    _, units, half = pos_ref.shape
    parts = index_ref.shape[1] // half
    gb = units // parts
    blocks = meta_ref.shape[2]
    low = lambda value: value.astype(F32).astype(BF16)
    eighth = low(lax.broadcasted_iota(jnp.int32, (blocks, half), 0))
    lane_of = low(lax.broadcasted_iota(jnp.int32, (OB, half), 0) % 8)
    one, none = jnp.bfloat16(1.0), jnp.bfloat16(0.0)
    for u in range(units):
        g, h = u // parts, u % parts
        line = pl.ds(own_row(here_ref, step * gb + g, per, slabs), 1)
        span = slice(h * half, (h + 1) * half)
        pos = pos_ref[0, u : u + 1, :]
        here = lane_of == low(pos & 7)
        spots = jnp.where(eighth == low(lax.shift_right_logical(pos, 3)), one, none)
        terms = [
            jnp.where(here, low(index_ref[line, span]), none),
            jnp.where(here, low(frac_ref[line, span]), none),
        ]
        meta_ref[0, u] = lax.dot_general(
            jnp.concatenate([spots, spots], axis=1),
            jnp.concatenate(terms, axis=1),
            (((1,), (1,)), ((), ())),
            preferred_element_type=F32,
        )


def up_to(value, step):
    return -(-value // step) * step


def sort_sizes(orients, owners):
    slots = orients + 7 * owners
    sure = orients + 144
    blocks = up_to((sure + up_to(max(0, slots - sure), 128)) // 8, 8)
    return slots, sure, blocks


def planned(shape):
    return pl.BlockSpec((1,) + shape[1:], lambda i, here: (i,) + (0,) * (len(shape) - 1))


def plan_call(here, destination, groups, gb, mesh_sizes):
    orients = destination.shape[1]
    half = min(256, orients)
    owners = mesh_sizes[0] * mesh_sizes[1]
    steps, units = groups // 2 // gb, gb * (orients // half)
    slots, _, blocks = sort_sizes(half, owners)
    shapes = [
        (steps, units, half),
        (steps, units, up_to(blocks + 1, 128)),
        (steps, 5, up_to(owners + units * slots // RD + 8, 128)),
    ]
    return pl.pallas_call(
        functools.partial(plan_kernel, sizes=mesh_sizes, per=group_block(groups) // 2),
        grid_spec=pltpu.PrefetchScalarGridSpec(
            num_scalar_prefetch=1,
            grid=(steps,),
            in_specs=[
                pl.BlockSpec(
                    (groups, orients), lambda i, here: (lax.rem(here[0], mesh_sizes[1]), 0)
                )
            ],
            out_specs=[planned(shape) for shape in shapes],
            scratch_shapes=[
                pltpu.VMEM((groups, orients), jnp.int32),
                pltpu.VMEM((units * owners, half), BF16),
                pltpu.VMEM((units * owners, half), F32),
            ],
        ),
        out_shape=[jax.ShapeDtypeStruct(shape, jnp.int32) for shape in shapes],
        compiler_params=pltpu.CompilerParams(vmem_limit_bytes=55 * MB),
        cost_estimate=pl.CostEstimate(
            flops=8 * steps * units * owners * half * half,
            bytes_accessed=8 * groups * orients,
            transcendentals=0,
        ),
    )(here, destination)


def meta_call(here, row_index, fraction, pos, owners, slabs):
    steps, units, half = pos.shape
    orients = row_index.shape[1]
    groups = 2 * steps * units * half // orients
    blocks = sort_sizes(half, owners)[2]
    shape = (steps, units, blocks, OB)
    table = pl.BlockSpec((groups, orients), lambda i, here: (lax.rem(here[0], slabs), 0))
    return pl.pallas_call(
        functools.partial(meta_kernel, per=group_block(groups) // 2, slabs=slabs),
        grid_spec=pltpu.PrefetchScalarGridSpec(
            num_scalar_prefetch=1,
            grid=(steps,),
            in_specs=[table, table, planned(pos.shape)],
            out_specs=planned(shape),
        ),
        out_shape=jax.ShapeDtypeStruct(shape, F32),
        compiler_params=pltpu.CompilerParams(vmem_limit_bytes=16 * MB),
        cost_estimate=pl.CostEstimate(
            flops=8 * steps * units * blocks * half * OB,
            bytes_accessed=8 * steps * units * blocks * OB,
            transcendentals=0,
        ),
    )(here, row_index, fraction, pos)


def insert_kernel(
    addr_ref, item_ref, x_ref, y_ref, pos_ref, meta_ref, blk_ref, more_blk_ref, *rest
):
    post_ref, more_ref, send_ref, keep_ref = rest[:-8]
    post_t, slice_a, slice_b, buf_s, buf_m, volume, stage, sem = rest[-8:]
    step = pl.program_id(0)
    count = x_ref.shape[0]
    orients = post_t.shape[0]
    units, half = pos_ref.shape[1:]
    parts = orients // half
    gb = units // parts
    width = x_ref.shape[1] // gb
    share = post_ref.shape[1]
    lanes = addr_ref.shape[2]

    @pl.when(step == 0)
    def _():
        volume[...] = jnp.zeros_like(volume)
        for who, (lists, pieces) in enumerate(((blk_ref, post_ref), (more_blk_ref, more_ref))):
            for k in range(pieces.shape[0]):
                lanes = slice(k * share, (k + 1) * share)
                turned = pieces[k].astype(F32).T
                for b in range(orients // OB):
                    value = jnp.where(
                        lists[0:1, lanes] == b,
                        turned[:OB],
                        jnp.where(lists[1:2, lanes] == b, turned[OB:], 0.0),
                    )
                    at = slice(who * count + k * share, who * count + (k + 1) * share)
                    post_t[b * OB : (b + 1) * OB, at] = value.astype(BF16)

    tail = pl.ds(pl.multiple_of(item_ref[0, 4, 0] * 8, 8), RD)
    buf_s[tail, :] = jnp.zeros((RD, width), F32)
    one, none = jnp.bfloat16(1.0), jnp.bfloat16(0.0)
    slots, sure, _ = sort_sizes(half, volume.shape[0] // RD)
    per = slice_a.shape[1] // width
    number = gb // per

    def slices(q, dst_ref):
        at = pl.ds(pl.multiple_of(q * (per * width), per * width), per * width)
        images = jnp.concatenate([x_ref[:, at], y_ref[:, at]], axis=0)
        value = jnp.dot(post_t[...], images, preferred_element_type=F32)
        dst_ref[...] = value.astype(BF16)

    def emit(u, piece, base, size):
        pos = pos_ref[0, pl.ds(u, 1), :]
        order = []
        for at in range(0, size, 128):
            high = min(128, size - at)
            slot = lax.broadcasted_iota(jnp.int32, (high, half), 0).astype(F32).astype(BF16)
            near = jnp.clip(pos - (base + at), -1, 128).astype(F32).astype(BF16)
            order.append(jnp.where(slot == near, one, none))
        order = jnp.concatenate(order, axis=0)
        rows = jnp.dot(order, piece, preferred_element_type=F32)
        for i in range(size // 8):
            at = addr_ref[0, u, base // 8 + i]
            buf_s[pl.ds(pl.multiple_of(at * 8, 8), 8), :] = rows[8 * i : 8 * i + 8]
            buf_m[pl.ds(at, 1), :] = meta_ref[0, u, pl.ds(base // 8 + i, 1), :]

    def sort(q, src_ref):
        for g in range(per):
            for h in range(parts):
                piece = src_ref[h * half : (h + 1) * half, g * width : (g + 1) * width]
                emit((q * per + g) * parts + h, piece, 0, sure)

    def rest_of(q, src_ref):
        for g in range(per):
            for h in range(parts):
                u = (q * per + g) * parts + h

                def more(e, c, u=u, g=g, h=h):
                    piece = src_ref[h * half : (h + 1) * half, g * width : (g + 1) * width]
                    emit(u, piece, sure + e * 128, 128)
                    return c

                used = addr_ref[0, u, lanes - 1]
                lax.fori_loop(0, lax.div(jnp.maximum(used - sure, 0) + 127, 128), more, 0)

    def most_used(q):
        most = addr_ref[0, q * per * parts, lanes - 1]
        for u in range(1, per * parts):
            most = jnp.maximum(most, addr_ref[0, q * per * parts + u, lanes - 1])
        return most

    def two(j, carry):
        q = j * 2
        sort(q, slice_a)
        slices(q + 1, slice_b)

        @pl.when(most_used(q) > sure)
        def _():
            rest_of(q, slice_a)

        sort(q + 1, slice_b)
        slices(jnp.minimum(q + 2, number - 1), slice_a)

        @pl.when(most_used(q + 1) > sure)
        def _():
            rest_of(q + 1, slice_b)

        return carry

    slices(0, slice_a)
    lax.fori_loop(0, number // 2, two, 0)
    if number % 2:
        sort(number - 1, slice_a)
        rest_of(number - 1, slice_a)

    bins = lax.broadcasted_iota(jnp.int32, (RD, RD), 0).astype(F32).astype(BF16)
    side = RD // 2
    at_lane = lax.broadcasted_iota(jnp.int32, (side // 8, side), 1) // 8
    own_lane = at_lane == lax.broadcasted_iota(jnp.int32, (side // 8, side), 0)
    line = lax.broadcasted_iota(jnp.int32, (1, RD), 1)
    together = 8

    def some_items(q, carry):
        for u in range(together):
            j = q * together + u
            owner, at, left = item_ref[0, 0, j], item_ref[0, 1, j], item_ref[0, 2, j]
            places = [
                jnp.sum(
                    jnp.where(own_lane, buf_m[pl.ds(at + h * (side // 8), side // 8), :], 0.0),
                    axis=0,
                    keepdims=True,
                )
                for h in range(2)
            ]
            place = jnp.where(line < left, jnp.concatenate(places, axis=1), -9.0)
            whole = jnp.floor(place)
            apart = (bins - whole.astype(BF16)) - (place - whole).astype(BF16)
            weights = jnp.maximum(one - jnp.abs(apart), none)
            values = buf_s[pl.ds(pl.multiple_of(at * 8, 8), RD), :].astype(BF16)
            goal = pl.ds(pl.multiple_of(owner * RD, RD), RD)
            volume[goal, :] += jnp.dot(weights, values, preferred_element_type=F32)
        return carry

    count_items = lax.div(item_ref[0, 3, 0] + together - 1, together)
    lax.fori_loop(0, count_items, some_items, 0)

    @pl.when(step == pl.num_programs(0) - 1)
    def _():
        side_rows = keep_ref.shape[1]
        slots_out, _, tile, _ = stage.shape
        copies = []
        for base, out_ref in ((side_rows, send_ref), (0, keep_ref)):
            for at in range(0, side_rows, tile):
                slot = len(copies) % slots_out
                if len(copies) >= slots_out:
                    copies[len(copies) - slots_out].wait()
                value = volume[base + at : base + at + tile, :].astype(BF16)
                for c in range(2):
                    stage[slot, c] = value[:, c * OB : (c + 1) * OB]
                copy = pltpu.make_async_copy(
                    stage.at[slot], out_ref.at[:, pl.ds(at, tile)], sem.at[slot]
                )
                copy.start()
                copies.append(copy)
        for copy in copies[-slots_out:]:
            copy.wait()


def group_pair(gb):
    return 2 if gb % 2 == 0 else 1


def insert_block(groups, orients, owners, count, width):
    half = min(256, orients)
    slots, _, blocks = sort_sizes(half, owners)
    room = max(32 * MB - owners * RD * width * 4, 18 * MB)
    best = 1
    for gb in range(1, groups + 1):
        units = gb * (orients // half)
        rows = units * slots + RD + 8
        need = rows * (width * 4 + OB // 2) + 8 * count * gb * width + units * blocks * OB * 8
        if groups % gb == 0 and need <= room:
            best = gb
    return best


def insert_call(addr, items, flats, pos, meta, blocks, posts, orients, owners):
    count, length = flats[0].shape
    steps, units, half = pos.shape
    gb = units * half // orients
    width = length // (steps * gb)
    total = owners * RD
    rows = units * sort_sizes(half, owners)[0] + RD + 8
    limit = total * width * 4 // MB + 30
    block = lambda shape, **kw: pl.BlockSpec(
        (1,) + shape[1:], lambda i: (i,) + (0,) * (len(shape) - 1), **kw
    )
    return pl.pallas_call(
        insert_kernel,
        grid=(steps,),
        out_shape=[jax.ShapeDtypeStruct((2, total // 2, OB), BF16)] * 2,
        in_specs=[
            block(addr.shape, memory_space=pltpu.SMEM),
            block(items.shape, memory_space=pltpu.SMEM),
            pl.BlockSpec((count, gb * width), lambda i: (0, i)),
            pl.BlockSpec((count, gb * width), lambda i: (0, i)),
            block(pos.shape),
            block(meta.shape),
            pl.BlockSpec((2, count), lambda i: (0, 0)),
            pl.BlockSpec((2, count), lambda i: (0, 0)),
        ]
        + [pl.BlockSpec(posts[0].shape, lambda i: (0, 0, 0))] * 2,
        out_specs=[pl.BlockSpec(memory_space=pl.ANY)] * 2,
        scratch_shapes=[
            pltpu.VMEM((orients, 2 * count), BF16),
            pltpu.VMEM((orients, group_pair(gb) * width), BF16),
            pltpu.VMEM((orients, group_pair(gb) * width), BF16),
            pltpu.VMEM((rows, width), F32),
            pltpu.VMEM((rows // 8, OB), F32),
            pltpu.VMEM((total, width), F32),
            pltpu.VMEM((OUT_SLOTS, 2, OUT_TILE, OB), BF16),
            pltpu.SemaphoreType.DMA((OUT_SLOTS,)),
        ],
        compiler_params=pltpu.CompilerParams(vmem_limit_bytes=limit * MB),
        cost_estimate=pl.CostEstimate(
            flops=8 * count * orients * length,
            bytes_accessed=2 * count * length,
            transcendentals=0,
        ),
    )(addr, items, *flats, pos, meta, *blocks, *posts)


def flip(value, axis, bit):
    size = lax.axis_size(axis)
    return lax.ppermute(value, axis, [(i, i ^ bit) for i in range(size)])


def shards(particles, blocks, references, inv_noise, destination, row_index, fraction):
    groups, width = particles.shape[1:]
    orients = references.shape[0]
    dom_size = lax.axis_size("dom")
    slab_size = lax.axis_size("slab")
    devices = dom_size * slab_size
    dom_pos = lax.axis_index("dom")
    slab_pos = lax.axis_index("slab")
    here = lax.axis_index(("dom", "slab")).astype(jnp.int32).reshape(1)
    dom_bits = [1 << i for i in range((dom_size - 1).bit_length())]
    slab_bits = [1 << i for i in range((slab_size - 1).bit_length())]

    blocks = blocks.T
    kept, sent, *scores = score_call(here, inv_noise, particles, references, blocks, slab_size)
    gb = insert_block(groups // 2, orients, devices, particles.shape[0], width)
    here, own = lax.optimization_barrier((here, scores[0]))
    plan = plan_call(here, destination, groups, gb, (dom_size, slab_size))
    own, *plan = lax.optimization_barrier((own, *plan))
    pos, addr, items = plan
    parts = [own] + [flip(scores[k], "slab", k) for k in range(1, slab_size)]
    flats = [kept, flip(sent, "dom", dom_bits[0])]
    post = softmax_call(parts)
    more_blocks = flip(blocks, "dom", dom_bits[0])
    post, more_blocks, later = lax.optimization_barrier((post, more_blocks, here))
    meta = meta_call(later, row_index, fraction, pos, devices, slab_size)
    posts = [post] + [flip(post, "slab", k) for k in range(1, slab_size)]
    ordered = []
    for k in range(slab_size):
        value = posts[0]
        for j in range(1, slab_size):
            value = jnp.where(slab_pos ^ j == k, posts[j], value)
        ordered.append(value)
    pile, meta = lax.optimization_barrier((jnp.stack(ordered), meta))
    posts = [pile, flip(pile, "dom", dom_bits[0])]
    lists = [blocks, more_blocks]
    send, keep = insert_call(addr, items, flats, pos, meta, lists, posts, orients, devices)

    def added(terms):
        return functools.reduce(jnp.add, [term.astype(F32) for term in terms])

    def halve(terms, axis_name, axis, bit):
        size = terms[0].shape[axis] // 2
        pick = lambda term, at: lax.slice_in_dim(term, at, at + size, axis=axis)
        sent = added([pick(term, size) for term in terms]).astype(BF16)
        return [pick(term, 0) for term in terms] + [flip(sent, axis_name, bit)]

    terms = [keep, flip(send, "dom", dom_bits[0])]
    rest = dom_bits[1:]
    columns = []
    for part in range(2):
        columns.append(
            [term[part].reshape((2,) * len(rest) + (slab_size * RD, OB)) for term in terms]
        )
    for stage in range(len(rest)):
        for part in range(2):
            axis = stage if part == 0 else len(rest) - 1 - stage
            columns[part] = halve(columns[part], "dom", axis, rest[axis])
    terms = [jnp.stack([t.reshape(slab_size * RD, OB) for t in pair]) for pair in zip(*columns)]
    for bit in slab_bits:
        terms = halve(terms, "slab", 1, bit)
    volume = jnp.concatenate([added([term[part] for term in terms]) for part in range(2)], axis=1)

    own = volume.astype(BF16)
    plane = [own] + [flip(own, "dom", 2 * k) for k in range(1, dom_size // 2)]
    chip = dom_pos // 2
    placed = []
    for k in range(dom_size // 2):
        value = plane[0]
        for j in range(1, dom_size // 2):
            value = jnp.where(chip ^ j == k, plane[j], value)
        placed.append(value)
    value = jnp.stack(placed)
    got = flip(value, "dom", dom_bits[0])
    value = jnp.where(
        dom_pos & dom_bits[0] == 0,
        jnp.stack([value, got], 1),
        jnp.stack([got, value], 1),
    )
    return volume, value.reshape(dom_size * RD, width)


def solution(mesh):
    return jax.shard_map(
        shards,
        mesh=mesh,
        in_specs=(
            P("dom", "slab", None),
            P("dom", None),
            P(None, "slab", None),
            P("slab"),
            P(),
            P(),
            P(),
        ),
        out_specs=(P(("dom", "slab"), None), P(None, "slab")),
        check_vma=False,
    )
```

```python
import functools

import jax
import jax.numpy as jnp
from jax import lax
from jax.experimental import pallas as pl
from jax.experimental.pallas import tpu as pltpu
from jax.sharding import PartitionSpec as P

OB = 128
RD = 256
MB = 2**20
OUT_SLOTS = 4
STREAMS = 4
OUT_TILE = 1024
F32 = jnp.float32
BF16 = jnp.bfloat16


def group_block(groups):
    return 16 if groups % 16 == 0 else 8


def spread_columns(blk_ref, cols_ref):
    count = blk_ref.shape[1]
    for j in range(2):
        for at in range(0, count, OB):
            line = blk_ref[j : j + 1, at : at + OB].astype(F32)
            cols_ref[j, at : at + OB, :] = jnp.broadcast_to(line, (OB, OB)).T


def score_kernel(here_ref, noise_ref, blk_ref, *rest):
    x_refs, r_refs = rest[:STREAMS], rest[STREAMS : 2 * STREAMS]
    keep_ref, send_ref = rest[2 * STREAMS : 2 * STREAMS + 2]
    out_refs = rest[2 * STREAMS + 2 : -8]
    flat_a, flat_b, w_a, w_b, acc_ref, perm_ref, cols_ref, sem = rest[-8:]
    step = pl.program_id(0)
    steps = pl.num_programs(0) - 1
    gb, width = x_refs[0].shape[1:]
    particles, orients = acc_ref.shape
    side = 16 * gb
    per = gb // 2
    slabs = len(out_refs)
    core = lax.div(here_ref[0], slabs) & 1
    rounds = 4

    def copies(flat_ref, slot, at_step, swap):
        lanes = pl.ds(pl.multiple_of(at_step * (per * width), per * width), per * width)
        goals = (send_ref, keep_ref) if swap else (keep_ref, send_ref)
        return [
            pltpu.make_async_copy(flat_ref.at[h], goals[h].at[:, lanes], sem.at[slot, h])
            for h in range(2)
        ]

    def send_out(flat_ref, slot):
        for which in range(2):

            @pl.when(core == which)
            def _(which=which):
                for copy in copies(flat_ref, slot, step, which == 1):
                    copy.start()

    def wait_out(flat_ref, slot):
        for copy in copies(flat_ref, slot, 0, False):
            copy.wait()

    def regroup(jobs):
        wide = [ref[pl.ds(first * 16, 16)].reshape(side, width) for ref, first, *_ in jobs]
        moved = jnp.dot(perm_ref[...], jnp.concatenate(wide, axis=1), preferred_element_type=F32)
        for g in range(gb):
            lanes = slice(g % per * width, (g % per + 1) * width)
            for t, (_, first, base, goal_ref, scaled) in enumerate(jobs):
                part = moved[g * 16 : (g + 1) * 16, t * width : (t + 1) * width]
                if scaled:
                    part = part * noise_ref[step * gb + g]
                at = pl.ds(pl.multiple_of(base + first * 16, 16), 16)
                goal_ref[g // per, at, lanes] = part.astype(BF16)

    def turn(src_ref, first, base, goal_ref):
        turned = jnp.swapaxes(src_ref[pl.ds(first * 16, 16)], 0, 1)
        at = pl.ds(pl.multiple_of(base + first * 16, 16), 16)
        for g in range(gb):
            goal_ref[g // per, at, g % per * width : (g % per + 1) * width] = turned[g]

    def tiles(i, flat_ref, w_ref):
        jobs, turns = [], []
        for s in range(STREAMS):
            rows = orients // STREAMS
            for t in range(rows // 16 // rounds):
                jobs.append((r_refs[s], i * (rows // 16 // rounds) + t, s * rows, w_ref, True))
            rows = particles // STREAMS
            for t in range(rows // 16 // rounds):
                job = (x_refs[s], i * (rows // 16 // rounds) + t, s * rows, flat_ref)
                if (s * (rows // 16 // rounds) + t) % 4:
                    turns.append(job)
                else:
                    jobs.append(job + (False,))
        for at in range(0, len(jobs), 5):
            regroup(jobs[at : at + 5])
        for job in turns:
            turn(*job)

    def product(left, right):
        acc_ref[...] += lax.dot_general(
            left, right, (((1,), (1,)), ((), ())), preferred_element_type=F32
        )

    def both(i, flat_ref, w_ref, last_flat, last_w):
        span = 2 * per * width // rounds
        at = pl.ds(pl.multiple_of(lax.rem(i, rounds // 2) * span, span), span)
        h = lax.div(i, rounds // 2)
        product(last_flat[h, :, at], last_w[h, :, at])
        tiles(i, flat_ref, w_ref)

    def loop(body, *refs):
        lax.fori_loop(0, rounds, lambda i, c: (body(i, *refs), c)[1], 0)

    @pl.when(step == 0)
    def _():
        row = lax.broadcasted_iota(jnp.int32, (side, side), 0)
        col = lax.broadcasted_iota(jnp.int32, (side, side), 1)
        same = ((row // 16) == (col % gb)) & ((row % 16) == (col // gb))
        perm_ref[...] = jnp.where(same, 1.0, 0.0).astype(BF16)
        acc_ref[...] = jnp.zeros_like(acc_ref)
        spread_columns(blk_ref, cols_ref)
        loop(tiles, flat_a, w_a)
        send_out(flat_a, 0)

    inner = (step > 0) & (step < steps)

    @pl.when(inner & (lax.rem(step, 2) == 1))
    def _():
        @pl.when(step > 1)
        def _():
            wait_out(flat_b, 1)

        loop(both, flat_b, w_b, flat_a, w_a)
        send_out(flat_b, 1)

    @pl.when(inner & (lax.rem(step, 2) == 0))
    def _():
        wait_out(flat_a, 0)
        loop(both, flat_a, w_a, flat_b, w_b)
        send_out(flat_a, 0)

    def finish(last_flat, last_w):
        for h in range(2):
            product(last_flat[h], last_w[h])
        me = lax.rem(here_ref[0], slabs)
        share = particles // len(out_refs)
        for k, out_ref in enumerate(out_refs):
            at = pl.multiple_of((me ^ k) * share, share)
            for j in range(2):
                wanted = cols_ref[j, pl.ds(at, share), :]
                chosen = jnp.zeros((share, OB), F32)
                for b in range(orients // OB):
                    value = acc_ref[pl.ds(at, share), b * OB : (b + 1) * OB]
                    chosen = jnp.where(wanted == b, value, chosen)
                out_ref[:, j * OB : (j + 1) * OB] = chosen
        wait_out(flat_a, 0)

        @pl.when(steps > 1)
        def _():
            wait_out(flat_b, 1)

    @pl.when((step == steps) & (lax.rem(step, 2) == 1))
    def _():
        finish(flat_a, w_a)

    @pl.when((step == steps) & (lax.rem(step, 2) == 0))
    def _():
        finish(flat_b, w_b)


def score_call(here, inv_noise, particles, references, blocks, slab_size):
    count, groups, width = particles.shape
    orients = references.shape[0]
    gb = group_block(groups)
    side = 16 * gb
    share = count // slab_size
    smem = pl.BlockSpec(memory_space=pltpu.SMEM)
    steps = groups // gb
    return pl.pallas_call(
        score_kernel,
        grid=(steps + 1,),
        out_shape=[jax.ShapeDtypeStruct((count, groups // 2 * width), BF16)] * 2
        + [jax.ShapeDtypeStruct((share, 2 * OB), F32)] * slab_size,
        in_specs=[
            smem,
            smem,
            pl.BlockSpec((2, count), lambda i: (0, 0)),
        ]
        + [
            pl.BlockSpec(
                (rows // STREAMS, gb, width), lambda i, s=s: (s, jnp.minimum(i, steps - 1), 0)
            )
            for rows in (count, orients)
            for s in range(STREAMS)
        ],
        out_specs=[pl.BlockSpec(memory_space=pl.ANY)] * 2
        + [pl.BlockSpec((share, 2 * OB), lambda i: (0, 0))] * slab_size,
        scratch_shapes=[
            pltpu.VMEM((2, count, gb // 2 * width), BF16),
            pltpu.VMEM((2, count, gb // 2 * width), BF16),
            pltpu.VMEM((2, orients, gb // 2 * width), BF16),
            pltpu.VMEM((2, orients, gb // 2 * width), BF16),
            pltpu.VMEM((count, orients), F32),
            pltpu.VMEM((side, side), BF16),
            pltpu.VMEM((2, count, OB), F32),
            pltpu.SemaphoreType.DMA((2, 2)),
        ],
        compiler_params=pltpu.CompilerParams(vmem_limit_bytes=56 * MB),
        cost_estimate=pl.CostEstimate(
            flops=4 * count * orients * groups * width,
            bytes_accessed=6 * count * groups * width,
            transcendentals=0,
        ),
    )(here, inv_noise, blocks, *[particles] * STREAMS, *[references] * STREAMS)


def softmax_kernel(*refs):
    *parts, out_ref = refs
    total = parts[0][...]
    for part in parts[1:]:
        total = total + part[...]
    highest = jnp.max(total, axis=1, keepdims=True)
    weights = jnp.exp(total - highest)
    out_ref[...] = (weights / jnp.sum(weights, axis=1, keepdims=True)).astype(BF16)


def softmax_call(parts):
    return pl.pallas_call(
        softmax_kernel,
        out_shape=jax.ShapeDtypeStruct(parts[0].shape, BF16),
        compiler_params=pltpu.CompilerParams(vmem_limit_bytes=8 * MB),
    )(*parts)


def own_row(here_ref, local, per, slabs):
    core = lax.div(here_ref[0], slabs) & 1
    return lax.div(local, per) * (2 * per) + core * per + lax.rem(local, per)


def plan_kernel(
    here_ref, dest_ref, pos_ref, addr_ref, item_ref, place_ref, hot_ref, count_ref, *, sizes, per
):
    step = pl.program_id(0)
    dom_size, slab_size = sizes
    owners = dom_size * slab_size
    _, units, half = pos_ref.shape
    lanes = addr_ref.shape[2]
    parts = dest_ref.shape[1] // half
    gb = units // parts
    dom_log, slab_log = (dom_size - 1).bit_length(), (slab_size - 1).bit_length()

    @pl.when(step == 0)
    def _():
        off = dest_ref[...] ^ here_ref[0]
        place = jnp.zeros_like(off)
        for bit in list(range(slab_log, slab_log + dom_log)) + list(range(slab_log)):
            place = place * 2 + (lax.shift_right_logical(off, bit) & 1)
        place_ref[...] = place

    owner = lax.broadcasted_iota(jnp.int32, (owners, 1), 0)
    for u in range(units):
        g, h = u // parts, u % parts
        at = pl.ds(own_row(here_ref, step * gb + g, per, slab_size), 1)
        line = place_ref[at, h * half : (h + 1) * half]
        hot = jnp.where(line == owner, 1.0, 0.0)
        hot_ref[u * owners : (u + 1) * owners, :] = hot.astype(BF16)
    before = lax.broadcasted_iota(jnp.int32, (half, half), 0)
    after = lax.broadcasted_iota(jnp.int32, (half, half), 1)
    upto = jnp.where(before <= after, 1.0, 0.0).astype(BF16)
    count_ref[...] = jnp.dot(hot_ref[...], upto, preferred_element_type=F32)

    exact = functools.partial(
        jnp.dot, preferred_element_type=F32, precision=lax.Precision.HIGHEST
    )
    row = lax.broadcasted_iota(jnp.int32, (owners, owners), 0)
    col = lax.broadcasted_iota(jnp.int32, (owners, owners), 1)
    below = jnp.where(row > col, 1.0, 0.0)
    row = lax.broadcasted_iota(jnp.int32, (OB, OB), 0)
    col = lax.broadcasted_iota(jnp.int32, (OB, OB), 1)
    earlier = jnp.where(row < col, 1.0, 0.0)
    lane = lax.broadcasted_iota(jnp.int32, (owners, OB), 1)
    runs = jnp.zeros((owners, OB), F32)
    for u in range(units):
        size = count_ref[u * owners : (u + 1) * owners, half - 1 : half]
        runs = jnp.where(lane == u, size, runs)
    runs = jnp.floor((runs + 7.0) * 0.125) * 8.0
    base = exact(below, runs)
    ahead = exact(runs, earlier)
    total = jnp.sum(runs, axis=1, keepdims=True)
    start = exact(below, jnp.broadcast_to(total, (owners, OB)))[:, :1]
    blocks = jnp.floor((total + (RD - 1.0)) * (1.0 / RD))
    first = exact(below, jnp.broadcast_to(blocks, (owners, OB)))[:, :1]
    shift = start + ahead - base
    used = jnp.sum(runs, axis=0, keepdims=True)

    slot = (lax.broadcasted_iota(jnp.int32, (1, lanes), 1) * 8).astype(F32)
    is_last = lax.broadcasted_iota(jnp.int32, (1, lanes), 1) == lanes - 1
    rows = units * (half + 7 * owners)
    for u in range(units):
        low, size = base[:, u : u + 1], runs[:, u : u + 1]
        hot = hot_ref[u * owners : (u + 1) * owners, :].astype(F32)
        rank = count_ref[u * owners : (u + 1) * owners, :] + (low - 1.0)
        pos_ref[0, u : u + 1, :] = jnp.sum(hot * rank, axis=0, keepdims=True).astype(jnp.int32)
        inside = (slot >= low) & (slot < low + size)
        goal = jnp.where(inside, shift[:, u : u + 1] + slot - rows, 0.0)
        goal = (jnp.sum(goal, axis=0, keepdims=True) + rows) * 0.125
        addr_ref[0, u : u + 1, :] = jnp.where(is_last, used[:, u : u + 1], goal).astype(jnp.int32)

    wide = item_ref.shape[2]
    number = lax.broadcasted_iota(jnp.int32, (1, wide), 1).astype(F32)
    inside = (number >= first) & (number < first + blocks)
    done = (number - first) * RD
    pick = lambda value: jnp.sum(jnp.where(inside, value, 0.0), axis=0, keepdims=True)
    every = lambda value: jnp.sum(
        jnp.broadcast_to(value, (owners, wide)), axis=0, keepdims=True
    )
    lines = (
        pick(jnp.broadcast_to(owner.astype(F32), (owners, wide))),
        pick((start + done) * 0.125),
        pick(total - done),
        every(blocks),
        every(total * 0.125),
    )
    for i, value in enumerate(lines):
        item_ref[0, i : i + 1, :] = value.astype(jnp.int32)


def meta_kernel(here_ref, index_ref, frac_ref, pos_ref, meta_ref, *, per, slabs):
    step = pl.program_id(0)
    _, units, half = pos_ref.shape
    parts = index_ref.shape[1] // half
    gb = units // parts
    blocks = meta_ref.shape[2]
    low = lambda value: value.astype(F32).astype(BF16)
    eighth = low(lax.broadcasted_iota(jnp.int32, (blocks, half), 0))
    lane_of = low(lax.broadcasted_iota(jnp.int32, (OB, half), 0) % 8)
    one, none = jnp.bfloat16(1.0), jnp.bfloat16(0.0)
    for u in range(units):
        g, h = u // parts, u % parts
        line = pl.ds(own_row(here_ref, step * gb + g, per, slabs), 1)
        span = slice(h * half, (h + 1) * half)
        pos = pos_ref[0, u : u + 1, :]
        here = lane_of == low(pos & 7)
        spots = jnp.where(eighth == low(lax.shift_right_logical(pos, 3)), one, none)
        terms = [
            jnp.where(here, low(index_ref[line, span]), none),
            jnp.where(here, low(frac_ref[line, span]), none),
        ]
        meta_ref[0, u] = lax.dot_general(
            jnp.concatenate([spots, spots], axis=1),
            jnp.concatenate(terms, axis=1),
            (((1,), (1,)), ((), ())),
            preferred_element_type=F32,
        )


def up_to(value, step):
    return -(-value // step) * step


def sort_sizes(orients, owners):
    slots = orients + 7 * owners
    sure = orients + 144
    blocks = up_to((sure + up_to(max(0, slots - sure), 128)) // 8, 8)
    return slots, sure, blocks


def planned(shape):
    return pl.BlockSpec((1,) + shape[1:], lambda i, here: (i,) + (0,) * (len(shape) - 1))


def plan_call(here, destination, groups, gb, mesh_sizes):
    orients = destination.shape[1]
    half = min(256, orients)
    owners = mesh_sizes[0] * mesh_sizes[1]
    steps, units = groups // 2 // gb, gb * (orients // half)
    slots, _, blocks = sort_sizes(half, owners)
    shapes = [
        (steps, units, half),
        (steps, units, up_to(blocks + 1, 128)),
        (steps, 5, up_to(owners + units * slots // RD + 8, 128)),
    ]
    return pl.pallas_call(
        functools.partial(plan_kernel, sizes=mesh_sizes, per=group_block(groups) // 2),
        grid_spec=pltpu.PrefetchScalarGridSpec(
            num_scalar_prefetch=1,
            grid=(steps,),
            in_specs=[
                pl.BlockSpec(
                    (groups, orients), lambda i, here: (lax.rem(here[0], mesh_sizes[1]), 0)
                )
            ],
            out_specs=[planned(shape) for shape in shapes],
            scratch_shapes=[
                pltpu.VMEM((groups, orients), jnp.int32),
                pltpu.VMEM((units * owners, half), BF16),
                pltpu.VMEM((units * owners, half), F32),
            ],
        ),
        out_shape=[jax.ShapeDtypeStruct(shape, jnp.int32) for shape in shapes],
        compiler_params=pltpu.CompilerParams(vmem_limit_bytes=55 * MB),
        cost_estimate=pl.CostEstimate(
            flops=8 * steps * units * owners * half * half,
            bytes_accessed=8 * groups * orients,
            transcendentals=0,
        ),
    )(here, destination)


def meta_call(here, row_index, fraction, pos, owners, slabs):
    steps, units, half = pos.shape
    orients = row_index.shape[1]
    groups = 2 * steps * units * half // orients
    blocks = sort_sizes(half, owners)[2]
    shape = (steps, units, blocks, OB)
    table = pl.BlockSpec((groups, orients), lambda i, here: (lax.rem(here[0], slabs), 0))
    return pl.pallas_call(
        functools.partial(meta_kernel, per=group_block(groups) // 2, slabs=slabs),
        grid_spec=pltpu.PrefetchScalarGridSpec(
            num_scalar_prefetch=1,
            grid=(steps,),
            in_specs=[table, table, planned(pos.shape)],
            out_specs=planned(shape),
        ),
        out_shape=jax.ShapeDtypeStruct(shape, F32),
        compiler_params=pltpu.CompilerParams(vmem_limit_bytes=16 * MB),
        cost_estimate=pl.CostEstimate(
            flops=8 * steps * units * blocks * half * OB,
            bytes_accessed=8 * steps * units * blocks * OB,
            transcendentals=0,
        ),
    )(here, row_index, fraction, pos)


def insert_kernel(
    addr_ref, item_ref, x_ref, y_ref, pos_ref, meta_ref, blk_ref, more_blk_ref, *rest
):
    post_ref, more_ref, send_ref, keep_ref = rest[:-8]
    post_t, slice_a, slice_b, buf_s, buf_m, volume, stage, sem = rest[-8:]
    step = pl.program_id(0)
    count = x_ref.shape[0]
    orients = post_t.shape[0]
    units, half = pos_ref.shape[1:]
    parts = orients // half
    gb = units // parts
    width = x_ref.shape[1] // gb
    share = post_ref.shape[1]
    lanes = addr_ref.shape[2]

    @pl.when(step == 0)
    def _():
        volume[...] = jnp.zeros_like(volume)
        for who, (lists, pieces) in enumerate(((blk_ref, post_ref), (more_blk_ref, more_ref))):
            for k in range(pieces.shape[0]):
                lanes = slice(k * share, (k + 1) * share)
                turned = pieces[k].astype(F32).T
                for b in range(orients // OB):
                    value = jnp.where(
                        lists[0:1, lanes] == b,
                        turned[:OB],
                        jnp.where(lists[1:2, lanes] == b, turned[OB:], 0.0),
                    )
                    at = slice(who * count + k * share, who * count + (k + 1) * share)
                    post_t[b * OB : (b + 1) * OB, at] = value.astype(BF16)

    tail = pl.ds(pl.multiple_of(item_ref[0, 4, 0] * 8, 8), RD)
    buf_s[tail, :] = jnp.zeros((RD, width), F32)
    one, none = jnp.bfloat16(1.0), jnp.bfloat16(0.0)
    slots, sure, _ = sort_sizes(half, volume.shape[0] // RD)
    per = slice_a.shape[1] // width
    number = gb // per

    def slices(q, dst_ref):
        at = pl.ds(pl.multiple_of(q * (per * width), per * width), per * width)
        images = jnp.concatenate([x_ref[:, at], y_ref[:, at]], axis=0)
        value = jnp.dot(post_t[...], images, preferred_element_type=F32)
        dst_ref[...] = value.astype(BF16)

    def emit(u, piece, base, size):
        pos = pos_ref[0, pl.ds(u, 1), :]
        order = []
        for at in range(0, size, 128):
            high = min(128, size - at)
            slot = lax.broadcasted_iota(jnp.int32, (high, half), 0).astype(F32).astype(BF16)
            near = jnp.clip(pos - (base + at), -1, 128).astype(F32).astype(BF16)
            order.append(jnp.where(slot == near, one, none))
        order = jnp.concatenate(order, axis=0)
        rows = jnp.dot(order, piece, preferred_element_type=F32)
        for i in range(size // 8):
            at = addr_ref[0, u, base // 8 + i]
            buf_s[pl.ds(pl.multiple_of(at * 8, 8), 8), :] = rows[8 * i : 8 * i + 8]
            buf_m[pl.ds(at, 1), :] = meta_ref[0, u, pl.ds(base // 8 + i, 1), :]

    def sort(q, src_ref):
        for g in range(per):
            for h in range(parts):
                piece = src_ref[h * half : (h + 1) * half, g * width : (g + 1) * width]
                emit((q * per + g) * parts + h, piece, 0, sure)

    def rest_of(q, src_ref):
        for g in range(per):
            for h in range(parts):
                u = (q * per + g) * parts + h

                def more(e, c, u=u, g=g, h=h):
                    piece = src_ref[h * half : (h + 1) * half, g * width : (g + 1) * width]
                    emit(u, piece, sure + e * 128, 128)
                    return c

                used = addr_ref[0, u, lanes - 1]
                lax.fori_loop(0, lax.div(jnp.maximum(used - sure, 0) + 127, 128), more, 0)

    def most_used(q):
        most = addr_ref[0, q * per * parts, lanes - 1]
        for u in range(1, per * parts):
            most = jnp.maximum(most, addr_ref[0, q * per * parts + u, lanes - 1])
        return most

    def two(j, carry):
        q = j * 2
        sort(q, slice_a)
        slices(q + 1, slice_b)

        @pl.when(most_used(q) > sure)
        def _():
            rest_of(q, slice_a)

        sort(q + 1, slice_b)
        slices(jnp.minimum(q + 2, number - 1), slice_a)

        @pl.when(most_used(q + 1) > sure)
        def _():
            rest_of(q + 1, slice_b)

        return carry

    slices(0, slice_a)
    lax.fori_loop(0, number // 2, two, 0)
    if number % 2:
        sort(number - 1, slice_a)
        rest_of(number - 1, slice_a)

    bins = lax.broadcasted_iota(jnp.int32, (RD, RD), 0).astype(F32).astype(BF16)
    side = RD // 2
    at_lane = lax.broadcasted_iota(jnp.int32, (side // 8, side), 1) // 8
    own_lane = at_lane == lax.broadcasted_iota(jnp.int32, (side // 8, side), 0)
    line = lax.broadcasted_iota(jnp.int32, (1, RD), 1)
    together = 8

    def some_items(q, carry):
        for u in range(together):
            j = q * together + u
            owner, at, left = item_ref[0, 0, j], item_ref[0, 1, j], item_ref[0, 2, j]
            places = [
                jnp.sum(
                    jnp.where(own_lane, buf_m[pl.ds(at + h * (side // 8), side // 8), :], 0.0),
                    axis=0,
                    keepdims=True,
                )
                for h in range(2)
            ]
            place = jnp.where(line < left, jnp.concatenate(places, axis=1), -9.0)
            whole = jnp.floor(place)
            apart = (bins - whole.astype(BF16)) - (place - whole).astype(BF16)
            weights = jnp.maximum(one - jnp.abs(apart), none)
            values = buf_s[pl.ds(pl.multiple_of(at * 8, 8), RD), :].astype(BF16)
            goal = pl.ds(pl.multiple_of(owner * RD, RD), RD)
            volume[goal, :] += jnp.dot(weights, values, preferred_element_type=F32)
        return carry

    count_items = lax.div(item_ref[0, 3, 0] + together - 1, together)
    lax.fori_loop(0, count_items, some_items, 0)

    @pl.when(step == pl.num_programs(0) - 1)
    def _():
        side_rows = keep_ref.shape[1]
        slots_out, _, tile, _ = stage.shape
        copies = []
        for base, out_ref in ((side_rows, send_ref), (0, keep_ref)):
            for at in range(0, side_rows, tile):
                slot = len(copies) % slots_out
                if len(copies) >= slots_out:
                    copies[len(copies) - slots_out].wait()
                value = volume[base + at : base + at + tile, :].astype(BF16)
                for c in range(2):
                    stage[slot, c] = value[:, c * OB : (c + 1) * OB]
                copy = pltpu.make_async_copy(
                    stage.at[slot], out_ref.at[:, pl.ds(at, tile)], sem.at[slot]
                )
                copy.start()
                copies.append(copy)
        for copy in copies[-slots_out:]:
            copy.wait()


def group_pair(gb):
    return 2 if gb % 2 == 0 else 1


def insert_block(groups, orients, owners, count, width):
    half = min(256, orients)
    slots, _, blocks = sort_sizes(half, owners)
    room = max(32 * MB - owners * RD * width * 4, 18 * MB)
    best = 1
    for gb in range(1, groups + 1):
        units = gb * (orients // half)
        rows = units * slots + RD + 8
        need = rows * (width * 4 + OB // 2) + 8 * count * gb * width + units * blocks * OB * 8
        if groups % gb == 0 and need <= room:
            best = gb
    return best


def insert_call(addr, items, flats, pos, meta, blocks, posts, orients, owners):
    count, length = flats[0].shape
    steps, units, half = pos.shape
    gb = units * half // orients
    width = length // (steps * gb)
    total = owners * RD
    rows = units * sort_sizes(half, owners)[0] + RD + 8
    limit = total * width * 4 // MB + 30
    block = lambda shape, **kw: pl.BlockSpec(
        (1,) + shape[1:], lambda i: (i,) + (0,) * (len(shape) - 1), **kw
    )
    return pl.pallas_call(
        insert_kernel,
        grid=(steps,),
        out_shape=[jax.ShapeDtypeStruct((2, total // 2, OB), BF16)] * 2,
        in_specs=[
            block(addr.shape, memory_space=pltpu.SMEM),
            block(items.shape, memory_space=pltpu.SMEM),
            pl.BlockSpec((count, gb * width), lambda i: (0, i)),
            pl.BlockSpec((count, gb * width), lambda i: (0, i)),
            block(pos.shape),
            block(meta.shape),
            pl.BlockSpec((2, count), lambda i: (0, 0)),
            pl.BlockSpec((2, count), lambda i: (0, 0)),
        ]
        + [pl.BlockSpec(posts[0].shape, lambda i: (0, 0, 0))] * 2,
        out_specs=[pl.BlockSpec(memory_space=pl.ANY)] * 2,
        scratch_shapes=[
            pltpu.VMEM((orients, 2 * count), BF16),
            pltpu.VMEM((orients, group_pair(gb) * width), BF16),
            pltpu.VMEM((orients, group_pair(gb) * width), BF16),
            pltpu.VMEM((rows, width), F32),
            pltpu.VMEM((rows // 8, OB), F32),
            pltpu.VMEM((total, width), F32),
            pltpu.VMEM((OUT_SLOTS, 2, OUT_TILE, OB), BF16),
            pltpu.SemaphoreType.DMA((OUT_SLOTS,)),
        ],
        compiler_params=pltpu.CompilerParams(vmem_limit_bytes=limit * MB),
        cost_estimate=pl.CostEstimate(
            flops=8 * count * orients * length,
            bytes_accessed=2 * count * length,
            transcendentals=0,
        ),
    )(addr, items, *flats, pos, meta, *blocks, *posts)


def flip(value, axis, bit):
    size = lax.axis_size(axis)
    return lax.ppermute(value, axis, [(i, i ^ bit) for i in range(size)])


def shards(particles, blocks, references, inv_noise, destination, row_index, fraction):
    groups, width = particles.shape[1:]
    orients = references.shape[0]
    dom_size = lax.axis_size("dom")
    slab_size = lax.axis_size("slab")
    devices = dom_size * slab_size
    dom_pos = lax.axis_index("dom")
    slab_pos = lax.axis_index("slab")
    here = lax.axis_index(("dom", "slab")).astype(jnp.int32).reshape(1)
    dom_bits = [1 << i for i in range((dom_size - 1).bit_length())]
    slab_bits = [1 << i for i in range((slab_size - 1).bit_length())]

    blocks = blocks.T
    kept, sent, *scores = score_call(here, inv_noise, particles, references, blocks, slab_size)
    gb = insert_block(groups // 2, orients, devices, particles.shape[0], width)
    here, own = lax.optimization_barrier((here, scores[0]))
    plan = plan_call(here, destination, groups, gb, (dom_size, slab_size))
    own, *plan = lax.optimization_barrier((own, *plan))
    pos, addr, items = plan
    parts = [own] + [flip(scores[k], "slab", k) for k in range(1, slab_size)]
    flats = [kept, flip(sent, "dom", dom_bits[0])]
    post = softmax_call(parts)
    more_blocks = flip(blocks, "dom", dom_bits[0])
    post, more_blocks, later = lax.optimization_barrier((post, more_blocks, here))
    meta = meta_call(later, row_index, fraction, pos, devices, slab_size)
    posts = [post] + [flip(post, "slab", k) for k in range(1, slab_size)]
    ordered = []
    for k in range(slab_size):
        value = posts[0]
        for j in range(1, slab_size):
            value = jnp.where(slab_pos ^ j == k, posts[j], value)
        ordered.append(value)
    pile, meta = lax.optimization_barrier((jnp.stack(ordered), meta))
    posts = [pile, flip(pile, "dom", dom_bits[0])]
    lists = [blocks, more_blocks]
    send, keep = insert_call(addr, items, flats, pos, meta, lists, posts, orients, devices)

    def added(terms):
        return functools.reduce(jnp.add, [term.astype(F32) for term in terms])

    def halve(terms, axis_name, axis, bit):
        size = terms[0].shape[axis] // 2
        pick = lambda term, at: lax.slice_in_dim(term, at, at + size, axis=axis)
        sent = added([pick(term, size) for term in terms]).astype(BF16)
        return [pick(term, 0) for term in terms] + [flip(sent, axis_name, bit)]

    terms = [keep, flip(send, "dom", dom_bits[0])]
    rest = dom_bits[1:]
    columns = []
    for part in range(2):
        columns.append(
            [term[part].reshape((2,) * len(rest) + (slab_size * RD, OB)) for term in terms]
        )
    for stage in range(len(rest)):
        for part in range(2):
            axis = stage if part == 0 else len(rest) - 1 - stage
            columns[part] = halve(columns[part], "dom", axis, rest[axis])
    terms = [jnp.stack([t.reshape(slab_size * RD, OB) for t in pair]) for pair in zip(*columns)]
    for bit in slab_bits:
        terms = halve(terms, "slab", 1, bit)
    volume = jnp.concatenate([added([term[part] for term in terms]) for part in range(2)], axis=1)

    own = volume.astype(BF16)
    plane = [own] + [flip(own, "dom", 2 * k) for k in range(1, dom_size // 2)]
    chip = dom_pos // 2
    placed = []
    for k in range(dom_size // 2):
        value = plane[0]
        for j in range(1, dom_size // 2):
            value = jnp.where(chip ^ j == k, plane[j], value)
        placed.append(value)
    value = jnp.stack(placed)
    got = flip(value, "dom", dom_bits[0])
    value = jnp.where(
        dom_pos & dom_bits[0] == 0,
        jnp.stack([value, got], 1),
        jnp.stack([got, value], 1),
    )
    return volume, value.reshape(dom_size * RD, width)


def solution(mesh):
    return jax.shard_map(
        shards,
        mesh=mesh,
        in_specs=(
            P("dom", "slab", None),
            P("dom", None),
            P(None, "slab", None),
            P("slab"),
            P(),
            P(),
            P(),
        ),
        out_specs=(P(("dom", "slab"), None), P(None, "slab")),
        check_vma=False,
    )
```

```python
import functools

import jax
import jax.numpy as jnp
from jax import lax
from jax.experimental import pallas as pl
from jax.experimental.pallas import tpu as pltpu
from jax.sharding import PartitionSpec as P

OB = 128
RD = 256
MB = 2**20
OUT_SLOTS = 4
STREAMS = 4
OUT_TILE = 1024
F32 = jnp.float32
BF16 = jnp.bfloat16


def group_block(groups):
    return 16 if groups % 16 == 0 else 8


def spread_columns(blk_ref, cols_ref):
    count = blk_ref.shape[1]
    for j in range(2):
        for at in range(0, count, OB):
            line = blk_ref[j : j + 1, at : at + OB].astype(F32)
            cols_ref[j, at : at + OB, :] = jnp.broadcast_to(line, (OB, OB)).T


def score_kernel(here_ref, noise_ref, blk_ref, *rest):
    x_refs, r_refs = rest[:STREAMS], rest[STREAMS : 2 * STREAMS]
    keep_ref, send_ref = rest[2 * STREAMS : 2 * STREAMS + 2]
    out_refs = rest[2 * STREAMS + 2 : -8]
    flat_a, flat_b, w_a, w_b, acc_ref, perm_ref, cols_ref, sem = rest[-8:]
    step = pl.program_id(0)
    steps = pl.num_programs(0) - 1
    gb, width = x_refs[0].shape[1:]
    particles, orients = acc_ref.shape
    side = 16 * gb
    per = gb // 2
    slabs = len(out_refs)
    core = lax.div(here_ref[0], slabs) & 1
    rounds = 2

    def copies(flat_ref, slot, at_step, swap):
        lanes = pl.ds(pl.multiple_of(at_step * (per * width), per * width), per * width)
        goals = (send_ref, keep_ref) if swap else (keep_ref, send_ref)
        return [
            pltpu.make_async_copy(flat_ref.at[h], goals[h].at[:, lanes], sem.at[slot, h])
            for h in range(2)
        ]

    def send_out(flat_ref, slot):
        for which in range(2):

            @pl.when(core == which)
            def _(which=which):
                for copy in copies(flat_ref, slot, step, which == 1):
                    copy.start()

    def wait_out(flat_ref, slot):
        for copy in copies(flat_ref, slot, 0, False):
            copy.wait()

    def regroup(jobs):
        wide = [ref[pl.ds(first * 16, 16)].reshape(side, width) for ref, first, *_ in jobs]
        moved = jnp.dot(perm_ref[...], jnp.concatenate(wide, axis=1), preferred_element_type=F32)
        for g in range(gb):
            lanes = slice(g % per * width, (g % per + 1) * width)
            for t, (_, first, base, goal_ref, scaled) in enumerate(jobs):
                part = moved[g * 16 : (g + 1) * 16, t * width : (t + 1) * width]
                if scaled:
                    part = part * noise_ref[step * gb + g]
                at = pl.ds(pl.multiple_of(base + first * 16, 16), 16)
                goal_ref[g // per, at, lanes] = part.astype(BF16)

    def turn(src_ref, first, base, goal_ref):
        turned = jnp.swapaxes(src_ref[pl.ds(first * 16, 16)], 0, 1)
        at = pl.ds(pl.multiple_of(base + first * 16, 16), 16)
        for g in range(gb):
            goal_ref[g // per, at, g % per * width : (g % per + 1) * width] = turned[g]

    def tiles(i, flat_ref, w_ref):
        jobs, turns = [], []
        for s in range(STREAMS):
            rows = orients // STREAMS
            for t in range(rows // 16 // rounds):
                jobs.append((r_refs[s], i * (rows // 16 // rounds) + t, s * rows, w_ref, True))
            rows = particles // STREAMS
            for t in range(rows // 16 // rounds):
                job = (x_refs[s], i * (rows // 16 // rounds) + t, s * rows, flat_ref)
                if (s * (rows // 16 // rounds) + t) % 4:
                    turns.append(job)
                else:
                    jobs.append(job + (False,))
        for at in range(0, len(jobs), 5):
            regroup(jobs[at : at + 5])
        for job in turns:
            turn(*job)

    def product(left, right):
        acc_ref[...] += lax.dot_general(
            left, right, (((1,), (1,)), ((), ())), preferred_element_type=F32
        )

    def both(i, flat_ref, w_ref, last_flat, last_w):
        span = 2 * per * width // rounds
        at = pl.ds(pl.multiple_of(lax.rem(i, rounds // 2) * span, span), span)
        h = lax.div(i, rounds // 2)
        product(last_flat[h, :, at], last_w[h, :, at])
        tiles(i, flat_ref, w_ref)

    def loop(body, *refs):
        lax.fori_loop(0, rounds, lambda i, c: (body(i, *refs), c)[1], 0)

    @pl.when(step == 0)
    def _():
        row = lax.broadcasted_iota(jnp.int32, (side, side), 0)
        col = lax.broadcasted_iota(jnp.int32, (side, side), 1)
        same = ((row // 16) == (col % gb)) & ((row % 16) == (col // gb))
        perm_ref[...] = jnp.where(same, 1.0, 0.0).astype(BF16)
        acc_ref[...] = jnp.zeros_like(acc_ref)
        spread_columns(blk_ref, cols_ref)
        loop(tiles, flat_a, w_a)
        send_out(flat_a, 0)

    inner = (step > 0) & (step < steps)

    @pl.when(inner & (lax.rem(step, 2) == 1))
    def _():
        @pl.when(step > 1)
        def _():
            wait_out(flat_b, 1)

        loop(both, flat_b, w_b, flat_a, w_a)
        send_out(flat_b, 1)

    @pl.when(inner & (lax.rem(step, 2) == 0))
    def _():
        wait_out(flat_a, 0)
        loop(both, flat_a, w_a, flat_b, w_b)
        send_out(flat_a, 0)

    def finish(last_flat, last_w):
        for h in range(2):
            product(last_flat[h], last_w[h])
        me = lax.rem(here_ref[0], slabs)
        share = particles // len(out_refs)
        for k, out_ref in enumerate(out_refs):
            at = pl.multiple_of((me ^ k) * share, share)
            for j in range(2):
                wanted = cols_ref[j, pl.ds(at, share), :]
                chosen = jnp.zeros((share, OB), F32)
                for b in range(orients // OB):
                    value = acc_ref[pl.ds(at, share), b * OB : (b + 1) * OB]
                    chosen = jnp.where(wanted == b, value, chosen)
                out_ref[:, j * OB : (j + 1) * OB] = chosen
        wait_out(flat_a, 0)

        @pl.when(steps > 1)
        def _():
            wait_out(flat_b, 1)

    @pl.when((step == steps) & (lax.rem(step, 2) == 1))
    def _():
        finish(flat_a, w_a)

    @pl.when((step == steps) & (lax.rem(step, 2) == 0))
    def _():
        finish(flat_b, w_b)


def score_call(here, inv_noise, particles, references, blocks, slab_size):
    count, groups, width = particles.shape
    orients = references.shape[0]
    gb = group_block(groups)
    side = 16 * gb
    share = count // slab_size
    smem = pl.BlockSpec(memory_space=pltpu.SMEM)
    steps = groups // gb
    return pl.pallas_call(
        score_kernel,
        grid=(steps + 1,),
        out_shape=[jax.ShapeDtypeStruct((count, groups // 2 * width), BF16)] * 2
        + [jax.ShapeDtypeStruct((share, 2 * OB), F32)] * slab_size,
        in_specs=[
            smem,
            smem,
            pl.BlockSpec((2, count), lambda i: (0, 0)),
        ]
        + [
            pl.BlockSpec(
                (rows // STREAMS, gb, width), lambda i, s=s: (s, jnp.minimum(i, steps - 1), 0)
            )
            for rows in (count, orients)
            for s in range(STREAMS)
        ],
        out_specs=[pl.BlockSpec(memory_space=pl.ANY)] * 2
        + [pl.BlockSpec((share, 2 * OB), lambda i: (0, 0))] * slab_size,
        scratch_shapes=[
            pltpu.VMEM((2, count, gb // 2 * width), BF16),
            pltpu.VMEM((2, count, gb // 2 * width), BF16),
            pltpu.VMEM((2, orients, gb // 2 * width), BF16),
            pltpu.VMEM((2, orients, gb // 2 * width), BF16),
            pltpu.VMEM((count, orients), F32),
            pltpu.VMEM((side, side), BF16),
            pltpu.VMEM((2, count, OB), F32),
            pltpu.SemaphoreType.DMA((2, 2)),
        ],
        compiler_params=pltpu.CompilerParams(vmem_limit_bytes=56 * MB),
        cost_estimate=pl.CostEstimate(
            flops=4 * count * orients * groups * width,
            bytes_accessed=6 * count * groups * width,
            transcendentals=0,
        ),
    )(here, inv_noise, blocks, *[particles] * STREAMS, *[references] * STREAMS)


def softmax_kernel(*refs):
    *parts, out_ref = refs
    total = parts[0][...]
    for part in parts[1:]:
        total = total + part[...]
    highest = jnp.max(total, axis=1, keepdims=True)
    weights = jnp.exp(total - highest)
    out_ref[...] = (weights / jnp.sum(weights, axis=1, keepdims=True)).astype(BF16)


def softmax_call(parts):
    return pl.pallas_call(
        softmax_kernel,
        out_shape=jax.ShapeDtypeStruct(parts[0].shape, BF16),
        compiler_params=pltpu.CompilerParams(vmem_limit_bytes=8 * MB),
    )(*parts)


def own_row(here_ref, local, per, slabs):
    core = lax.div(here_ref[0], slabs) & 1
    return lax.div(local, per) * (2 * per) + core * per + lax.rem(local, per)


def plan_kernel(
    here_ref, dest_ref, pos_ref, addr_ref, item_ref, place_ref, hot_ref, count_ref, *, sizes, per
):
    step = pl.program_id(0)
    dom_size, slab_size = sizes
    owners = dom_size * slab_size
    _, units, half = pos_ref.shape
    lanes = addr_ref.shape[2]
    parts = dest_ref.shape[1] // half
    gb = units // parts
    dom_log, slab_log = (dom_size - 1).bit_length(), (slab_size - 1).bit_length()

    @pl.when(step == 0)
    def _():
        off = dest_ref[...] ^ here_ref[0]
        place = jnp.zeros_like(off)
        for bit in list(range(slab_log, slab_log + dom_log)) + list(range(slab_log)):
            place = place * 2 + (lax.shift_right_logical(off, bit) & 1)
        place_ref[...] = place

    owner = lax.broadcasted_iota(jnp.int32, (owners, 1), 0)
    for u in range(units):
        g, h = u // parts, u % parts
        at = pl.ds(own_row(here_ref, step * gb + g, per, slab_size), 1)
        line = place_ref[at, h * half : (h + 1) * half]
        hot = jnp.where(line == owner, 1.0, 0.0)
        hot_ref[u * owners : (u + 1) * owners, :] = hot.astype(BF16)
    before = lax.broadcasted_iota(jnp.int32, (half, half), 0)
    after = lax.broadcasted_iota(jnp.int32, (half, half), 1)
    upto = jnp.where(before <= after, 1.0, 0.0).astype(BF16)
    count_ref[...] = jnp.dot(hot_ref[...], upto, preferred_element_type=F32)

    exact = functools.partial(
        jnp.dot, preferred_element_type=F32, precision=lax.Precision.HIGHEST
    )
    row = lax.broadcasted_iota(jnp.int32, (owners, owners), 0)
    col = lax.broadcasted_iota(jnp.int32, (owners, owners), 1)
    below = jnp.where(row > col, 1.0, 0.0)
    row = lax.broadcasted_iota(jnp.int32, (OB, OB), 0)
    col = lax.broadcasted_iota(jnp.int32, (OB, OB), 1)
    earlier = jnp.where(row < col, 1.0, 0.0)
    lane = lax.broadcasted_iota(jnp.int32, (owners, OB), 1)
    runs = jnp.zeros((owners, OB), F32)
    for u in range(units):
        size = count_ref[u * owners : (u + 1) * owners, half - 1 : half]
        runs = jnp.where(lane == u, size, runs)
    runs = jnp.floor((runs + 7.0) * 0.125) * 8.0
    base = exact(below, runs)
    ahead = exact(runs, earlier)
    total = jnp.sum(runs, axis=1, keepdims=True)
    start = exact(below, jnp.broadcast_to(total, (owners, OB)))[:, :1]
    blocks = jnp.floor((total + (RD - 1.0)) * (1.0 / RD))
    first = exact(below, jnp.broadcast_to(blocks, (owners, OB)))[:, :1]
    shift = start + ahead - base
    used = jnp.sum(runs, axis=0, keepdims=True)

    slot = (lax.broadcasted_iota(jnp.int32, (1, lanes), 1) * 8).astype(F32)
    is_last = lax.broadcasted_iota(jnp.int32, (1, lanes), 1) == lanes - 1
    rows = units * (half + 7 * owners)
    for u in range(units):
        low, size = base[:, u : u + 1], runs[:, u : u + 1]
        hot = hot_ref[u * owners : (u + 1) * owners, :].astype(F32)
        rank = count_ref[u * owners : (u + 1) * owners, :] + (low - 1.0)
        pos_ref[0, u : u + 1, :] = jnp.sum(hot * rank, axis=0, keepdims=True).astype(jnp.int32)
        inside = (slot >= low) & (slot < low + size)
        goal = jnp.where(inside, shift[:, u : u + 1] + slot - rows, 0.0)
        goal = (jnp.sum(goal, axis=0, keepdims=True) + rows) * 0.125
        addr_ref[0, u : u + 1, :] = jnp.where(is_last, used[:, u : u + 1], goal).astype(jnp.int32)

    wide = item_ref.shape[2]
    number = lax.broadcasted_iota(jnp.int32, (1, wide), 1).astype(F32)
    inside = (number >= first) & (number < first + blocks)
    done = (number - first) * RD
    pick = lambda value: jnp.sum(jnp.where(inside, value, 0.0), axis=0, keepdims=True)
    every = lambda value: jnp.sum(
        jnp.broadcast_to(value, (owners, wide)), axis=0, keepdims=True
    )
    lines = (
        pick(jnp.broadcast_to(owner.astype(F32), (owners, wide))),
        pick((start + done) * 0.125),
        pick(total - done),
        every(blocks),
        every(total * 0.125),
    )
    for i, value in enumerate(lines):
        item_ref[0, i : i + 1, :] = value.astype(jnp.int32)


def meta_kernel(here_ref, index_ref, frac_ref, pos_ref, meta_ref, *, per, slabs):
    step = pl.program_id(0)
    _, units, half = pos_ref.shape
    parts = index_ref.shape[1] // half
    gb = units // parts
    blocks = meta_ref.shape[2]
    low = lambda value: value.astype(F32).astype(BF16)
    eighth = low(lax.broadcasted_iota(jnp.int32, (blocks, half), 0))
    lane_of = low(lax.broadcasted_iota(jnp.int32, (OB, half), 0) % 8)
    one, none = jnp.bfloat16(1.0), jnp.bfloat16(0.0)
    for u in range(units):
        g, h = u // parts, u % parts
        line = pl.ds(own_row(here_ref, step * gb + g, per, slabs), 1)
        span = slice(h * half, (h + 1) * half)
        pos = pos_ref[0, u : u + 1, :]
        here = lane_of == low(pos & 7)
        spots = jnp.where(eighth == low(lax.shift_right_logical(pos, 3)), one, none)
        terms = [
            jnp.where(here, low(index_ref[line, span]), none),
            jnp.where(here, low(frac_ref[line, span]), none),
        ]
        meta_ref[0, u] = lax.dot_general(
            jnp.concatenate([spots, spots], axis=1),
            jnp.concatenate(terms, axis=1),
            (((1,), (1,)), ((), ())),
            preferred_element_type=F32,
        )


def up_to(value, step):
    return -(-value // step) * step


def sort_sizes(orients, owners):
    slots = orients + 7 * owners
    sure = orients + 144
    blocks = up_to((sure + up_to(max(0, slots - sure), 128)) // 8, 8)
    return slots, sure, blocks


def planned(shape):
    return pl.BlockSpec((1,) + shape[1:], lambda i, here: (i,) + (0,) * (len(shape) - 1))


def plan_call(here, destination, groups, gb, mesh_sizes):
    orients = destination.shape[1]
    half = min(256, orients)
    owners = mesh_sizes[0] * mesh_sizes[1]
    steps, units = groups // 2 // gb, gb * (orients // half)
    slots, _, blocks = sort_sizes(half, owners)
    shapes = [
        (steps, units, half),
        (steps, units, up_to(blocks + 1, 128)),
        (steps, 5, up_to(owners + units * slots // RD + 8, 128)),
    ]
    return pl.pallas_call(
        functools.partial(plan_kernel, sizes=mesh_sizes, per=group_block(groups) // 2),
        grid_spec=pltpu.PrefetchScalarGridSpec(
            num_scalar_prefetch=1,
            grid=(steps,),
            in_specs=[
                pl.BlockSpec(
                    (groups, orients), lambda i, here: (lax.rem(here[0], mesh_sizes[1]), 0)
                )
            ],
            out_specs=[planned(shape) for shape in shapes],
            scratch_shapes=[
                pltpu.VMEM((groups, orients), jnp.int32),
                pltpu.VMEM((units * owners, half), BF16),
                pltpu.VMEM((units * owners, half), F32),
            ],
        ),
        out_shape=[jax.ShapeDtypeStruct(shape, jnp.int32) for shape in shapes],
        compiler_params=pltpu.CompilerParams(vmem_limit_bytes=55 * MB),
        cost_estimate=pl.CostEstimate(
            flops=8 * steps * units * owners * half * half,
            bytes_accessed=8 * groups * orients,
            transcendentals=0,
        ),
    )(here, destination)


def meta_call(here, row_index, fraction, pos, owners, slabs):
    steps, units, half = pos.shape
    orients = row_index.shape[1]
    groups = 2 * steps * units * half // orients
    blocks = sort_sizes(half, owners)[2]
    shape = (steps, units, blocks, OB)
    table = pl.BlockSpec((groups, orients), lambda i, here: (lax.rem(here[0], slabs), 0))
    return pl.pallas_call(
        functools.partial(meta_kernel, per=group_block(groups) // 2, slabs=slabs),
        grid_spec=pltpu.PrefetchScalarGridSpec(
            num_scalar_prefetch=1,
            grid=(steps,),
            in_specs=[table, table, planned(pos.shape)],
            out_specs=planned(shape),
        ),
        out_shape=jax.ShapeDtypeStruct(shape, F32),
        compiler_params=pltpu.CompilerParams(vmem_limit_bytes=16 * MB),
        cost_estimate=pl.CostEstimate(
            flops=8 * steps * units * blocks * half * OB,
            bytes_accessed=8 * steps * units * blocks * OB,
            transcendentals=0,
        ),
    )(here, row_index, fraction, pos)


def insert_kernel(
    addr_ref, item_ref, x_ref, y_ref, pos_ref, meta_ref, blk_ref, more_blk_ref, *rest
):
    post_ref, more_ref, send_ref, keep_ref = rest[:-8]
    post_t, slice_a, slice_b, buf_s, buf_m, volume, stage, sem = rest[-8:]
    step = pl.program_id(0)
    count = x_ref.shape[0]
    orients = post_t.shape[0]
    units, half = pos_ref.shape[1:]
    parts = orients // half
    gb = units // parts
    width = x_ref.shape[1] // gb
    share = post_ref.shape[1]
    lanes = addr_ref.shape[2]

    @pl.when(step == 0)
    def _():
        volume[...] = jnp.zeros_like(volume)
        for who, (lists, pieces) in enumerate(((blk_ref, post_ref), (more_blk_ref, more_ref))):
            for k in range(pieces.shape[0]):
                lanes = slice(k * share, (k + 1) * share)
                turned = pieces[k].astype(F32).T
                for b in range(orients // OB):
                    value = jnp.where(
                        lists[0:1, lanes] == b,
                        turned[:OB],
                        jnp.where(lists[1:2, lanes] == b, turned[OB:], 0.0),
                    )
                    at = slice(who * count + k * share, who * count + (k + 1) * share)
                    post_t[b * OB : (b + 1) * OB, at] = value.astype(BF16)

    tail = pl.ds(pl.multiple_of(item_ref[0, 4, 0] * 8, 8), RD)
    buf_s[tail, :] = jnp.zeros((RD, width), F32)
    one, none = jnp.bfloat16(1.0), jnp.bfloat16(0.0)
    slots, sure, _ = sort_sizes(half, volume.shape[0] // RD)
    per = slice_a.shape[1] // width
    number = gb // per

    def slices(q, dst_ref):
        at = pl.ds(pl.multiple_of(q * (per * width), per * width), per * width)
        images = jnp.concatenate([x_ref[:, at], y_ref[:, at]], axis=0)
        value = jnp.dot(post_t[...], images, preferred_element_type=F32)
        dst_ref[...] = value.astype(BF16)

    def emit(u, piece, base, size):
        pos = pos_ref[0, pl.ds(u, 1), :]
        order = []
        for at in range(0, size, 128):
            high = min(128, size - at)
            slot = lax.broadcasted_iota(jnp.int32, (high, half), 0).astype(F32).astype(BF16)
            near = jnp.clip(pos - (base + at), -1, 128).astype(F32).astype(BF16)
            order.append(jnp.where(slot == near, one, none))
        order = jnp.concatenate(order, axis=0)
        rows = jnp.dot(order, piece, preferred_element_type=F32)
        for i in range(size // 8):
            at = addr_ref[0, u, base // 8 + i]
            buf_s[pl.ds(pl.multiple_of(at * 8, 8), 8), :] = rows[8 * i : 8 * i + 8]
            buf_m[pl.ds(at, 1), :] = meta_ref[0, u, pl.ds(base // 8 + i, 1), :]

    def sort(q, src_ref):
        for g in range(per):
            for h in range(parts):
                piece = src_ref[h * half : (h + 1) * half, g * width : (g + 1) * width]
                emit((q * per + g) * parts + h, piece, 0, sure)

    def rest_of(q, src_ref):
        for g in range(per):
            for h in range(parts):
                u = (q * per + g) * parts + h

                def more(e, c, u=u, g=g, h=h):
                    piece = src_ref[h * half : (h + 1) * half, g * width : (g + 1) * width]
                    emit(u, piece, sure + e * 128, 128)
                    return c

                used = addr_ref[0, u, lanes - 1]
                lax.fori_loop(0, lax.div(jnp.maximum(used - sure, 0) + 127, 128), more, 0)

    def most_used(q):
        most = addr_ref[0, q * per * parts, lanes - 1]
        for u in range(1, per * parts):
            most = jnp.maximum(most, addr_ref[0, q * per * parts + u, lanes - 1])
        return most

    def two(j, carry):
        q = j * 2
        sort(q, slice_a)
        slices(q + 1, slice_b)

        @pl.when(most_used(q) > sure)
        def _():
            rest_of(q, slice_a)

        sort(q + 1, slice_b)
        slices(jnp.minimum(q + 2, number - 1), slice_a)

        @pl.when(most_used(q + 1) > sure)
        def _():
            rest_of(q + 1, slice_b)

        return carry

    slices(0, slice_a)
    lax.fori_loop(0, number // 2, two, 0)
    if number % 2:
        sort(number - 1, slice_a)
        rest_of(number - 1, slice_a)

    bins = lax.broadcasted_iota(jnp.int32, (RD, RD), 0).astype(F32).astype(BF16)
    side = RD // 2
    at_lane = lax.broadcasted_iota(jnp.int32, (side // 8, side), 1) // 8
    own_lane = at_lane == lax.broadcasted_iota(jnp.int32, (side // 8, side), 0)
    line = lax.broadcasted_iota(jnp.int32, (1, RD), 1)
    together = 8

    def some_items(q, carry):
        for u in range(together):
            j = q * together + u
            owner, at, left = item_ref[0, 0, j], item_ref[0, 1, j], item_ref[0, 2, j]
            places = [
                jnp.sum(
                    jnp.where(own_lane, buf_m[pl.ds(at + h * (side // 8), side // 8), :], 0.0),
                    axis=0,
                    keepdims=True,
                )
                for h in range(2)
            ]
            place = jnp.where(line < left, jnp.concatenate(places, axis=1), -9.0)
            whole = jnp.floor(place)
            apart = (bins - whole.astype(BF16)) - (place - whole).astype(BF16)
            weights = jnp.maximum(one - jnp.abs(apart), none)
            values = buf_s[pl.ds(pl.multiple_of(at * 8, 8), RD), :].astype(BF16)
            goal = pl.ds(pl.multiple_of(owner * RD, RD), RD)
            volume[goal, :] += jnp.dot(weights, values, preferred_element_type=F32)
        return carry

    count_items = lax.div(item_ref[0, 3, 0] + together - 1, together)
    lax.fori_loop(0, count_items, some_items, 0)

    @pl.when(step == pl.num_programs(0) - 1)
    def _():
        side_rows = keep_ref.shape[1]
        slots_out, _, tile, _ = stage.shape
        copies = []
        for base, out_ref in ((side_rows, send_ref), (0, keep_ref)):
            for at in range(0, side_rows, tile):
                slot = len(copies) % slots_out
                if len(copies) >= slots_out:
                    copies[len(copies) - slots_out].wait()
                value = volume[base + at : base + at + tile, :].astype(BF16)
                for c in range(2):
                    stage[slot, c] = value[:, c * OB : (c + 1) * OB]
                copy = pltpu.make_async_copy(
                    stage.at[slot], out_ref.at[:, pl.ds(at, tile)], sem.at[slot]
                )
                copy.start()
                copies.append(copy)
        for copy in copies[-slots_out:]:
            copy.wait()


def group_pair(gb):
    return 2 if gb % 2 == 0 else 1


def insert_block(groups, orients, owners, count, width):
    half = min(256, orients)
    slots, _, blocks = sort_sizes(half, owners)
    room = max(32 * MB - owners * RD * width * 4, 18 * MB)
    best = 1
    for gb in range(1, groups + 1):
        units = gb * (orients // half)
        rows = units * slots + RD + 8
        need = rows * (width * 4 + OB // 2) + 8 * count * gb * width + units * blocks * OB * 8
        if groups % gb == 0 and need <= room:
            best = gb
    return best


def insert_call(addr, items, flats, pos, meta, blocks, posts, orients, owners):
    count, length = flats[0].shape
    steps, units, half = pos.shape
    gb = units * half // orients
    width = length // (steps * gb)
    total = owners * RD
    rows = units * sort_sizes(half, owners)[0] + RD + 8
    limit = total * width * 4 // MB + 30
    block = lambda shape, **kw: pl.BlockSpec(
        (1,) + shape[1:], lambda i: (i,) + (0,) * (len(shape) - 1), **kw
    )
    return pl.pallas_call(
        insert_kernel,
        grid=(steps,),
        out_shape=[jax.ShapeDtypeStruct((2, total // 2, OB), BF16)] * 2,
        in_specs=[
            block(addr.shape, memory_space=pltpu.SMEM),
            block(items.shape, memory_space=pltpu.SMEM),
            pl.BlockSpec((count, gb * width), lambda i: (0, i)),
            pl.BlockSpec((count, gb * width), lambda i: (0, i)),
            block(pos.shape),
            block(meta.shape),
            pl.BlockSpec((2, count), lambda i: (0, 0)),
            pl.BlockSpec((2, count), lambda i: (0, 0)),
        ]
        + [pl.BlockSpec(posts[0].shape, lambda i: (0, 0, 0))] * 2,
        out_specs=[pl.BlockSpec(memory_space=pl.ANY)] * 2,
        scratch_shapes=[
            pltpu.VMEM((orients, 2 * count), BF16),
            pltpu.VMEM((orients, group_pair(gb) * width), BF16),
            pltpu.VMEM((orients, group_pair(gb) * width), BF16),
            pltpu.VMEM((rows, width), F32),
            pltpu.VMEM((rows // 8, OB), F32),
            pltpu.VMEM((total, width), F32),
            pltpu.VMEM((OUT_SLOTS, 2, OUT_TILE, OB), BF16),
            pltpu.SemaphoreType.DMA((OUT_SLOTS,)),
        ],
        compiler_params=pltpu.CompilerParams(vmem_limit_bytes=limit * MB),
        cost_estimate=pl.CostEstimate(
            flops=8 * count * orients * length,
            bytes_accessed=2 * count * length,
            transcendentals=0,
        ),
    )(addr, items, *flats, pos, meta, *blocks, *posts)


def flip(value, axis, bit):
    size = lax.axis_size(axis)
    return lax.ppermute(value, axis, [(i, i ^ bit) for i in range(size)])


def shards(particles, blocks, references, inv_noise, destination, row_index, fraction):
    groups, width = particles.shape[1:]
    orients = references.shape[0]
    dom_size = lax.axis_size("dom")
    slab_size = lax.axis_size("slab")
    devices = dom_size * slab_size
    dom_pos = lax.axis_index("dom")
    slab_pos = lax.axis_index("slab")
    here = lax.axis_index(("dom", "slab")).astype(jnp.int32).reshape(1)
    dom_bits = [1 << i for i in range((dom_size - 1).bit_length())]
    slab_bits = [1 << i for i in range((slab_size - 1).bit_length())]

    blocks = blocks.T
    kept, sent, *scores = score_call(here, inv_noise, particles, references, blocks, slab_size)
    gb = insert_block(groups // 2, orients, devices, particles.shape[0], width)
    here, own = lax.optimization_barrier((here, scores[0]))
    plan = plan_call(here, destination, groups, gb, (dom_size, slab_size))
    own, *plan = lax.optimization_barrier((own, *plan))
    pos, addr, items = plan
    parts = [own] + [flip(scores[k], "slab", k) for k in range(1, slab_size)]
    flats = [kept, flip(sent, "dom", dom_bits[0])]
    post = softmax_call(parts)
    more_blocks = flip(blocks, "dom", dom_bits[0])
    post, more_blocks, later = lax.optimization_barrier((post, more_blocks, here))
    meta = meta_call(later, row_index, fraction, pos, devices, slab_size)
    posts = [post] + [flip(post, "slab", k) for k in range(1, slab_size)]
    ordered = []
    for k in range(slab_size):
        value = posts[0]
        for j in range(1, slab_size):
            value = jnp.where(slab_pos ^ j == k, posts[j], value)
        ordered.append(value)
    pile, meta = lax.optimization_barrier((jnp.stack(ordered), meta))
    posts = [pile, flip(pile, "dom", dom_bits[0])]
    lists = [blocks, more_blocks]
    send, keep = insert_call(addr, items, flats, pos, meta, lists, posts, orients, devices)

    def added(terms):
        return functools.reduce(jnp.add, [term.astype(F32) for term in terms])

    def halve(terms, axis_name, axis, bit):
        size = terms[0].shape[axis] // 2
        pick = lambda term, at: lax.slice_in_dim(term, at, at + size, axis=axis)
        sent = added([pick(term, size) for term in terms]).astype(BF16)
        return [pick(term, 0) for term in terms] + [flip(sent, axis_name, bit)]

    terms = [keep, flip(send, "dom", dom_bits[0])]
    rest = dom_bits[1:]
    columns = []
    for part in range(2):
        columns.append(
            [term[part].reshape((2,) * len(rest) + (slab_size * RD, OB)) for term in terms]
        )
    for stage in range(len(rest)):
        for part in range(2):
            axis = stage if part == 0 else len(rest) - 1 - stage
            columns[part] = halve(columns[part], "dom", axis, rest[axis])
    terms = [jnp.stack([t.reshape(slab_size * RD, OB) for t in pair]) for pair in zip(*columns)]
    for bit in slab_bits:
        terms = halve(terms, "slab", 1, bit)
    volume = jnp.concatenate([added([term[part] for term in terms]) for part in range(2)], axis=1)

    own = volume.astype(BF16)
    plane = [own] + [flip(own, "dom", 2 * k) for k in range(1, dom_size // 2)]
    chip = dom_pos // 2
    placed = []
    for k in range(dom_size // 2):
        value = plane[0]
        for j in range(1, dom_size // 2):
            value = jnp.where(chip ^ j == k, plane[j], value)
        placed.append(value)
    value = jnp.stack(placed)
    got = flip(value, "dom", dom_bits[0])
    value = jnp.where(
        dom_pos & dom_bits[0] == 0,
        jnp.stack([value, got], 1),
        jnp.stack([got, value], 1),
    )
    return volume, value.reshape(dom_size * RD, width)


def solution(mesh):
    return jax.shard_map(
        shards,
        mesh=mesh,
        in_specs=(
            P("dom", "slab", None),
            P("dom", None),
            P(None, "slab", None),
            P("slab"),
            P(),
            P(),
            P(),
        ),
        out_specs=(P(("dom", "slab"), None), P(None, "slab")),
        check_vma=False,
    )
```
